32 devices in a mesh: fsdp: 8 (over y, x, core), rep: 4 (over z).
Axes of the slice: x: 2, y: 2, z: 4, core: 2. Of those that a mesh axis runs over, the one named last changes fastest.
Arguments:
- images: bfloat16 [160, 197, 768], P(('fsdp', 'rep')), may hold values from -6 to 6
- cotangent: bfloat16 [160, 197, 768], P(('fsdp', 'rep')), may hold values from -6 to 6
- weight_in: float32 [2, 768, 5376], P(None, 'fsdp'), may hold values from -0.21875 to 0.21875
- weight_out: float32 [2, 3840, 768], P(None, 'fsdp'), may hold values from -0.3125 to 0.3125
- vector_params: float32 [2, 9216], P(None, 'fsdp'), may hold values from 0.5 to 1.5
- first_in: float32 [2, 768, 5376], P(None, 'fsdp'), may hold values from -56 to 56
- first_out: float32 [2, 3840, 768], P(None, 'fsdp'), may hold values from -56 to 56
- first_vec: float32 [2, 9216], P(None, 'fsdp'), may hold values from -56 to 56
- second_in: float32 [2, 768, 5376], P(None, 'fsdp'), may hold values from 3.152 to 12.608
- second_out: float32 [2, 3840, 768], P(None, 'fsdp'), may hold values from 3.152 to 12.608
- second_vec: float32 [2, 9216], P(None, 'fsdp'), may hold values from 3.152 to 12.608
Outputs:
- encoded: bfloat16 [160, 197, 768], P(('fsdp', 'rep'))
- image_grad: float32 [160, 197, 768], P(('fsdp', 'rep'))
- grad_in: float32 [2, 768, 5376], P(None, 'fsdp')
- grad_out: float32 [2, 3840, 768], P(None, 'fsdp')
- grad_vec: float32 [2, 9216], P(None, 'fsdp')
- new_in: float32 [2, 768, 5376], P(None, 'fsdp')
- new_out: float32 [2, 3840, 768], P(None, 'fsdp')
- new_vec: float32 [2, 9216], P(None, 'fsdp')
- moment_in: float32 [2, 768, 5376], P(None, 'fsdp')
- moment_out: float32 [2, 3840, 768], P(None, 'fsdp')
- moment_vec: float32 [2, 9216], P(None, 'fsdp')
- square_in: float32 [2, 768, 5376], P(None, 'fsdp')
- square_out: float32 [2, 3840, 768], P(None, 'fsdp')
- square_vec: float32 [2, 9216], P(None, 'fsdp')
The draws below stay inside these ranges and needn't reach their ends.
All inputs are finite; a program needn't handle non-finite values.
Results may differ from the reference program's by a relative error of at most 0.013.
The reference program's roundings to bfloat16 on the way count: a program that leaves them out, or rounds other values in their place, can miss the bound.
Values may be sent and summed in bfloat16 or wider, within the bound.
A program may use at most 320 MiB of HBM per device.

```python
import math
import jax
import jax.numpy as jnp
from jax import lax

D = 768
HEADS = 12
HEAD_DIM = 64
FF = 3072
SEQ = 197
LAYERS = 2
STEP = 3
IMG_DEV = 5
IMAGES = 160
N_REP = 4


def steps_of(rng, shape, pieces, smallest, largest):
    def one(dim, blocks):
        steps = jax.random.uniform(jax.random.fold_in(jax.random.fold_in(rng, 6), dim), (blocks,), jnp.float32, smallest / len(pieces), largest / len(pieces))
        return jnp.repeat(jnp.exp(steps), shape[dim] // blocks).reshape((-1,) + (1,) * (len(shape) - dim - 1))

    level = one(*pieces[0])
    for cut in pieces[1:]:
        level = level * one(*cut)
    return level


def noise(stream_key, dims, deviation, reach, split=(), dtype=jnp.bfloat16):
    array = jax.random.normal(stream_key, dims, jnp.float32) * deviation
    if len(split) > 0:
        array = steps_of(stream_key, dims, split, -0.22, 0.18) * array
    return jnp.clip(array, min=-reach, max=reach).astype(dtype)


def setup_inputs(seed: int = 0) -> dict:
    key_list = jax.random.split(jax.random.key(seed), 12)
    images = noise(key_list[0], (IMAGES, SEQ, D), 1.0, 6.0, ((0, 32),))
    cotangent = noise(key_list[1], (IMAGES, SEQ, D), 1.0, 6.0, ((0, 32),))
    weight_in = noise(key_list[2], (LAYERS, D, 3 * D + FF), D ** -0.5, 0.21875, ((1, 8),), jnp.float32)
    weight_out = noise(key_list[3], (LAYERS, D + FF, D), (D // 2) ** -0.5, 0.3125, ((1, 8),), jnp.float32)
    vector_params = jnp.clip(0.5 + 1.0 * jax.random.uniform(key_list[4], (LAYERS, 8 * D + FF), jnp.float32) ** steps_of(key_list[4], (LAYERS, 8 * D + FF), ((1, 8),), -0.2, 0.2), 0.5, 1.5)
    first_in = noise(key_list[5], (LAYERS, D, 3 * D + FF), (0.05 * (IMAGES * SEQ) ** 0.5), 56.0, ((1, 8),), jnp.float32)
    first_out = noise(key_list[6], (LAYERS, D + FF, D), (0.05 * (IMAGES * SEQ) ** 0.5), 56.0, ((1, 8),), jnp.float32)
    first_vec = noise(key_list[7], (LAYERS, 8 * D + FF), (0.05 * (IMAGES * SEQ) ** 0.5), 56.0, ((1, 8),), jnp.float32)
    second_in = jnp.clip(jnp.exp(math.log(12.608) - 1.3862944 * jax.random.uniform(key_list[8], (LAYERS, D, 3 * D + FF), jnp.float32) ** steps_of(key_list[8], (LAYERS, D, 3 * D + FF), ((1, 8),), -0.2, 0.2)), 3.152, 12.608)
    second_out = jnp.clip(jnp.exp(math.log(12.608) - 1.3862944 * jax.random.uniform(key_list[9], (LAYERS, D + FF, D), jnp.float32) ** steps_of(key_list[9], (LAYERS, D + FF, D), ((1, 8),), -0.2, 0.2)), 3.152, 12.608)
    second_vec = jnp.clip(jnp.exp(math.log(12.608) - 1.3862944 * jax.random.uniform(key_list[10], (LAYERS, 8 * D + FF), jnp.float32) ** steps_of(key_list[10], (LAYERS, 8 * D + FF), ((1, 8),), -0.2, 0.2)), 3.152, 12.608)
    return {"images": images, "cotangent": cotangent, "weight_in": weight_in, "weight_out": weight_out, "vector_params": vector_params, "first_in": first_in, "first_out": first_out, "first_vec": first_vec, "second_in": second_in, "second_out": second_out, "second_vec": second_vec}


@jax.custom_vjp
def low(v):
    return lax.optimization_barrier(v.astype(jnp.bfloat16)).astype(jnp.float32)

@jax.custom_vjp
def low_back(v):
    return v

def low_keep(v):
    return (low(v), None)

def low_pass(kept, grad):
    return (grad,)

def back_keep(v):
    return (v, None)

def back_low(kept, grad):
    return (low(grad),)
low.defvjp(low_keep, low_pass)
low_back.defvjp(back_keep, back_low)
norm_eps = 1e-06
beta_one = 0.9
beta_two = 0.999
matrix_rate = 0.03
vector_rate = 0.2
matrix_decay = 0.05
adam_eps = 1e-08
highest = lax.Precision.HIGHEST

def layer_norm(hidden, gain_row, shift_row):
    average = lax.optimization_barrier(jnp.mean(hidden, axis=-1, keepdims=True))
    centred = hidden - average
    spread = lax.optimization_barrier(jnp.mean(centred * centred, axis=-1, keepdims=True))
    return centred * lax.rsqrt(spread + norm_eps) * gain_row + shift_row

def heads_view(matrix_a):
    return matrix_a.reshape(-1, SEQ, HEADS, HEAD_DIM)

def ref_layer(hidden, in_weight, out_weight, vec_weight):
    row_list = [vec_weight[slot_index * D:(slot_index + 1) * D] for slot_index in range(8)]
    ff_bias = vec_weight[8 * D:]
    normed = low(layer_norm(hidden, row_list[0], row_list[1]))
    mixed = low_back(jnp.dot(normed, in_weight[:, :3 * D], precision=highest))
    queries = low(mixed[:, :D] + row_list[2])
    key_rows = low(mixed[:, D:2 * D])
    values = low(mixed[:, 2 * D:] + row_list[3])
    score_scale = HEAD_DIM ** (-0.5)
    scores = low_back(jnp.einsum('bqhd,bkhd->bhqk', heads_view(queries), heads_view(key_rows), precision=highest) * score_scale)
    soft_weights = low(jax.nn.softmax(scores, axis=-1))
    attended = jnp.einsum('bhqk,bkhd->bqhd', soft_weights, heads_view(values), precision=highest)
    attended = low(low_back(attended.reshape(-1, D)))
    inner = hidden + low_back(jnp.dot(attended, out_weight[:D], precision=highest)) + row_list[4]
    normed_two = low(layer_norm(inner, row_list[5], row_list[6]))
    pre_act = low_back(jnp.dot(normed_two, in_weight[:, 3 * D:], precision=highest)) + ff_bias
    activated = low(jax.nn.gelu(pre_act, approximate=False))
    return inner + low_back(jnp.dot(activated, out_weight[D:], precision=highest)) + row_list[7]

def adam_update(master, gradient, moment_one, moment_two, rate, decay_rate):
    moment_one = beta_one * moment_one + (1.0 - beta_one) * gradient
    moment_two = beta_two * moment_two + (1.0 - beta_two) * gradient * gradient
    corr_one = 1.0 - beta_one ** STEP
    corr_two = 1.0 - beta_two ** STEP
    adam_move = moment_one / corr_one / (jnp.sqrt(moment_two / corr_two) + adam_eps)
    return (master - rate * (adam_move + decay_rate * master), moment_one, moment_two)

def reference(images, cotangent, weight_in, weight_out, vector_params, first_in, first_out, first_vec, second_in, second_out, second_vec):

    def forward(tokens_all, master_in, master_out, master_vec):
        in_low = low(master_in)
        out_low = low(master_out)
        vec_low = low(master_vec)
        group_rows = IMG_DEV * N_REP * SEQ
        blocks = tokens_all.reshape(-1, group_rows, D)

        def run_block(block):
            hidden = block
            for depth_index in range(LAYERS):
                hidden = ref_layer(hidden, in_low[depth_index], out_low[depth_index], vec_low[depth_index])
            return hidden
        result = lax.map(jax.checkpoint(run_block), blocks)
        return result.reshape(tokens_all.shape)
    tokens_all = images.astype(jnp.float32)
    result, back_fn = jax.vjp(forward, tokens_all, weight_in, weight_out, vector_params)
    image_grad, grad_in, grad_out, grad_vec = back_fn(cotangent.astype(jnp.float32))
    new_in, moment_in, square_in = adam_update(weight_in, grad_in, first_in, second_in, matrix_rate, matrix_decay)
    new_out, moment_out, square_out = adam_update(weight_out, grad_out, first_out, second_out, matrix_rate, matrix_decay)
    new_vec, moment_vec, square_vec = adam_update(vector_params, grad_vec, first_vec, second_vec, vector_rate, 0.0)
    return (result.astype(jnp.bfloat16), image_grad, grad_in, grad_out, grad_vec, new_in, new_out, new_vec, moment_in, moment_out, moment_vec, square_in, square_out, square_vec)
```

```python
import functools
import jax, jax.numpy as jnp
from jax import lax
from jax.experimental import pallas as pl
from jax.experimental.pallas import tpu as pltpu
from jax.sharding import PartitionSpec as P

D=768; HD=64; SEQ=197; RP=208; EPS=1e-6
BF=jnp.bfloat16; F32=jnp.float32
def dot(a,b): return jnp.dot(a,b,preferred_element_type=F32)
def dot_t(a,b): return lax.dot_general(a,b,(((1,),(1,)),((),())),preferred_element_type=F32)
def dot_0(a,b): return lax.dot_general(a,b,(((0,),(0,)),((),())),preferred_element_type=F32)

def norm_stats(x):
    mean=jnp.mean(x,axis=-1,keepdims=True); xc=x-mean
    var=jnp.mean(xc*xc,axis=-1,keepdims=True)
    return xc, lax.rsqrt(var+EPS)

def attn_fwd(q,k,v):
    lane=lax.broadcasted_iota(jnp.int32,(1,128),1)
    col=lax.broadcasted_iota(jnp.int32,(1,RP),1)
    os=[]
    for half in range(2):
        m=jnp.where((lane<64) if half==0 else (lane>=64),0.125,0.0).astype(BF)
        s=dot_t(q*m,k)
        s=jnp.where(col<SEQ,s,-1e30)
        mx=jnp.max(s,axis=-1,keepdims=True)
        e=jnp.exp(s-mx)
        p=(e*(1.0/jnp.sum(e,axis=-1,keepdims=True))).astype(BF)
        os.append(dot(p,v))
    return jnp.where(lane<64,os[0],os[1]).astype(BF)

def attn_bwd(q,k,v,do):
    lane=lax.broadcasted_iota(jnp.int32,(1,128),1)
    row=lax.broadcasted_iota(jnp.int32,(RP,1),0)
    r=[]
    for half in range(2):
        sel=(lane<64) if half==0 else (lane>=64)
        m=jnp.where(sel,0.125,0.0).astype(BF)
        m1=jnp.where(sel,1.0,0.0).astype(BF)
        qs=q*m
        s=dot_t(k,qs)
        s=jnp.where(row<SEQ,s,-1e30)
        mx=jnp.max(s,axis=0,keepdims=True)
        e=jnp.exp(s-mx)
        p=e*(1.0/jnp.sum(e,axis=0,keepdims=True))
        pb=p.astype(BF)
        dp=dot_t(v,do*m1)
        dl=jnp.sum(p*dp,axis=0,keepdims=True)
        ds=(p*(dp-dl)).astype(BF)
        dv=dot(pb,do)
        dk=dot(ds,qs)
        dq=dot_0(ds,k)*0.125
        r.append((dq,dk,dv))
    return tuple(jnp.where(lane<64,a,b) for a,b in zip(*r))

def ka_kernel(h_ref,w_ref,vec_ref,qkv_ref,o_ref,a_ref):
    h=h_ref[0].astype(F32)
    xc,rs=norm_stats(h)
    a_ref[0]=(xc*rs*vec_ref[0:1]+vec_ref[1:2]).astype(BF)
    a=a_ref[0]
    for c in range(3):
        cs=slice(256*c,256*c+256)
        qkv_ref[0,:,256*c:256*c+256]=(dot(a,w_ref[:,256*c:256*c+256])+vec_ref[2:3,cs]).astype(BF)
        qkv_ref[0,:,D+256*c:D+256*c+256]=dot(a,w_ref[:,D+256*c:D+256*c+256]).astype(BF)
        qkv_ref[0,:,2*D+256*c:2*D+256*c+256]=(dot(a,w_ref[:,2*D+256*c:2*D+256*c+256])+vec_ref[3:4,cs]).astype(BF)
        for p in range(2):
            b=256*c+128*p
            o_ref[0,:,b:b+128]=attn_fwd(qkv_ref[0,:,b:b+128],qkv_ref[0,:,D+b:D+b+128],qkv_ref[0,:,2*D+b:2*D+b+128])

def img(n,dt=None): return pl.BlockSpec((1,RP,n),lambda i:(i,0,0))
def full(shape): return pl.BlockSpec(shape,lambda i:(0,)*len(shape))
PAR=pltpu.CompilerParams(vmem_limit_bytes=60*2**20)

def ka(h,w,vec):
    n=h.shape[0]
    return pl.pallas_call(ka_kernel,grid=(n,),in_specs=[img(D),full(w.shape),full(vec.shape)],
        out_specs=[img(3*D),img(D),img(D)],
        out_shape=[jax.ShapeDtypeStruct((n,RP,3*D),BF),jax.ShapeDtypeStruct((n,RP,D),BF),jax.ShapeDtypeStruct((n,RP,D),BF)],
        compiler_params=PAR)(h,w,vec)

def gelu_parts(u):
    c=0.5*(1.0+lax.erf(u*0.7071067811865476))
    g=c+u*(jnp.exp(-0.5*u*u)*0.3989422804014327)
    return u*c,g

def kb_kernel(FC,h_ref,o_ref,wo_ref,w1_ref,w2_ref,vec_ref,h1_ref,a_ref,e_ref,g_ref,h2_ref):
    h1=h_ref[0].astype(F32)+dot(o_ref[0],wo_ref[...])+vec_ref[4:5]
    h1_ref[0]=h1
    xc,rs=norm_stats(h1)
    a_ref[0]=(xc*rs*vec_ref[5:6]+vec_ref[6:7]).astype(BF)
    a=a_ref[0]
    h2_ref[0]=h1+vec_ref[7:8]
    for j in range(3072//FC):
        lo=FC*j
        u=dot(a,w1_ref[:,lo:lo+FC])+vec_ref[8+lo//D:9+lo//D,lo%D:lo%D+FC]
        e,g=gelu_parts(u)
        e_ref[0,:,lo:lo+FC]=e.astype(BF); g_ref[0,:,lo:lo+FC]=g.astype(BF)
        h2_ref[0]+=dot(e_ref[0,:,lo:lo+FC],w2_ref[lo:lo+FC,:])

def kb(h,o,wo,w1,w2,vec,FC=256):
    n=h.shape[0]
    S=jax.ShapeDtypeStruct
    return pl.pallas_call(functools.partial(kb_kernel,FC),grid=(n,),in_specs=[img(D),img(D),full(wo.shape),full(w1.shape),full(w2.shape),full(vec.shape)],
        out_specs=[img(D),img(D),img(3072),img(3072),img(D)],
        out_shape=[S((n,RP,D),F32),S((n,RP,D),BF),S((n,RP,3072),BF),S((n,RP,3072),BF),S((n,RP,D),F32)],
        compiler_params=PAR)(h,o,wo,w1,w2,vec)

def rsum(x): return jnp.sum(x,axis=0,keepdims=True)
def norm_back(x,gain,dy):
    xc,rs=norm_stats(x); xh=xc*rs
    dyg=dy*gain
    dx=rs*(dyg-jnp.mean(dyg,axis=-1,keepdims=True)-xh*jnp.mean(dyg*xh,axis=-1,keepdims=True))
    return dx, rsum(dy*xh), rsum(dy)

def kc_kernel(FC,d_ref,h1_ref,g_ref,wo_ref,w1_ref,w2_ref,vec_ref,db_ref,du_ref,dh1_ref,dh1b_ref,do_ref,dv_ref,acc_ref):
    @pl.when(pl.program_id(0)==0)
    def _(): dv_ref[...]=jnp.zeros_like(dv_ref)
    d=d_ref[0].astype(F32)
    db_ref[0]=d.astype(BF)
    db=db_ref[0]
    dv_ref[7:8]+=rsum(d)
    for j in range(3072//FC):
        lo=FC*j
        du=dot_t(db,w2_ref[lo:lo+FC,:])*g_ref[0,:,lo:lo+FC].astype(F32)
        dv_ref[8+lo//D:9+lo//D,lo%D:lo%D+FC]+=rsum(du)
        du_ref[0,:,lo:lo+FC]=du.astype(BF)
        t=dot_t(du_ref[0,:,lo:lo+FC],w1_ref[:,lo:lo+FC])
        if j==0: acc_ref[...]=t
        else: acc_ref[...]+=t
    dx,dg,dc=norm_back(h1_ref[0],vec_ref[5:6],acc_ref[...])
    dv_ref[5:6]+=dg; dv_ref[6:7]+=dc
    dh1=d_ref[0].astype(F32)+dx
    dh1_ref[0]=dh1
    dv_ref[4:5]+=rsum(dh1)
    dh1b_ref[0]=dh1.astype(BF)
    do_ref[0]=dot_t(dh1b_ref[0],wo_ref[...]).astype(BF)

def kc(d,h1,g,wo,w1,w2,vec,FC=256):
    n=d.shape[0]; S=jax.ShapeDtypeStruct
    return pl.pallas_call(functools.partial(kc_kernel,FC),grid=(n,),in_specs=[img(D),img(D),img(3072),full(wo.shape),full(w1.shape),full(w2.shape),full(vec.shape)],
        out_specs=[img(D),img(3072),img(D),img(D),img(D),full((16,D))],
        out_shape=[S((n,RP,D),BF),S((n,RP,3072),BF),S((n,RP,D),F32),S((n,RP,D),BF),S((n,RP,D),BF),S((16,D),F32)],
        scratch_shapes=[pltpu.VMEM((RP,D),F32)],
        compiler_params=PAR)(d,h1,g,wo,w1,w2,vec)

def kd_kernel(qkv_ref,do_ref,dz_ref,dv_ref):
    @pl.when(pl.program_id(0)==0)
    def _(): dv_ref[...]=jnp.zeros_like(dv_ref)
    for p in range(6):
        b=128*p
        dq,dk,dv=attn_bwd(qkv_ref[0,:,b:b+128],qkv_ref[0,:,D+b:D+b+128],qkv_ref[0,:,2*D+b:2*D+b+128],do_ref[0,:,b:b+128])
        dv_ref[2:3,b:b+128]+=rsum(dq); dv_ref[3:4,b:b+128]+=rsum(dv)
        dz_ref[0,:,b:b+128]=dq.astype(BF); dz_ref[0,:,D+b:D+b+128]=dk.astype(BF); dz_ref[0,:,2*D+b:2*D+b+128]=dv.astype(BF)

def kd(qkv,do):
    n=do.shape[0]; S=jax.ShapeDtypeStruct
    return pl.pallas_call(kd_kernel,grid=(n,),in_specs=[img(3*D),img(D)],out_specs=[img(3*D),full((16,D))],
        out_shape=[S((n,RP,3*D),BF),S((16,D),F32)],compiler_params=PAR)(qkv,do)

def kf_kernel(dz_ref,h_ref,dh1_ref,w_ref,vec_ref,dh_ref,dv_ref):
    @pl.when(pl.program_id(0)==0)
    def _(): dv_ref[...]=jnp.zeros_like(dv_ref)
    da=dot_t(dz_ref[0],w_ref[...])
    dx,dg,dc=norm_back(h_ref[0].astype(F32),vec_ref[0:1],da)
    dv_ref[0:1]+=dg; dv_ref[1:2]+=dc
    rows=dh_ref.shape[1]
    dh_ref[0]=(dh1_ref[0]+dx)[:rows]

def kf(dz,h,dh1,w,vec,rows=RP):
    n=dz.shape[0]; S=jax.ShapeDtypeStruct
    return pl.pallas_call(kf_kernel,grid=(n,),in_specs=[img(3*D),img(D),img(D),full(w.shape),full(vec.shape)],
        out_specs=[pl.BlockSpec((1,rows,D),lambda i:(i,0,0)),full((16,D))],
        out_shape=[S((n,rows,D),F32),S((16,D),F32)],compiler_params=PAR)(dz,h,dh1,w,vec)

def dw_kernel(l_ref,r_ref,o_ref):
    o_ref[...]=dot_0(l_ref[...],r_ref[...]).astype(BF)
def dw(l,r,MB=256):
    M=l.shape[-1]; N=r.shape[-1]; K=l.shape[0]*RP
    l=l.reshape(K,M); r=r.reshape(K,N)
    return pl.pallas_call(dw_kernel,grid=(M//MB,),in_specs=[pl.BlockSpec((K,MB),lambda i:(0,i)),pl.BlockSpec((K,N),lambda i:(0,0))],
       out_specs=pl.BlockSpec((MB,N),lambda i:(i,0)),out_shape=jax.ShapeDtypeStruct((M,N),BF),compiler_params=PAR)(l,r)


LAYERS = 2
STEP = 3
beta_one = 0.9
beta_two = 0.999
matrix_rate = 0.03
vector_rate = 0.2
matrix_decay = 0.05
adam_eps = 1e-8


def adam_update(master, gradient, moment_one, moment_two, rate, decay_rate):
    moment_one = beta_one * moment_one + (1.0 - beta_one) * gradient
    moment_two = beta_two * moment_two + (1.0 - beta_two) * gradient * gradient
    corr_one = 1.0 - beta_one**STEP
    corr_two = 1.0 - beta_two**STEP
    adam_move = moment_one / corr_one / (jnp.sqrt(moment_two / corr_two) + adam_eps)
    return (master - rate * (adam_move + decay_rate * master), moment_one, moment_two)


def swap(x, axis, size, mask):
    return lax.ppermute(x, axis, [(i, i ^ mask) for i in range(size)])


def halve(x, order, size):
    bits = size.bit_length() - 1
    me = lax.axis_index("fsdp")
    x = x.reshape((2,) * bits + x.shape[1:])
    left = list(range(bits))[::-1]
    for bit in order:
        at = left.index(bit)
        mine = (me >> bit) & 1
        keep = lax.dynamic_index_in_dim(x, mine, at, keepdims=False)
        send = lax.dynamic_index_in_dim(x, 1 - mine, at, keepdims=False)
        got = swap(send, "fsdp", size, 1 << bit)
        x = (keep.astype(F32) + got.astype(F32)).astype(BF)
        left.remove(bit)
    return x


def reduce_all(x, nf, nr):
    bits = nf.bit_length() - 1
    rows, cols = x.shape
    x = x.reshape(nf, rows // nf, cols)
    half = cols // 2 // 128 * 128
    up = [0] + list(range(1, bits))
    down = [0] + list(range(1, bits))[::-1]
    x = jnp.concatenate([halve(x[..., :half], up, nf), halve(x[..., half:], down, nf)], axis=-1)
    mask = 1
    while mask < nr:
        got = swap(x, "rep", nr, 2 * mask - 1)
        y = x.astype(F32) + got.astype(F32)
        x = y.astype(BF)
        mask *= 2
    return y


def make_shards(nf, nr):
    def shards(images, cotangent, weight_in, weight_out, vector_params, first_in, first_out, first_vec, second_in, second_out, second_vec):
        pad = lambda a: jnp.pad(a, ((0, 0), (0, RP - SEQ), (0, 0)))
        vec_all = lax.all_gather(vector_params.astype(BF), "fsdp", axis=1, tiled=True).astype(F32)
        h = pad(images)
        ct = pad(cotangent)
        saved = []
        for l in range(LAYERS):
            win = lax.all_gather(weight_in[l].astype(BF), "fsdp", axis=0, tiled=True)
            wout = lax.all_gather(weight_out[l].astype(BF), "fsdp", axis=0, tiled=True)
            vec = jnp.pad(vec_all[l].reshape(12, D), ((0, 4), (0, 0)))
            wqkv, w1, wo, w2 = win[:, : 3 * D], win[:, 3 * D :], wout[:D], wout[D:]
            qkv, o, a1 = ka(h, wqkv, vec)
            h1, a2, e, g, h2 = kb(h, o, wo, w1, w2, vec)
            saved.append((h, wqkv, w1, wo, w2, vec, qkv, o, a1, h1, a2, e, g))
            h = h2
        encoded = h[:, :SEQ].astype(BF)
        d = ct
        gin, gout, gvec = [None] * LAYERS, [None] * LAYERS, [None] * LAYERS
        for l in reversed(range(LAYERS)):
            h, wqkv, w1, wo, w2, vec, qkv, o, a1, h1, a2, e, g = saved[l]
            db, du, dh1, dh1b, do, dv1 = kc(d, h1, g, wo, w1, w2, vec)
            g1 = reduce_all(dw(a2, du), nf, nr)
            go = reduce_all(jnp.concatenate([dw(o, dh1b), dw(e, db)], axis=0), nf, nr)
            dz, dv2 = kd(qkv, do)
            gq = reduce_all(dw(a1, dz), nf, nr)
            d, dv3 = kf(dz, h, dh1, wqkv, vec, RP if l else SEQ)
            gin[l] = jnp.concatenate([gq, g1], axis=1)
            gout[l] = go
            gvec[l] = (dv1 + dv2 + dv3)[:12].reshape(-1)
        gv = lax.psum(jnp.stack(gvec), ("fsdp", "rep"))
        wide = gv.shape[1] // nf
        gv = lax.dynamic_slice_in_dim(gv, lax.axis_index("fsdp") * wide, wide, 1)
        gi, go = jnp.stack(gin), jnp.stack(gout)
        new_in, moment_in, square_in = adam_update(weight_in, gi, first_in, second_in, matrix_rate, matrix_decay)
        new_out, moment_out, square_out = adam_update(weight_out, go, first_out, second_out, matrix_rate, matrix_decay)
        new_vec, moment_vec, square_vec = adam_update(vector_params, gv, first_vec, second_vec, vector_rate, 0.0)
        return (encoded, d, gi, go, gv, new_in, new_out, new_vec, moment_in, moment_out, moment_vec, square_in, square_out, square_vec)

    return shards


def solution(mesh):
    tokens = P(("fsdp", "rep"), None, None)
    matrix = P(None, "fsdp", None)
    vector = P(None, "fsdp")
    in_specs = (tokens, tokens) + (matrix, matrix, vector) * 3
    out_specs = (tokens, tokens) + (matrix, matrix, vector) * 4
    return jax.shard_map(make_shards(mesh.shape["fsdp"], mesh.shape["rep"]), mesh=mesh, in_specs=in_specs, out_specs=out_specs, check_vma=False)
```

```python
import functools
import jax, jax.numpy as jnp
from jax import lax
from jax.experimental import pallas as pl
from jax.experimental.pallas import tpu as pltpu
from jax.sharding import PartitionSpec as P

D=768; HD=64; SEQ=197; RP=208; EPS=1e-6
BF=jnp.bfloat16; F32=jnp.float32
def dot(a,b): return jnp.dot(a,b,preferred_element_type=F32)
def dot_t(a,b): return lax.dot_general(a,b,(((1,),(1,)),((),())),preferred_element_type=F32)
def dot_0(a,b): return lax.dot_general(a,b,(((0,),(0,)),((),())),preferred_element_type=F32)

def norm_stats(x):
    mean=jnp.mean(x,axis=-1,keepdims=True); xc=x-mean
    var=jnp.mean(xc*xc,axis=-1,keepdims=True)
    return xc, lax.rsqrt(var+EPS)

def attn_fwd(q,k,v):
    lane=lax.broadcasted_iota(jnp.int32,(1,128),1)
    col=lax.broadcasted_iota(jnp.int32,(1,RP),1)
    os=[]
    for half in range(2):
        m=jnp.where((lane<64) if half==0 else (lane>=64),0.125,0.0).astype(BF)
        s=dot_t(q*m,k)
        s=jnp.where(col<SEQ,s,-1e30)
        mx=jnp.max(s,axis=-1,keepdims=True)
        e=jnp.exp(s-mx)
        p=(e*(1.0/jnp.sum(e,axis=-1,keepdims=True))).astype(BF)
        os.append(dot(p,v))
    return jnp.where(lane<64,os[0],os[1]).astype(BF)

def attn_bwd(q,k,v,do):
    lane=lax.broadcasted_iota(jnp.int32,(1,128),1)
    row=lax.broadcasted_iota(jnp.int32,(RP,1),0)
    r=[]
    for half in range(2):
        sel=(lane<64) if half==0 else (lane>=64)
        m=jnp.where(sel,0.125,0.0).astype(BF)
        m1=jnp.where(sel,1.0,0.0).astype(BF)
        qs=q*m
        s=dot_t(k,qs)
        s=jnp.where(row<SEQ,s,-1e30)
        mx=jnp.max(s,axis=0,keepdims=True)
        e=jnp.exp(s-mx)
        p=e*(1.0/jnp.sum(e,axis=0,keepdims=True))
        pb=p.astype(BF)
        dp=dot_t(v,do*m1)
        dl=jnp.sum(p*dp,axis=0,keepdims=True)
        ds=(p*(dp-dl)).astype(BF)
        dv=dot(pb,do)
        dk=dot(ds,qs)
        dq=dot_0(ds,k)*0.125
        r.append((dq,dk,dv))
    return tuple(jnp.where(lane<64,a,b) for a,b in zip(*r))

def ka_kernel(h_ref,w_ref,vec_ref,qkv_ref,o_ref,a_ref):
    h=h_ref[0].astype(F32)
    xc,rs=norm_stats(h)
    a_ref[0]=(xc*rs*vec_ref[0:1]+vec_ref[1:2]).astype(BF)
    a=a_ref[0]
    for c in range(3):
        cs=slice(256*c,256*c+256)
        qkv_ref[0,:,256*c:256*c+256]=(dot(a,w_ref[:,256*c:256*c+256])+vec_ref[2:3,cs]).astype(BF)
        qkv_ref[0,:,D+256*c:D+256*c+256]=dot(a,w_ref[:,D+256*c:D+256*c+256]).astype(BF)
        qkv_ref[0,:,2*D+256*c:2*D+256*c+256]=(dot(a,w_ref[:,2*D+256*c:2*D+256*c+256])+vec_ref[3:4,cs]).astype(BF)
        for p in range(2):
            b=256*c+128*p
            o_ref[0,:,b:b+128]=attn_fwd(qkv_ref[0,:,b:b+128],qkv_ref[0,:,D+b:D+b+128],qkv_ref[0,:,2*D+b:2*D+b+128])

def img(n,dt=None): return pl.BlockSpec((1,RP,n),lambda i:(i,0,0))
def full(shape): return pl.BlockSpec(shape,lambda i:(0,)*len(shape))
PAR=pltpu.CompilerParams(vmem_limit_bytes=60*2**20)

def ka(h,w,vec):
    n=h.shape[0]
    return pl.pallas_call(ka_kernel,grid=(n,),in_specs=[img(D),full(w.shape),full(vec.shape)],
        out_specs=[img(3*D),img(D),img(D)],
        out_shape=[jax.ShapeDtypeStruct((n,RP,3*D),BF),jax.ShapeDtypeStruct((n,RP,D),BF),jax.ShapeDtypeStruct((n,RP,D),BF)],
        compiler_params=PAR)(h,w,vec)

def gelu_parts(u):
    c=0.5*(1.0+lax.erf(u*0.7071067811865476))
    g=c+u*(jnp.exp(-0.5*u*u)*0.3989422804014327)
    return u*c,g

def kb_kernel(FC,h_ref,o_ref,wo_ref,w1_ref,w2_ref,vec_ref,h1_ref,a_ref,e_ref,g_ref,h2_ref):
    h1=h_ref[0].astype(F32)+dot(o_ref[0],wo_ref[...])+vec_ref[4:5]
    h1_ref[0]=h1
    xc,rs=norm_stats(h1)
    a_ref[0]=(xc*rs*vec_ref[5:6]+vec_ref[6:7]).astype(BF)
    a=a_ref[0]
    h2_ref[0]=h1+vec_ref[7:8]
    for j in range(3072//FC):
        lo=FC*j
        u=dot(a,w1_ref[:,lo:lo+FC])+vec_ref[8+lo//D:9+lo//D,lo%D:lo%D+FC]
        e,g=gelu_parts(u)
        e_ref[0,:,lo:lo+FC]=e.astype(BF); g_ref[0,:,lo:lo+FC]=g.astype(BF)
        h2_ref[0]+=dot(e_ref[0,:,lo:lo+FC],w2_ref[lo:lo+FC,:])

def kb(h,o,wo,w1,w2,vec,FC=256):
    n=h.shape[0]
    S=jax.ShapeDtypeStruct
    return pl.pallas_call(functools.partial(kb_kernel,FC),grid=(n,),in_specs=[img(D),img(D),full(wo.shape),full(w1.shape),full(w2.shape),full(vec.shape)],
        out_specs=[img(D),img(D),img(3072),img(3072),img(D)],
        out_shape=[S((n,RP,D),F32),S((n,RP,D),BF),S((n,RP,3072),BF),S((n,RP,3072),BF),S((n,RP,D),F32)],
        compiler_params=PAR)(h,o,wo,w1,w2,vec)

def rsum(x): return jnp.sum(x,axis=0,keepdims=True)
def norm_back(x,gain,dy):
    xc,rs=norm_stats(x); xh=xc*rs
    dyg=dy*gain
    dx=rs*(dyg-jnp.mean(dyg,axis=-1,keepdims=True)-xh*jnp.mean(dyg*xh,axis=-1,keepdims=True))
    return dx, rsum(dy*xh), rsum(dy)

def kc_kernel(FC,d_ref,h1_ref,g_ref,wo_ref,w1_ref,w2_ref,vec_ref,db_ref,du_ref,dh1_ref,dh1b_ref,do_ref,dv_ref,acc_ref):
    @pl.when(pl.program_id(0)==0)
    def _(): dv_ref[...]=jnp.zeros_like(dv_ref)
    d=d_ref[0].astype(F32)
    db_ref[0]=d.astype(BF)
    db=db_ref[0]
    dv_ref[7:8]+=rsum(d)
    for j in range(3072//FC):
        lo=FC*j
        du=dot_t(db,w2_ref[lo:lo+FC,:])*g_ref[0,:,lo:lo+FC].astype(F32)
        dv_ref[8+lo//D:9+lo//D,lo%D:lo%D+FC]+=rsum(du)
        du_ref[0,:,lo:lo+FC]=du.astype(BF)
        t=dot_t(du_ref[0,:,lo:lo+FC],w1_ref[:,lo:lo+FC])
        if j==0: acc_ref[...]=t
        else: acc_ref[...]+=t
    dx,dg,dc=norm_back(h1_ref[0],vec_ref[5:6],acc_ref[...])
    dv_ref[5:6]+=dg; dv_ref[6:7]+=dc
    dh1=d_ref[0].astype(F32)+dx
    dh1_ref[0]=dh1
    dv_ref[4:5]+=rsum(dh1)
    dh1b_ref[0]=dh1.astype(BF)
    do_ref[0]=dot_t(dh1b_ref[0],wo_ref[...]).astype(BF)

def kc(d,h1,g,wo,w1,w2,vec,FC=256):
    n=d.shape[0]; S=jax.ShapeDtypeStruct
    return pl.pallas_call(functools.partial(kc_kernel,FC),grid=(n,),in_specs=[img(D),img(D),img(3072),full(wo.shape),full(w1.shape),full(w2.shape),full(vec.shape)],
        out_specs=[img(D),img(3072),img(D),img(D),img(D),full((16,D))],
        out_shape=[S((n,RP,D),BF),S((n,RP,3072),BF),S((n,RP,D),F32),S((n,RP,D),BF),S((n,RP,D),BF),S((16,D),F32)],
        scratch_shapes=[pltpu.VMEM((RP,D),F32)],
        compiler_params=PAR)(d,h1,g,wo,w1,w2,vec)

def kd_kernel(qkv_ref,do_ref,dz_ref,dv_ref):
    @pl.when(pl.program_id(0)==0)
    def _(): dv_ref[...]=jnp.zeros_like(dv_ref)
    for p in range(6):
        b=128*p
        dq,dk,dv=attn_bwd(qkv_ref[0,:,b:b+128],qkv_ref[0,:,D+b:D+b+128],qkv_ref[0,:,2*D+b:2*D+b+128],do_ref[0,:,b:b+128])
        dv_ref[2:3,b:b+128]+=rsum(dq); dv_ref[3:4,b:b+128]+=rsum(dv)
        dz_ref[0,:,b:b+128]=dq.astype(BF); dz_ref[0,:,D+b:D+b+128]=dk.astype(BF); dz_ref[0,:,2*D+b:2*D+b+128]=dv.astype(BF)

def kd(qkv,do):
    n=do.shape[0]; S=jax.ShapeDtypeStruct
    return pl.pallas_call(kd_kernel,grid=(n,),in_specs=[img(3*D),img(D)],out_specs=[img(3*D),full((16,D))],
        out_shape=[S((n,RP,3*D),BF),S((16,D),F32)],compiler_params=PAR)(qkv,do)

def kf_kernel(dz_ref,h_ref,dh1_ref,w_ref,vec_ref,dh_ref,dv_ref):
    @pl.when(pl.program_id(0)==0)
    def _(): dv_ref[...]=jnp.zeros_like(dv_ref)
    da=dot_t(dz_ref[0],w_ref[...])
    dx,dg,dc=norm_back(h_ref[0].astype(F32),vec_ref[0:1],da)
    dv_ref[0:1]+=dg; dv_ref[1:2]+=dc
    rows=dh_ref.shape[1]
    dh_ref[0]=(dh1_ref[0]+dx)[:rows]

def kf(dz,h,dh1,w,vec,rows=RP):
    n=dz.shape[0]; S=jax.ShapeDtypeStruct
    return pl.pallas_call(kf_kernel,grid=(n,),in_specs=[img(3*D),img(D),img(D),full(w.shape),full(vec.shape)],
        out_specs=[pl.BlockSpec((1,rows,D),lambda i:(i,0,0)),full((16,D))],
        out_shape=[S((n,rows,D),F32),S((16,D),F32)],compiler_params=PAR)(dz,h,dh1,w,vec)

def dw_kernel(l_ref,r_ref,o_ref):
    o_ref[...]=dot_0(l_ref[...],r_ref[...]).astype(BF)
def dw(l,r,MB=256):
    M=l.shape[-1]; N=r.shape[-1]; K=l.shape[0]*RP
    l=l.reshape(K,M); r=r.reshape(K,N)
    return pl.pallas_call(dw_kernel,grid=(M//MB,),in_specs=[pl.BlockSpec((K,MB),lambda i:(0,i)),pl.BlockSpec((K,N),lambda i:(0,0))],
       out_specs=pl.BlockSpec((MB,N),lambda i:(i,0)),out_shape=jax.ShapeDtypeStruct((M,N),BF),compiler_params=PAR)(l,r)


LAYERS = 2
MESH = pl.DeviceIdType.MESH
CH = 96
NC = 12


def plane():
    f = lax.axis_index("fsdp")
    core, x, y = f % 2, (f // 2) % 2, f // 4
    return f, core, x, y


def chunk_rows(c, f):
    layer, j = c // NC, c % NC
    early = 1 - (j + 9) // 12
    late = j // 8
    mid = 1 - early - late
    base = layer * NC * D
    return pl.multiple_of(base + early * (j * D + CH * f) + late * ((j - 5) * D + CH * f)
                          + mid * (7 * D + 5 * CH * f + CH * (j - 3)), 16)


def fwd_kernel(img_ref, ws_ref, vs_ref, hs_ref, qkv_ref, a1_ref, o_ref, h1_ref, a2_ref, e_ref, g_ref, enc_ref, wo_ref, vo_ref,
               w, hb, ob, ab, vg, vec, lsem, ssem, rsem, vssem, vrsem, osem, vosem):
    l, s = pl.program_id(0), pl.program_id(1)
    f, core, x, y = plane()
    fc, fx, fy = f + 1 - 2 * core, f + 2 - 4 * x, f + 4 - 8 * y
    fd = fx + fy - f

    def wrow(c, who, lo=0, n=CH):
        return w.at[pl.ds(pl.multiple_of(chunk_rows(c, who) + lo, 16), n)]

    def send(c, kind, src, dst, to):
        return pltpu.make_async_remote_copy(src_ref=src, dst_ref=dst, send_sem=ssem.at[c % 4, kind], recv_sem=rsem.at[c % 4, kind],
                                            device_id={"fsdp": to}, device_id_type=MESH)

    def kinds(c):
        own, mine, half = ws_ref.at[c], wrow(c, f), CH // 2
        return [lambda: send(c, 0, own, mine, fx), lambda: send(c, 1, own, mine, fy), lambda: send(c, 2, own, mine, fc),
                lambda: send(c, 3, wrow(c, fx, 0, half), wrow(c, fx, 0, half), fy),
                lambda: send(c, 4, wrow(c, fy, half, half), wrow(c, fy, half, half), fx),
                lambda: send(c, 5, wrow(c, fx), wrow(c, fx), fc), lambda: send(c, 6, wrow(c, fy), wrow(c, fy), fc),
                lambda: send(c, 7, wrow(c, fd), wrow(c, fd), fc), lambda: pltpu.make_async_copy(own, mine, lsem.at[c % 4])]

    def start(c, which):
        k = kinds(c)
        for i in which:
            k[i]().start()

    def wait(c, which):
        k = kinds(c)
        for i in which:
            k[i]().wait()

    def tick(t):
        @pl.when((t >= 3) & (t < 27))
        def _():
            wait(t - 3, (2, 5, 6, 7, 8))

        @pl.when((t >= 2) & (t < 26))
        def _():
            wait(t - 2, (3, 4))
            start(t - 2, (7,))

        @pl.when((t >= 1) & (t < 25))
        def _():
            wait(t - 1, (0, 1))
            start(t - 1, (3, 4, 5, 6))

        @pl.when(t < 24)
        def _():
            start(t, (0, 1, 2, 8))

    def out_copy(b, n):
        return pltpu.make_async_copy(w.at[pl.ds(b, n)], wo_ref.at[pl.ds(b, n)], osem)

    @pl.when((l == 0) & (s == 0))
    def _():
        bar = pltpu.get_barrier_semaphore()
        for k in range(1, 8):
            pl.semaphore_signal(bar, inc=1, device_id={"fsdp": (f + k) % 8}, device_id_type=MESH)
        pl.semaphore_wait(bar, 7)

        def vcopy(k):
            return pltpu.make_async_remote_copy(src_ref=vs_ref, dst_ref=vg.at[f], send_sem=vssem.at[k - 1], recv_sem=vrsem.at[k - 1],
                                                device_id={"fsdp": (f + k) % 8}, device_id_type=MESH)
        for k in range(1, 8):
            vcopy(k).start()
        vg[f] = vs_ref[...]

        @pl.loop(0, 6)
        def _(t):
            tick(t)
        for k in range(1, 8):
            vcopy(k).wait()
        for layer in range(LAYERS):
            for c in range(72):
                vec[layer, c // 6:c // 6 + 1, 128 * (c % 6):128 * (c % 6) + 128] = vg[c // 9, layer, c % 9:c % 9 + 1, :]
        hb[...] = jnp.zeros_like(hb)
        cp = pltpu.make_async_copy(vec, vo_ref, vosem)
        cp.start()
        cp.wait()

    early = (1 - l) * (s + 5) + l * (s + 17)
    late = (1 - l) * (s + 1 + s // 11 + s // 13) + l * (s + 13)

    @pl.when((s <= 5) & (l + s > 0))
    def _():
        tick(early)

    @pl.when(s >= 10)
    def _():
        tick(late)

    @pl.when(s < 5)
    def _():
        @pl.when(l == 0)
        def _():
            hb[s, 0:SEQ, :] = img_ref[s].astype(F32)
        h = hb[s]
        hs_ref[0, 0] = h
        xc, rs = norm_stats(h)
        a1_ref[0, 0] = (xc * rs * vec[l, 0:1] + vec[l, 1:2]).astype(BF)
        a = a1_ref[0, 0]
        wb = l * NC * D

        def wq(part, c):
            return w[pl.ds(pl.multiple_of(wb + part * D, 16), D), 256 * c:256 * c + 256]
        for c in range(3):
            cs = slice(256 * c, 256 * c + 256)
            qkv_ref[0, 0, :, cs] = (dot(a, wq(0, c)) + vec[l, 2:3, cs]).astype(BF)
            qkv_ref[0, 0, :, D + 256 * c:D + 256 * c + 256] = dot(a, wq(1, c)).astype(BF)
            qkv_ref[0, 0, :, 2 * D + 256 * c:2 * D + 256 * c + 256] = (dot(a, wq(2, c)) + vec[l, 3:4, cs]).astype(BF)
            for p in range(2):
                b = 256 * c + 128 * p
                o = attn_fwd(qkv_ref[0, 0, :, b:b + 128], qkv_ref[0, 0, :, D + b:D + b + 128], qkv_ref[0, 0, :, 2 * D + b:2 * D + b + 128])
                o_ref[0, 0, :, b:b + 128] = o
                ob[s, :, b:b + 128] = o

    @pl.when((s >= 5) & (s < 10))
    def _():
        i = s - 5
        wo = w[pl.ds(pl.multiple_of((l * NC + 7) * D, 16), D), :]
        h1 = hb[i] + dot(ob[i], wo) + vec[l, 4:5]
        h1_ref[0, 0] = h1
        hb[i] = h1 + vec[l, 7:8]
        xc, rs = norm_stats(h1)
        a = (xc * rs * vec[l, 5:6] + vec[l, 6:7]).astype(BF)
        a2_ref[0, 0] = a
        ab[i] = a

    @pl.when(s >= 10)
    def _():
        j = s - 10
        up = pl.multiple_of((l * NC + 3 + j) * D, 16)
        down = pl.multiple_of((l * NC + 8 + j) * D, 16)

        @pl.loop(0, 5)
        def _(i):
            @pl.when((i == 3) & (l == 0) & ((s == 10) | (s == 12)))
            def _():
                tick(12 + 3 * ((s - 10) // 2))
            for q in range(3):
                cs = slice(256 * q, 256 * q + 256)
                u = dot(ab[i], w[pl.ds(up, D), cs]) + vec[l, pl.ds(8 + j, 1), cs]
                e, g = gelu_parts(u)
                e_ref[0, i, :, cs] = e.astype(BF)
                g_ref[0, i, :, cs] = g.astype(BF)
                hb[i] += dot(e_ref[0, i, :, cs], w[pl.ds(pl.multiple_of(down + 256 * q, 16), 256), :])

            @pl.when((l == 1) & (s == 13))
            def _():
                enc_ref[i] = hb[i, 0:SEQ, :].astype(BF)

    for layer in range(LAYERS):
        base = layer * NC * D

        @pl.when((l == layer) & (s == 4))
        def _():
            out_copy(base, 3 * D).start()

        @pl.when((l == layer) & (s == 9))
        def _():
            out_copy(base + 7 * D, 5 * D).start()

        for j in range(4):
            @pl.when((l == layer) & (s == 10 + j))
            def _():
                out_copy(base + (3 + j) * D, D).start()

    @pl.when((l == 1) & (s == 13))
    def _():
        pltpu.make_async_copy(w, wo_ref, osem).wait()


def fwd(images, shard, vshard):
    n = images.shape[0]
    S = jax.ShapeDtypeStruct
    one = lambda cols: pl.BlockSpec((1, 1, RP, cols), lambda l, s: (l, jnp.minimum(s, 4), 0, 0))
    two = lambda cols: pl.BlockSpec((1, 1, RP, cols), lambda l, s: (l, jnp.clip(s - 5, 0, 4), 0, 0))
    wide = pl.BlockSpec((1, n, RP, D), lambda l, s: (l, 0, 0, jnp.clip(s - 10, 0, 3)))
    anyw = pl.BlockSpec(memory_space=pl.ANY)
    rows = LAYERS * NC * D
    return pl.pallas_call(
        fwd_kernel, grid=(LAYERS, 14),
        in_specs=[pl.BlockSpec(images.shape, lambda l, s: (0, 0, 0)), anyw, pl.BlockSpec(vshard.shape, lambda l, s: (0, 0, 0))],
        out_specs=[one(D), one(3 * D), one(D), one(D), two(D), two(D), wide, wide, pl.BlockSpec(images.shape, lambda l, s: (0, 0, 0)), anyw, anyw],
        out_shape=[S((LAYERS, n, RP, D), F32), S((LAYERS, n, RP, 3 * D), BF), S((LAYERS, n, RP, D), BF), S((LAYERS, n, RP, D), BF),
                   S((LAYERS, n, RP, D), F32), S((LAYERS, n, RP, D), BF), S((LAYERS, n, RP, 4 * D), BF), S((LAYERS, n, RP, 4 * D), BF),
                   S(images.shape, BF), S((rows, D), BF), S((LAYERS, 16, D), F32)],
        scratch_shapes=[pltpu.VMEM((rows, D), BF), pltpu.VMEM((n, RP, D), F32), pltpu.VMEM((n, RP, D), BF), pltpu.VMEM((n, RP, D), BF),
                        pltpu.VMEM((8, LAYERS, 16, 128), F32), pltpu.VMEM((LAYERS, 16, D), F32),
                        pltpu.SemaphoreType.DMA((4,)), pltpu.SemaphoreType.DMA((4, 8)), pltpu.SemaphoreType.DMA((4, 8)),
                        pltpu.SemaphoreType.DMA((7,)), pltpu.SemaphoreType.DMA((7,)), pltpu.SemaphoreType.DMA, pltpu.SemaphoreType.DMA],
        compiler_params=pltpu.CompilerParams(collective_id=0, has_side_effects=True, vmem_limit_bytes=62 * 2**20),
    )(images, shard, vshard)


STEP = 3
beta_one = 0.9
beta_two = 0.999
matrix_rate = 0.03
vector_rate = 0.2
matrix_decay = 0.05
adam_eps = 1e-8


def adam_update(master, gradient, moment_one, moment_two, rate, decay_rate):
    moment_one = beta_one * moment_one + (1.0 - beta_one) * gradient
    moment_two = beta_two * moment_two + (1.0 - beta_two) * gradient * gradient
    corr_one = 1.0 - beta_one**STEP
    corr_two = 1.0 - beta_two**STEP
    adam_move = moment_one / corr_one / (jnp.sqrt(moment_two / corr_two) + adam_eps)
    return (master - rate * (adam_move + decay_rate * master), moment_one, moment_two)


def swap(x, axis, size, mask):
    return lax.ppermute(x, axis, [(i, i ^ mask) for i in range(size)])


def halve(x, order, size):
    bits = size.bit_length() - 1
    me = lax.axis_index("fsdp")
    x = x.reshape((2,) * bits + x.shape[1:])
    left = list(range(bits))[::-1]
    for bit in order:
        at = left.index(bit)
        mine = (me >> bit) & 1
        keep = lax.dynamic_index_in_dim(x, mine, at, keepdims=False)
        send = lax.dynamic_index_in_dim(x, 1 - mine, at, keepdims=False)
        got = swap(send, "fsdp", size, 1 << bit)
        x = (keep.astype(F32) + got.astype(F32)).astype(BF)
        left.remove(bit)
    return x


def reduce_all(x, nf, nr):
    bits = nf.bit_length() - 1
    rows, cols = x.shape
    x = x.reshape(nf, rows // nf, cols)
    half = cols // 2 // 128 * 128
    up = [0] + list(range(1, bits))
    down = [0] + list(range(1, bits))[::-1]
    x = jnp.concatenate([halve(x[..., :half], up, nf), halve(x[..., half:], down, nf)], axis=-1)
    mask = 1
    while mask < nr:
        got = swap(x, "rep", nr, 2 * mask - 1)
        y = x.astype(F32) + got.astype(F32)
        x = y.astype(BF)
        mask *= 2
    return y


def own_shard(weight_in, weight_out):
    a = weight_in.astype(BF).reshape(LAYERS, CH, 7, D).transpose(0, 2, 1, 3)
    b = weight_out.astype(BF).reshape(LAYERS, 5, CH, D)
    return jnp.concatenate([a[:, :3], b, a[:, 3:]], axis=1).reshape(LAYERS * NC, CH, D)


def fused_forward(images, weight_in, weight_out, vector_params):
    vs = jnp.pad(vector_params.astype(BF).astype(F32).reshape(LAYERS, 9, 128), ((0, 0), (0, 7), (0, 0)))
    hs, qkv, a1, o, h1, a2, e, g, encoded, w, vec = fwd(images, own_shard(weight_in, weight_out), vs)
    saved = []
    for l in range(LAYERS):
        blk = lambda b, n: w[(l * NC + b) * D : (l * NC + b + n) * D]
        wqkv = jnp.concatenate([blk(0, 1), blk(1, 1), blk(2, 1)], axis=1)
        w1 = jnp.concatenate([blk(3 + j, 1) for j in range(4)], axis=1)
        saved.append((hs[l], wqkv, w1, blk(7, 1), blk(8, 4), vec[l], qkv[l], o[l], a1[l], h1[l], a2[l], e[l], g[l]))
    return encoded, saved


def make_shards(nf, nr):
    def shards(images, cotangent, weight_in, weight_out, vector_params, first_in, first_out, first_vec, second_in, second_out, second_vec):
        pad = lambda a: jnp.pad(a, ((0, 0), (0, RP - SEQ), (0, 0)))
        ct = pad(cotangent)
        if nf == 8:
            encoded, saved = fused_forward(images, weight_in, weight_out, vector_params)
        else:
            vec_all = lax.all_gather(vector_params.astype(BF), "fsdp", axis=1, tiled=True).astype(F32)
            h = pad(images)
            ct = pad(cotangent)
            saved = []
            for l in range(LAYERS):
                win = lax.all_gather(weight_in[l].astype(BF), "fsdp", axis=0, tiled=True)
                wout = lax.all_gather(weight_out[l].astype(BF), "fsdp", axis=0, tiled=True)
                vec = jnp.pad(vec_all[l].reshape(12, D), ((0, 4), (0, 0)))
                wqkv, w1, wo, w2 = win[:, : 3 * D], win[:, 3 * D :], wout[:D], wout[D:]
                qkv, o, a1 = ka(h, wqkv, vec)
                h1, a2, e, g, h2 = kb(h, o, wo, w1, w2, vec)
                saved.append((h, wqkv, w1, wo, w2, vec, qkv, o, a1, h1, a2, e, g))
                h = h2
            encoded = h[:, :SEQ].astype(BF)
        d = ct
        gin, gout, gvec = [None] * LAYERS, [None] * LAYERS, [None] * LAYERS
        for l in reversed(range(LAYERS)):
            h, wqkv, w1, wo, w2, vec, qkv, o, a1, h1, a2, e, g = saved[l]
            db, du, dh1, dh1b, do, dv1 = kc(d, h1, g, wo, w1, w2, vec)
            g1 = reduce_all(dw(a2, du), nf, nr)
            go = reduce_all(jnp.concatenate([dw(o, dh1b), dw(e, db)], axis=0), nf, nr)
            dz, dv2 = kd(qkv, do)
            gq = reduce_all(dw(a1, dz), nf, nr)
            d, dv3 = kf(dz, h, dh1, wqkv, vec, RP if l else SEQ)
            gin[l] = jnp.concatenate([gq, g1], axis=1)
            gout[l] = go
            gvec[l] = (dv1 + dv2 + dv3)[:12].reshape(-1)
        gv = lax.psum(jnp.stack(gvec), ("fsdp", "rep"))
        wide = gv.shape[1] // nf
        gv = lax.dynamic_slice_in_dim(gv, lax.axis_index("fsdp") * wide, wide, 1)
        gi, go = jnp.stack(gin), jnp.stack(gout)
        new_in, moment_in, square_in = adam_update(weight_in, gi, first_in, second_in, matrix_rate, matrix_decay)
        new_out, moment_out, square_out = adam_update(weight_out, go, first_out, second_out, matrix_rate, matrix_decay)
        new_vec, moment_vec, square_vec = adam_update(vector_params, gv, first_vec, second_vec, vector_rate, 0.0)
        return (encoded, d, gi, go, gv, new_in, new_out, new_vec, moment_in, moment_out, moment_vec, square_in, square_out, square_vec)

    return shards


def solution(mesh):
    tokens = P(("fsdp", "rep"), None, None)
    matrix = P(None, "fsdp", None)
    vector = P(None, "fsdp")
    in_specs = (tokens, tokens) + (matrix, matrix, vector) * 3
    out_specs = (tokens, tokens) + (matrix, matrix, vector) * 4
    return jax.shard_map(make_shards(mesh.shape["fsdp"], mesh.shape["rep"]), mesh=mesh, in_specs=in_specs, out_specs=out_specs, check_vma=False)
```

```python
import functools
import jax, jax.numpy as jnp
from jax import lax
from jax.experimental import pallas as pl
from jax.experimental.pallas import tpu as pltpu
from jax.sharding import PartitionSpec as P

D=768; HD=64; SEQ=197; RP=208; EPS=1e-6
BF=jnp.bfloat16; F32=jnp.float32
def dot(a,b): return jnp.dot(a,b,preferred_element_type=F32)
def dot_t(a,b): return lax.dot_general(a,b,(((1,),(1,)),((),())),preferred_element_type=F32)
def dot_0(a,b): return lax.dot_general(a,b,(((0,),(0,)),((),())),preferred_element_type=F32)

def norm_stats(x):
    mean=jnp.mean(x,axis=-1,keepdims=True); xc=x-mean
    var=jnp.mean(xc*xc,axis=-1,keepdims=True)
    return xc, lax.rsqrt(var+EPS)

def attn_fwd(q,k,v):
    lane=lax.broadcasted_iota(jnp.int32,(1,128),1)
    col=lax.broadcasted_iota(jnp.int32,(1,RP),1)
    os=[]
    for half in range(2):
        m=jnp.where((lane<64) if half==0 else (lane>=64),0.125,0.0).astype(BF)
        s=dot_t(q*m,k)
        s=jnp.where(col<SEQ,s,-1e30)
        mx=jnp.max(s,axis=-1,keepdims=True)
        e=jnp.exp(s-mx)
        p=(e*(1.0/jnp.sum(e,axis=-1,keepdims=True))).astype(BF)
        os.append(dot(p,v))
    return jnp.where(lane<64,os[0],os[1]).astype(BF)

def attn_bwd(q,k,v,do):
    lane=lax.broadcasted_iota(jnp.int32,(1,128),1)
    row=lax.broadcasted_iota(jnp.int32,(RP,1),0)
    r=[]
    for half in range(2):
        sel=(lane<64) if half==0 else (lane>=64)
        m=jnp.where(sel,0.125,0.0).astype(BF)
        m1=jnp.where(sel,1.0,0.0).astype(BF)
        qs=q*m
        s=dot_t(k,qs)
        s=jnp.where(row<SEQ,s,-1e30)
        mx=jnp.max(s,axis=0,keepdims=True)
        e=jnp.exp(s-mx)
        p=e*(1.0/jnp.sum(e,axis=0,keepdims=True))
        pb=p.astype(BF)
        dp=dot_t(v,do*m1)
        dl=jnp.sum(p*dp,axis=0,keepdims=True)
        ds=(p*(dp-dl)).astype(BF)
        dv=dot(pb,do)
        dk=dot(ds,qs)
        dq=dot_0(ds,k)*0.125
        r.append((dq,dk,dv))
    return tuple(jnp.where(lane<64,a,b) for a,b in zip(*r))

def ka_kernel(h_ref,w_ref,vec_ref,qkv_ref,o_ref,a_ref):
    h=h_ref[0].astype(F32)
    xc,rs=norm_stats(h)
    a_ref[0]=(xc*rs*vec_ref[0:1]+vec_ref[1:2]).astype(BF)
    a=a_ref[0]
    for c in range(3):
        cs=slice(256*c,256*c+256)
        qkv_ref[0,:,256*c:256*c+256]=(dot(a,w_ref[:,256*c:256*c+256])+vec_ref[2:3,cs]).astype(BF)
        qkv_ref[0,:,D+256*c:D+256*c+256]=dot(a,w_ref[:,D+256*c:D+256*c+256]).astype(BF)
        qkv_ref[0,:,2*D+256*c:2*D+256*c+256]=(dot(a,w_ref[:,2*D+256*c:2*D+256*c+256])+vec_ref[3:4,cs]).astype(BF)
        for p in range(2):
            b=256*c+128*p
            o_ref[0,:,b:b+128]=attn_fwd(qkv_ref[0,:,b:b+128],qkv_ref[0,:,D+b:D+b+128],qkv_ref[0,:,2*D+b:2*D+b+128])

def img(n,dt=None): return pl.BlockSpec((1,RP,n),lambda i:(i,0,0))
def full(shape): return pl.BlockSpec(shape,lambda i:(0,)*len(shape))
PAR=pltpu.CompilerParams(vmem_limit_bytes=60*2**20)

def ka(h,w,vec):
    n=h.shape[0]
    return pl.pallas_call(ka_kernel,grid=(n,),in_specs=[img(D),full(w.shape),full(vec.shape)],
        out_specs=[img(3*D),img(D),img(D)],
        out_shape=[jax.ShapeDtypeStruct((n,RP,3*D),BF),jax.ShapeDtypeStruct((n,RP,D),BF),jax.ShapeDtypeStruct((n,RP,D),BF)],
        compiler_params=PAR)(h,w,vec)

def gelu_parts(u):
    c=0.5*(1.0+lax.erf(u*0.7071067811865476))
    g=c+u*(jnp.exp(-0.5*u*u)*0.3989422804014327)
    return u*c,g

def kb_kernel(FC,h_ref,o_ref,wo_ref,w1_ref,w2_ref,vec_ref,h1_ref,a_ref,e_ref,g_ref,h2_ref):
    h1=h_ref[0].astype(F32)+dot(o_ref[0],wo_ref[...])+vec_ref[4:5]
    h1_ref[0]=h1
    xc,rs=norm_stats(h1)
    a_ref[0]=(xc*rs*vec_ref[5:6]+vec_ref[6:7]).astype(BF)
    a=a_ref[0]
    h2_ref[0]=h1+vec_ref[7:8]
    for j in range(3072//FC):
        lo=FC*j
        u=dot(a,w1_ref[:,lo:lo+FC])+vec_ref[8+lo//D:9+lo//D,lo%D:lo%D+FC]
        e,g=gelu_parts(u)
        e_ref[0,:,lo:lo+FC]=e.astype(BF); g_ref[0,:,lo:lo+FC]=g.astype(BF)
        h2_ref[0]+=dot(e_ref[0,:,lo:lo+FC],w2_ref[lo:lo+FC,:])

def kb(h,o,wo,w1,w2,vec,FC=256):
    n=h.shape[0]
    S=jax.ShapeDtypeStruct
    return pl.pallas_call(functools.partial(kb_kernel,FC),grid=(n,),in_specs=[img(D),img(D),full(wo.shape),full(w1.shape),full(w2.shape),full(vec.shape)],
        out_specs=[img(D),img(D),img(3072),img(3072),img(D)],
        out_shape=[S((n,RP,D),F32),S((n,RP,D),BF),S((n,RP,3072),BF),S((n,RP,3072),BF),S((n,RP,D),F32)],
        compiler_params=PAR)(h,o,wo,w1,w2,vec)

def rsum(x): return jnp.sum(x,axis=0,keepdims=True)
def norm_back(x,gain,dy):
    xc,rs=norm_stats(x); xh=xc*rs
    dyg=dy*gain
    dx=rs*(dyg-jnp.mean(dyg,axis=-1,keepdims=True)-xh*jnp.mean(dyg*xh,axis=-1,keepdims=True))
    return dx, rsum(dy*xh), rsum(dy)

def kc_kernel(FC,d_ref,h1_ref,g_ref,wo_ref,w1_ref,w2_ref,vec_ref,db_ref,du_ref,dh1_ref,dh1b_ref,do_ref,dv_ref,acc_ref):
    @pl.when(pl.program_id(0)==0)
    def _(): dv_ref[...]=jnp.zeros_like(dv_ref)
    d=d_ref[0].astype(F32)
    db_ref[0]=d.astype(BF)
    db=db_ref[0]
    dv_ref[7:8]+=rsum(d)
    for j in range(3072//FC):
        lo=FC*j
        du=dot_t(db,w2_ref[lo:lo+FC,:])*g_ref[0,:,lo:lo+FC].astype(F32)
        dv_ref[8+lo//D:9+lo//D,lo%D:lo%D+FC]+=rsum(du)
        du_ref[0,:,lo:lo+FC]=du.astype(BF)
        t=dot_t(du_ref[0,:,lo:lo+FC],w1_ref[:,lo:lo+FC])
        if j==0: acc_ref[...]=t
        else: acc_ref[...]+=t
    dx,dg,dc=norm_back(h1_ref[0],vec_ref[5:6],acc_ref[...])
    dv_ref[5:6]+=dg; dv_ref[6:7]+=dc
    dh1=d_ref[0].astype(F32)+dx
    dh1_ref[0]=dh1
    dv_ref[4:5]+=rsum(dh1)
    dh1b_ref[0]=dh1.astype(BF)
    do_ref[0]=dot_t(dh1b_ref[0],wo_ref[...]).astype(BF)

def kc(d,h1,g,wo,w1,w2,vec,FC=256):
    n=d.shape[0]; S=jax.ShapeDtypeStruct
    return pl.pallas_call(functools.partial(kc_kernel,FC),grid=(n,),in_specs=[img(D),img(D),img(3072),full(wo.shape),full(w1.shape),full(w2.shape),full(vec.shape)],
        out_specs=[img(D),img(3072),img(D),img(D),img(D),full((16,D))],
        out_shape=[S((n,RP,D),BF),S((n,RP,3072),BF),S((n,RP,D),F32),S((n,RP,D),BF),S((n,RP,D),BF),S((16,D),F32)],
        scratch_shapes=[pltpu.VMEM((RP,D),F32)],
        compiler_params=PAR)(d,h1,g,wo,w1,w2,vec)

def kd_kernel(qkv_ref,do_ref,dz_ref,dv_ref):
    @pl.when(pl.program_id(0)==0)
    def _(): dv_ref[...]=jnp.zeros_like(dv_ref)
    for p in range(6):
        b=128*p
        dq,dk,dv=attn_bwd(qkv_ref[0,:,b:b+128],qkv_ref[0,:,D+b:D+b+128],qkv_ref[0,:,2*D+b:2*D+b+128],do_ref[0,:,b:b+128])
        dv_ref[2:3,b:b+128]+=rsum(dq); dv_ref[3:4,b:b+128]+=rsum(dv)
        dz_ref[0,:,b:b+128]=dq.astype(BF); dz_ref[0,:,D+b:D+b+128]=dk.astype(BF); dz_ref[0,:,2*D+b:2*D+b+128]=dv.astype(BF)

def kd(qkv,do):
    n=do.shape[0]; S=jax.ShapeDtypeStruct
    return pl.pallas_call(kd_kernel,grid=(n,),in_specs=[img(3*D),img(D)],out_specs=[img(3*D),full((16,D))],
        out_shape=[S((n,RP,3*D),BF),S((16,D),F32)],compiler_params=PAR)(qkv,do)

def kf_kernel(dz_ref,h_ref,dh1_ref,w_ref,vec_ref,dh_ref,dv_ref):
    @pl.when(pl.program_id(0)==0)
    def _(): dv_ref[...]=jnp.zeros_like(dv_ref)
    da=dot_t(dz_ref[0],w_ref[...])
    dx,dg,dc=norm_back(h_ref[0].astype(F32),vec_ref[0:1],da)
    dv_ref[0:1]+=dg; dv_ref[1:2]+=dc
    rows=dh_ref.shape[1]
    dh_ref[0]=(dh1_ref[0]+dx)[:rows]

def kf(dz,h,dh1,w,vec,rows=RP):
    n=dz.shape[0]; S=jax.ShapeDtypeStruct
    return pl.pallas_call(kf_kernel,grid=(n,),in_specs=[img(3*D),img(D),img(D),full(w.shape),full(vec.shape)],
        out_specs=[pl.BlockSpec((1,rows,D),lambda i:(i,0,0)),full((16,D))],
        out_shape=[S((n,rows,D),F32),S((16,D),F32)],compiler_params=PAR)(dz,h,dh1,w,vec)

def dw_kernel(l_ref,r_ref,o_ref):
    o_ref[...]=dot_0(l_ref[...],r_ref[...]).astype(BF)
def dw(l,r,MB=256):
    M=l.shape[-1]; N=r.shape[-1]; K=l.shape[0]*RP
    l=l.reshape(K,M); r=r.reshape(K,N)
    return pl.pallas_call(dw_kernel,grid=(M//MB,),in_specs=[pl.BlockSpec((K,MB),lambda i:(0,i)),pl.BlockSpec((K,N),lambda i:(0,0))],
       out_specs=pl.BlockSpec((MB,N),lambda i:(i,0)),out_shape=jax.ShapeDtypeStruct((M,N),BF),compiler_params=PAR)(l,r)


LAYERS = 2
MESH = pl.DeviceIdType.MESH
CH = 96
NC = 12


def plane():
    f = lax.axis_index("fsdp")
    core, x, y = f % 2, (f // 2) % 2, f // 4
    return f, core, x, y


def chunk_rows(c, f):
    layer, j = c // NC, c % NC
    early = 1 - (j + 9) // 12
    late = j // 8
    mid = 1 - early - late
    base = layer * NC * D
    return pl.multiple_of(base + early * (j * D + CH * f) + late * ((j - 5) * D + CH * f)
                          + mid * (7 * D + 5 * CH * f + CH * (j - 3)), 16)


def fwd_kernel(img_ref, ws_ref, vs_ref, hs_ref, qkv_ref, a1_ref, o_ref, h1_ref, a2_ref, e_ref, g_ref, enc_ref, wo_ref, vo_ref,
               w, hb, ob, ab, vg, vec, lsem, ssem, rsem, vssem, vrsem, osem, vosem):
    l, s = pl.program_id(0), pl.program_id(1)
    f, core, x, y = plane()
    fc, fx, fy = f + 1 - 2 * core, f + 2 - 4 * x, f + 4 - 8 * y
    fd = fx + fy - f

    def wrow(c, who, lo=0, n=CH):
        return w.at[pl.ds(pl.multiple_of(chunk_rows(c, who) + lo, 16), n)]

    def send(c, kind, src, dst, to):
        return pltpu.make_async_remote_copy(src_ref=src, dst_ref=dst, send_sem=ssem.at[c % 4, kind], recv_sem=rsem.at[c % 4, kind],
                                            device_id={"fsdp": to}, device_id_type=MESH)

    def kinds(c):
        own, mine, half = ws_ref.at[c], wrow(c, f), CH // 2
        return [lambda: send(c, 0, own, mine, fx), lambda: send(c, 1, own, mine, fy), lambda: send(c, 2, own, mine, fc),
                lambda: send(c, 3, wrow(c, fx, 0, half), wrow(c, fx, 0, half), fy),
                lambda: send(c, 4, wrow(c, fy, half, half), wrow(c, fy, half, half), fx),
                lambda: send(c, 5, wrow(c, fx), wrow(c, fx), fc), lambda: send(c, 6, wrow(c, fy), wrow(c, fy), fc),
                lambda: send(c, 7, wrow(c, fd), wrow(c, fd), fc), lambda: pltpu.make_async_copy(own, mine, lsem.at[c % 4])]

    def start(c, which):
        k = kinds(c)
        for i in which:
            k[i]().start()

    def wait(c, which):
        k = kinds(c)
        for i in which:
            k[i]().wait()

    def tick(t):
        @pl.when((t >= 3) & (t < 27))
        def _():
            wait(t - 3, (2, 5, 6, 7, 8))

        @pl.when((t >= 2) & (t < 26))
        def _():
            wait(t - 2, (3, 4))
            start(t - 2, (7,))

        @pl.when((t >= 1) & (t < 25))
        def _():
            wait(t - 1, (0, 1))
            start(t - 1, (3, 4, 5, 6))

        @pl.when(t < 24)
        def _():
            start(t, (0, 1, 2, 8))

    def out_copy(b, n):
        return pltpu.make_async_copy(w.at[pl.ds(b, n)], wo_ref.at[pl.ds(b, n)], osem)

    @pl.when((l == 0) & (s == 0))
    def _():
        bar = pltpu.get_barrier_semaphore()
        for k in range(1, 8):
            pl.semaphore_signal(bar, inc=1, device_id={"fsdp": (f + k) % 8}, device_id_type=MESH)
        pl.semaphore_wait(bar, 7)

        def vcopy(k):
            return pltpu.make_async_remote_copy(src_ref=vs_ref, dst_ref=vg.at[f], send_sem=vssem.at[k - 1], recv_sem=vrsem.at[k - 1],
                                                device_id={"fsdp": (f + k) % 8}, device_id_type=MESH)
        for k in range(1, 8):
            vcopy(k).start()
        vg[f] = vs_ref[...]

        @pl.loop(0, 6)
        def _(t):
            tick(t)
        for k in range(1, 8):
            vcopy(k).wait()
        for layer in range(LAYERS):
            for c in range(72):
                vec[layer, c // 6:c // 6 + 1, 128 * (c % 6):128 * (c % 6) + 128] = vg[c // 9, layer, c % 9:c % 9 + 1, :]
        hb[...] = jnp.zeros_like(hb)
        cp = pltpu.make_async_copy(vec, vo_ref, vosem)
        cp.start()
        cp.wait()

    early = (1 - l) * (s + 5) + l * (s + 17)
    late = (1 - l) * (s + 1 + s // 11 + s // 13) + l * (s + 13)

    @pl.when((s <= 5) & (l + s > 0))
    def _():
        tick(early)

    @pl.when(s >= 10)
    def _():
        tick(late)

    @pl.when(s < 5)
    def _():
        @pl.when(l == 0)
        def _():
            hb[s, 0:SEQ, :] = img_ref[s].astype(F32)
        h = hb[s]
        hs_ref[0, 0] = h
        xc, rs = norm_stats(h)
        a1_ref[0, 0] = (xc * rs * vec[l, 0:1] + vec[l, 1:2]).astype(BF)
        a = a1_ref[0, 0]
        wb = l * NC * D

        def wq(part, c):
            return w[pl.ds(pl.multiple_of(wb + part * D, 16), D), 256 * c:256 * c + 256]
        for c in range(3):
            cs = slice(256 * c, 256 * c + 256)
            qkv_ref[0, 0, :, cs] = (dot(a, wq(0, c)) + vec[l, 2:3, cs]).astype(BF)
            qkv_ref[0, 0, :, D + 256 * c:D + 256 * c + 256] = dot(a, wq(1, c)).astype(BF)
            qkv_ref[0, 0, :, 2 * D + 256 * c:2 * D + 256 * c + 256] = (dot(a, wq(2, c)) + vec[l, 3:4, cs]).astype(BF)
            for p in range(2):
                b = 256 * c + 128 * p
                o = attn_fwd(qkv_ref[0, 0, :, b:b + 128], qkv_ref[0, 0, :, D + b:D + b + 128], qkv_ref[0, 0, :, 2 * D + b:2 * D + b + 128])
                o_ref[0, 0, :, b:b + 128] = o
                ob[s, :, b:b + 128] = o

    @pl.when((s >= 5) & (s < 10))
    def _():
        i = s - 5
        wo = w[pl.ds(pl.multiple_of((l * NC + 7) * D, 16), D), :]
        h1 = hb[i] + dot(ob[i], wo) + vec[l, 4:5]
        h1_ref[0, 0] = h1
        hb[i] = h1 + vec[l, 7:8]
        xc, rs = norm_stats(h1)
        a = (xc * rs * vec[l, 5:6] + vec[l, 6:7]).astype(BF)
        a2_ref[0, 0] = a
        ab[i] = a

    @pl.when(s >= 10)
    def _():
        j = s - 10
        up = pl.multiple_of((l * NC + 3 + j) * D, 16)
        down = pl.multiple_of((l * NC + 8 + j) * D, 16)

        @pl.loop(0, 5)
        def _(i):
            @pl.when((i == 3) & (l == 0) & ((s == 10) | (s == 12)))
            def _():
                tick(12 + 3 * ((s - 10) // 2))
            for q in range(3):
                cs = slice(256 * q, 256 * q + 256)
                u = dot(ab[i], w[pl.ds(up, D), cs]) + vec[l, pl.ds(8 + j, 1), cs]
                e, g = gelu_parts(u)
                e_ref[0, i, :, cs] = e.astype(BF)
                g_ref[0, i, :, cs] = g.astype(BF)
                hb[i] += dot(e_ref[0, i, :, cs], w[pl.ds(pl.multiple_of(down + 256 * q, 16), 256), :])

            @pl.when((l == 1) & (s == 13))
            def _():
                enc_ref[i] = hb[i, 0:SEQ, :].astype(BF)

    for layer in range(LAYERS):
        base = layer * NC * D

        @pl.when((l == layer) & (s == 4))
        def _():
            out_copy(base, 3 * D).start()

        @pl.when((l == layer) & (s == 9))
        def _():
            out_copy(base + 7 * D, 5 * D).start()

        for j in range(4):
            @pl.when((l == layer) & (s == 10 + j))
            def _():
                out_copy(base + (3 + j) * D, D).start()

    @pl.when((l == 1) & (s == 13))
    def _():
        pltpu.make_async_copy(w, wo_ref, osem).wait()


def fwd(images, shard, vshard):
    n = images.shape[0]
    S = jax.ShapeDtypeStruct
    one = lambda cols: pl.BlockSpec((1, 1, RP, cols), lambda l, s: (l, jnp.minimum(s, 4), 0, 0))
    two = lambda cols: pl.BlockSpec((1, 1, RP, cols), lambda l, s: (l, jnp.clip(s - 5, 0, 4), 0, 0))
    wide = pl.BlockSpec((1, n, RP, D), lambda l, s: (l, 0, 0, jnp.clip(s - 10, 0, 3)))
    anyw = pl.BlockSpec(memory_space=pl.ANY)
    rows = LAYERS * NC * D
    return pl.pallas_call(
        fwd_kernel, grid=(LAYERS, 14),
        in_specs=[pl.BlockSpec(images.shape, lambda l, s: (0, 0, 0)), anyw, pl.BlockSpec(vshard.shape, lambda l, s: (0, 0, 0))],
        out_specs=[one(D), one(3 * D), one(D), one(D), two(D), two(D), wide, wide, pl.BlockSpec(images.shape, lambda l, s: (0, 0, 0)), anyw, anyw],
        out_shape=[S((LAYERS, n, RP, D), F32), S((LAYERS, n, RP, 3 * D), BF), S((LAYERS, n, RP, D), BF), S((LAYERS, n, RP, D), BF),
                   S((LAYERS, n, RP, D), F32), S((LAYERS, n, RP, D), BF), S((LAYERS, n, RP, 4 * D), BF), S((LAYERS, n, RP, 4 * D), BF),
                   S(images.shape, BF), S((rows, D), BF), S((LAYERS, 16, D), F32)],
        scratch_shapes=[pltpu.VMEM((rows, D), BF), pltpu.VMEM((n, RP, D), F32), pltpu.VMEM((n, RP, D), BF), pltpu.VMEM((n, RP, D), BF),
                        pltpu.VMEM((8, LAYERS, 16, 128), F32), pltpu.VMEM((LAYERS, 16, D), F32),
                        pltpu.SemaphoreType.DMA((4,)), pltpu.SemaphoreType.DMA((4, 8)), pltpu.SemaphoreType.DMA((4, 8)),
                        pltpu.SemaphoreType.DMA((7,)), pltpu.SemaphoreType.DMA((7,)), pltpu.SemaphoreType.DMA, pltpu.SemaphoreType.DMA],
        compiler_params=pltpu.CompilerParams(collective_id=0, has_side_effects=True, vmem_limit_bytes=62 * 2**20),
    )(images, shard, vshard)


def bwd_kernel(cot_ref, w_ref, vec_ref, hs_ref, h1_ref, g_ref, e_ref, qkv_ref, a2_ref, o_ref, a1_ref,
               di_ref, gin_ref, gout_ref, gv_ref,
               wk, d, db, dhb, do, du, ab, gb, dv, rc, s2, ra, rb, s3a, s3b, r3a, r3b, s4, rz, s5, ry, fin,
               vs, vr, vz, wsem, asem, ssem, rsem, osem, vssem, vrsem):
    lr, s = pl.program_id(0), pl.program_id(1)
    l = LAYERS - 1 - lr
    f, core, x, y = plane()
    z = lax.axis_index("rep")
    fc, fx, fy = f + 1 - 2 * core, f + 2 - 4 * x, f + 4 - 8 * y
    z1, z3 = z + 1 - 2 * (z % 2), 3 - z
    half = CH // 2
    rows = d.shape[0] * RP

    def load(layer, block, n, at):
        return pltpu.make_async_copy(w_ref.at[pl.ds(pl.multiple_of((layer * NC + block) * D, 16), n * D)], wk.at[pl.ds(at * D, n * D)], wsem.at[0 if at else 1])

    def fetch(src, slot):
        return pltpu.make_async_copy(src.at[l], ab.at[slot], asem.at[slot])

    def remote(kind, p, src, dst, **to):
        return pltpu.make_async_remote_copy(src_ref=src, dst_ref=dst, send_sem=ssem.at[p, kind], recv_sem=rsem.at[p, kind],
                                            device_id=to, device_id_type=MESH)

    def chunk(v):
        return v - 6 * (v // 18)

    def live(v):
        return ((v >= 0) & (v < 12)) | ((v >= 18) & (v < 30))

    def kind(n, v):
        p = v % 2
        if n == 0:
            lc = chunk(v) % NC
            return remote(0, p, gb.at[lc - 9 * (lc // 9), :, 1 - core], rc.at[p], fsdp=fc)
        if n == 1:
            return remote(1, p, s2.at[p, :, 1 - x, pl.ds(0, half)], ra.at[p], fsdp=fx)
        if n == 2:
            return remote(2, p, s2.at[p, 1 - y, :, pl.ds(half, half)], rb.at[p], fsdp=fy)
        if n == 3:
            return remote(3, p, s3a.at[p, 1 - y], r3a.at[p], fsdp=fy)
        if n == 4:
            return remote(4, p, s3b.at[p, 1 - x], r3b.at[p], fsdp=fx)
        if n == 5:
            return remote(5, p, s4.at[p], rz.at[p], rep=z1)
        return remote(6, p, s5.at[p], ry.at[p], rep=z3)

    def put(v, act):
        c = chunk(v)
        lc, layer = c % NC, LAYERS - 1 - c // NC
        p = v % 2
        out = (lc >= 4) & (lc < 9)

        @pl.when(out)
        def _():
            act(pltpu.make_async_copy(fin.at[p], gout_ref.at[layer, pl.ds(pl.multiple_of((lc - 4) * CH, 8), CH)], osem.at[p]))

        @pl.when(jnp.logical_not(out))
        def _():
            j = lc + 3 - 9 * (lc // 9)
            j = j - 3 * (lc // 9)
            act(pltpu.make_async_copy(fin.at[p], gin_ref.at[layer, :, pl.ds(pl.multiple_of(j * D, 128), D)], osem.at[p]))

    def add(a, b):
        return a.astype(F32) + b.astype(F32)

    def tick(t):
        @pl.when(live(t - 6))
        def _():
            put(t - 6, lambda a: a.wait())

        @pl.when(live(t - 5))
        def _():
            v = t - 5
            p = v % 2
            kind(6, v).wait()
            fin[p] = add(s5[p], ry[p])
            put(v, lambda a: a.start())

        @pl.when(live(t - 4))
        def _():
            v = t - 4
            p = v % 2
            kind(5, v).wait()
            s5[p] = add(s4[p], rz[p]).astype(BF)
            kind(6, v).start()

        @pl.when(live(t - 3))
        def _():
            v = t - 3
            p = v % 2
            kind(3, v).wait()
            kind(4, v).wait()
            s4[p, 0:half] = add(s3a[p, y], r3a[p]).astype(BF)
            s4[p, half:CH] = add(s3b[p, x], r3b[p]).astype(BF)
            kind(5, v).start()

        @pl.when(live(t - 2))
        def _():
            v = t - 2
            p = v % 2
            kind(1, v).wait()
            kind(2, v).wait()
            for i in range(2):
                s3a[p, i] = add(s2[p, i, x, 0:half], ra[p, i]).astype(BF)
                s3b[p, i] = add(s2[p, y, i, half:CH], rb[p, i]).astype(BF)
            kind(3, v).start()
            kind(4, v).start()

        @pl.when(live(t - 1))
        def _():
            v = t - 1
            p = v % 2
            kind(0, v).wait()
            lc = chunk(v) % NC
            for i in range(4):
                s2[p, i // 2, i % 2] = add(gb[lc - 9 * (lc // 9), i, core], rc[p, i]).astype(BF)
            kind(1, v).start()
            kind(2, v).start()

        @pl.when(live(t))
        def _():
            kind(0, t).start()

    @pl.when((lr == 0) & (s == 0))
    def _():
        load(l, 3, 9, 0).start()
        bar = pltpu.get_barrier_semaphore()
        for k in range(1, 8):
            pl.semaphore_signal(bar, inc=1, device_id={"fsdp": (f + k) % 8}, device_id_type=MESH)
        for k in range(1, 4):
            pl.semaphore_signal(bar, inc=1, device_id={"rep": (z + k) % 4}, device_id_type=MESH)
        pl.semaphore_wait(bar, 10)
        dv[...] = jnp.zeros_like(dv)
        load(l, 3, 9, 0).wait()

    @pl.when((lr == 1) & (s == 0))
    def _():
        load(l, 3, 3, 0).start()
        load(l, 3, 3, 0).wait()
        load(l, 6, 6, 3).wait()

    @pl.when(s == 0)
    def _():
        fetch(a2_ref, 0).start()
        fetch(o_ref, 1).start()

    @pl.when(s == 5)
    def _():
        fetch(a2_ref, 0).wait()
        load(l, 0, 3, 0).start()

        @pl.when(lr == 0)
        def _():
            load(l - 1, 6, 6, 3).start()

    @pl.when(s == 9)
    def _():
        fetch(o_ref, 1).wait()

    @pl.when(s == 10)
    def _():
        fetch(a1_ref, 0).start()

    @pl.when(s == 19)
    def _():
        fetch(a1_ref, 0).wait()

    @pl.when(s == 22)
    def _():
        load(l, 0, 3, 0).wait()

    even = 1 - s % 2
    first = (s >= 6) & (s <= 12) & (even == 1)
    second = (s >= 14) & (s <= 18)
    third = (s >= 20) & ((even == 1) | (lr == 1))
    start = (s <= 4) & (lr == 1)
    t = jnp.where(first, 18 * lr + (s - 6) // 2, jnp.where(second, 18 * lr + s - 10, jnp.where(start, 13 + s, lr * (s + 7) + (1 - lr) * ((s - 20) // 2 + 9))))

    @pl.when(first | second | third | start)
    def _():
        tick(t)

    @pl.when(s < 5)
    def _():
        i = s

        @pl.when(lr == 0)
        def _():
            d[i] = jnp.zeros((RP, D), F32)
            d[i, 0:SEQ, :] = cot_ref[0].astype(F32)
        up = d[i]
        db[i] = up.astype(BF)
        dv[l, 7:8] += rsum(up)
        acc = None
        for j in range(12):
            cs = slice(256 * j, 256 * j + 256)
            r = (5 * D + 256 * j)
            t1 = dot_t(db[i], wk[r:r + 256, :]) * g_ref[0, 0, :, cs].astype(F32)
            dv[l, 8 + j // 3:9 + j // 3, 256 * (j % 3):256 * (j % 3) + 256] += rsum(t1)
            du[i, :, cs] = t1.astype(BF)
            t2 = dot_t(du[i, :, cs], wk[(j // 3) * D:(j // 3) * D + D, 256 * (j % 3):256 * (j % 3) + 256])
            acc = t2 if acc is None else acc + t2
        dx, dg, dc = norm_back(h1_ref[0, 0], vec_ref[l, 5:6], acc)
        dv[l, 5:6] += dg
        dv[l, 6:7] += dc
        dh1 = d[i] + dx
        d[i] = dh1
        dv[l, 4:5] += rsum(dh1)
        dhb[i] = dh1.astype(BF)
        do[i] = dot_t(dhb[i], wk[4 * D:5 * D, :]).astype(BF)

    def grad(lhs, rhs, store):
        for m in range(2):
            r = dot_0(lhs(384 * m), rhs).astype(BF).reshape(4, CH, D)
            store(4 * m, r)

    def inner(slot, j):
        def store(m, r):
            gb[slot, m // 2, 0] = r[0]
            gb[slot, m // 2, 1] = r[1]
            gb[slot, m // 2 + 1, 0] = r[2]
            gb[slot, m // 2 + 1, 1] = r[3]
        grad(lambda m: ab[0, :, :, m:m + 384].reshape(rows, 384), du[:, :, pl.ds(pl.multiple_of(D * j, 128), D)].reshape(rows, D), store)

    def outer(step, lhs, rhs):
        def store(m, r):
            for q in range(4):
                b = 8 * step + m + q
                gb[4 + b % 5, b // 10, (b // 5) % 2] = r[q]
        grad(lhs, rhs[...].reshape(rows, D), store)

    @pl.when((s >= 5) & (s < 9))
    def _():
        inner(s - 5, s - 5)

    @pl.when(s == 9)
    def _():
        outer(0, lambda m: ab[1, :, :, m:m + 384].reshape(rows, 384), dhb)

    @pl.when((s >= 10) & (s < 14))
    def _():
        outer(s - 9, lambda m: e_ref[0, :, :, m:m + 384].reshape(rows, 384), db)

    @pl.when((s >= 14) & (s < 19))
    def _():
        i = s - 14
        for p in range(6):
            b = 128 * p
            dq, dk, dvv = attn_bwd(qkv_ref[0, 0, :, b:b + 128], qkv_ref[0, 0, :, D + b:D + b + 128], qkv_ref[0, 0, :, 2 * D + b:2 * D + b + 128],
                                   do[i, :, b:b + 128])
            dv[l, 2:3, b:b + 128] += rsum(dq)
            dv[l, 3:4, b:b + 128] += rsum(dvv)
            du[i, :, b:b + 128] = dq.astype(BF)
            du[i, :, D + b:D + b + 128] = dk.astype(BF)
            du[i, :, 2 * D + b:2 * D + b + 128] = dvv.astype(BF)

    @pl.when((s >= 19) & (s < 22))
    def _():
        inner(s - 19, s - 19)

    @pl.when(s >= 22)
    def _():
        i = s - 22
        da = dot_t(du[i, :, 0:D], wk[0:D, :]) + dot_t(du[i, :, D:2 * D], wk[D:2 * D, :]) + dot_t(du[i, :, 2 * D:3 * D], wk[2 * D:3 * D, :])
        dx, dg, dc = norm_back(hs_ref[0, 0], vec_ref[l, 0:1], da)
        dv[l, 0:1] += dg
        dv[l, 1:2] += dc
        dh = d[i] + dx
        d[i] = dh
        di_ref[0] = dh[0:SEQ]

    @pl.when((lr == 1) & (s == 26))
    def _():
        for layer in range(LAYERS):
            for c in range(72):
                vs[c // 9, layer, c % 9:c % 9 + 1, :] = dv[layer, c // 6:c // 6 + 1, 128 * (c % 6):128 * (c % 6) + 128]

        def vcopy(k):
            to = (f + k) % 8
            return pltpu.make_async_remote_copy(src_ref=vs.at[to], dst_ref=vr.at[k - 1], send_sem=vssem.at[k - 1], recv_sem=vrsem.at[k - 1],
                                                device_id={"fsdp": to}, device_id_type=MESH)

        def zcopy(k):
            return pltpu.make_async_remote_copy(src_ref=vz.at[z], dst_ref=vz.at[z], send_sem=vssem.at[6 + k], recv_sem=vrsem.at[6 + k],
                                                device_id={"rep": (z + k) % 4}, device_id_type=MESH)
        for k in range(1, 8):
            vcopy(k).start()
        tick(34)
        for k in range(1, 8):
            vcopy(k).wait()
        total = vs[f]
        for k in range(7):
            total = total + vr[k]
        vz[z] = total
        for k in range(1, 4):
            zcopy(k).start()
        for k in range(1, 4):
            zcopy(k).wait()
        gv_ref[...] = (vz[0] + vz[1]) + (vz[2] + vz[3])
        put(29, lambda a: a.wait())


def bwd(cotangent, w, vec, hs, h1, g, e, qkv, a2, o, a1, shard_in, shard_out):
    n = cotangent.shape[0]
    S = jax.ShapeDtypeStruct
    anyw = pl.BlockSpec(memory_space=pl.ANY)
    row = lambda cols, at: pl.BlockSpec((1, 1, RP, cols), lambda lr, s: (LAYERS - 1 - lr, jnp.clip(s - at, 0, 4), 0, 0))
    tok = lambda index: pl.BlockSpec((1, SEQ, D), index)
    VB = lambda *shape: pltpu.VMEM(shape, BF)
    half = CH // 2
    return pl.pallas_call(
        bwd_kernel, grid=(LAYERS, 27),
        in_specs=[tok(lambda lr, s: (jnp.minimum(s + 4 * lr, 4), 0, 0)), anyw, pl.BlockSpec(vec.shape, lambda lr, s: (0, 0, 0)),
                  row(D, 22), row(D, 0), row(4 * D, 0),
                  pl.BlockSpec((1, n, RP, D), lambda lr, s: (LAYERS - 1 - lr, 0, 0, jnp.clip(s - 10, 0, 3))),
                  row(3 * D, 14), anyw, anyw, anyw],
        out_specs=[tok(lambda lr, s: (lr * jnp.clip(s - 22, 0, 4), 0, 0)), anyw, anyw, pl.BlockSpec((LAYERS, 16, 128), lambda lr, s: (0, 0, 0))],
        out_shape=[S(cotangent.shape, F32), S(shard_in, F32), S(shard_out, F32), S((LAYERS, 16, 128), F32)],
        scratch_shapes=[VB(9 * D, D), pltpu.VMEM((n, RP, D), F32), VB(n, RP, D), VB(n, RP, D), VB(n, RP, D), VB(n, RP, 4 * D), VB(2, n, RP, D),
                        VB(9, 4, 2, CH, D), pltpu.VMEM((LAYERS, 16, D), F32),
                        VB(2, 4, CH, D), VB(2, 2, 2, CH, D), VB(2, 2, half, D), VB(2, 2, half, D), VB(2, 2, half, D), VB(2, 2, half, D),
                        VB(2, half, D), VB(2, half, D), VB(2, CH, D), VB(2, CH, D), VB(2, CH, D), VB(2, CH, D), pltpu.VMEM((2, CH, D), F32),
                        pltpu.VMEM((8, LAYERS, 16, 128), F32), pltpu.VMEM((7, LAYERS, 16, 128), F32), pltpu.VMEM((4, LAYERS, 16, 128), F32),
                        pltpu.SemaphoreType.DMA((2,)), pltpu.SemaphoreType.DMA((2,)), pltpu.SemaphoreType.DMA((2, 7)), pltpu.SemaphoreType.DMA((2, 7)),
                        pltpu.SemaphoreType.DMA((2,)), pltpu.SemaphoreType.DMA((10,)), pltpu.SemaphoreType.DMA((10,))],
        compiler_params=pltpu.CompilerParams(collective_id=1, has_side_effects=True, vmem_limit_bytes=63 * 2**20),
    )(cotangent, w, vec, hs, h1, g, e, qkv, a2, o, a1)


STEP = 3
beta_one = 0.9
beta_two = 0.999
matrix_rate = 0.03
vector_rate = 0.2
matrix_decay = 0.05
adam_eps = 1e-8


def adam_update(master, gradient, moment_one, moment_two, rate, decay_rate):
    moment_one = beta_one * moment_one + (1.0 - beta_one) * gradient
    moment_two = beta_two * moment_two + (1.0 - beta_two) * gradient * gradient
    corr_one = 1.0 - beta_one**STEP
    corr_two = 1.0 - beta_two**STEP
    adam_move = moment_one / corr_one / (jnp.sqrt(moment_two / corr_two) + adam_eps)
    return (master - rate * (adam_move + decay_rate * master), moment_one, moment_two)


def swap(x, axis, size, mask):
    return lax.ppermute(x, axis, [(i, i ^ mask) for i in range(size)])


def halve(x, order, size):
    bits = size.bit_length() - 1
    me = lax.axis_index("fsdp")
    x = x.reshape((2,) * bits + x.shape[1:])
    left = list(range(bits))[::-1]
    for bit in order:
        at = left.index(bit)
        mine = (me >> bit) & 1
        keep = lax.dynamic_index_in_dim(x, mine, at, keepdims=False)
        send = lax.dynamic_index_in_dim(x, 1 - mine, at, keepdims=False)
        got = swap(send, "fsdp", size, 1 << bit)
        x = (keep.astype(F32) + got.astype(F32)).astype(BF)
        left.remove(bit)
    return x


def reduce_all(x, nf, nr):
    bits = nf.bit_length() - 1
    rows, cols = x.shape
    x = x.reshape(nf, rows // nf, cols)
    half = cols // 2 // 128 * 128
    up = [0] + list(range(1, bits))
    down = [0] + list(range(1, bits))[::-1]
    x = jnp.concatenate([halve(x[..., :half], up, nf), halve(x[..., half:], down, nf)], axis=-1)
    mask = 1
    while mask < nr:
        got = swap(x, "rep", nr, 2 * mask - 1)
        y = x.astype(F32) + got.astype(F32)
        x = y.astype(BF)
        mask *= 2
    return y


def own_shard(weight_in, weight_out):
    a = weight_in.astype(BF).reshape(LAYERS, CH, 7, D).transpose(0, 2, 1, 3)
    b = weight_out.astype(BF).reshape(LAYERS, 5, CH, D)
    return jnp.concatenate([a[:, :3], b, a[:, 3:]], axis=1).reshape(LAYERS * NC, CH, D)


def fused_step(images, cotangent, weight_in, weight_out, vector_params):
    vs = jnp.pad(vector_params.astype(BF).astype(F32).reshape(LAYERS, 9, 128), ((0, 0), (0, 7), (0, 0)))
    hs, qkv, a1, o, h1, a2, e, g, encoded, w, vec = fwd(images, own_shard(weight_in, weight_out), vs)
    dimg, gi, go, gv = bwd(cotangent, w, vec, hs, h1, g, e, qkv, a2, o, a1, weight_in.shape, weight_out.shape)
    return encoded, dimg, gi, go, gv[:, :9].reshape(vector_params.shape)


def plain_step(nf, nr, images, cotangent, weight_in, weight_out, vector_params):
    pad = lambda a: jnp.pad(a, ((0, 0), (0, RP - SEQ), (0, 0)))
    vec_all = lax.all_gather(vector_params.astype(BF), "fsdp", axis=1, tiled=True).astype(F32)
    h = pad(images)
    ct = pad(cotangent)
    saved = []
    for l in range(LAYERS):
        win = lax.all_gather(weight_in[l].astype(BF), "fsdp", axis=0, tiled=True)
        wout = lax.all_gather(weight_out[l].astype(BF), "fsdp", axis=0, tiled=True)
        vec = jnp.pad(vec_all[l].reshape(12, D), ((0, 4), (0, 0)))
        wqkv, w1, wo, w2 = win[:, : 3 * D], win[:, 3 * D :], wout[:D], wout[D:]
        qkv, o, a1 = ka(h, wqkv, vec)
        h1, a2, e, g, h2 = kb(h, o, wo, w1, w2, vec)
        saved.append((h, wqkv, w1, wo, w2, vec, qkv, o, a1, h1, a2, e, g))
        h = h2
    encoded = h[:, :SEQ].astype(BF)
    d = ct
    gin, gout, gvec = [None] * LAYERS, [None] * LAYERS, [None] * LAYERS
    for l in reversed(range(LAYERS)):
        h, wqkv, w1, wo, w2, vec, qkv, o, a1, h1, a2, e, g = saved[l]
        db, du, dh1, dh1b, do, dv1 = kc(d, h1, g, wo, w1, w2, vec)
        g1 = reduce_all(dw(a2, du), nf, nr)
        go = reduce_all(jnp.concatenate([dw(o, dh1b), dw(e, db)], axis=0), nf, nr)
        dz, dv2 = kd(qkv, do)
        gq = reduce_all(dw(a1, dz), nf, nr)
        d, dv3 = kf(dz, h, dh1, wqkv, vec, RP if l else SEQ)
        gin[l] = jnp.concatenate([gq, g1], axis=1)
        gout[l] = go
        gvec[l] = (dv1 + dv2 + dv3)[:12].reshape(-1)
    gv = lax.psum(jnp.stack(gvec), ("fsdp", "rep"))
    wide = gv.shape[1] // nf
    gv = lax.dynamic_slice_in_dim(gv, lax.axis_index("fsdp") * wide, wide, 1)
    return encoded, d, jnp.stack(gin), jnp.stack(gout), gv


def make_shards(nf, nr):
    def shards(images, cotangent, weight_in, weight_out, vector_params, first_in, first_out, first_vec, second_in, second_out, second_vec):
        if nf == 8 and nr == 4:
            encoded, d, gi, go, gv = fused_step(images, cotangent, weight_in, weight_out, vector_params)
        else:
            encoded, d, gi, go, gv = plain_step(nf, nr, images, cotangent, weight_in, weight_out, vector_params)
        new_in, moment_in, square_in = adam_update(weight_in, gi, first_in, second_in, matrix_rate, matrix_decay)
        new_out, moment_out, square_out = adam_update(weight_out, go, first_out, second_out, matrix_rate, matrix_decay)
        new_vec, moment_vec, square_vec = adam_update(vector_params, gv, first_vec, second_vec, vector_rate, 0.0)
        return (encoded, d, gi, go, gv, new_in, new_out, new_vec, moment_in, moment_out, moment_vec, square_in, square_out, square_vec)

    return shards


def solution(mesh):
    tokens = P(("fsdp", "rep"), None, None)
    matrix = P(None, "fsdp", None)
    vector = P(None, "fsdp")
    in_specs = (tokens, tokens) + (matrix, matrix, vector) * 3
    out_specs = (tokens, tokens) + (matrix, matrix, vector) * 4
    return jax.shard_map(make_shards(mesh.shape["fsdp"], mesh.shape["rep"]), mesh=mesh, in_specs=in_specs, out_specs=out_specs, check_vma=False)
```

```python
import functools
import jax, jax.numpy as jnp
from jax import lax
from jax.experimental import pallas as pl
from jax.experimental.pallas import tpu as pltpu
from jax.sharding import PartitionSpec as P

D=768; HD=64; SEQ=197; RP=208; EPS=1e-6
BF=jnp.bfloat16; F32=jnp.float32
def dot(a,b): return jnp.dot(a,b,preferred_element_type=F32)
def dot_t(a,b): return lax.dot_general(a,b,(((1,),(1,)),((),())),preferred_element_type=F32)
def dot_0(a,b): return lax.dot_general(a,b,(((0,),(0,)),((),())),preferred_element_type=F32)

def norm_stats(x):
    mean=jnp.mean(x,axis=-1,keepdims=True); xc=x-mean
    var=jnp.mean(xc*xc,axis=-1,keepdims=True)
    return xc, lax.rsqrt(var+EPS)

def attn_fwd(q,k,v):
    lane=lax.broadcasted_iota(jnp.int32,(1,128),1)
    col=lax.broadcasted_iota(jnp.int32,(1,RP),1)
    os=[]
    for half in range(2):
        m=jnp.where((lane<64) if half==0 else (lane>=64),0.125,0.0).astype(BF)
        s=dot_t(q*m,k)
        s=jnp.where(col<SEQ,s,-1e30)
        mx=jnp.max(s,axis=-1,keepdims=True)
        e=jnp.exp(s-mx)
        p=(e*(1.0/jnp.sum(e,axis=-1,keepdims=True))).astype(BF)
        os.append(dot(p,v))
    return jnp.where(lane<64,os[0],os[1]).astype(BF)

def attn_bwd(q,k,v,do):
    lane=lax.broadcasted_iota(jnp.int32,(1,128),1)
    row=lax.broadcasted_iota(jnp.int32,(RP,1),0)
    r=[]
    for half in range(2):
        sel=(lane<64) if half==0 else (lane>=64)
        m=jnp.where(sel,0.125,0.0).astype(BF)
        m1=jnp.where(sel,1.0,0.0).astype(BF)
        qs=q*m
        s=dot_t(k,qs)
        s=jnp.where(row<SEQ,s,-1e30)
        mx=jnp.max(s,axis=0,keepdims=True)
        e=jnp.exp(s-mx)
        p=e*(1.0/jnp.sum(e,axis=0,keepdims=True))
        pb=p.astype(BF)
        dp=dot_t(v,do*m1)
        dl=jnp.sum(p*dp,axis=0,keepdims=True)
        ds=(p*(dp-dl)).astype(BF)
        dv=dot(pb,do)
        dk=dot(ds,qs)
        dq=dot_0(ds,k)*0.125
        r.append((dq,dk,dv))
    return tuple(jnp.where(lane<64,a,b) for a,b in zip(*r))

def ka_kernel(h_ref,w_ref,vec_ref,qkv_ref,o_ref,a_ref):
    h=h_ref[0].astype(F32)
    xc,rs=norm_stats(h)
    a_ref[0]=(xc*rs*vec_ref[0:1]+vec_ref[1:2]).astype(BF)
    a=a_ref[0]
    for c in range(3):
        cs=slice(256*c,256*c+256)
        qkv_ref[0,:,256*c:256*c+256]=(dot(a,w_ref[:,256*c:256*c+256])+vec_ref[2:3,cs]).astype(BF)
        qkv_ref[0,:,D+256*c:D+256*c+256]=dot(a,w_ref[:,D+256*c:D+256*c+256]).astype(BF)
        qkv_ref[0,:,2*D+256*c:2*D+256*c+256]=(dot(a,w_ref[:,2*D+256*c:2*D+256*c+256])+vec_ref[3:4,cs]).astype(BF)
        for p in range(2):
            b=256*c+128*p
            o_ref[0,:,b:b+128]=attn_fwd(qkv_ref[0,:,b:b+128],qkv_ref[0,:,D+b:D+b+128],qkv_ref[0,:,2*D+b:2*D+b+128])

def img(n,dt=None): return pl.BlockSpec((1,RP,n),lambda i:(i,0,0))
def full(shape): return pl.BlockSpec(shape,lambda i:(0,)*len(shape))
PAR=pltpu.CompilerParams(vmem_limit_bytes=60*2**20)

def ka(h,w,vec):
    n=h.shape[0]
    return pl.pallas_call(ka_kernel,grid=(n,),in_specs=[img(D),full(w.shape),full(vec.shape)],
        out_specs=[img(3*D),img(D),img(D)],
        out_shape=[jax.ShapeDtypeStruct((n,RP,3*D),BF),jax.ShapeDtypeStruct((n,RP,D),BF),jax.ShapeDtypeStruct((n,RP,D),BF)],
        compiler_params=PAR)(h,w,vec)

def gelu_parts(u):
    c=0.5*(1.0+lax.erf(u*0.7071067811865476))
    g=c+u*(jnp.exp(-0.5*u*u)*0.3989422804014327)
    return u*c,g

def kb_kernel(FC,h_ref,o_ref,wo_ref,w1_ref,w2_ref,vec_ref,h1_ref,a_ref,e_ref,g_ref,h2_ref):
    h1=h_ref[0].astype(F32)+dot(o_ref[0],wo_ref[...])+vec_ref[4:5]
    h1_ref[0]=h1
    xc,rs=norm_stats(h1)
    a_ref[0]=(xc*rs*vec_ref[5:6]+vec_ref[6:7]).astype(BF)
    a=a_ref[0]
    h2_ref[0]=h1+vec_ref[7:8]
    for j in range(3072//FC):
        lo=FC*j
        u=dot(a,w1_ref[:,lo:lo+FC])+vec_ref[8+lo//D:9+lo//D,lo%D:lo%D+FC]
        e,g=gelu_parts(u)
        e_ref[0,:,lo:lo+FC]=e.astype(BF); g_ref[0,:,lo:lo+FC]=g.astype(BF)
        h2_ref[0]+=dot(e_ref[0,:,lo:lo+FC],w2_ref[lo:lo+FC,:])

def kb(h,o,wo,w1,w2,vec,FC=256):
    n=h.shape[0]
    S=jax.ShapeDtypeStruct
    return pl.pallas_call(functools.partial(kb_kernel,FC),grid=(n,),in_specs=[img(D),img(D),full(wo.shape),full(w1.shape),full(w2.shape),full(vec.shape)],
        out_specs=[img(D),img(D),img(3072),img(3072),img(D)],
        out_shape=[S((n,RP,D),F32),S((n,RP,D),BF),S((n,RP,3072),BF),S((n,RP,3072),BF),S((n,RP,D),F32)],
        compiler_params=PAR)(h,o,wo,w1,w2,vec)

def rsum(x): return jnp.sum(x,axis=0,keepdims=True)
def norm_back(x,gain,dy):
    xc,rs=norm_stats(x); xh=xc*rs
    dyg=dy*gain
    dx=rs*(dyg-jnp.mean(dyg,axis=-1,keepdims=True)-xh*jnp.mean(dyg*xh,axis=-1,keepdims=True))
    return dx, rsum(dy*xh), rsum(dy)

def kc_kernel(FC,d_ref,h1_ref,g_ref,wo_ref,w1_ref,w2_ref,vec_ref,db_ref,du_ref,dh1_ref,dh1b_ref,do_ref,dv_ref,acc_ref):
    @pl.when(pl.program_id(0)==0)
    def _(): dv_ref[...]=jnp.zeros_like(dv_ref)
    d=d_ref[0].astype(F32)
    db_ref[0]=d.astype(BF)
    db=db_ref[0]
    dv_ref[7:8]+=rsum(d)
    for j in range(3072//FC):
        lo=FC*j
        du=dot_t(db,w2_ref[lo:lo+FC,:])*g_ref[0,:,lo:lo+FC].astype(F32)
        dv_ref[8+lo//D:9+lo//D,lo%D:lo%D+FC]+=rsum(du)
        du_ref[0,:,lo:lo+FC]=du.astype(BF)
        t=dot_t(du_ref[0,:,lo:lo+FC],w1_ref[:,lo:lo+FC])
        if j==0: acc_ref[...]=t
        else: acc_ref[...]+=t
    dx,dg,dc=norm_back(h1_ref[0],vec_ref[5:6],acc_ref[...])
    dv_ref[5:6]+=dg; dv_ref[6:7]+=dc
    dh1=d_ref[0].astype(F32)+dx
    dh1_ref[0]=dh1
    dv_ref[4:5]+=rsum(dh1)
    dh1b_ref[0]=dh1.astype(BF)
    do_ref[0]=dot_t(dh1b_ref[0],wo_ref[...]).astype(BF)

def kc(d,h1,g,wo,w1,w2,vec,FC=256):
    n=d.shape[0]; S=jax.ShapeDtypeStruct
    return pl.pallas_call(functools.partial(kc_kernel,FC),grid=(n,),in_specs=[img(D),img(D),img(3072),full(wo.shape),full(w1.shape),full(w2.shape),full(vec.shape)],
        out_specs=[img(D),img(3072),img(D),img(D),img(D),full((16,D))],
        out_shape=[S((n,RP,D),BF),S((n,RP,3072),BF),S((n,RP,D),F32),S((n,RP,D),BF),S((n,RP,D),BF),S((16,D),F32)],
        scratch_shapes=[pltpu.VMEM((RP,D),F32)],
        compiler_params=PAR)(d,h1,g,wo,w1,w2,vec)

def kd_kernel(qkv_ref,do_ref,dz_ref,dv_ref):
    @pl.when(pl.program_id(0)==0)
    def _(): dv_ref[...]=jnp.zeros_like(dv_ref)
    for p in range(6):
        b=128*p
        dq,dk,dv=attn_bwd(qkv_ref[0,:,b:b+128],qkv_ref[0,:,D+b:D+b+128],qkv_ref[0,:,2*D+b:2*D+b+128],do_ref[0,:,b:b+128])
        dv_ref[2:3,b:b+128]+=rsum(dq); dv_ref[3:4,b:b+128]+=rsum(dv)
        dz_ref[0,:,b:b+128]=dq.astype(BF); dz_ref[0,:,D+b:D+b+128]=dk.astype(BF); dz_ref[0,:,2*D+b:2*D+b+128]=dv.astype(BF)

def kd(qkv,do):
    n=do.shape[0]; S=jax.ShapeDtypeStruct
    return pl.pallas_call(kd_kernel,grid=(n,),in_specs=[img(3*D),img(D)],out_specs=[img(3*D),full((16,D))],
        out_shape=[S((n,RP,3*D),BF),S((16,D),F32)],compiler_params=PAR)(qkv,do)

def kf_kernel(dz_ref,h_ref,dh1_ref,w_ref,vec_ref,dh_ref,dv_ref):
    @pl.when(pl.program_id(0)==0)
    def _(): dv_ref[...]=jnp.zeros_like(dv_ref)
    da=dot_t(dz_ref[0],w_ref[...])
    dx,dg,dc=norm_back(h_ref[0].astype(F32),vec_ref[0:1],da)
    dv_ref[0:1]+=dg; dv_ref[1:2]+=dc
    rows=dh_ref.shape[1]
    dh_ref[0]=(dh1_ref[0]+dx)[:rows]

def kf(dz,h,dh1,w,vec,rows=RP):
    n=dz.shape[0]; S=jax.ShapeDtypeStruct
    return pl.pallas_call(kf_kernel,grid=(n,),in_specs=[img(3*D),img(D),img(D),full(w.shape),full(vec.shape)],
        out_specs=[pl.BlockSpec((1,rows,D),lambda i:(i,0,0)),full((16,D))],
        out_shape=[S((n,rows,D),F32),S((16,D),F32)],compiler_params=PAR)(dz,h,dh1,w,vec)

def dw_kernel(l_ref,r_ref,o_ref):
    o_ref[...]=dot_0(l_ref[...],r_ref[...]).astype(BF)
def dw(l,r,MB=256):
    M=l.shape[-1]; N=r.shape[-1]; K=l.shape[0]*RP
    l=l.reshape(K,M); r=r.reshape(K,N)
    return pl.pallas_call(dw_kernel,grid=(M//MB,),in_specs=[pl.BlockSpec((K,MB),lambda i:(0,i)),pl.BlockSpec((K,N),lambda i:(0,0))],
       out_specs=pl.BlockSpec((MB,N),lambda i:(i,0)),out_shape=jax.ShapeDtypeStruct((M,N),BF),compiler_params=PAR)(l,r)


LAYERS = 2
MESH = pl.DeviceIdType.MESH
CH = 96
NC = 12


def plane():
    f = lax.axis_index("fsdp")
    core, x, y = f % 2, (f // 2) % 2, f // 4
    return f, core, x, y


def chunk_rows(c, f):
    layer, j = c // NC, c % NC
    early = 1 - (j + 9) // 12
    late = j // 8
    mid = 1 - early - late
    base = layer * NC * D
    return pl.multiple_of(base + early * (j * D + CH * f) + late * ((j - 5) * D + CH * f)
                          + mid * (7 * D + 5 * CH * f + CH * (j - 3)), 16)


def fwd_kernel(img_ref, ws_ref, vs_ref, hs_ref, qkv_ref, a1_ref, o_ref, h1_ref, a2_ref, e_ref, g_ref, enc_ref, wo_ref, vo_ref,
               w, hb, ob, ab, vg, vec, lsem, ssem, rsem, vssem, vrsem, osem, vosem):
    l, s = pl.program_id(0), pl.program_id(1)
    f, core, x, y = plane()
    fc, fx, fy = f + 1 - 2 * core, f + 2 - 4 * x, f + 4 - 8 * y
    fd = fx + fy - f

    def wrow(c, who, lo=0, n=CH):
        return w.at[pl.ds(pl.multiple_of(chunk_rows(c, who) + lo, 16), n)]

    def send(c, kind, src, dst, to):
        return pltpu.make_async_remote_copy(src_ref=src, dst_ref=dst, send_sem=ssem.at[c % 8, kind], recv_sem=rsem.at[c % 8, kind],
                                            device_id={"fsdp": to}, device_id_type=MESH)

    def kinds(c):
        own, mine, half = ws_ref.at[c], wrow(c, f), CH // 2
        return [lambda: send(c, 0, own, mine, fx), lambda: send(c, 1, own, mine, fy), lambda: send(c, 2, own, mine, fc),
                lambda: send(c, 3, wrow(c, fx, 0, half), wrow(c, fx, 0, half), fy),
                lambda: send(c, 4, wrow(c, fy, half, half), wrow(c, fy, half, half), fx),
                lambda: send(c, 5, wrow(c, fx), wrow(c, fx), fc), lambda: send(c, 6, wrow(c, fy), wrow(c, fy), fc),
                lambda: send(c, 7, wrow(c, fd), wrow(c, fd), fc), lambda: pltpu.make_async_copy(own, mine, lsem.at[c % 8])]

    def start(c, which):
        k = kinds(c)
        for i in which:
            k[i]().start()

    def wait(c, which):
        k = kinds(c)
        for i in which:
            k[i]().wait()

    def tick(t):
        @pl.when((t >= 4) & (t < 28))
        def _():
            wait(t - 4, (2, 5, 6, 7, 8))

        @pl.when((t >= 3) & (t < 27))
        def _():
            wait(t - 3, (3, 4))
            start(t - 3, (7,))

        @pl.when((t >= 2) & (t < 26))
        def _():
            wait(t - 2, (0, 1))
            start(t - 2, (3, 4, 5, 6))

        @pl.when(t < 24)
        def _():
            start(t, (0, 1, 2, 8))

    def out_copy(b, n):
        return pltpu.make_async_copy(w.at[pl.ds(b, n)], wo_ref.at[pl.ds(b, n)], osem)

    @pl.when((l == 0) & (s == 0))
    def _():
        bar = pltpu.get_barrier_semaphore()
        for k in range(1, 8):
            pl.semaphore_signal(bar, inc=1, device_id={"fsdp": (f + k) % 8}, device_id_type=MESH)
        pl.semaphore_wait(bar, 7)

        def vcopy(k):
            return pltpu.make_async_remote_copy(src_ref=vs_ref, dst_ref=vg.at[f], send_sem=vssem.at[k - 1], recv_sem=vrsem.at[k - 1],
                                                device_id={"fsdp": (f + k) % 8}, device_id_type=MESH)
        for k in range(1, 8):
            vcopy(k).start()
        vg[f] = vs_ref[...]

        @pl.loop(0, 7)
        def _(t):
            tick(t)
        for k in range(1, 8):
            vcopy(k).wait()
        for layer in range(LAYERS):
            for c in range(72):
                vec[layer, c // 6:c // 6 + 1, 128 * (c % 6):128 * (c % 6) + 128] = vg[c // 9, layer, c % 9:c % 9 + 1, :]
        hb[...] = jnp.zeros_like(hb)
        cp = pltpu.make_async_copy(vec, vo_ref, vosem)
        cp.start()
        cp.wait()

    early = (1 - l) * (s + 6) + l * (s + 18)
    late = (1 - l) * (s + 2 + s // 11 + s // 13) + l * (s + 14)

    @pl.when((s <= 5) & (l + s > 0))
    def _():
        tick(early)

    @pl.when(s >= 10)
    def _():
        tick(late)

    @pl.when(s < 5)
    def _():
        @pl.when(l == 0)
        def _():
            hb[s, 0:SEQ, :] = img_ref[s].astype(F32)
        h = hb[s]
        hs_ref[0, 0] = h
        xc, rs = norm_stats(h)
        a1_ref[0, 0] = (xc * rs * vec[l, 0:1] + vec[l, 1:2]).astype(BF)
        a = a1_ref[0, 0]
        wb = l * NC * D

        def wq(part, c):
            return w[pl.ds(pl.multiple_of(wb + part * D, 16), D), 256 * c:256 * c + 256]
        for c in range(3):
            cs = slice(256 * c, 256 * c + 256)
            qkv_ref[0, 0, :, cs] = (dot(a, wq(0, c)) + vec[l, 2:3, cs]).astype(BF)
            qkv_ref[0, 0, :, D + 256 * c:D + 256 * c + 256] = dot(a, wq(1, c)).astype(BF)
            qkv_ref[0, 0, :, 2 * D + 256 * c:2 * D + 256 * c + 256] = (dot(a, wq(2, c)) + vec[l, 3:4, cs]).astype(BF)
            for p in range(2):
                b = 256 * c + 128 * p
                o = attn_fwd(qkv_ref[0, 0, :, b:b + 128], qkv_ref[0, 0, :, D + b:D + b + 128], qkv_ref[0, 0, :, 2 * D + b:2 * D + b + 128])
                o_ref[0, 0, :, b:b + 128] = o
                ob[s, :, b:b + 128] = o

    @pl.when((s >= 5) & (s < 10))
    def _():
        i = s - 5
        wo = w[pl.ds(pl.multiple_of((l * NC + 7) * D, 16), D), :]
        h1 = hb[i] + dot(ob[i], wo) + vec[l, 4:5]
        h1_ref[0, 0] = h1
        hb[i] = h1 + vec[l, 7:8]
        xc, rs = norm_stats(h1)
        a = (xc * rs * vec[l, 5:6] + vec[l, 6:7]).astype(BF)
        a2_ref[0, 0] = a
        ab[i] = a

    @pl.when(s >= 10)
    def _():
        j = s - 10
        up = pl.multiple_of((l * NC + 3 + j) * D, 16)
        down = pl.multiple_of((l * NC + 8 + j) * D, 16)

        @pl.loop(0, 5)
        def _(i):
            @pl.when((i == 3) & (l == 0) & ((s == 10) | (s == 12)))
            def _():
                tick(13 + 3 * ((s - 10) // 2))
            for q in range(3):
                cs = slice(256 * q, 256 * q + 256)
                u = dot(ab[i], w[pl.ds(up, D), cs]) + vec[l, pl.ds(8 + j, 1), cs]
                e, g = gelu_parts(u)
                e_ref[0, i, :, cs] = e.astype(BF)
                g_ref[0, i, :, cs] = g.astype(BF)
                hb[i] += dot(e_ref[0, i, :, cs], w[pl.ds(pl.multiple_of(down + 256 * q, 16), 256), :])

            @pl.when((l == 1) & (s == 13))
            def _():
                enc_ref[i] = hb[i, 0:SEQ, :].astype(BF)

    for layer in range(LAYERS):
        base = layer * NC * D

        @pl.when((l == layer) & (s == 4))
        def _():
            out_copy(base, 3 * D).start()

        @pl.when((l == layer) & (s == 9))
        def _():
            out_copy(base + 7 * D, 5 * D).start()

        for j in range(4):
            @pl.when((l == layer) & (s == 10 + j))
            def _():
                out_copy(base + (3 + j) * D, D).start()

    @pl.when((l == 1) & (s == 13))
    def _():
        pltpu.make_async_copy(w, wo_ref, osem).wait()


def fwd(images, shard, vshard):
    n = images.shape[0]
    S = jax.ShapeDtypeStruct
    one = lambda cols: pl.BlockSpec((1, 1, RP, cols), lambda l, s: (l, jnp.minimum(s, 4), 0, 0))
    two = lambda cols: pl.BlockSpec((1, 1, RP, cols), lambda l, s: (l, jnp.clip(s - 5, 0, 4), 0, 0))
    wide = pl.BlockSpec((1, n, RP, D), lambda l, s: (l, 0, 0, jnp.clip(s - 10, 0, 3)))
    anyw = pl.BlockSpec(memory_space=pl.ANY)
    rows = LAYERS * NC * D
    return pl.pallas_call(
        fwd_kernel, grid=(LAYERS, 14),
        in_specs=[pl.BlockSpec(images.shape, lambda l, s: (0, 0, 0)), anyw, pl.BlockSpec(vshard.shape, lambda l, s: (0, 0, 0))],
        out_specs=[one(D), one(3 * D), one(D), one(D), two(D), two(D), wide, wide, pl.BlockSpec(images.shape, lambda l, s: (0, 0, 0)), anyw, anyw],
        out_shape=[S((LAYERS, n, RP, D), F32), S((LAYERS, n, RP, 3 * D), BF), S((LAYERS, n, RP, D), BF), S((LAYERS, n, RP, D), BF),
                   S((LAYERS, n, RP, D), F32), S((LAYERS, n, RP, D), BF), S((LAYERS, n, RP, 4 * D), BF), S((LAYERS, n, RP, 4 * D), BF),
                   S(images.shape, BF), S((rows, D), BF), S((LAYERS, 16, D), F32)],
        scratch_shapes=[pltpu.VMEM((rows, D), BF), pltpu.VMEM((n, RP, D), F32), pltpu.VMEM((n, RP, D), BF), pltpu.VMEM((n, RP, D), BF),
                        pltpu.VMEM((8, LAYERS, 16, 128), F32), pltpu.VMEM((LAYERS, 16, D), F32),
                        pltpu.SemaphoreType.DMA((8,)), pltpu.SemaphoreType.DMA((8, 8)), pltpu.SemaphoreType.DMA((8, 8)),
                        pltpu.SemaphoreType.DMA((7,)), pltpu.SemaphoreType.DMA((7,)), pltpu.SemaphoreType.DMA, pltpu.SemaphoreType.DMA],
        compiler_params=pltpu.CompilerParams(collective_id=0, has_side_effects=True, vmem_limit_bytes=62 * 2**20),
    )(images, shard, vshard)


def bwd_kernel(cot_ref, w_ref, vec_ref, hs_ref, h1_ref, g_ref, e_ref, qkv_ref, a2_ref, o_ref, a1_ref,
               di_ref, gin_ref, gout_ref, gv_ref,
               wk, d, db, dhb, do, du, ab, gb, dv, rc, s2, ra, rb, s3a, s3b, r3a, r3b, s4, rz, s5, ry, s6, rw, fin,
               vs, vr, vz, wsem, asem, ssem, rsem, osem, vssem, vrsem):
    lr, s = pl.program_id(0), pl.program_id(1)
    l = LAYERS - 1 - lr
    f, core, x, y = plane()
    z = lax.axis_index("rep")
    fc, fx, fy = f + 1 - 2 * core, f + 2 - 4 * x, f + 4 - 8 * y
    z1, z3 = z + 1 - 2 * (z % 2), 3 - z
    half = CH // 2
    mine = pl.multiple_of(((z + 1) // 2 % 2) * half, 16)
    theirs = pl.multiple_of(half - (z + 1) // 2 % 2 * half, 16)
    rows = d.shape[0] * RP

    def load(layer, block, n, at):
        return pltpu.make_async_copy(w_ref.at[pl.ds(pl.multiple_of((layer * NC + block) * D, 16), n * D)], wk.at[pl.ds(at * D, n * D)], wsem.at[0 if at else 1])

    def fetch(src, slot):
        return pltpu.make_async_copy(src.at[l], ab.at[slot], asem.at[slot])

    def remote(kind, p, src, dst, **to):
        return pltpu.make_async_remote_copy(src_ref=src, dst_ref=dst, send_sem=ssem.at[p, kind], recv_sem=rsem.at[p, kind],
                                            device_id=to, device_id_type=MESH)

    def live(v):
        return (v >= 0) & (v < 24)

    def kind(n, v):
        p, q = v % 2, v % 4
        if n == 0:
            lc = v % NC
            return remote(0, q, gb.at[lc - 9 * (lc // 9), :, 1 - core], rc.at[p], fsdp=fc)
        if n == 1:
            return remote(1, q, s2.at[p, :, 1 - x, pl.ds(0, half)], ra.at[q], fsdp=fx)
        if n == 2:
            return remote(2, q, s2.at[p, 1 - y, :, pl.ds(half, half)], rb.at[q], fsdp=fy)
        if n == 3:
            return remote(3, q, s3a.at[p, 1 - y], r3a.at[p], fsdp=fy)
        if n == 4:
            return remote(4, q, s3b.at[p, 1 - x], r3b.at[p], fsdp=fx)
        if n == 5:
            return remote(5, q, s4.at[p, pl.ds(theirs, half)], rz.at[q], rep=z1)
        if n == 6:
            return remote(6, q, s5.at[p], ry.at[q], rep=z3)
        return remote(7, q, s6.at[p], rw.at[p], rep=z1)

    def put(v, act):
        lc, layer = v % NC, LAYERS - 1 - v // NC
        p = v % 2
        out = (lc >= 4) & (lc < 9)

        @pl.when(out)
        def _():
            act(pltpu.make_async_copy(fin.at[p], gout_ref.at[layer, pl.ds(pl.multiple_of((lc - 4) * CH, 8), CH)], osem.at[p]))

        @pl.when(jnp.logical_not(out))
        def _():
            j = lc + 3 - 9 * (lc // 9)
            j = j - 3 * (lc // 9)
            act(pltpu.make_async_copy(fin.at[p], gin_ref.at[layer, :, pl.ds(pl.multiple_of(j * D, 128), D)], osem.at[p]))

    def add(a, b):
        return a.astype(F32) + b.astype(F32)

    def tick(t):
        @pl.when(live(t - 10))
        def _():
            put(t - 10, lambda a: a.wait())

        @pl.when(live(t - 9))
        def _():
            v = t - 9
            p = v % 2
            kind(7, v).wait()
            fin[p, pl.ds(mine, half)] = s6[p].astype(F32)
            fin[p, pl.ds(theirs, half)] = rw[p].astype(F32)
            put(v, lambda a: a.start())

        @pl.when(live(t - 8))
        def _():
            v = t - 8
            p = v % 2
            kind(6, v).wait()
            s6[p] = add(s5[p], ry[v % 4]).astype(BF)
            kind(7, v).start()

        @pl.when(live(t - 6))
        def _():
            v = t - 6
            p = v % 2
            kind(5, v).wait()
            s5[p] = add(s4[p, pl.ds(mine, half)], rz[v % 4]).astype(BF)
            kind(6, v).start()

        @pl.when(live(t - 4))
        def _():
            v = t - 4
            p = v % 2
            kind(3, v).wait()
            kind(4, v).wait()
            s4[p, 0:half] = add(s3a[p, y], r3a[p]).astype(BF)
            s4[p, half:CH] = add(s3b[p, x], r3b[p]).astype(BF)
            kind(5, v).start()

        @pl.when(live(t - 3))
        def _():
            v = t - 3
            p, q = v % 2, v % 4
            kind(1, v).wait()
            kind(2, v).wait()
            for i in range(2):
                s3a[p, i] = add(s2[p, i, x, 0:half], ra[q, i]).astype(BF)
                s3b[p, i] = add(s2[p, y, i, half:CH], rb[q, i]).astype(BF)
            kind(3, v).start()
            kind(4, v).start()

        @pl.when(live(t - 1))
        def _():
            v = t - 1
            p = v % 2
            kind(0, v).wait()
            lc = v % NC
            for i in range(4):
                s2[p, i // 2, i % 2] = add(gb[lc - 9 * (lc // 9), i, core], rc[p, i]).astype(BF)
            kind(1, v).start()
            kind(2, v).start()

        @pl.when(live(t))
        def _():
            kind(0, t).start()

    @pl.when((lr == 0) & (s == 0))
    def _():
        load(l, 3, 9, 0).start()
        bar = pltpu.get_barrier_semaphore()
        for k in range(1, 8):
            pl.semaphore_signal(bar, inc=1, device_id={"fsdp": (f + k) % 8}, device_id_type=MESH)
        for k in range(1, 4):
            pl.semaphore_signal(bar, inc=1, device_id={"rep": (z + k) % 4}, device_id_type=MESH)
        pl.semaphore_wait(bar, 10)
        dv[...] = jnp.zeros_like(dv)
        load(l, 3, 9, 0).wait()

    @pl.when((lr == 1) & (s == 0))
    def _():
        load(l, 3, 3, 0).start()
        load(l, 3, 3, 0).wait()
        load(l, 6, 6, 3).wait()

    @pl.when(s == 0)
    def _():
        fetch(a2_ref, 0).start()
        fetch(o_ref, 1).start()

    @pl.when(s == 5)
    def _():
        fetch(a2_ref, 0).wait()
        load(l, 0, 3, 0).start()

        @pl.when(lr == 0)
        def _():
            load(l - 1, 6, 6, 3).start()

    @pl.when(s == 9)
    def _():
        fetch(o_ref, 1).wait()

    @pl.when(s == 10)
    def _():
        fetch(a1_ref, 0).start()

    @pl.when(s == 19)
    def _():
        fetch(a1_ref, 0).wait()

    @pl.when(s == 22)
    def _():
        load(l, 0, 3, 0).wait()

    odd = s % 2
    first = (s >= 6) & (s <= 13) & (odd == 1 - lr)
    second = (s >= 14) & (s <= 18)
    third = (s >= 20) & (lr == 1)
    start = (s <= 4) & (odd == 0) & (lr == 1)
    t = jnp.where(first, 12 * lr + (s - 6) // 2, jnp.where(second, 12 * lr + s - 10, jnp.where(start, 9 + s // 2, s + 1)))

    @pl.when(first | second | third | start)
    def _():
        tick(t)

    @pl.when(s < 5)
    def _():
        i = s

        @pl.when(lr == 0)
        def _():
            d[i] = jnp.zeros((RP, D), F32)
            d[i, 0:SEQ, :] = cot_ref[0].astype(F32)
        up = d[i]
        db[i] = up.astype(BF)
        dv[l, 7:8] += rsum(up)
        acc = None
        for j in range(12):
            cs = slice(256 * j, 256 * j + 256)
            r = (5 * D + 256 * j)
            t1 = dot_t(db[i], wk[r:r + 256, :]) * g_ref[0, 0, :, cs].astype(F32)
            dv[l, 8 + j // 3:9 + j // 3, 256 * (j % 3):256 * (j % 3) + 256] += rsum(t1)
            du[i, :, cs] = t1.astype(BF)
            t2 = dot_t(du[i, :, cs], wk[(j // 3) * D:(j // 3) * D + D, 256 * (j % 3):256 * (j % 3) + 256])
            acc = t2 if acc is None else acc + t2
        dx, dg, dc = norm_back(h1_ref[0, 0], vec_ref[l, 5:6], acc)
        dv[l, 5:6] += dg
        dv[l, 6:7] += dc
        dh1 = d[i] + dx
        d[i] = dh1
        dv[l, 4:5] += rsum(dh1)
        dhb[i] = dh1.astype(BF)
        do[i] = dot_t(dhb[i], wk[4 * D:5 * D, :]).astype(BF)

    def grad(lhs, rhs, store):
        for m in range(2):
            r = dot_0(lhs(384 * m), rhs).astype(BF).reshape(4, CH, D)
            store(4 * m, r)

    def inner(slot, j):
        def store(m, r):
            gb[slot, m // 2, 0] = r[0]
            gb[slot, m // 2, 1] = r[1]
            gb[slot, m // 2 + 1, 0] = r[2]
            gb[slot, m // 2 + 1, 1] = r[3]
        grad(lambda m: ab[0, :, :, m:m + 384].reshape(rows, 384), du[:, :, pl.ds(pl.multiple_of(D * j, 128), D)].reshape(rows, D), store)

    def outer(step, lhs, rhs):
        def store(m, r):
            for q in range(4):
                b = 8 * step + m + q
                gb[4 + b % 5, b // 10, (b // 5) % 2] = r[q]
        grad(lhs, rhs[...].reshape(rows, D), store)

    @pl.when((s >= 5) & (s < 9))
    def _():
        inner(s - 5, s - 5)

    @pl.when(s == 9)
    def _():
        outer(0, lambda m: ab[1, :, :, m:m + 384].reshape(rows, 384), dhb)

    @pl.when((s >= 10) & (s < 14))
    def _():
        outer(s - 9, lambda m: e_ref[0, :, :, m:m + 384].reshape(rows, 384), db)

    @pl.when((s >= 14) & (s < 19))
    def _():
        i = s - 14
        for p in range(6):
            b = 128 * p
            dq, dk, dvv = attn_bwd(qkv_ref[0, 0, :, b:b + 128], qkv_ref[0, 0, :, D + b:D + b + 128], qkv_ref[0, 0, :, 2 * D + b:2 * D + b + 128],
                                   do[i, :, b:b + 128])
            dv[l, 2:3, b:b + 128] += rsum(dq)
            dv[l, 3:4, b:b + 128] += rsum(dvv)
            du[i, :, b:b + 128] = dq.astype(BF)
            du[i, :, D + b:D + b + 128] = dk.astype(BF)
            du[i, :, 2 * D + b:2 * D + b + 128] = dvv.astype(BF)

    @pl.when((s >= 19) & (s < 22))
    def _():
        inner(s - 19, s - 19)

    @pl.when(s >= 22)
    def _():
        i = s - 22
        da = dot_t(du[i, :, 0:D], wk[0:D, :]) + dot_t(du[i, :, D:2 * D], wk[D:2 * D, :]) + dot_t(du[i, :, 2 * D:3 * D], wk[2 * D:3 * D, :])
        dx, dg, dc = norm_back(hs_ref[0, 0], vec_ref[l, 0:1], da)
        dv[l, 0:1] += dg
        dv[l, 1:2] += dc
        dh = d[i] + dx
        d[i] = dh
        di_ref[0] = dh[0:SEQ]

    @pl.when((lr == 1) & (s == 26))
    def _():
        for layer in range(LAYERS):
            for c in range(72):
                vs[c // 9, layer, c % 9:c % 9 + 1, :] = dv[layer, c // 6:c // 6 + 1, 128 * (c % 6):128 * (c % 6) + 128]

        def vcopy(k):
            to = (f + k) % 8
            return pltpu.make_async_remote_copy(src_ref=vs.at[to], dst_ref=vr.at[k - 1], send_sem=vssem.at[k - 1], recv_sem=vrsem.at[k - 1],
                                                device_id={"fsdp": to}, device_id_type=MESH)

        def zcopy(k):
            return pltpu.make_async_remote_copy(src_ref=vz.at[z], dst_ref=vz.at[z], send_sem=vssem.at[6 + k], recv_sem=vrsem.at[6 + k],
                                                device_id={"rep": (z + k) % 4}, device_id_type=MESH)
        for k in range(1, 8):
            vcopy(k).start()
        for t in range(28, 34):
            tick(jnp.int32(t))
        for k in range(1, 8):
            vcopy(k).wait()
        total = vs[f]
        for k in range(7):
            total = total + vr[k]
        vz[z] = total
        for k in range(1, 4):
            zcopy(k).start()
        for k in range(1, 4):
            zcopy(k).wait()
        gv_ref[...] = (vz[0] + vz[1]) + (vz[2] + vz[3])


def bwd(cotangent, w, vec, hs, h1, g, e, qkv, a2, o, a1, shard_in, shard_out):
    n = cotangent.shape[0]
    S = jax.ShapeDtypeStruct
    anyw = pl.BlockSpec(memory_space=pl.ANY)
    row = lambda cols, at: pl.BlockSpec((1, 1, RP, cols), lambda lr, s: (LAYERS - 1 - lr, jnp.clip(s - at, 0, 4), 0, 0))
    tok = lambda index: pl.BlockSpec((1, SEQ, D), index)
    VB = lambda *shape: pltpu.VMEM(shape, BF)
    half = CH // 2
    return pl.pallas_call(
        bwd_kernel, grid=(LAYERS, 27),
        in_specs=[tok(lambda lr, s: (jnp.minimum(s + 4 * lr, 4), 0, 0)), anyw, pl.BlockSpec(vec.shape, lambda lr, s: (0, 0, 0)),
                  row(D, 22), row(D, 0), row(4 * D, 0),
                  pl.BlockSpec((1, n, RP, D), lambda lr, s: (LAYERS - 1 - lr, 0, 0, jnp.clip(s - 10, 0, 3))),
                  row(3 * D, 14), anyw, anyw, anyw],
        out_specs=[tok(lambda lr, s: (lr * jnp.clip(s - 22, 0, 4), 0, 0)), anyw, anyw, pl.BlockSpec((LAYERS, 16, 128), lambda lr, s: (0, 0, 0))],
        out_shape=[S(cotangent.shape, F32), S(shard_in, F32), S(shard_out, F32), S((LAYERS, 16, 128), F32)],
        scratch_shapes=[VB(9 * D, D), pltpu.VMEM((n, RP, D), F32), VB(n, RP, D), VB(n, RP, D), VB(n, RP, D), VB(n, RP, 4 * D), VB(2, n, RP, D),
                        VB(9, 4, 2, CH, D), pltpu.VMEM((LAYERS, 16, D), F32),
                        VB(2, 4, CH, D), VB(2, 2, 2, CH, D), VB(4, 2, half, D), VB(4, 2, half, D), VB(2, 2, half, D), VB(2, 2, half, D),
                        VB(2, half, D), VB(2, half, D), VB(2, CH, D), VB(4, half, D), VB(2, half, D), VB(4, half, D), VB(2, half, D), VB(2, half, D),
                        pltpu.VMEM((2, CH, D), F32),
                        pltpu.VMEM((8, LAYERS, 16, 128), F32), pltpu.VMEM((7, LAYERS, 16, 128), F32), pltpu.VMEM((4, LAYERS, 16, 128), F32),
                        pltpu.SemaphoreType.DMA((2,)), pltpu.SemaphoreType.DMA((2,)), pltpu.SemaphoreType.DMA((4, 8)), pltpu.SemaphoreType.DMA((4, 8)),
                        pltpu.SemaphoreType.DMA((2,)), pltpu.SemaphoreType.DMA((10,)), pltpu.SemaphoreType.DMA((10,))],
        compiler_params=pltpu.CompilerParams(collective_id=1, has_side_effects=True, vmem_limit_bytes=63 * 2**20),
    )(cotangent, w, vec, hs, h1, g, e, qkv, a2, o, a1)


STEP = 3
beta_one = 0.9
beta_two = 0.999
matrix_rate = 0.03
vector_rate = 0.2
matrix_decay = 0.05
adam_eps = 1e-8


def adam_update(master, gradient, moment_one, moment_two, rate, decay_rate):
    moment_one = beta_one * moment_one + (1.0 - beta_one) * gradient
    moment_two = beta_two * moment_two + (1.0 - beta_two) * gradient * gradient
    corr_one = 1.0 - beta_one**STEP
    corr_two = 1.0 - beta_two**STEP
    adam_move = moment_one / corr_one / (jnp.sqrt(moment_two / corr_two) + adam_eps)
    return (master - rate * (adam_move + decay_rate * master), moment_one, moment_two)


def swap(x, axis, size, mask):
    return lax.ppermute(x, axis, [(i, i ^ mask) for i in range(size)])


def halve(x, order, size):
    bits = size.bit_length() - 1
    me = lax.axis_index("fsdp")
    x = x.reshape((2,) * bits + x.shape[1:])
    left = list(range(bits))[::-1]
    for bit in order:
        at = left.index(bit)
        mine = (me >> bit) & 1
        keep = lax.dynamic_index_in_dim(x, mine, at, keepdims=False)
        send = lax.dynamic_index_in_dim(x, 1 - mine, at, keepdims=False)
        got = swap(send, "fsdp", size, 1 << bit)
        x = (keep.astype(F32) + got.astype(F32)).astype(BF)
        left.remove(bit)
    return x


def reduce_all(x, nf, nr):
    bits = nf.bit_length() - 1
    rows, cols = x.shape
    x = x.reshape(nf, rows // nf, cols)
    half = cols // 2 // 128 * 128
    up = [0] + list(range(1, bits))
    down = [0] + list(range(1, bits))[::-1]
    x = jnp.concatenate([halve(x[..., :half], up, nf), halve(x[..., half:], down, nf)], axis=-1)
    mask = 1
    while mask < nr:
        got = swap(x, "rep", nr, 2 * mask - 1)
        y = x.astype(F32) + got.astype(F32)
        x = y.astype(BF)
        mask *= 2
    return y


def own_shard(weight_in, weight_out):
    a = weight_in.astype(BF).reshape(LAYERS, CH, 7, D).transpose(0, 2, 1, 3)
    b = weight_out.astype(BF).reshape(LAYERS, 5, CH, D)
    return jnp.concatenate([a[:, :3], b, a[:, 3:]], axis=1).reshape(LAYERS * NC, CH, D)


def fused_step(images, cotangent, weight_in, weight_out, vector_params):
    vs = jnp.pad(vector_params.astype(BF).astype(F32).reshape(LAYERS, 9, 128), ((0, 0), (0, 7), (0, 0)))
    hs, qkv, a1, o, h1, a2, e, g, encoded, w, vec = fwd(images, own_shard(weight_in, weight_out), vs)
    dimg, gi, go, gv = bwd(cotangent, w, vec, hs, h1, g, e, qkv, a2, o, a1, weight_in.shape, weight_out.shape)
    return encoded, dimg, gi, go, gv[:, :9].reshape(vector_params.shape)


def plain_step(nf, nr, images, cotangent, weight_in, weight_out, vector_params):
    pad = lambda a: jnp.pad(a, ((0, 0), (0, RP - SEQ), (0, 0)))
    vec_all = lax.all_gather(vector_params.astype(BF), "fsdp", axis=1, tiled=True).astype(F32)
    h = pad(images)
    ct = pad(cotangent)
    saved = []
    for l in range(LAYERS):
        win = lax.all_gather(weight_in[l].astype(BF), "fsdp", axis=0, tiled=True)
        wout = lax.all_gather(weight_out[l].astype(BF), "fsdp", axis=0, tiled=True)
        vec = jnp.pad(vec_all[l].reshape(12, D), ((0, 4), (0, 0)))
        wqkv, w1, wo, w2 = win[:, : 3 * D], win[:, 3 * D :], wout[:D], wout[D:]
        qkv, o, a1 = ka(h, wqkv, vec)
        h1, a2, e, g, h2 = kb(h, o, wo, w1, w2, vec)
        saved.append((h, wqkv, w1, wo, w2, vec, qkv, o, a1, h1, a2, e, g))
        h = h2
    encoded = h[:, :SEQ].astype(BF)
    d = ct
    gin, gout, gvec = [None] * LAYERS, [None] * LAYERS, [None] * LAYERS
    for l in reversed(range(LAYERS)):
        h, wqkv, w1, wo, w2, vec, qkv, o, a1, h1, a2, e, g = saved[l]
        db, du, dh1, dh1b, do, dv1 = kc(d, h1, g, wo, w1, w2, vec)
        g1 = reduce_all(dw(a2, du), nf, nr)
        go = reduce_all(jnp.concatenate([dw(o, dh1b), dw(e, db)], axis=0), nf, nr)
        dz, dv2 = kd(qkv, do)
        gq = reduce_all(dw(a1, dz), nf, nr)
        d, dv3 = kf(dz, h, dh1, wqkv, vec, RP if l else SEQ)
        gin[l] = jnp.concatenate([gq, g1], axis=1)
        gout[l] = go
        gvec[l] = (dv1 + dv2 + dv3)[:12].reshape(-1)
    gv = lax.psum(jnp.stack(gvec), ("fsdp", "rep"))
    wide = gv.shape[1] // nf
    gv = lax.dynamic_slice_in_dim(gv, lax.axis_index("fsdp") * wide, wide, 1)
    return encoded, d, jnp.stack(gin), jnp.stack(gout), gv


def make_shards(nf, nr):
    def shards(images, cotangent, weight_in, weight_out, vector_params, first_in, first_out, first_vec, second_in, second_out, second_vec):
        if nf == 8 and nr == 4:
            encoded, d, gi, go, gv = fused_step(images, cotangent, weight_in, weight_out, vector_params)
        else:
            encoded, d, gi, go, gv = plain_step(nf, nr, images, cotangent, weight_in, weight_out, vector_params)
        new_in, moment_in, square_in = adam_update(weight_in, gi, first_in, second_in, matrix_rate, matrix_decay)
        new_out, moment_out, square_out = adam_update(weight_out, go, first_out, second_out, matrix_rate, matrix_decay)
        new_vec, moment_vec, square_vec = adam_update(vector_params, gv, first_vec, second_vec, vector_rate, 0.0)
        return (encoded, d, gi, go, gv, new_in, new_out, new_vec, moment_in, moment_out, moment_vec, square_in, square_out, square_vec)

    return shards


def solution(mesh):
    tokens = P(("fsdp", "rep"), None, None)
    matrix = P(None, "fsdp", None)
    vector = P(None, "fsdp")
    in_specs = (tokens, tokens) + (matrix, matrix, vector) * 3
    out_specs = (tokens, tokens) + (matrix, matrix, vector) * 4
    return jax.shard_map(make_shards(mesh.shape["fsdp"], mesh.shape["rep"]), mesh=mesh, in_specs=in_specs, out_specs=out_specs, check_vma=False)
```

```python
import functools
import jax, jax.numpy as jnp
from jax import lax
from jax.experimental import pallas as pl
from jax.experimental.pallas import tpu as pltpu
from jax.sharding import PartitionSpec as P

D=768; HD=64; SEQ=197; RP=208; EPS=1e-6
BF=jnp.bfloat16; F32=jnp.float32
def dot(a,b): return jnp.dot(a,b,preferred_element_type=F32)
def dot_t(a,b): return lax.dot_general(a,b,(((1,),(1,)),((),())),preferred_element_type=F32)
def dot_0(a,b): return lax.dot_general(a,b,(((0,),(0,)),((),())),preferred_element_type=F32)

def norm_stats(x):
    mean=jnp.mean(x,axis=-1,keepdims=True); xc=x-mean
    var=jnp.mean(xc*xc,axis=-1,keepdims=True)
    return xc, lax.rsqrt(var+EPS)

def head_masks(scale):
    lane = lax.broadcasted_iota(jnp.int32, (1, 128), 1)
    return jnp.where(lane < 64, scale, 0.0).astype(BF), jnp.where(lane < 64, 0.0, scale).astype(BF)


def weights_t(q, k, masks):
    row = lax.broadcasted_iota(jnp.int32, (RP, 1), 0)
    s = [jnp.where(row < SEQ, dot_t(k, q * m), -1e30) for m in masks]
    e = [jnp.exp(x - jnp.max(x, axis=0, keepdims=True)) for x in s]
    return [x * (1.0 / jnp.sum(x, axis=0, keepdims=True)) for x in e]


def attn_fwd(q, k, v):
    ones = head_masks(1.0)
    row = lax.broadcasted_iota(jnp.int32, (16, 1), 0)
    ps = []
    for m in head_masks(0.125):
        s = dot_t(k, q * m)
        s = jnp.concatenate([s[:RP - 16], jnp.where(row < SEQ - RP + 16, s[RP - 16:], -1e30)], axis=0)
        e = jnp.exp(s - jnp.max(s, axis=0, keepdims=True))
        ps.append((e * (1.0 / jnp.sum(e, axis=0, keepdims=True))).astype(BF))
    return (dot_0(ps[0], v * ones[0]) + dot_0(ps[1], v * ones[1])).astype(BF)


def attn_bwd(q, k, v, do):
    scaled, ones = head_masks(0.125), head_masks(1.0)
    p = weights_t(q, k, scaled)
    dos = [do * m for m in ones]
    dp = [dot_t(v, x) for x in dos]
    pb = [x.astype(BF) for x in p]
    ds = [(a * (b - jnp.sum(a * b, axis=0, keepdims=True))).astype(BF) for a, b in zip(p, dp)]
    dv = dot(pb[0], dos[0]) + dot(pb[1], dos[1])
    dk = dot(ds[0], q * scaled[0]) + dot(ds[1], q * scaled[1])
    dq = dot_0(ds[0], k * scaled[0]) + dot_0(ds[1], k * scaled[1])
    return dq, dk, dv


def ka_kernel(h_ref,w_ref,vec_ref,qkv_ref,o_ref,a_ref):
    h=h_ref[0].astype(F32)
    xc,rs=norm_stats(h)
    a_ref[0]=(xc*rs*vec_ref[0:1]+vec_ref[1:2]).astype(BF)
    a=a_ref[0]
    for c in range(3):
        cs=slice(256*c,256*c+256)
        qkv_ref[0,:,256*c:256*c+256]=(dot(a,w_ref[:,256*c:256*c+256])+vec_ref[2:3,cs]).astype(BF)
        qkv_ref[0,:,D+256*c:D+256*c+256]=dot(a,w_ref[:,D+256*c:D+256*c+256]).astype(BF)
        qkv_ref[0,:,2*D+256*c:2*D+256*c+256]=(dot(a,w_ref[:,2*D+256*c:2*D+256*c+256])+vec_ref[3:4,cs]).astype(BF)
        for p in range(2):
            b=256*c+128*p
            o_ref[0,:,b:b+128]=attn_fwd(qkv_ref[0,:,b:b+128],qkv_ref[0,:,D+b:D+b+128],qkv_ref[0,:,2*D+b:2*D+b+128])

def img(n,dt=None): return pl.BlockSpec((1,RP,n),lambda i:(i,0,0))
def full(shape): return pl.BlockSpec(shape,lambda i:(0,)*len(shape))
PAR=pltpu.CompilerParams(vmem_limit_bytes=60*2**20)

def ka(h,w,vec):
    n=h.shape[0]
    return pl.pallas_call(ka_kernel,grid=(n,),in_specs=[img(D),full(w.shape),full(vec.shape)],
        out_specs=[img(3*D),img(D),img(D)],
        out_shape=[jax.ShapeDtypeStruct((n,RP,3*D),BF),jax.ShapeDtypeStruct((n,RP,D),BF),jax.ShapeDtypeStruct((n,RP,D),BF)],
        compiler_params=PAR)(h,w,vec)

def gelu_parts(u):
    c=0.5*(1.0+lax.erf(u*0.7071067811865476))
    g=c+u*(jnp.exp(-0.5*u*u)*0.3989422804014327)
    return u*c,g

def kb_kernel(FC,h_ref,o_ref,wo_ref,w1_ref,w2_ref,vec_ref,h1_ref,a_ref,e_ref,g_ref,h2_ref):
    h1=h_ref[0].astype(F32)+dot(o_ref[0],wo_ref[...])+vec_ref[4:5]
    h1_ref[0]=h1
    xc,rs=norm_stats(h1)
    a_ref[0]=(xc*rs*vec_ref[5:6]+vec_ref[6:7]).astype(BF)
    a=a_ref[0]
    h2_ref[0]=h1+vec_ref[7:8]
    for j in range(3072//FC):
        lo=FC*j
        u=dot(a,w1_ref[:,lo:lo+FC])+vec_ref[8+lo//D:9+lo//D,lo%D:lo%D+FC]
        e,g=gelu_parts(u)
        e_ref[0,:,lo:lo+FC]=e.astype(BF); g_ref[0,:,lo:lo+FC]=g.astype(BF)
        h2_ref[0]+=dot(e_ref[0,:,lo:lo+FC],w2_ref[lo:lo+FC,:])

def kb(h,o,wo,w1,w2,vec,FC=256):
    n=h.shape[0]
    S=jax.ShapeDtypeStruct
    return pl.pallas_call(functools.partial(kb_kernel,FC),grid=(n,),in_specs=[img(D),img(D),full(wo.shape),full(w1.shape),full(w2.shape),full(vec.shape)],
        out_specs=[img(D),img(D),img(3072),img(3072),img(D)],
        out_shape=[S((n,RP,D),F32),S((n,RP,D),BF),S((n,RP,3072),BF),S((n,RP,3072),BF),S((n,RP,D),F32)],
        compiler_params=PAR)(h,o,wo,w1,w2,vec)

def rsum(x): return jnp.sum(x,axis=0,keepdims=True)
def norm_back(x,gain,dy):
    xc,rs=norm_stats(x); xh=xc*rs
    dyg=dy*gain
    dx=rs*(dyg-jnp.mean(dyg,axis=-1,keepdims=True)-xh*jnp.mean(dyg*xh,axis=-1,keepdims=True))
    return dx, rsum(dy*xh), rsum(dy)

def kc_kernel(FC,d_ref,h1_ref,g_ref,wo_ref,w1_ref,w2_ref,vec_ref,db_ref,du_ref,dh1_ref,dh1b_ref,do_ref,dv_ref,acc_ref):
    @pl.when(pl.program_id(0)==0)
    def _(): dv_ref[...]=jnp.zeros_like(dv_ref)
    d=d_ref[0].astype(F32)
    db_ref[0]=d.astype(BF)
    db=db_ref[0]
    dv_ref[7:8]+=rsum(d)
    for j in range(3072//FC):
        lo=FC*j
        du=dot_t(db,w2_ref[lo:lo+FC,:])*g_ref[0,:,lo:lo+FC].astype(F32)
        dv_ref[8+lo//D:9+lo//D,lo%D:lo%D+FC]+=rsum(du)
        du_ref[0,:,lo:lo+FC]=du.astype(BF)
        t=dot_t(du_ref[0,:,lo:lo+FC],w1_ref[:,lo:lo+FC])
        if j==0: acc_ref[...]=t
        else: acc_ref[...]+=t
    dx,dg,dc=norm_back(h1_ref[0],vec_ref[5:6],acc_ref[...])
    dv_ref[5:6]+=dg; dv_ref[6:7]+=dc
    dh1=d_ref[0].astype(F32)+dx
    dh1_ref[0]=dh1
    dv_ref[4:5]+=rsum(dh1)
    dh1b_ref[0]=dh1.astype(BF)
    do_ref[0]=dot_t(dh1b_ref[0],wo_ref[...]).astype(BF)

def kc(d,h1,g,wo,w1,w2,vec,FC=256):
    n=d.shape[0]; S=jax.ShapeDtypeStruct
    return pl.pallas_call(functools.partial(kc_kernel,FC),grid=(n,),in_specs=[img(D),img(D),img(3072),full(wo.shape),full(w1.shape),full(w2.shape),full(vec.shape)],
        out_specs=[img(D),img(3072),img(D),img(D),img(D),full((16,D))],
        out_shape=[S((n,RP,D),BF),S((n,RP,3072),BF),S((n,RP,D),F32),S((n,RP,D),BF),S((n,RP,D),BF),S((16,D),F32)],
        scratch_shapes=[pltpu.VMEM((RP,D),F32)],
        compiler_params=PAR)(d,h1,g,wo,w1,w2,vec)

def kd_kernel(qkv_ref,do_ref,dz_ref,dv_ref):
    @pl.when(pl.program_id(0)==0)
    def _(): dv_ref[...]=jnp.zeros_like(dv_ref)
    for p in range(6):
        b=128*p
        dq,dk,dv=attn_bwd(qkv_ref[0,:,b:b+128],qkv_ref[0,:,D+b:D+b+128],qkv_ref[0,:,2*D+b:2*D+b+128],do_ref[0,:,b:b+128])
        dv_ref[2:3,b:b+128]+=rsum(dq); dv_ref[3:4,b:b+128]+=rsum(dv)
        dz_ref[0,:,b:b+128]=dq.astype(BF); dz_ref[0,:,D+b:D+b+128]=dk.astype(BF); dz_ref[0,:,2*D+b:2*D+b+128]=dv.astype(BF)

def kd(qkv,do):
    n=do.shape[0]; S=jax.ShapeDtypeStruct
    return pl.pallas_call(kd_kernel,grid=(n,),in_specs=[img(3*D),img(D)],out_specs=[img(3*D),full((16,D))],
        out_shape=[S((n,RP,3*D),BF),S((16,D),F32)],compiler_params=PAR)(qkv,do)

def kf_kernel(dz_ref,h_ref,dh1_ref,w_ref,vec_ref,dh_ref,dv_ref):
    @pl.when(pl.program_id(0)==0)
    def _(): dv_ref[...]=jnp.zeros_like(dv_ref)
    da=dot_t(dz_ref[0],w_ref[...])
    dx,dg,dc=norm_back(h_ref[0].astype(F32),vec_ref[0:1],da)
    dv_ref[0:1]+=dg; dv_ref[1:2]+=dc
    rows=dh_ref.shape[1]
    dh_ref[0]=(dh1_ref[0]+dx)[:rows]

def kf(dz,h,dh1,w,vec,rows=RP):
    n=dz.shape[0]; S=jax.ShapeDtypeStruct
    return pl.pallas_call(kf_kernel,grid=(n,),in_specs=[img(3*D),img(D),img(D),full(w.shape),full(vec.shape)],
        out_specs=[pl.BlockSpec((1,rows,D),lambda i:(i,0,0)),full((16,D))],
        out_shape=[S((n,rows,D),F32),S((16,D),F32)],compiler_params=PAR)(dz,h,dh1,w,vec)

def dw_kernel(l_ref,r_ref,o_ref):
    o_ref[...]=dot_0(l_ref[...],r_ref[...]).astype(BF)
def dw(l,r,MB=256):
    M=l.shape[-1]; N=r.shape[-1]; K=l.shape[0]*RP
    l=l.reshape(K,M); r=r.reshape(K,N)
    return pl.pallas_call(dw_kernel,grid=(M//MB,),in_specs=[pl.BlockSpec((K,MB),lambda i:(0,i)),pl.BlockSpec((K,N),lambda i:(0,0))],
       out_specs=pl.BlockSpec((MB,N),lambda i:(i,0)),out_shape=jax.ShapeDtypeStruct((M,N),BF),compiler_params=PAR)(l,r)


LAYERS = 2
MESH = pl.DeviceIdType.MESH
CH = 96
NC = 12


def plane():
    f = lax.axis_index("fsdp")
    core, x, y = f % 2, (f // 2) % 2, f // 4
    return f, core, x, y


def chunk_rows(c, f):
    layer, j = c // NC, c % NC
    early = 1 - (j + 9) // 12
    late = j // 8
    mid = 1 - early - late
    base = layer * NC * D
    return pl.multiple_of(base + early * (j * D + CH * f) + late * ((j - 5) * D + CH * f)
                          + mid * (7 * D + 5 * CH * f + CH * (j - 3)), 16)


def fwd_kernel(img_ref, win_ref, wout_ref, vs_ref, hs_ref, qkv_ref, a1_ref, o_ref, h1_ref, a2_ref, e_ref, g_ref, enc_ref, wo_ref, vo_ref,
               w, hb, ob, ab, vg, vec, st, lsem, ssem, rsem, vssem, vrsem, osem, vosem):
    l, s = pl.program_id(0), pl.program_id(1)
    f, core, x, y = plane()
    fc, fx, fy = f + 1 - 2 * core, f + 2 - 4 * x, f + 4 - 8 * y
    fd = fx + fy - f

    def wrow(c, who, lo=0, n=CH):
        return w.at[pl.ds(pl.multiple_of(chunk_rows(c, who) + lo, 16), n)]

    def send(c, kind, src, dst, to):
        return pltpu.make_async_remote_copy(src_ref=src, dst_ref=dst, send_sem=ssem.at[c % 8, kind], recv_sem=rsem.at[c % 8, kind],
                                            device_id={"fsdp": to}, device_id_type=MESH)

    def fetch(c, act):
        layer, j = c // NC, c % NC
        mid = (j >= 3) & (j < 8)

        @pl.when(mid)
        def _():
            act(pltpu.make_async_copy(wout_ref.at[layer, pl.ds(pl.multiple_of((j - 3) * CH, 8), CH)], st.at[c % 4], lsem.at[c % 4]))

        @pl.when(jnp.logical_not(mid))
        def _():
            act(pltpu.make_async_copy(win_ref.at[layer, :, pl.ds(pl.multiple_of((j - 5 * (j // 8)) * D, 128), D)], st.at[c % 4], lsem.at[c % 4]))

    def kinds(c):
        mine, half = wrow(c, f), CH // 2
        return [lambda: send(c, 0, mine, mine, fx), lambda: send(c, 1, mine, mine, fy), lambda: send(c, 2, mine, mine, fc),
                lambda: send(c, 3, wrow(c, fx, 0, half), wrow(c, fx, 0, half), fy),
                lambda: send(c, 4, wrow(c, fy, half, half), wrow(c, fy, half, half), fx),
                lambda: send(c, 5, wrow(c, fx), wrow(c, fx), fc), lambda: send(c, 6, wrow(c, fy), wrow(c, fy), fc),
                lambda: send(c, 7, wrow(c, fd), wrow(c, fd), fc)]

    def start(c, which):
        k = kinds(c)
        for i in which:
            k[i]().start()

    def wait(c, which):
        k = kinds(c)
        for i in which:
            k[i]().wait()

    def tick(t):
        @pl.when((t >= 4) & (t < 28))
        def _():
            wait(t - 4, (2, 5, 6, 7))

        @pl.when((t >= 3) & (t < 27))
        def _():
            wait(t - 3, (3, 4))
            start(t - 3, (7,))

        @pl.when((t >= 2) & (t < 26))
        def _():
            wait(t - 2, (0, 1))
            start(t - 2, (3, 4, 5, 6))

        @pl.when(t < 24)
        def _():
            fetch(t, lambda a: a.wait())
            w[pl.ds(chunk_rows(t, f), CH)] = st[t % 4].astype(BF)
            start(t, (0, 1, 2))

        @pl.when(t < 21)
        def _():
            fetch(t + 3, lambda a: a.start())

    def out_copy(b, n):
        return pltpu.make_async_copy(w.at[pl.ds(b, n)], wo_ref.at[pl.ds(b, n)], osem)

    @pl.when((l == 0) & (s == 0))
    def _():
        for c in range(3):
            fetch(jnp.int32(c), lambda a: a.start())
        bar = pltpu.get_barrier_semaphore()
        for k in range(1, 8):
            pl.semaphore_signal(bar, inc=1, device_id={"fsdp": (f + k) % 8}, device_id_type=MESH)
        pl.semaphore_wait(bar, 7)

        def vcopy(k):
            return pltpu.make_async_remote_copy(src_ref=vs_ref, dst_ref=vg.at[f], send_sem=vssem.at[k - 1], recv_sem=vrsem.at[k - 1],
                                                device_id={"fsdp": (f + k) % 8}, device_id_type=MESH)
        for k in range(1, 8):
            vcopy(k).start()
        vg[f] = vs_ref[...]

        @pl.loop(0, 7)
        def _(t):
            tick(t)
        for k in range(1, 8):
            vcopy(k).wait()
        for layer in range(LAYERS):
            for c in range(72):
                vec[layer, c // 6:c // 6 + 1, 128 * (c % 6):128 * (c % 6) + 128] = vg[c // 9, layer, c % 9:c % 9 + 1, :]
        hb[...] = jnp.zeros_like(hb)
        cp = pltpu.make_async_copy(vec, vo_ref, vosem)
        cp.start()
        cp.wait()

    early = (1 - l) * (s + 6) + l * (s + 18)
    late = (1 - l) * (s + 2) + l * (s + 14)

    @pl.when((s == 0) & (l == 1))
    def _():
        tick(16)
        tick(17)

    @pl.when((s <= 5) & (l + s > 0))
    def _():
        tick(early)

    @pl.when(s >= 10)
    def _():
        tick(late)

    @pl.when(s < 5)
    def _():
        @pl.when(l == 0)
        def _():
            hb[s, 0:SEQ, :] = img_ref[s].astype(F32)
        h = hb[s]
        hs_ref[0, 0] = h
        xc, rs = norm_stats(h)
        a1_ref[0, 0] = (xc * rs * vec[l, 0:1] + vec[l, 1:2]).astype(BF)
        a = a1_ref[0, 0]
        wb = l * NC * D

        def wq(part, c):
            return w[pl.ds(pl.multiple_of(wb + part * D, 16), D), 256 * c:256 * c + 256]
        for c in range(3):
            cs = slice(256 * c, 256 * c + 256)
            qkv_ref[0, 0, :, cs] = (dot(a, wq(0, c)) + vec[l, 2:3, cs]).astype(BF)
            qkv_ref[0, 0, :, D + 256 * c:D + 256 * c + 256] = dot(a, wq(1, c)).astype(BF)
            qkv_ref[0, 0, :, 2 * D + 256 * c:2 * D + 256 * c + 256] = (dot(a, wq(2, c)) + vec[l, 3:4, cs]).astype(BF)
            for p in range(2):
                b = 256 * c + 128 * p
                o = attn_fwd(qkv_ref[0, 0, :, b:b + 128], qkv_ref[0, 0, :, D + b:D + b + 128], qkv_ref[0, 0, :, 2 * D + b:2 * D + b + 128])
                o_ref[0, 0, :, b:b + 128] = o
                ob[s, :, b:b + 128] = o

    @pl.when((s >= 5) & (s < 10))
    def _():
        i = s - 5
        wo = w[pl.ds(pl.multiple_of((l * NC + 7) * D, 16), D), :]
        h1 = hb[i] + dot(ob[i], wo) + vec[l, 4:5]
        h1_ref[0, 0] = h1
        hb[i] = h1 + vec[l, 7:8]
        xc, rs = norm_stats(h1)
        a = (xc * rs * vec[l, 5:6] + vec[l, 6:7]).astype(BF)
        a2_ref[0, 0] = a
        ab[i] = a

    @pl.when(s >= 10)
    def _():
        j = s - 10
        up = pl.multiple_of((l * NC + 3 + j) * D, 16)
        down = pl.multiple_of((l * NC + 8 + j) * D, 16)

        bias = vec[l, pl.ds(8 + j, 1), :]
        n = hb.shape[0]
        u = dot(ab[0], w[pl.ds(up, D), :])
        for i in range(n):
            later = dot(ab[i + 1], w[pl.ds(up, D), :]) if i < n - 1 else None
            e, g = gelu_parts(u + bias)
            e = e.astype(BF)
            e_ref[0, i] = e
            g_ref[0, i] = g.astype(BF)
            hb[i] += dot(e, w[pl.ds(down, D), :])
            u = later

        @pl.when((l == 1) & (s == 13))
        def _():
            for i in range(n):
                enc_ref[i] = hb[i, 0:SEQ, :].astype(BF)

    for layer in range(LAYERS):
        base = layer * NC * D

        @pl.when((l == layer) & (s == 4))
        def _():
            out_copy(base, 3 * D).start()

        @pl.when((l == layer) & (s == 9))
        def _():
            out_copy(base + 7 * D, 5 * D).start()

        for j in range(4):
            @pl.when((l == layer) & (s == 10 + j))
            def _():
                out_copy(base + (3 + j) * D, D).start()

    @pl.when((l == 1) & (s == 13))
    def _():
        pltpu.make_async_copy(w, wo_ref, osem).wait()


def fwd(images, weight_in, weight_out, vshard):
    n = images.shape[0]
    S = jax.ShapeDtypeStruct
    one = lambda cols: pl.BlockSpec((1, 1, RP, cols), lambda l, s: (l, jnp.minimum(s, 4), 0, 0))
    two = lambda cols: pl.BlockSpec((1, 1, RP, cols), lambda l, s: (l, jnp.clip(s - 5, 0, 4), 0, 0))
    wide = pl.BlockSpec((1, n, RP, D), lambda l, s: (l, 0, 0, jnp.clip(s - 10, 0, 3)))
    anyw = pl.BlockSpec(memory_space=pl.ANY)
    rows = LAYERS * NC * D
    return pl.pallas_call(
        fwd_kernel, grid=(LAYERS, 14),
        in_specs=[pl.BlockSpec(images.shape, lambda l, s: (0, 0, 0)), anyw, anyw, pl.BlockSpec(vshard.shape, lambda l, s: (0, 0, 0))],
        out_specs=[one(D), one(3 * D), one(D), one(D), two(D), two(D), wide, wide, pl.BlockSpec(images.shape, lambda l, s: (0, 0, 0)), anyw, anyw],
        out_shape=[S((LAYERS, n, RP, D), F32), S((LAYERS, n, RP, 3 * D), BF), S((LAYERS, n, RP, D), BF), S((LAYERS, n, RP, D), BF),
                   S((LAYERS, n, RP, D), F32), S((LAYERS, n, RP, D), BF), S((LAYERS, n, RP, 4 * D), BF), S((LAYERS, n, RP, 4 * D), BF),
                   S(images.shape, BF), S((rows, D), BF), S((LAYERS, 16, D), F32)],
        scratch_shapes=[pltpu.VMEM((rows, D), BF), pltpu.VMEM((n, RP, D), F32), pltpu.VMEM((n, RP, D), BF), pltpu.VMEM((n, RP, D), BF),
                        pltpu.VMEM((8, LAYERS, 16, 128), F32), pltpu.VMEM((LAYERS, 16, D), F32), pltpu.VMEM((4, CH, D), F32),
                        pltpu.SemaphoreType.DMA((4,)), pltpu.SemaphoreType.DMA((8, 8)), pltpu.SemaphoreType.DMA((8, 8)),
                        pltpu.SemaphoreType.DMA((7,)), pltpu.SemaphoreType.DMA((7,)), pltpu.SemaphoreType.DMA, pltpu.SemaphoreType.DMA],
        compiler_params=pltpu.CompilerParams(collective_id=0, has_side_effects=True, vmem_limit_bytes=62 * 2**20),
    )(images, weight_in, weight_out, vshard)


def bwd_kernel(cot_ref, w_ref, vec_ref, hs_ref, h1_ref, g_ref, e_ref, qkv_ref, a2_ref, o_ref, a1_ref,
               di_ref, gin_ref, gout_ref, gv_ref,
               wk, d, acc, db, dhb, du, ab, gb, dv, rc, s2, ra, rb, s3a, s3b, r3a, r3b, s4, rz, s5, ry, s6, rw, fin,
               vs, vr, vz, wsem, asem, ssem, rsem, osem, vssem, vrsem):
    lr, s = pl.program_id(0), pl.program_id(1)
    l = LAYERS - 1 - lr
    f, core, x, y = plane()
    z = lax.axis_index("rep")
    fc, fx, fy = f + 1 - 2 * core, f + 2 - 4 * x, f + 4 - 8 * y
    z1, z3 = z + 1 - 2 * (z % 2), 3 - z
    half = CH // 2
    mine = pl.multiple_of(((z + 1) // 2 % 2) * half, 16)
    theirs = pl.multiple_of(half - (z + 1) // 2 % 2 * half, 16)
    n = d.shape[0]
    rows = n * RP

    def load(layer, block, n, at):
        return pltpu.make_async_copy(w_ref.at[pl.ds(pl.multiple_of((layer * NC + block) * D, 16), n * D)], wk.at[pl.ds(at * D, n * D)], wsem.at[0 if at else 1])

    def fetch(src, slot, layer):
        return pltpu.make_async_copy(src.at[layer], ab.at[slot], asem.at[slot])

    def remote(kind, p, src, dst, **to):
        return pltpu.make_async_remote_copy(src_ref=src, dst_ref=dst, send_sem=ssem.at[p, kind], recv_sem=rsem.at[p, kind],
                                            device_id=to, device_id_type=MESH)

    def live(v):
        return (v >= 0) & (v < 24)

    def kind(n, v):
        p, q = v % 2, v % 4
        if n == 0:
            lc = v % NC
            return remote(0, q, gb.at[lc - 9 * (lc // 9), :, 1 - core], rc.at[p], fsdp=fc)
        if n == 1:
            return remote(1, q, s2.at[p, :, 1 - x, pl.ds(0, half)], ra.at[q], fsdp=fx)
        if n == 2:
            return remote(2, q, s2.at[p, 1 - y, :, pl.ds(half, half)], rb.at[q], fsdp=fy)
        if n == 3:
            return remote(3, q, s3a.at[p, 1 - y], r3a.at[p], fsdp=fy)
        if n == 4:
            return remote(4, q, s3b.at[p, 1 - x], r3b.at[p], fsdp=fx)
        if n == 5:
            return remote(5, q, s4.at[p, pl.ds(theirs, half)], rz.at[q], rep=z1)
        if n == 6:
            return remote(6, q, s5.at[p], ry.at[q], rep=z3)
        return remote(7, q, s6.at[p], rw.at[p], rep=z1)

    def put(v, act):
        lc, layer = v % NC, LAYERS - 1 - v // NC
        p = v % 2
        out = (lc >= 4) & (lc < 9)

        @pl.when(out)
        def _():
            act(pltpu.make_async_copy(fin.at[p], gout_ref.at[layer, pl.ds(pl.multiple_of((lc - 4) * CH, 8), CH)], osem.at[p]))

        @pl.when(jnp.logical_not(out))
        def _():
            j = lc + 3 - 9 * (lc // 9)
            j = j - 3 * (lc // 9)
            act(pltpu.make_async_copy(fin.at[p], gin_ref.at[layer, :, pl.ds(pl.multiple_of(j * D, 128), D)], osem.at[p]))

    def add(a, b):
        return a + b

    def tick(t):
        @pl.when(live(t - 10))
        def _():
            put(t - 10, lambda a: a.wait())

        @pl.when(live(t - 9))
        def _():
            v = t - 9
            p = v % 2
            kind(7, v).wait()
            fin[p, pl.ds(mine, half)] = s6[p].astype(F32)
            fin[p, pl.ds(theirs, half)] = rw[p].astype(F32)
            put(v, lambda a: a.start())

        @pl.when(live(t - 8))
        def _():
            v = t - 8
            p = v % 2
            kind(6, v).wait()
            s6[p] = add(s5[p], ry[v % 4]).astype(BF)
            kind(7, v).start()

        @pl.when(live(t - 6))
        def _():
            v = t - 6
            p = v % 2
            kind(5, v).wait()
            s5[p] = add(s4[p, pl.ds(mine, half)], rz[v % 4]).astype(BF)
            kind(6, v).start()

        @pl.when(live(t - 4))
        def _():
            v = t - 4
            p = v % 2
            kind(3, v).wait()
            kind(4, v).wait()
            s4[p, 0:half] = add(s3a[p, y], r3a[p]).astype(BF)
            s4[p, half:CH] = add(s3b[p, x], r3b[p]).astype(BF)
            kind(5, v).start()

        @pl.when(live(t - 3))
        def _():
            v = t - 3
            p, q = v % 2, v % 4
            kind(1, v).wait()
            kind(2, v).wait()
            for i in range(2):
                s3a[p, i] = add(s2[p, i, x, 0:half], ra[q, i]).astype(BF)
                s3b[p, i] = add(s2[p, y, i, half:CH], rb[q, i]).astype(BF)
            kind(3, v).start()
            kind(4, v).start()

        @pl.when(live(t - 1))
        def _():
            v = t - 1
            p = v % 2
            kind(0, v).wait()
            lc = v % NC
            for i in range(4):
                s2[p, i // 2, i % 2] = add(gb[lc - 9 * (lc // 9), i, core], rc[p, i]).astype(BF)
            kind(1, v).start()
            kind(2, v).start()

        @pl.when(live(t))
        def _():
            kind(0, t).start()

    @pl.when((lr == 0) & (s == 0))
    def _():
        load(l, 3, 9, 0).start()
        bar = pltpu.get_barrier_semaphore()
        for k in range(1, 8):
            pl.semaphore_signal(bar, inc=1, device_id={"fsdp": (f + k) % 8}, device_id_type=MESH)
        for k in range(1, 4):
            pl.semaphore_signal(bar, inc=1, device_id={"rep": (z + k) % 4}, device_id_type=MESH)
        pl.semaphore_wait(bar, 10)
        dv[...] = jnp.zeros_like(dv)
        fetch(a2_ref, 0, l).start()
        for i in range(n):
            d[i] = jnp.zeros((RP, D), F32)
            d[i, 0:SEQ, :] = cot_ref[i].astype(F32)
        load(l, 3, 9, 0).wait()

    @pl.when((lr == 1) & (s == 0))
    def _():
        load(l, 3, 3, 0).wait()
        load(l, 6, 6, 3).wait()

    @pl.when(s == 0)
    def _():
        fetch(o_ref, 1, l).start()

    @pl.when(s == 1)
    def _():
        fetch(a2_ref, 0, l).wait()

    @pl.when(s == 8)
    def _():
        fetch(a1_ref, 0, l).start()

    @pl.when(s == 13)
    def _():
        fetch(o_ref, 1, l).wait()
        load(l, 0, 3, 0).start()

        @pl.when(lr == 0)
        def _():
            load(l - 1, 6, 6, 3).start()

    @pl.when(s == 23)
    def _():
        fetch(a1_ref, 0, l).wait()

    @pl.when(s == 26)
    def _():
        load(l, 0, 3, 0).wait()

    @pl.when((s == 27) & (lr == 0))
    def _():
        fetch(a2_ref, 0, l - 1).start()
        load(l - 1, 3, 3, 0).start()

    one = (s >= 2) & (s <= 8) & (s % 2 == 0)
    two = (s >= 18) & (s <= 22) & (s != 20)
    three = s == 24
    four = (lr == 0) & ((s == 26) | (s == 28))
    five = (lr == 1) & (s >= 25)
    six = (lr == 1) & (s == 0)
    back = s - 18
    t = jnp.where(one, 12 * lr + s // 2 - 1, jnp.where(two, 12 * lr + 4 + back - back // 3, jnp.where(three, 12 * lr + 8, jnp.where(
        four, 9 + (s - 26) // 2, jnp.where(five, s - 4, 11)))))

    @pl.when(one | two | three | four | five | six)
    def _():
        tick(t)

    @pl.when(s == 0)
    def _():
        for i in range(n):
            up = d[i]
            db[i] = up.astype(BF)
            acc[i] = jnp.zeros((RP, D), F32)
            dv[l, 7:8] += rsum(up)

    @pl.when((s < 8) & (s % 2 == 0))
    def _():
        j = s // 2
        whole = db[...].reshape(rows, D)
        cols = pl.multiple_of(j * D, 128)
        for q in range(3):
            t1 = dot_t(whole, wk[pl.ds(pl.multiple_of((5 + j) * D + 256 * q, 16), 256), :])
            t1 = t1 * g_ref[0, :, :, 256 * q:256 * q + 256].reshape(rows, 256).astype(F32)
            dv[l, pl.ds(8 + j, 1), 256 * q:256 * q + 256] += rsum(t1)
            du[:, :, pl.ds(pl.multiple_of(cols + 256 * q, 128), 256)] = t1.astype(BF).reshape(n, RP, 256)
        acc[...] += dot_t(du[:, :, pl.ds(cols, D)].reshape(rows, D), wk[pl.ds(pl.multiple_of(j * D, 16), D), :]).reshape(n, RP, D)

    @pl.when((s >= 8) & (s < 13))
    def _():
        i = s - 8
        dx, dg, dc = norm_back(h1_ref[0, 0], vec_ref[l, 5:6], acc[i])
        dv[l, 5:6] += dg
        dv[l, 6:7] += dc
        dh1 = d[i] + dx
        d[i] = dh1
        dv[l, 4:5] += rsum(dh1)
        dhb[i] = dh1.astype(BF)
        du[i, :, 3 * D:4 * D] = dot_t(dhb[i], wk[4 * D:5 * D, :]).astype(BF)

    def grad(lhs, rhs, store):
        for m in range(2):
            r = dot_0(lhs(384 * m), rhs).astype(BF).reshape(4, CH, D)
            store(4 * m, r)

    def inner(slot, j):
        def store(m, r):
            gb[slot, m // 2, 0] = r[0]
            gb[slot, m // 2, 1] = r[1]
            gb[slot, m // 2 + 1, 0] = r[2]
            gb[slot, m // 2 + 1, 1] = r[3]
        grad(lambda m: ab[0, :, :, m:m + 384].reshape(rows, 384), du[:, :, pl.ds(pl.multiple_of(D * j, 128), D)].reshape(rows, D), store)

    def outer(step, lhs, rhs):
        def store(m, r):
            for q in range(4):
                b = 8 * step + m + q
                gb[4 + b % 5, b // 10, (b // 5) % 2] = r[q]
        grad(lhs, rhs[...].reshape(rows, D), store)

    @pl.when((s < 8) & (s % 2 == 1))
    def _():
        inner(s // 2, s // 2)

    @pl.when(s == 13)
    def _():
        outer(0, lambda m: ab[1, :, :, m:m + 384].reshape(rows, 384), dhb)

    @pl.when((s >= 14) & (s < 18))
    def _():
        outer(s - 13, lambda m: e_ref[0, :, :, m:m + 384].reshape(rows, 384), db)

    @pl.when((s >= 18) & (s < 23))
    def _():
        i = s - 18
        for p in range(6):
            b = 128 * p
            dq, dk, dvv = attn_bwd(qkv_ref[0, 0, :, b:b + 128], qkv_ref[0, 0, :, D + b:D + b + 128], qkv_ref[0, 0, :, 2 * D + b:2 * D + b + 128],
                                   du[i, :, 3 * D + b:3 * D + b + 128])
            dv[l, 2:3, b:b + 128] += rsum(dq)
            dv[l, 3:4, b:b + 128] += rsum(dvv)
            du[i, :, b:b + 128] = dq.astype(BF)
            du[i, :, D + b:D + b + 128] = dk.astype(BF)
            du[i, :, 2 * D + b:2 * D + b + 128] = dvv.astype(BF)

    @pl.when((s >= 23) & (s < 26))
    def _():
        inner(s - 23, s - 23)

    @pl.when(s == 26)
    def _():
        acc[...] = dot_t(du[:, :, 0:D].reshape(rows, D), wk[0:D, :]).reshape(n, RP, D)
        acc[...] += dot_t(du[:, :, D:2 * D].reshape(rows, D), wk[D:2 * D, :]).reshape(n, RP, D)
        acc[...] += dot_t(du[:, :, 2 * D:3 * D].reshape(rows, D), wk[2 * D:3 * D, :]).reshape(n, RP, D)

    @pl.when(s >= 27)
    def _():
        i = s - 27
        dx, dg, dc = norm_back(hs_ref[0, 0], vec_ref[l, 0:1], acc[i])
        dv[l, 0:1] += dg
        dv[l, 1:2] += dc
        dh = d[i] + dx
        d[i] = dh
        di_ref[0] = dh[0:SEQ]

    @pl.when((lr == 1) & (s == 31))
    def _():
        for layer in range(LAYERS):
            for c in range(72):
                vs[c // 9, layer, c % 9:c % 9 + 1, :] = dv[layer, c // 6:c // 6 + 1, 128 * (c % 6):128 * (c % 6) + 128]

        def vcopy(k):
            to = (f + k) % 8
            return pltpu.make_async_remote_copy(src_ref=vs.at[to], dst_ref=vr.at[k - 1], send_sem=vssem.at[k - 1], recv_sem=vrsem.at[k - 1],
                                                device_id={"fsdp": to}, device_id_type=MESH)

        def zcopy(k):
            return pltpu.make_async_remote_copy(src_ref=vz.at[z], dst_ref=vz.at[z], send_sem=vssem.at[6 + k], recv_sem=vrsem.at[6 + k],
                                                device_id={"rep": (z + k) % 4}, device_id_type=MESH)
        for k in range(1, 8):
            vcopy(k).start()
        for t in range(28, 34):
            tick(jnp.int32(t))
        for k in range(1, 8):
            vcopy(k).wait()
        total = vs[f]
        for k in range(7):
            total = total + vr[k]
        vz[z] = total
        for k in range(1, 4):
            zcopy(k).start()
        for k in range(1, 4):
            zcopy(k).wait()
        gv_ref[...] = (vz[0] + vz[1]) + (vz[2] + vz[3])


def bwd(cotangent, w, vec, hs, h1, g, e, qkv, a2, o, a1, shard_in, shard_out):
    n = cotangent.shape[0]
    S = jax.ShapeDtypeStruct
    anyw = pl.BlockSpec(memory_space=pl.ANY)
    row = lambda cols, at: pl.BlockSpec((1, 1, RP, cols), lambda lr, s: (LAYERS - 1 - lr, jnp.clip(s - at, 0, 4), 0, 0))
    tok = lambda index: pl.BlockSpec((1, SEQ, D), index)
    VB = lambda *shape: pltpu.VMEM(shape, BF)
    half = CH // 2
    return pl.pallas_call(
        bwd_kernel, grid=(LAYERS, 32),
        in_specs=[pl.BlockSpec(cotangent.shape, lambda lr, s: (0, 0, 0), pipeline_mode=pl.Buffered(1)), anyw, pl.BlockSpec(vec.shape, lambda lr, s: (0, 0, 0)),
                  row(D, 27), row(D, 8), pl.BlockSpec((1, n, RP, D), lambda lr, s: (LAYERS - 1 - lr, 0, 0, jnp.minimum(s // 2, 3))),
                  pl.BlockSpec((1, n, RP, D), lambda lr, s: (LAYERS - 1 - lr, 0, 0, jnp.clip(s - 14, 0, 3))),
                  row(3 * D, 18), anyw, anyw, anyw],
        out_specs=[tok(lambda lr, s: (lr * jnp.clip(s - 27, 0, 4), 0, 0)), anyw, anyw, pl.BlockSpec((LAYERS, 16, 128), lambda lr, s: (0, 0, 0))],
        out_shape=[S(cotangent.shape, F32), S(shard_in, F32), S(shard_out, F32), S((LAYERS, 16, 128), F32)],
        scratch_shapes=[VB(9 * D, D), pltpu.VMEM((n, RP, D), F32), pltpu.VMEM((n, RP, D), F32), VB(n, RP, D), VB(n, RP, D), VB(n, RP, 4 * D), VB(2, n, RP, D),
                        VB(9, 4, 2, CH, D), pltpu.VMEM((LAYERS, 16, D), F32),
                        VB(2, 4, CH, D), VB(2, 2, 2, CH, D), VB(4, 2, half, D), VB(4, 2, half, D), VB(2, 2, half, D), VB(2, 2, half, D),
                        VB(2, half, D), VB(2, half, D), VB(2, CH, D), VB(4, half, D), VB(2, half, D), VB(4, half, D), VB(2, half, D), VB(2, half, D),
                        pltpu.VMEM((2, CH, D), F32),
                        pltpu.VMEM((8, LAYERS, 16, 128), F32), pltpu.VMEM((7, LAYERS, 16, 128), F32), pltpu.VMEM((4, LAYERS, 16, 128), F32),
                        pltpu.SemaphoreType.DMA((2,)), pltpu.SemaphoreType.DMA((2,)), pltpu.SemaphoreType.DMA((4, 8)), pltpu.SemaphoreType.DMA((4, 8)),
                        pltpu.SemaphoreType.DMA((2,)), pltpu.SemaphoreType.DMA((10,)), pltpu.SemaphoreType.DMA((10,))],
        compiler_params=pltpu.CompilerParams(collective_id=1, has_side_effects=True, vmem_limit_bytes=63 * 2**20),
    )(cotangent, w, vec, hs, h1, g, e, qkv, a2, o, a1)


STEP = 3
beta_one = 0.9
beta_two = 0.999
matrix_rate = 0.03
vector_rate = 0.2
matrix_decay = 0.05
adam_eps = 1e-8


def adam_update(master, gradient, moment_one, moment_two, rate, decay_rate):
    moment_one = beta_one * moment_one + (1.0 - beta_one) * gradient
    moment_two = beta_two * moment_two + (1.0 - beta_two) * gradient * gradient
    corr_one = 1.0 - beta_one**STEP
    corr_two = 1.0 - beta_two**STEP
    adam_move = moment_one / corr_one / (jnp.sqrt(moment_two / corr_two) + adam_eps)
    return (master - rate * (adam_move + decay_rate * master), moment_one, moment_two)


def adam_kernel(g_ref, w_ref, m_ref, v_ref, go_ref, wo_ref, mo_ref, vo_ref, enc_ref, dim_ref,
                g_out, w_out, m_out, v_out, go_out, wo_out, mo_out, vo_out, enc_out, dim_out, steps):
    i = pl.program_id(0)

    def update(g, w, m, v, outs):
        grad = g[...]
        new, moment, square = adam_update(w[...], grad, m[...], v[...], matrix_rate, matrix_decay)
        outs[0][...], outs[1][...], outs[2][...], outs[3][...] = grad, new, moment, square

    @pl.when(i < steps)
    def _():
        update(g_ref, w_ref, m_ref, v_ref, (g_out, w_out, m_out, v_out))

    @pl.when(i >= steps)
    def _():
        update(go_ref, wo_ref, mo_ref, vo_ref, (go_out, wo_out, mo_out, vo_out))

    @pl.when(i < enc_steps)
    def _():
        enc_out[...] = enc_ref[...]
        dim_out[...] = dim_ref[...]


enc_steps = 5


def adam_all(ins, outs, encoded, dimg):
    a, b = ins[0].shape, outs[0].shape
    steps = 3 * LAYERS
    first = pl.BlockSpec((1, a[1], a[2] // 3), lambda i: (jnp.minimum(i, steps - 1) // 3, 0, jnp.minimum(i, steps - 1) % 3))
    second = pl.BlockSpec((1, b[1] // 3, b[2]), lambda i: (jnp.maximum(i - steps, 0) // 3, jnp.maximum(i - steps, 0) % 3, 0))
    tok = pl.BlockSpec((1,) + encoded.shape[1:], lambda i: (jnp.minimum(i, enc_steps - 1), 0, 0))
    S = jax.ShapeDtypeStruct
    return pl.pallas_call(
        functools.partial(adam_kernel, steps=steps), grid=(2 * steps,),
        in_specs=[first] * 4 + [second] * 4 + [tok] * 2, out_specs=[first] * 4 + [second] * 4 + [tok] * 2,
        out_shape=[S(a, F32)] * 4 + [S(b, F32)] * 4 + [S(encoded.shape, BF), S(dimg.shape, F32)],
        compiler_params=PAR,
    )(*ins, *outs, encoded, dimg)


def swap(x, axis, size, mask):
    return lax.ppermute(x, axis, [(i, i ^ mask) for i in range(size)])


def halve(x, order, size):
    bits = size.bit_length() - 1
    me = lax.axis_index("fsdp")
    x = x.reshape((2,) * bits + x.shape[1:])
    left = list(range(bits))[::-1]
    for bit in order:
        at = left.index(bit)
        mine = (me >> bit) & 1
        keep = lax.dynamic_index_in_dim(x, mine, at, keepdims=False)
        send = lax.dynamic_index_in_dim(x, 1 - mine, at, keepdims=False)
        got = swap(send, "fsdp", size, 1 << bit)
        x = (keep.astype(F32) + got.astype(F32)).astype(BF)
        left.remove(bit)
    return x


def reduce_all(x, nf, nr):
    bits = nf.bit_length() - 1
    rows, cols = x.shape
    x = x.reshape(nf, rows // nf, cols)
    half = cols // 2 // 128 * 128
    up = [0] + list(range(1, bits))
    down = [0] + list(range(1, bits))[::-1]
    x = jnp.concatenate([halve(x[..., :half], up, nf), halve(x[..., half:], down, nf)], axis=-1)
    mask = 1
    while mask < nr:
        got = swap(x, "rep", nr, 2 * mask - 1)
        y = x.astype(F32) + got.astype(F32)
        x = y.astype(BF)
        mask *= 2
    return y


def fused_step(images, cotangent, weight_in, weight_out, vector_params):
    vs = jnp.pad(vector_params.astype(BF).astype(F32).reshape(LAYERS, 9, 128), ((0, 0), (0, 7), (0, 0)))
    hs, qkv, a1, o, h1, a2, e, g, encoded, w, vec = fwd(images, weight_in, weight_out, vs)
    dimg, gi, go, gv = bwd(cotangent, w, vec, hs, h1, g, e, qkv, a2, o, a1, weight_in.shape, weight_out.shape)
    return encoded, dimg, gi, go, gv[:, :9].reshape(vector_params.shape)


def plain_step(nf, nr, images, cotangent, weight_in, weight_out, vector_params):
    pad = lambda a: jnp.pad(a, ((0, 0), (0, RP - SEQ), (0, 0)))
    vec_all = lax.all_gather(vector_params.astype(BF), "fsdp", axis=1, tiled=True).astype(F32)
    h = pad(images)
    ct = pad(cotangent)
    saved = []
    for l in range(LAYERS):
        win = lax.all_gather(weight_in[l].astype(BF), "fsdp", axis=0, tiled=True)
        wout = lax.all_gather(weight_out[l].astype(BF), "fsdp", axis=0, tiled=True)
        vec = jnp.pad(vec_all[l].reshape(12, D), ((0, 4), (0, 0)))
        wqkv, w1, wo, w2 = win[:, : 3 * D], win[:, 3 * D :], wout[:D], wout[D:]
        qkv, o, a1 = ka(h, wqkv, vec)
        h1, a2, e, g, h2 = kb(h, o, wo, w1, w2, vec)
        saved.append((h, wqkv, w1, wo, w2, vec, qkv, o, a1, h1, a2, e, g))
        h = h2
    encoded = h[:, :SEQ].astype(BF)
    d = ct
    gin, gout, gvec = [None] * LAYERS, [None] * LAYERS, [None] * LAYERS
    for l in reversed(range(LAYERS)):
        h, wqkv, w1, wo, w2, vec, qkv, o, a1, h1, a2, e, g = saved[l]
        db, du, dh1, dh1b, do, dv1 = kc(d, h1, g, wo, w1, w2, vec)
        g1 = reduce_all(dw(a2, du), nf, nr)
        go = reduce_all(jnp.concatenate([dw(o, dh1b), dw(e, db)], axis=0), nf, nr)
        dz, dv2 = kd(qkv, do)
        gq = reduce_all(dw(a1, dz), nf, nr)
        d, dv3 = kf(dz, h, dh1, wqkv, vec, RP if l else SEQ)
        gin[l] = jnp.concatenate([gq, g1], axis=1)
        gout[l] = go
        gvec[l] = (dv1 + dv2 + dv3)[:12].reshape(-1)
    gv = lax.psum(jnp.stack(gvec), ("fsdp", "rep"))
    wide = gv.shape[1] // nf
    gv = lax.dynamic_slice_in_dim(gv, lax.axis_index("fsdp") * wide, wide, 1)
    return encoded, d, jnp.stack(gin), jnp.stack(gout), gv


def make_shards(nf, nr):
    def shards(images, cotangent, weight_in, weight_out, vector_params, first_in, first_out, first_vec, second_in, second_out, second_vec):
        if nf == 8 and nr == 4:
            encoded, d, gi, go, gv = fused_step(images, cotangent, weight_in, weight_out, vector_params)
            gi, new_in, moment_in, square_in, go, new_out, moment_out, square_out, encoded, d = adam_all(
                (gi, weight_in, first_in, second_in), (go, weight_out, first_out, second_out), encoded, d)
        else:
            encoded, d, gi, go, gv = plain_step(nf, nr, images, cotangent, weight_in, weight_out, vector_params)
            new_in, moment_in, square_in = adam_update(weight_in, gi, first_in, second_in, matrix_rate, matrix_decay)
            new_out, moment_out, square_out = adam_update(weight_out, go, first_out, second_out, matrix_rate, matrix_decay)
        new_vec, moment_vec, square_vec = adam_update(vector_params, gv, first_vec, second_vec, vector_rate, 0.0)
        return (encoded, d, gi, go, gv, new_in, new_out, new_vec, moment_in, moment_out, moment_vec, square_in, square_out, square_vec)

    return shards


def solution(mesh):
    tokens = P(("fsdp", "rep"), None, None)
    matrix = P(None, "fsdp", None)
    vector = P(None, "fsdp")
    in_specs = (tokens, tokens) + (matrix, matrix, vector) * 3
    out_specs = (tokens, tokens) + (matrix, matrix, vector) * 4
    return jax.shard_map(make_shards(mesh.shape["fsdp"], mesh.shape["rep"]), mesh=mesh, in_specs=in_specs, out_specs=out_specs, check_vma=False)
```

```python
import functools
import jax, jax.numpy as jnp
from jax import lax
from jax.experimental import pallas as pl
from jax.experimental.pallas import tpu as pltpu
from jax.sharding import PartitionSpec as P

D=768; HD=64; SEQ=197; RP=208; EPS=1e-6
BF=jnp.bfloat16; F32=jnp.float32
def dot(a,b): return jnp.dot(a,b,preferred_element_type=F32)
def dot_t(a,b): return lax.dot_general(a,b,(((1,),(1,)),((),())),preferred_element_type=F32)
def dot_0(a,b): return lax.dot_general(a,b,(((0,),(0,)),((),())),preferred_element_type=F32)

def norm_stats(x):
    mean=jnp.mean(x,axis=-1,keepdims=True); xc=x-mean
    var=jnp.mean(xc*xc,axis=-1,keepdims=True)
    return xc, lax.rsqrt(var+EPS)

def head_masks(scale):
    lane = lax.broadcasted_iota(jnp.int32, (1, 128), 1)
    return jnp.where(lane < 64, scale, 0.0).astype(BF), jnp.where(lane < 64, 0.0, scale).astype(BF)


def weights_t(q, k, masks):
    row = lax.broadcasted_iota(jnp.int32, (RP, 1), 0)
    s = [jnp.where(row < SEQ, dot_t(k, q * m), -1e30) for m in masks]
    e = [jnp.exp(x - jnp.max(x, axis=0, keepdims=True)) for x in s]
    return [x * (1.0 / jnp.sum(x, axis=0, keepdims=True)) for x in e]


def attn_fwd(q, k, v):
    ones = head_masks(1.0)
    row = lax.broadcasted_iota(jnp.int32, (16, 1), 0)
    ps = []
    for m in head_masks(0.125):
        s = dot_t(k, q * m)
        s = jnp.concatenate([s[:RP - 16], jnp.where(row < SEQ - RP + 16, s[RP - 16:], -1e30)], axis=0)
        e = jnp.exp(s - jnp.max(s, axis=0, keepdims=True))
        ps.append((e * (1.0 / jnp.sum(e, axis=0, keepdims=True))).astype(BF))
    return (dot_0(ps[0], v * ones[0]) + dot_0(ps[1], v * ones[1])).astype(BF)


def attn_bwd(q, k, v, do):
    scaled, ones = head_masks(0.125), head_masks(1.0)
    p = weights_t(q, k, scaled)
    dos = [do * m for m in ones]
    dp = [dot_t(v, x) for x in dos]
    pb = [x.astype(BF) for x in p]
    ds = [(a * (b - jnp.sum(a * b, axis=0, keepdims=True))).astype(BF) for a, b in zip(p, dp)]
    dv = dot(pb[0], dos[0]) + dot(pb[1], dos[1])
    dk = dot(ds[0], q * scaled[0]) + dot(ds[1], q * scaled[1])
    dq = dot_0(ds[0], k * scaled[0]) + dot_0(ds[1], k * scaled[1])
    return dq, dk, dv


def ka_kernel(h_ref,w_ref,vec_ref,qkv_ref,o_ref,a_ref):
    h=h_ref[0].astype(F32)
    xc,rs=norm_stats(h)
    a_ref[0]=(xc*rs*vec_ref[0:1]+vec_ref[1:2]).astype(BF)
    a=a_ref[0]
    for c in range(3):
        cs=slice(256*c,256*c+256)
        qkv_ref[0,:,256*c:256*c+256]=(dot(a,w_ref[:,256*c:256*c+256])+vec_ref[2:3,cs]).astype(BF)
        qkv_ref[0,:,D+256*c:D+256*c+256]=dot(a,w_ref[:,D+256*c:D+256*c+256]).astype(BF)
        qkv_ref[0,:,2*D+256*c:2*D+256*c+256]=(dot(a,w_ref[:,2*D+256*c:2*D+256*c+256])+vec_ref[3:4,cs]).astype(BF)
        for p in range(2):
            b=256*c+128*p
            o_ref[0,:,b:b+128]=attn_fwd(qkv_ref[0,:,b:b+128],qkv_ref[0,:,D+b:D+b+128],qkv_ref[0,:,2*D+b:2*D+b+128])

def img(n,dt=None): return pl.BlockSpec((1,RP,n),lambda i:(i,0,0))
def full(shape): return pl.BlockSpec(shape,lambda i:(0,)*len(shape))
PAR=pltpu.CompilerParams(vmem_limit_bytes=60*2**20)

def ka(h,w,vec):
    n=h.shape[0]
    return pl.pallas_call(ka_kernel,grid=(n,),in_specs=[img(D),full(w.shape),full(vec.shape)],
        out_specs=[img(3*D),img(D),img(D)],
        out_shape=[jax.ShapeDtypeStruct((n,RP,3*D),BF),jax.ShapeDtypeStruct((n,RP,D),BF),jax.ShapeDtypeStruct((n,RP,D),BF)],
        compiler_params=PAR)(h,w,vec)

def gelu_parts(u):
    c=0.5*(1.0+lax.erf(u*0.7071067811865476))
    g=c+u*(jnp.exp(-0.5*u*u)*0.3989422804014327)
    return u*c,g

def kb_kernel(FC,h_ref,o_ref,wo_ref,w1_ref,w2_ref,vec_ref,h1_ref,a_ref,e_ref,g_ref,h2_ref):
    h1=h_ref[0].astype(F32)+dot(o_ref[0],wo_ref[...])+vec_ref[4:5]
    h1_ref[0]=h1
    xc,rs=norm_stats(h1)
    a_ref[0]=(xc*rs*vec_ref[5:6]+vec_ref[6:7]).astype(BF)
    a=a_ref[0]
    h2_ref[0]=h1+vec_ref[7:8]
    for j in range(3072//FC):
        lo=FC*j
        u=dot(a,w1_ref[:,lo:lo+FC])+vec_ref[8+lo//D:9+lo//D,lo%D:lo%D+FC]
        e,g=gelu_parts(u)
        e_ref[0,:,lo:lo+FC]=e.astype(BF); g_ref[0,:,lo:lo+FC]=g.astype(BF)
        h2_ref[0]+=dot(e_ref[0,:,lo:lo+FC],w2_ref[lo:lo+FC,:])

def kb(h,o,wo,w1,w2,vec,FC=256):
    n=h.shape[0]
    S=jax.ShapeDtypeStruct
    return pl.pallas_call(functools.partial(kb_kernel,FC),grid=(n,),in_specs=[img(D),img(D),full(wo.shape),full(w1.shape),full(w2.shape),full(vec.shape)],
        out_specs=[img(D),img(D),img(3072),img(3072),img(D)],
        out_shape=[S((n,RP,D),F32),S((n,RP,D),BF),S((n,RP,3072),BF),S((n,RP,3072),BF),S((n,RP,D),F32)],
        compiler_params=PAR)(h,o,wo,w1,w2,vec)

def rsum(x): return jnp.sum(x,axis=0,keepdims=True)
def norm_back(x,gain,dy):
    xc,rs=norm_stats(x); xh=xc*rs
    dyg=dy*gain
    dx=rs*(dyg-jnp.mean(dyg,axis=-1,keepdims=True)-xh*jnp.mean(dyg*xh,axis=-1,keepdims=True))
    return dx, rsum(dy*xh), rsum(dy)

def kc_kernel(FC,d_ref,h1_ref,g_ref,wo_ref,w1_ref,w2_ref,vec_ref,db_ref,du_ref,dh1_ref,dh1b_ref,do_ref,dv_ref,acc_ref):
    @pl.when(pl.program_id(0)==0)
    def _(): dv_ref[...]=jnp.zeros_like(dv_ref)
    d=d_ref[0].astype(F32)
    db_ref[0]=d.astype(BF)
    db=db_ref[0]
    dv_ref[7:8]+=rsum(d)
    for j in range(3072//FC):
        lo=FC*j
        du=dot_t(db,w2_ref[lo:lo+FC,:])*g_ref[0,:,lo:lo+FC].astype(F32)
        dv_ref[8+lo//D:9+lo//D,lo%D:lo%D+FC]+=rsum(du)
        du_ref[0,:,lo:lo+FC]=du.astype(BF)
        t=dot_t(du_ref[0,:,lo:lo+FC],w1_ref[:,lo:lo+FC])
        if j==0: acc_ref[...]=t
        else: acc_ref[...]+=t
    dx,dg,dc=norm_back(h1_ref[0],vec_ref[5:6],acc_ref[...])
    dv_ref[5:6]+=dg; dv_ref[6:7]+=dc
    dh1=d_ref[0].astype(F32)+dx
    dh1_ref[0]=dh1
    dv_ref[4:5]+=rsum(dh1)
    dh1b_ref[0]=dh1.astype(BF)
    do_ref[0]=dot_t(dh1b_ref[0],wo_ref[...]).astype(BF)

def kc(d,h1,g,wo,w1,w2,vec,FC=256):
    n=d.shape[0]; S=jax.ShapeDtypeStruct
    return pl.pallas_call(functools.partial(kc_kernel,FC),grid=(n,),in_specs=[img(D),img(D),img(3072),full(wo.shape),full(w1.shape),full(w2.shape),full(vec.shape)],
        out_specs=[img(D),img(3072),img(D),img(D),img(D),full((16,D))],
        out_shape=[S((n,RP,D),BF),S((n,RP,3072),BF),S((n,RP,D),F32),S((n,RP,D),BF),S((n,RP,D),BF),S((16,D),F32)],
        scratch_shapes=[pltpu.VMEM((RP,D),F32)],
        compiler_params=PAR)(d,h1,g,wo,w1,w2,vec)

def kd_kernel(qkv_ref,do_ref,dz_ref,dv_ref):
    @pl.when(pl.program_id(0)==0)
    def _(): dv_ref[...]=jnp.zeros_like(dv_ref)
    for p in range(6):
        b=128*p
        dq,dk,dv=attn_bwd(qkv_ref[0,:,b:b+128],qkv_ref[0,:,D+b:D+b+128],qkv_ref[0,:,2*D+b:2*D+b+128],do_ref[0,:,b:b+128])
        dv_ref[2:3,b:b+128]+=rsum(dq); dv_ref[3:4,b:b+128]+=rsum(dv)
        dz_ref[0,:,b:b+128]=dq.astype(BF); dz_ref[0,:,D+b:D+b+128]=dk.astype(BF); dz_ref[0,:,2*D+b:2*D+b+128]=dv.astype(BF)

def kd(qkv,do):
    n=do.shape[0]; S=jax.ShapeDtypeStruct
    return pl.pallas_call(kd_kernel,grid=(n,),in_specs=[img(3*D),img(D)],out_specs=[img(3*D),full((16,D))],
        out_shape=[S((n,RP,3*D),BF),S((16,D),F32)],compiler_params=PAR)(qkv,do)

def kf_kernel(dz_ref,h_ref,dh1_ref,w_ref,vec_ref,dh_ref,dv_ref):
    @pl.when(pl.program_id(0)==0)
    def _(): dv_ref[...]=jnp.zeros_like(dv_ref)
    da=dot_t(dz_ref[0],w_ref[...])
    dx,dg,dc=norm_back(h_ref[0].astype(F32),vec_ref[0:1],da)
    dv_ref[0:1]+=dg; dv_ref[1:2]+=dc
    rows=dh_ref.shape[1]
    dh_ref[0]=(dh1_ref[0]+dx)[:rows]

def kf(dz,h,dh1,w,vec,rows=RP):
    n=dz.shape[0]; S=jax.ShapeDtypeStruct
    return pl.pallas_call(kf_kernel,grid=(n,),in_specs=[img(3*D),img(D),img(D),full(w.shape),full(vec.shape)],
        out_specs=[pl.BlockSpec((1,rows,D),lambda i:(i,0,0)),full((16,D))],
        out_shape=[S((n,rows,D),F32),S((16,D),F32)],compiler_params=PAR)(dz,h,dh1,w,vec)

def dw_kernel(l_ref,r_ref,o_ref):
    o_ref[...]=dot_0(l_ref[...],r_ref[...]).astype(BF)
def dw(l,r,MB=256):
    M=l.shape[-1]; N=r.shape[-1]; K=l.shape[0]*RP
    l=l.reshape(K,M); r=r.reshape(K,N)
    return pl.pallas_call(dw_kernel,grid=(M//MB,),in_specs=[pl.BlockSpec((K,MB),lambda i:(0,i)),pl.BlockSpec((K,N),lambda i:(0,0))],
       out_specs=pl.BlockSpec((MB,N),lambda i:(i,0)),out_shape=jax.ShapeDtypeStruct((M,N),BF),compiler_params=PAR)(l,r)


LAYERS = 2
MESH = pl.DeviceIdType.MESH
CH = 96
NC = 12


def plane():
    f = lax.axis_index("fsdp")
    core, x, y = f % 2, (f // 2) % 2, f // 4
    return f, core, x, y


def chunk_rows(c, f):
    layer, j = c // NC, c % NC
    early = 1 - (j + 9) // 12
    late = j // 8
    mid = 1 - early - late
    base = layer * NC * D
    return pl.multiple_of(base + early * (j * D + CH * f) + late * ((j - 5) * D + CH * f)
                          + mid * (7 * D + 5 * CH * f + CH * (j - 3)), 16)


def fwd_kernel(img_ref, win_ref, wout_ref, vs_ref, hs_ref, qkv_ref, a1_ref, o_ref, h1_ref, a2_ref, e_ref, g_ref, enc_ref, wo_ref, vo_ref,
               w, hb, ob, ab, vg, vec, st, lsem, ssem, rsem, vssem, vrsem, osem, vosem):
    l, s = pl.program_id(0), pl.program_id(1)
    f, core, x, y = plane()
    fc, fx, fy = f + 1 - 2 * core, f + 2 - 4 * x, f + 4 - 8 * y
    fd = fx + fy - f
    z = lax.axis_index("rep")
    side = z % 2
    zp = z + 1 - 2 * side
    part = pl.ds(pl.multiple_of(256 * side, 128), 512)
    give = pl.ds(pl.multiple_of(512 * side, 128), 256)

    def wrow(c, who, lo=0, n=CH):
        return pl.ds(pl.multiple_of(chunk_rows(c, who) + lo, 16), n)

    def send(c, kind, where, **to):
        return pltpu.make_async_remote_copy(src_ref=w.at[where], dst_ref=w.at[where], send_sem=ssem.at[c % 8, kind], recv_sem=rsem.at[c % 8, kind],
                                            device_id=to, device_id_type=MESH)

    def fetch(c, act):
        layer, j = c // NC, c % NC
        mid = (j >= 3) & (j < 8)

        @pl.when(mid)
        def _():
            act(pltpu.make_async_copy(wout_ref.at[layer, pl.ds(pl.multiple_of((j - 3) * CH, 8), CH)], st.at[c % 4], lsem.at[c % 4]))

        @pl.when(jnp.logical_not(mid))
        def _():
            act(pltpu.make_async_copy(win_ref.at[layer, :, pl.ds(pl.multiple_of((j - 5 * (j // 8)) * D, 128), D)], st.at[c % 4], lsem.at[c % 4]))

    def kinds(c):
        half = CH // 2
        return [lambda: send(c, 0, (wrow(c, f), part), fsdp=fx), lambda: send(c, 1, (wrow(c, f), part), fsdp=fy),
                lambda: send(c, 2, (wrow(c, f),), fsdp=fc),
                lambda: send(c, 3, (wrow(c, fx, 0, half), part), fsdp=fy), lambda: send(c, 4, (wrow(c, fy, half, half), part), fsdp=fx),
                lambda: send(c, 5, (wrow(c, fx), give), rep=zp), lambda: send(c, 6, (wrow(c, fy), give), rep=zp),
                lambda: send(c, 7, (wrow(c, fd), give), rep=zp),
                lambda: send(c, 8, (wrow(c, fx),), fsdp=fc), lambda: send(c, 9, (wrow(c, fy),), fsdp=fc), lambda: send(c, 10, (wrow(c, fd),), fsdp=fc)]

    def start(c, which):
        k = kinds(c)
        for i in which:
            k[i]().start()

    def wait(c, which):
        k = kinds(c)
        for i in which:
            k[i]().wait()

    def tick(t):
        @pl.when((t >= 6) & (t < 30))
        def _():
            wait(t - 6, (2, 8, 9, 10))

        @pl.when((t >= 5) & (t < 29))
        def _():
            wait(t - 5, (7,))
            start(t - 5, (10,))

        @pl.when((t >= 4) & (t < 28))
        def _():
            wait(t - 4, (5, 6))
            start(t - 4, (8, 9))

        @pl.when((t >= 3) & (t < 27))
        def _():
            wait(t - 3, (3, 4))
            start(t - 3, (7,))

        @pl.when((t >= 2) & (t < 26))
        def _():
            wait(t - 2, (0, 1))
            start(t - 2, (3, 4, 5, 6))

        @pl.when(t < 24)
        def _():
            fetch(t, lambda a: a.wait())
            w[pl.ds(chunk_rows(t, f), CH)] = st[t % 4].astype(BF)
            start(t, (0, 1, 2))

        @pl.when(t < 21)
        def _():
            fetch(t + 3, lambda a: a.start())

    def out_copy(b, n):
        return pltpu.make_async_copy(w.at[pl.ds(b, n)], wo_ref.at[pl.ds(b, n)], osem)

    @pl.when((l == 0) & (s == 0))
    def _():
        for c in range(3):
            fetch(jnp.int32(c), lambda a: a.start())
        bar = pltpu.get_barrier_semaphore()
        for k in range(1, 8):
            pl.semaphore_signal(bar, inc=1, device_id={"fsdp": (f + k) % 8}, device_id_type=MESH)
        pl.semaphore_signal(bar, inc=1, device_id={"rep": zp}, device_id_type=MESH)
        pl.semaphore_wait(bar, 8)

        def vcopy(k):
            return pltpu.make_async_remote_copy(src_ref=vs_ref, dst_ref=vg.at[f], send_sem=vssem.at[k - 1], recv_sem=vrsem.at[k - 1],
                                                device_id={"fsdp": (f + k) % 8}, device_id_type=MESH)
        for k in range(1, 8):
            vcopy(k).start()
        vg[f] = vs_ref[...]

        @pl.loop(0, 9)
        def _(t):
            tick(t)
        for k in range(1, 8):
            vcopy(k).wait()
        for layer in range(LAYERS):
            for c in range(72):
                vec[layer, c // 6:c // 6 + 1, 128 * (c % 6):128 * (c % 6) + 128] = vg[c // 9, layer, c % 9:c % 9 + 1, :]
        hb[...] = jnp.zeros_like(hb)
        cp = pltpu.make_async_copy(vec, vo_ref, vosem)
        cp.start()
        cp.wait()

    early = (1 - l) * (s + 8) + l * (s + 20)
    late = (1 - l) * (s + 4 + s // 11) + l * (s + 16)

    @pl.when((s == 0) & (l == 1))
    def _():
        tick(19)

    @pl.when((s == 11) & (l == 0))
    def _():
        tick(15)

    @pl.when((s <= 5) & (l + s > 0))
    def _():
        tick(early)

    @pl.when(s >= 10)
    def _():
        tick(late)

    @pl.when(s < 5)
    def _():
        @pl.when(l == 0)
        def _():
            hb[s, 0:SEQ, :] = img_ref[s].astype(F32)
        h = hb[s]
        hs_ref[0, 0] = h
        xc, rs = norm_stats(h)
        a1_ref[0, 0] = (xc * rs * vec[l, 0:1] + vec[l, 1:2]).astype(BF)
        a = a1_ref[0, 0]
        wb = l * NC * D

        def wq(part, c):
            return w[pl.ds(pl.multiple_of(wb + part * D, 16), D), 256 * c:256 * c + 256]
        for c in range(3):
            cs = slice(256 * c, 256 * c + 256)
            qkv_ref[0, 0, :, cs] = (dot(a, wq(0, c)) + vec[l, 2:3, cs]).astype(BF)
            qkv_ref[0, 0, :, D + 256 * c:D + 256 * c + 256] = dot(a, wq(1, c)).astype(BF)
            qkv_ref[0, 0, :, 2 * D + 256 * c:2 * D + 256 * c + 256] = (dot(a, wq(2, c)) + vec[l, 3:4, cs]).astype(BF)
            for p in range(2):
                b = 256 * c + 128 * p
                o = attn_fwd(qkv_ref[0, 0, :, b:b + 128], qkv_ref[0, 0, :, D + b:D + b + 128], qkv_ref[0, 0, :, 2 * D + b:2 * D + b + 128])
                o_ref[0, 0, :, b:b + 128] = o
                ob[s, :, b:b + 128] = o

    @pl.when((s >= 5) & (s < 10))
    def _():
        i = s - 5
        wo = w[pl.ds(pl.multiple_of((l * NC + 7) * D, 16), D), :]
        h1 = hb[i] + dot(ob[i], wo) + vec[l, 4:5]
        h1_ref[0, 0] = h1
        hb[i] = h1 + vec[l, 7:8]
        xc, rs = norm_stats(h1)
        a = (xc * rs * vec[l, 5:6] + vec[l, 6:7]).astype(BF)
        a2_ref[0, 0] = a
        ab[i] = a

    @pl.when(s >= 10)
    def _():
        j = s - 10
        up = pl.multiple_of((l * NC + 3 + j) * D, 16)
        down = pl.multiple_of((l * NC + 8 + j) * D, 16)

        bias = vec[l, pl.ds(8 + j, 1), :]
        n = hb.shape[0]
        u = dot(ab[0], w[pl.ds(up, D), :])
        for i in range(n):
            later = dot(ab[i + 1], w[pl.ds(up, D), :]) if i < n - 1 else None
            e, g = gelu_parts(u + bias)
            e = e.astype(BF)
            e_ref[0, i] = e
            g_ref[0, i] = g.astype(BF)
            hb[i] += dot(e, w[pl.ds(down, D), :])
            u = later

        @pl.when((l == 1) & (s == 13))
        def _():
            for i in range(n):
                enc_ref[i] = hb[i, 0:SEQ, :].astype(BF)

    for layer in range(LAYERS):
        base = layer * NC * D

        @pl.when((l == layer) & (s == 4))
        def _():
            out_copy(base, 3 * D).start()

        @pl.when((l == layer) & (s == 9))
        def _():
            out_copy(base + 7 * D, 5 * D).start()

        for j in range(4):
            @pl.when((l == layer) & (s == 10 + j))
            def _():
                out_copy(base + (3 + j) * D, D).start()

    @pl.when((l == 1) & (s == 13))
    def _():
        pltpu.make_async_copy(w, wo_ref, osem).wait()


def fwd(images, weight_in, weight_out, vshard):
    n = images.shape[0]
    S = jax.ShapeDtypeStruct
    one = lambda cols: pl.BlockSpec((1, 1, RP, cols), lambda l, s: (l, jnp.minimum(s, 4), 0, 0))
    two = lambda cols: pl.BlockSpec((1, 1, RP, cols), lambda l, s: (l, jnp.clip(s - 5, 0, 4), 0, 0))
    wide = pl.BlockSpec((1, n, RP, D), lambda l, s: (l, 0, 0, jnp.clip(s - 10, 0, 3)))
    anyw = pl.BlockSpec(memory_space=pl.ANY)
    rows = LAYERS * NC * D
    return pl.pallas_call(
        fwd_kernel, grid=(LAYERS, 14),
        in_specs=[pl.BlockSpec(images.shape, lambda l, s: (0, 0, 0)), anyw, anyw, pl.BlockSpec(vshard.shape, lambda l, s: (0, 0, 0))],
        out_specs=[one(D), one(3 * D), one(D), one(D), two(D), two(D), wide, wide, pl.BlockSpec(images.shape, lambda l, s: (0, 0, 0)), anyw, anyw],
        out_shape=[S((LAYERS, n, RP, D), F32), S((LAYERS, n, RP, 3 * D), BF), S((LAYERS, n, RP, D), BF), S((LAYERS, n, RP, D), BF),
                   S((LAYERS, n, RP, D), F32), S((LAYERS, n, RP, D), BF), S((LAYERS, n, RP, 4 * D), BF), S((LAYERS, n, RP, 4 * D), BF),
                   S(images.shape, BF), S((rows, D), BF), S((LAYERS, 16, D), F32)],
        scratch_shapes=[pltpu.VMEM((rows, D), BF), pltpu.VMEM((n, RP, D), F32), pltpu.VMEM((n, RP, D), BF), pltpu.VMEM((n, RP, D), BF),
                        pltpu.VMEM((8, LAYERS, 16, 128), F32), pltpu.VMEM((LAYERS, 16, D), F32), pltpu.VMEM((4, CH, D), F32),
                        pltpu.SemaphoreType.DMA((4,)), pltpu.SemaphoreType.DMA((8, 11)), pltpu.SemaphoreType.DMA((8, 11)),
                        pltpu.SemaphoreType.DMA((7,)), pltpu.SemaphoreType.DMA((7,)), pltpu.SemaphoreType.DMA, pltpu.SemaphoreType.DMA],
        compiler_params=pltpu.CompilerParams(collective_id=0, has_side_effects=True, vmem_limit_bytes=62 * 2**20),
    )(images, weight_in, weight_out, vshard)


def bwd_kernel(cot_ref, w_ref, vec_ref, hs_ref, h1_ref, g_ref, e_ref, qkv_ref, a2_ref, o_ref, a1_ref,
               di_ref, gin_ref, gout_ref, gv_ref,
               wk, d, acc, db, dhb, du, ab, gb, dv, rc, s2, ra, rb, s3a, s3b, r3a, r3b, s4, rz, s5, ry, s6, rw, fin,
               vs, vr, vz, wsem, asem, ssem, rsem, osem, vssem, vrsem):
    lr, s = pl.program_id(0), pl.program_id(1)
    l = LAYERS - 1 - lr
    f, core, x, y = plane()
    z = lax.axis_index("rep")
    fc, fx, fy = f + 1 - 2 * core, f + 2 - 4 * x, f + 4 - 8 * y
    z1, z3 = z + 1 - 2 * (z % 2), 3 - z
    half = CH // 2
    mine = pl.multiple_of(((z + 1) // 2 % 2) * half, 16)
    theirs = pl.multiple_of(half - (z + 1) // 2 % 2 * half, 16)
    n = d.shape[0]
    rows = n * RP

    def load(layer, block, n, at):
        return pltpu.make_async_copy(w_ref.at[pl.ds(pl.multiple_of((layer * NC + block) * D, 16), n * D)], wk.at[pl.ds(at * D, n * D)], wsem.at[0 if at else 1])

    def fetch(src, slot, layer):
        return pltpu.make_async_copy(src.at[layer], ab.at[slot], asem.at[slot])

    def remote(kind, p, src, dst, **to):
        return pltpu.make_async_remote_copy(src_ref=src, dst_ref=dst, send_sem=ssem.at[p, kind], recv_sem=rsem.at[p, kind],
                                            device_id=to, device_id_type=MESH)

    def live(v):
        return (v >= 0) & (v < 24)

    def kind(n, v):
        p, q = v % 2, v % 4
        if n == 0:
            lc = v % NC
            return remote(0, q, gb.at[lc - 9 * (lc // 9), :, 1 - core], rc.at[p], fsdp=fc)
        if n == 1:
            return remote(1, q, s2.at[p, :, 1 - x, pl.ds(0, half)], ra.at[q], fsdp=fx)
        if n == 2:
            return remote(2, q, s2.at[p, 1 - y, :, pl.ds(half, half)], rb.at[q], fsdp=fy)
        if n == 3:
            return remote(3, q, s3a.at[p, 1 - y], r3a.at[p], fsdp=fy)
        if n == 4:
            return remote(4, q, s3b.at[p, 1 - x], r3b.at[p], fsdp=fx)
        if n == 5:
            return remote(5, q, s4.at[p, pl.ds(theirs, half)], rz.at[q], rep=z1)
        if n == 6:
            return remote(6, q, s5.at[p], ry.at[q], rep=z3)
        return remote(7, q, s6.at[p], rw.at[p], rep=z1)

    def put(v, act):
        lc, layer = v % NC, LAYERS - 1 - v // NC
        p = v % 2
        out = (lc >= 4) & (lc < 9)

        @pl.when(out)
        def _():
            act(pltpu.make_async_copy(fin.at[p], gout_ref.at[layer, pl.ds(pl.multiple_of((lc - 4) * CH, 8), CH)], osem.at[p]))

        @pl.when(jnp.logical_not(out))
        def _():
            j = lc + 3 - 9 * (lc // 9)
            j = j - 3 * (lc // 9)
            act(pltpu.make_async_copy(fin.at[p], gin_ref.at[layer, :, pl.ds(pl.multiple_of(j * D, 128), D)], osem.at[p]))

    def add(a, b):
        return a + b

    def tick(t):
        @pl.when(live(t - 10))
        def _():
            put(t - 10, lambda a: a.wait())

        @pl.when(live(t - 9))
        def _():
            v = t - 9
            p = v % 2
            kind(7, v).wait()
            fin[p, pl.ds(mine, half)] = s6[p].astype(F32)
            fin[p, pl.ds(theirs, half)] = rw[p].astype(F32)
            put(v, lambda a: a.start())

        @pl.when(live(t - 8))
        def _():
            v = t - 8
            p = v % 2
            kind(6, v).wait()
            s6[p] = add(s5[p], ry[v % 4]).astype(BF)
            kind(7, v).start()

        @pl.when(live(t - 6))
        def _():
            v = t - 6
            p = v % 2
            kind(5, v).wait()
            s5[p] = add(s4[p, pl.ds(mine, half)], rz[v % 4]).astype(BF)
            kind(6, v).start()

        @pl.when(live(t - 4))
        def _():
            v = t - 4
            p = v % 2
            kind(3, v).wait()
            kind(4, v).wait()
            s4[p, 0:half] = add(s3a[p, y], r3a[p]).astype(BF)
            s4[p, half:CH] = add(s3b[p, x], r3b[p]).astype(BF)
            kind(5, v).start()

        @pl.when(live(t - 3))
        def _():
            v = t - 3
            p, q = v % 2, v % 4
            kind(1, v).wait()
            kind(2, v).wait()
            for i in range(2):
                s3a[p, i] = add(s2[p, i, x, 0:half], ra[q, i]).astype(BF)
                s3b[p, i] = add(s2[p, y, i, half:CH], rb[q, i]).astype(BF)
            kind(3, v).start()
            kind(4, v).start()

        @pl.when(live(t - 1))
        def _():
            v = t - 1
            p = v % 2
            kind(0, v).wait()
            lc = v % NC
            for i in range(4):
                s2[p, i // 2, i % 2] = add(gb[lc - 9 * (lc // 9), i, core], rc[p, i]).astype(BF)
            kind(1, v).start()
            kind(2, v).start()

        @pl.when(live(t))
        def _():
            kind(0, t).start()

    @pl.when((lr == 0) & (s == 0))
    def _():
        load(l, 3, 9, 0).start()
        bar = pltpu.get_barrier_semaphore()
        for k in range(1, 8):
            pl.semaphore_signal(bar, inc=1, device_id={"fsdp": (f + k) % 8}, device_id_type=MESH)
        for k in range(1, 4):
            pl.semaphore_signal(bar, inc=1, device_id={"rep": (z + k) % 4}, device_id_type=MESH)
        pl.semaphore_wait(bar, 10)
        dv[...] = jnp.zeros_like(dv)
        fetch(a2_ref, 0, l).start()
        for i in range(n):
            d[i] = jnp.zeros((RP, D), F32)
            d[i, 0:SEQ, :] = cot_ref[i].astype(F32)
        load(l, 3, 9, 0).wait()

    @pl.when((lr == 1) & (s == 0))
    def _():
        load(l, 3, 3, 0).wait()
        load(l, 6, 6, 3).wait()

    @pl.when(s == 0)
    def _():
        fetch(o_ref, 1, l).start()

    @pl.when(s == 1)
    def _():
        fetch(a2_ref, 0, l).wait()

    @pl.when(s == 8)
    def _():
        fetch(a1_ref, 0, l).start()

    @pl.when(s == 13)
    def _():
        fetch(o_ref, 1, l).wait()
        load(l, 0, 3, 0).start()

        @pl.when(lr == 0)
        def _():
            load(l - 1, 6, 6, 3).start()

    @pl.when(s == 23)
    def _():
        fetch(a1_ref, 0, l).wait()

    @pl.when(s == 26)
    def _():
        load(l, 0, 3, 0).wait()

    @pl.when((s == 27) & (lr == 0))
    def _():
        fetch(a2_ref, 0, l - 1).start()
        load(l - 1, 3, 3, 0).start()

    one = (s >= 2) & (s <= 8) & (s % 2 == 0)
    two = (s >= 18) & (s <= 22) & (s != 20)
    three = s == 24
    four = (lr == 0) & ((s == 26) | (s == 28))
    five = (lr == 1) & (s >= 25)
    six = (lr == 1) & (s == 0)
    back = s - 18
    t = jnp.where(one, 12 * lr + s // 2 - 1, jnp.where(two, 12 * lr + 4 + back - back // 3, jnp.where(three, 12 * lr + 8, jnp.where(
        four, 9 + (s - 26) // 2, jnp.where(five, s - 4, 11)))))

    @pl.when(one | two | three | four | five | six)
    def _():
        tick(t)

    @pl.when(s == 0)
    def _():
        for i in range(n):
            up = d[i]
            db[i] = up.astype(BF)
            acc[i] = jnp.zeros((RP, D), F32)
            dv[l, 7:8] += rsum(up)

    @pl.when((s < 8) & (s % 2 == 0))
    def _():
        j = s // 2
        whole = db[...].reshape(rows, D)
        cols = pl.multiple_of(j * D, 128)
        for q in range(3):
            t1 = dot_t(whole, wk[pl.ds(pl.multiple_of((5 + j) * D + 256 * q, 16), 256), :])
            t1 = t1 * g_ref[0, :, :, 256 * q:256 * q + 256].reshape(rows, 256).astype(F32)
            dv[l, pl.ds(8 + j, 1), 256 * q:256 * q + 256] += rsum(t1)
            du[:, :, pl.ds(pl.multiple_of(cols + 256 * q, 128), 256)] = t1.astype(BF).reshape(n, RP, 256)
        acc[...] += dot_t(du[:, :, pl.ds(cols, D)].reshape(rows, D), wk[pl.ds(pl.multiple_of(j * D, 16), D), :]).reshape(n, RP, D)

    @pl.when((s >= 8) & (s < 13))
    def _():
        i = s - 8
        dx, dg, dc = norm_back(h1_ref[0, 0], vec_ref[l, 5:6], acc[i])
        dv[l, 5:6] += dg
        dv[l, 6:7] += dc
        dh1 = d[i] + dx
        d[i] = dh1
        dv[l, 4:5] += rsum(dh1)
        dhb[i] = dh1.astype(BF)
        du[i, :, 3 * D:4 * D] = dot_t(dhb[i], wk[4 * D:5 * D, :]).astype(BF)

    def grad(lhs, rhs, store):
        for m in range(2):
            r = dot_0(lhs(384 * m), rhs).astype(BF).reshape(4, CH, D)
            store(4 * m, r)

    def inner(slot, j):
        def store(m, r):
            gb[slot, m // 2, 0] = r[0]
            gb[slot, m // 2, 1] = r[1]
            gb[slot, m // 2 + 1, 0] = r[2]
            gb[slot, m // 2 + 1, 1] = r[3]
        grad(lambda m: ab[0, :, :, m:m + 384].reshape(rows, 384), du[:, :, pl.ds(pl.multiple_of(D * j, 128), D)].reshape(rows, D), store)

    def outer(step, lhs, rhs):
        def store(m, r):
            for q in range(4):
                b = 8 * step + m + q
                gb[4 + b % 5, b // 10, (b // 5) % 2] = r[q]
        grad(lhs, rhs[...].reshape(rows, D), store)

    @pl.when((s < 8) & (s % 2 == 1))
    def _():
        inner(s // 2, s // 2)

    @pl.when(s == 13)
    def _():
        outer(0, lambda m: ab[1, :, :, m:m + 384].reshape(rows, 384), dhb)

    @pl.when((s >= 14) & (s < 18))
    def _():
        outer(s - 13, lambda m: e_ref[0, :, :, m:m + 384].reshape(rows, 384), db)

    @pl.when((s >= 18) & (s < 23))
    def _():
        i = s - 18
        for p in range(6):
            b = 128 * p
            dq, dk, dvv = attn_bwd(qkv_ref[0, 0, :, b:b + 128], qkv_ref[0, 0, :, D + b:D + b + 128], qkv_ref[0, 0, :, 2 * D + b:2 * D + b + 128],
                                   du[i, :, 3 * D + b:3 * D + b + 128])
            dv[l, 2:3, b:b + 128] += rsum(dq)
            dv[l, 3:4, b:b + 128] += rsum(dvv)
            du[i, :, b:b + 128] = dq.astype(BF)
            du[i, :, D + b:D + b + 128] = dk.astype(BF)
            du[i, :, 2 * D + b:2 * D + b + 128] = dvv.astype(BF)

    @pl.when((s >= 23) & (s < 26))
    def _():
        inner(s - 23, s - 23)

    @pl.when(s == 26)
    def _():
        acc[...] = dot_t(du[:, :, 0:D].reshape(rows, D), wk[0:D, :]).reshape(n, RP, D)
        acc[...] += dot_t(du[:, :, D:2 * D].reshape(rows, D), wk[D:2 * D, :]).reshape(n, RP, D)
        acc[...] += dot_t(du[:, :, 2 * D:3 * D].reshape(rows, D), wk[2 * D:3 * D, :]).reshape(n, RP, D)

    @pl.when(s >= 27)
    def _():
        i = s - 27
        dx, dg, dc = norm_back(hs_ref[0, 0], vec_ref[l, 0:1], acc[i])
        dv[l, 0:1] += dg
        dv[l, 1:2] += dc
        dh = d[i] + dx
        d[i] = dh
        di_ref[0] = dh[0:SEQ]

    @pl.when((lr == 1) & (s == 31))
    def _():
        for layer in range(LAYERS):
            for c in range(72):
                vs[c // 9, layer, c % 9:c % 9 + 1, :] = dv[layer, c // 6:c // 6 + 1, 128 * (c % 6):128 * (c % 6) + 128]

        def vcopy(k):
            to = (f + k) % 8
            return pltpu.make_async_remote_copy(src_ref=vs.at[to], dst_ref=vr.at[k - 1], send_sem=vssem.at[k - 1], recv_sem=vrsem.at[k - 1],
                                                device_id={"fsdp": to}, device_id_type=MESH)

        def zcopy(k):
            return pltpu.make_async_remote_copy(src_ref=vz.at[z], dst_ref=vz.at[z], send_sem=vssem.at[6 + k], recv_sem=vrsem.at[6 + k],
                                                device_id={"rep": (z + k) % 4}, device_id_type=MESH)
        for k in range(1, 8):
            vcopy(k).start()
        for t in range(28, 34):
            tick(jnp.int32(t))
        for k in range(1, 8):
            vcopy(k).wait()
        total = vs[f]
        for k in range(7):
            total = total + vr[k]
        vz[z] = total
        for k in range(1, 4):
            zcopy(k).start()
        for k in range(1, 4):
            zcopy(k).wait()
        gv_ref[...] = (vz[0] + vz[1]) + (vz[2] + vz[3])


def bwd(cotangent, w, vec, hs, h1, g, e, qkv, a2, o, a1, shard_in, shard_out):
    n = cotangent.shape[0]
    S = jax.ShapeDtypeStruct
    anyw = pl.BlockSpec(memory_space=pl.ANY)
    row = lambda cols, at: pl.BlockSpec((1, 1, RP, cols), lambda lr, s: (LAYERS - 1 - lr, jnp.clip(s - at, 0, 4), 0, 0))
    tok = lambda index: pl.BlockSpec((1, SEQ, D), index)
    VB = lambda *shape: pltpu.VMEM(shape, BF)
    half = CH // 2
    return pl.pallas_call(
        bwd_kernel, grid=(LAYERS, 32),
        in_specs=[pl.BlockSpec(cotangent.shape, lambda lr, s: (0, 0, 0), pipeline_mode=pl.Buffered(1)), anyw, pl.BlockSpec(vec.shape, lambda lr, s: (0, 0, 0)),
                  row(D, 27), row(D, 8), pl.BlockSpec((1, n, RP, D), lambda lr, s: (LAYERS - 1 - lr, 0, 0, jnp.minimum(s // 2, 3))),
                  pl.BlockSpec((1, n, RP, D), lambda lr, s: (LAYERS - 1 - lr, 0, 0, jnp.clip(s - 14, 0, 3))),
                  row(3 * D, 18), anyw, anyw, anyw],
        out_specs=[tok(lambda lr, s: (lr * jnp.clip(s - 27, 0, 4), 0, 0)), anyw, anyw, pl.BlockSpec((LAYERS, 16, 128), lambda lr, s: (0, 0, 0))],
        out_shape=[S(cotangent.shape, F32), S(shard_in, F32), S(shard_out, F32), S((LAYERS, 16, 128), F32)],
        scratch_shapes=[VB(9 * D, D), pltpu.VMEM((n, RP, D), F32), pltpu.VMEM((n, RP, D), F32), VB(n, RP, D), VB(n, RP, D), VB(n, RP, 4 * D), VB(2, n, RP, D),
                        VB(9, 4, 2, CH, D), pltpu.VMEM((LAYERS, 16, D), F32),
                        VB(2, 4, CH, D), VB(2, 2, 2, CH, D), VB(4, 2, half, D), VB(4, 2, half, D), VB(2, 2, half, D), VB(2, 2, half, D),
                        VB(2, half, D), VB(2, half, D), VB(2, CH, D), VB(4, half, D), VB(2, half, D), VB(4, half, D), VB(2, half, D), VB(2, half, D),
                        pltpu.VMEM((2, CH, D), F32),
                        pltpu.VMEM((8, LAYERS, 16, 128), F32), pltpu.VMEM((7, LAYERS, 16, 128), F32), pltpu.VMEM((4, LAYERS, 16, 128), F32),
                        pltpu.SemaphoreType.DMA((2,)), pltpu.SemaphoreType.DMA((2,)), pltpu.SemaphoreType.DMA((4, 8)), pltpu.SemaphoreType.DMA((4, 8)),
                        pltpu.SemaphoreType.DMA((2,)), pltpu.SemaphoreType.DMA((10,)), pltpu.SemaphoreType.DMA((10,))],
        compiler_params=pltpu.CompilerParams(collective_id=1, has_side_effects=True, vmem_limit_bytes=63 * 2**20),
    )(cotangent, w, vec, hs, h1, g, e, qkv, a2, o, a1)


STEP = 3
beta_one = 0.9
beta_two = 0.999
matrix_rate = 0.03
vector_rate = 0.2
matrix_decay = 0.05
adam_eps = 1e-8


def adam_update(master, gradient, moment_one, moment_two, rate, decay_rate):
    moment_one = beta_one * moment_one + (1.0 - beta_one) * gradient
    moment_two = beta_two * moment_two + (1.0 - beta_two) * gradient * gradient
    corr_one = 1.0 - beta_one**STEP
    corr_two = 1.0 - beta_two**STEP
    adam_move = moment_one / corr_one / (jnp.sqrt(moment_two / corr_two) + adam_eps)
    return (master - rate * (adam_move + decay_rate * master), moment_one, moment_two)


def adam_kernel(g_ref, w_ref, m_ref, v_ref, go_ref, wo_ref, mo_ref, vo_ref, enc_ref, dim_ref,
                g_out, w_out, m_out, v_out, go_out, wo_out, mo_out, vo_out, enc_out, dim_out, steps):
    i = pl.program_id(0)

    def update(g, w, m, v, outs):
        grad = g[...]
        new, moment, square = adam_update(w[...], grad, m[...], v[...], matrix_rate, matrix_decay)
        outs[0][...], outs[1][...], outs[2][...], outs[3][...] = grad, new, moment, square

    @pl.when(i < steps)
    def _():
        update(g_ref, w_ref, m_ref, v_ref, (g_out, w_out, m_out, v_out))

    @pl.when(i >= steps)
    def _():
        update(go_ref, wo_ref, mo_ref, vo_ref, (go_out, wo_out, mo_out, vo_out))

    @pl.when(i < enc_steps)
    def _():
        enc_out[...] = enc_ref[...]
        dim_out[...] = dim_ref[...]


enc_steps = 5


def adam_all(ins, outs, encoded, dimg):
    a, b = ins[0].shape, outs[0].shape
    steps = 3 * LAYERS
    first = pl.BlockSpec((1, a[1], a[2] // 3), lambda i: (jnp.minimum(i, steps - 1) // 3, 0, jnp.minimum(i, steps - 1) % 3))
    second = pl.BlockSpec((1, b[1] // 3, b[2]), lambda i: (jnp.maximum(i - steps, 0) // 3, jnp.maximum(i - steps, 0) % 3, 0))
    tok = pl.BlockSpec((1,) + encoded.shape[1:], lambda i: (jnp.minimum(i, enc_steps - 1), 0, 0))
    S = jax.ShapeDtypeStruct
    return pl.pallas_call(
        functools.partial(adam_kernel, steps=steps), grid=(2 * steps,),
        in_specs=[first] * 4 + [second] * 4 + [tok] * 2, out_specs=[first] * 4 + [second] * 4 + [tok] * 2,
        out_shape=[S(a, F32)] * 4 + [S(b, F32)] * 4 + [S(encoded.shape, BF), S(dimg.shape, F32)],
        compiler_params=PAR,
    )(*ins, *outs, encoded, dimg)


def swap(x, axis, size, mask):
    return lax.ppermute(x, axis, [(i, i ^ mask) for i in range(size)])


def halve(x, order, size):
    bits = size.bit_length() - 1
    me = lax.axis_index("fsdp")
    x = x.reshape((2,) * bits + x.shape[1:])
    left = list(range(bits))[::-1]
    for bit in order:
        at = left.index(bit)
        mine = (me >> bit) & 1
        keep = lax.dynamic_index_in_dim(x, mine, at, keepdims=False)
        send = lax.dynamic_index_in_dim(x, 1 - mine, at, keepdims=False)
        got = swap(send, "fsdp", size, 1 << bit)
        x = (keep.astype(F32) + got.astype(F32)).astype(BF)
        left.remove(bit)
    return x


def reduce_all(x, nf, nr):
    bits = nf.bit_length() - 1
    rows, cols = x.shape
    x = x.reshape(nf, rows // nf, cols)
    half = cols // 2 // 128 * 128
    up = [0] + list(range(1, bits))
    down = [0] + list(range(1, bits))[::-1]
    x = jnp.concatenate([halve(x[..., :half], up, nf), halve(x[..., half:], down, nf)], axis=-1)
    mask = 1
    while mask < nr:
        got = swap(x, "rep", nr, 2 * mask - 1)
        y = x.astype(F32) + got.astype(F32)
        x = y.astype(BF)
        mask *= 2
    return y


def fused_step(images, cotangent, weight_in, weight_out, vector_params):
    vs = jnp.pad(vector_params.astype(BF).astype(F32).reshape(LAYERS, 9, 128), ((0, 0), (0, 7), (0, 0)))
    hs, qkv, a1, o, h1, a2, e, g, encoded, w, vec = fwd(images, weight_in, weight_out, vs)
    dimg, gi, go, gv = bwd(cotangent, w, vec, hs, h1, g, e, qkv, a2, o, a1, weight_in.shape, weight_out.shape)
    return encoded, dimg, gi, go, gv[:, :9].reshape(vector_params.shape)


def plain_step(nf, nr, images, cotangent, weight_in, weight_out, vector_params):
    pad = lambda a: jnp.pad(a, ((0, 0), (0, RP - SEQ), (0, 0)))
    vec_all = lax.all_gather(vector_params.astype(BF), "fsdp", axis=1, tiled=True).astype(F32)
    h = pad(images)
    ct = pad(cotangent)
    saved = []
    for l in range(LAYERS):
        win = lax.all_gather(weight_in[l].astype(BF), "fsdp", axis=0, tiled=True)
        wout = lax.all_gather(weight_out[l].astype(BF), "fsdp", axis=0, tiled=True)
        vec = jnp.pad(vec_all[l].reshape(12, D), ((0, 4), (0, 0)))
        wqkv, w1, wo, w2 = win[:, : 3 * D], win[:, 3 * D :], wout[:D], wout[D:]
        qkv, o, a1 = ka(h, wqkv, vec)
        h1, a2, e, g, h2 = kb(h, o, wo, w1, w2, vec)
        saved.append((h, wqkv, w1, wo, w2, vec, qkv, o, a1, h1, a2, e, g))
        h = h2
    encoded = h[:, :SEQ].astype(BF)
    d = ct
    gin, gout, gvec = [None] * LAYERS, [None] * LAYERS, [None] * LAYERS
    for l in reversed(range(LAYERS)):
        h, wqkv, w1, wo, w2, vec, qkv, o, a1, h1, a2, e, g = saved[l]
        db, du, dh1, dh1b, do, dv1 = kc(d, h1, g, wo, w1, w2, vec)
        g1 = reduce_all(dw(a2, du), nf, nr)
        go = reduce_all(jnp.concatenate([dw(o, dh1b), dw(e, db)], axis=0), nf, nr)
        dz, dv2 = kd(qkv, do)
        gq = reduce_all(dw(a1, dz), nf, nr)
        d, dv3 = kf(dz, h, dh1, wqkv, vec, RP if l else SEQ)
        gin[l] = jnp.concatenate([gq, g1], axis=1)
        gout[l] = go
        gvec[l] = (dv1 + dv2 + dv3)[:12].reshape(-1)
    gv = lax.psum(jnp.stack(gvec), ("fsdp", "rep"))
    wide = gv.shape[1] // nf
    gv = lax.dynamic_slice_in_dim(gv, lax.axis_index("fsdp") * wide, wide, 1)
    return encoded, d, jnp.stack(gin), jnp.stack(gout), gv


def make_shards(nf, nr):
    def shards(images, cotangent, weight_in, weight_out, vector_params, first_in, first_out, first_vec, second_in, second_out, second_vec):
        if nf == 8 and nr == 4:
            encoded, d, gi, go, gv = fused_step(images, cotangent, weight_in, weight_out, vector_params)
            gi, new_in, moment_in, square_in, go, new_out, moment_out, square_out, encoded, d = adam_all(
                (gi, weight_in, first_in, second_in), (go, weight_out, first_out, second_out), encoded, d)
        else:
            encoded, d, gi, go, gv = plain_step(nf, nr, images, cotangent, weight_in, weight_out, vector_params)
            new_in, moment_in, square_in = adam_update(weight_in, gi, first_in, second_in, matrix_rate, matrix_decay)
            new_out, moment_out, square_out = adam_update(weight_out, go, first_out, second_out, matrix_rate, matrix_decay)
        new_vec, moment_vec, square_vec = adam_update(vector_params, gv, first_vec, second_vec, vector_rate, 0.0)
        return (encoded, d, gi, go, gv, new_in, new_out, new_vec, moment_in, moment_out, moment_vec, square_in, square_out, square_vec)

    return shards


def solution(mesh):
    tokens = P(("fsdp", "rep"), None, None)
    matrix = P(None, "fsdp", None)
    vector = P(None, "fsdp")
    in_specs = (tokens, tokens) + (matrix, matrix, vector) * 3
    out_specs = (tokens, tokens) + (matrix, matrix, vector) * 4
    return jax.shard_map(make_shards(mesh.shape["fsdp"], mesh.shape["rep"]), mesh=mesh, in_specs=in_specs, out_specs=out_specs, check_vma=False)
```

```python
import functools
import jax, jax.numpy as jnp
from jax import lax
from jax.experimental import pallas as pl
from jax.experimental.pallas import tpu as pltpu
from jax.sharding import PartitionSpec as P

D=768; HD=64; SEQ=197; RP=208; EPS=1e-6
BF=jnp.bfloat16; F32=jnp.float32
def dot(a,b): return jnp.dot(a,b,preferred_element_type=F32)
def dot_t(a,b): return lax.dot_general(a,b,(((1,),(1,)),((),())),preferred_element_type=F32)
def dot_0(a,b): return lax.dot_general(a,b,(((0,),(0,)),((),())),preferred_element_type=F32)

def norm_stats(x):
    mean=jnp.mean(x,axis=-1,keepdims=True); xc=x-mean
    var=jnp.mean(xc*xc,axis=-1,keepdims=True)
    return xc, lax.rsqrt(var+EPS)

def head_masks(scale):
    lane = lax.broadcasted_iota(jnp.int32, (1, 128), 1)
    return jnp.where(lane < 64, scale, 0.0).astype(BF), jnp.where(lane < 64, 0.0, scale).astype(BF)


def weights_t(q, k, masks):
    row = lax.broadcasted_iota(jnp.int32, (RP, 1), 0)
    s = [jnp.where(row < SEQ, dot_t(k, q * m), -1e30) for m in masks]
    e = [jnp.exp(x - jnp.max(x, axis=0, keepdims=True)) for x in s]
    return [x * (1.0 / jnp.sum(x, axis=0, keepdims=True)) for x in e]


def attn_fwd(q, k, v):
    ones = head_masks(1.0)
    row = lax.broadcasted_iota(jnp.int32, (16, 1), 0)
    ps = []
    for m in head_masks(0.125):
        s = dot_t(k, q * m)
        s = jnp.concatenate([s[:RP - 16], jnp.where(row < SEQ - RP + 16, s[RP - 16:], -1e30)], axis=0)
        e = jnp.exp(s - jnp.max(s, axis=0, keepdims=True))
        ps.append((e * (1.0 / jnp.sum(e, axis=0, keepdims=True))).astype(BF))
    return (dot_0(ps[0], v * ones[0]) + dot_0(ps[1], v * ones[1])).astype(BF)


def attn_bwd(q, k, v, do):
    scaled, ones = head_masks(0.125), head_masks(1.0)
    p = weights_t(q, k, scaled)
    dos = [do * m for m in ones]
    dp = [dot_t(v, x) for x in dos]
    pb = [x.astype(BF) for x in p]
    ds = [(a * (b - jnp.sum(a * b, axis=0, keepdims=True))).astype(BF) for a, b in zip(p, dp)]
    dv = dot(pb[0], dos[0]) + dot(pb[1], dos[1])
    dk = dot(ds[0], q * scaled[0]) + dot(ds[1], q * scaled[1])
    dq = dot_0(ds[0], k * scaled[0]) + dot_0(ds[1], k * scaled[1])
    return dq, dk, dv


def ka_kernel(h_ref,w_ref,vec_ref,qkv_ref,o_ref,a_ref):
    h=h_ref[0].astype(F32)
    xc,rs=norm_stats(h)
    a_ref[0]=(xc*rs*vec_ref[0:1]+vec_ref[1:2]).astype(BF)
    a=a_ref[0]
    for c in range(3):
        cs=slice(256*c,256*c+256)
        qkv_ref[0,:,256*c:256*c+256]=(dot(a,w_ref[:,256*c:256*c+256])+vec_ref[2:3,cs]).astype(BF)
        qkv_ref[0,:,D+256*c:D+256*c+256]=dot(a,w_ref[:,D+256*c:D+256*c+256]).astype(BF)
        qkv_ref[0,:,2*D+256*c:2*D+256*c+256]=(dot(a,w_ref[:,2*D+256*c:2*D+256*c+256])+vec_ref[3:4,cs]).astype(BF)
        for p in range(2):
            b=256*c+128*p
            o_ref[0,:,b:b+128]=attn_fwd(qkv_ref[0,:,b:b+128],qkv_ref[0,:,D+b:D+b+128],qkv_ref[0,:,2*D+b:2*D+b+128])

def img(n,dt=None): return pl.BlockSpec((1,RP,n),lambda i:(i,0,0))
def full(shape): return pl.BlockSpec(shape,lambda i:(0,)*len(shape))
PAR=pltpu.CompilerParams(vmem_limit_bytes=60*2**20)

def ka(h,w,vec):
    n=h.shape[0]
    return pl.pallas_call(ka_kernel,grid=(n,),in_specs=[img(D),full(w.shape),full(vec.shape)],
        out_specs=[img(3*D),img(D),img(D)],
        out_shape=[jax.ShapeDtypeStruct((n,RP,3*D),BF),jax.ShapeDtypeStruct((n,RP,D),BF),jax.ShapeDtypeStruct((n,RP,D),BF)],
        compiler_params=PAR)(h,w,vec)

def gelu_parts(u):
    c=0.5*(1.0+lax.erf(u*0.7071067811865476))
    g=c+u*(jnp.exp(-0.5*u*u)*0.3989422804014327)
    return u*c,g

def kb_kernel(FC,h_ref,o_ref,wo_ref,w1_ref,w2_ref,vec_ref,h1_ref,a_ref,e_ref,g_ref,h2_ref):
    h1=h_ref[0].astype(F32)+dot(o_ref[0],wo_ref[...])+vec_ref[4:5]
    h1_ref[0]=h1
    xc,rs=norm_stats(h1)
    a_ref[0]=(xc*rs*vec_ref[5:6]+vec_ref[6:7]).astype(BF)
    a=a_ref[0]
    h2_ref[0]=h1+vec_ref[7:8]
    for j in range(3072//FC):
        lo=FC*j
        u=dot(a,w1_ref[:,lo:lo+FC])+vec_ref[8+lo//D:9+lo//D,lo%D:lo%D+FC]
        e,g=gelu_parts(u)
        e_ref[0,:,lo:lo+FC]=e.astype(BF); g_ref[0,:,lo:lo+FC]=g.astype(BF)
        h2_ref[0]+=dot(e_ref[0,:,lo:lo+FC],w2_ref[lo:lo+FC,:])

def kb(h,o,wo,w1,w2,vec,FC=256):
    n=h.shape[0]
    S=jax.ShapeDtypeStruct
    return pl.pallas_call(functools.partial(kb_kernel,FC),grid=(n,),in_specs=[img(D),img(D),full(wo.shape),full(w1.shape),full(w2.shape),full(vec.shape)],
        out_specs=[img(D),img(D),img(3072),img(3072),img(D)],
        out_shape=[S((n,RP,D),F32),S((n,RP,D),BF),S((n,RP,3072),BF),S((n,RP,3072),BF),S((n,RP,D),F32)],
        compiler_params=PAR)(h,o,wo,w1,w2,vec)

def rsum(x): return jnp.sum(x,axis=0,keepdims=True)
def norm_back(x,gain,dy):
    xc,rs=norm_stats(x); xh=xc*rs
    dyg=dy*gain
    dx=rs*(dyg-jnp.mean(dyg,axis=-1,keepdims=True)-xh*jnp.mean(dyg*xh,axis=-1,keepdims=True))
    return dx, rsum(dy*xh), rsum(dy)

def kc_kernel(FC,d_ref,h1_ref,g_ref,wo_ref,w1_ref,w2_ref,vec_ref,db_ref,du_ref,dh1_ref,dh1b_ref,do_ref,dv_ref,acc_ref):
    @pl.when(pl.program_id(0)==0)
    def _(): dv_ref[...]=jnp.zeros_like(dv_ref)
    d=d_ref[0].astype(F32)
    db_ref[0]=d.astype(BF)
    db=db_ref[0]
    dv_ref[7:8]+=rsum(d)
    for j in range(3072//FC):
        lo=FC*j
        du=dot_t(db,w2_ref[lo:lo+FC,:])*g_ref[0,:,lo:lo+FC].astype(F32)
        dv_ref[8+lo//D:9+lo//D,lo%D:lo%D+FC]+=rsum(du)
        du_ref[0,:,lo:lo+FC]=du.astype(BF)
        t=dot_t(du_ref[0,:,lo:lo+FC],w1_ref[:,lo:lo+FC])
        if j==0: acc_ref[...]=t
        else: acc_ref[...]+=t
    dx,dg,dc=norm_back(h1_ref[0],vec_ref[5:6],acc_ref[...])
    dv_ref[5:6]+=dg; dv_ref[6:7]+=dc
    dh1=d_ref[0].astype(F32)+dx
    dh1_ref[0]=dh1
    dv_ref[4:5]+=rsum(dh1)
    dh1b_ref[0]=dh1.astype(BF)
    do_ref[0]=dot_t(dh1b_ref[0],wo_ref[...]).astype(BF)

def kc(d,h1,g,wo,w1,w2,vec,FC=256):
    n=d.shape[0]; S=jax.ShapeDtypeStruct
    return pl.pallas_call(functools.partial(kc_kernel,FC),grid=(n,),in_specs=[img(D),img(D),img(3072),full(wo.shape),full(w1.shape),full(w2.shape),full(vec.shape)],
        out_specs=[img(D),img(3072),img(D),img(D),img(D),full((16,D))],
        out_shape=[S((n,RP,D),BF),S((n,RP,3072),BF),S((n,RP,D),F32),S((n,RP,D),BF),S((n,RP,D),BF),S((16,D),F32)],
        scratch_shapes=[pltpu.VMEM((RP,D),F32)],
        compiler_params=PAR)(d,h1,g,wo,w1,w2,vec)

def kd_kernel(qkv_ref,do_ref,dz_ref,dv_ref):
    @pl.when(pl.program_id(0)==0)
    def _(): dv_ref[...]=jnp.zeros_like(dv_ref)
    for p in range(6):
        b=128*p
        dq,dk,dv=attn_bwd(qkv_ref[0,:,b:b+128],qkv_ref[0,:,D+b:D+b+128],qkv_ref[0,:,2*D+b:2*D+b+128],do_ref[0,:,b:b+128])
        dv_ref[2:3,b:b+128]+=rsum(dq); dv_ref[3:4,b:b+128]+=rsum(dv)
        dz_ref[0,:,b:b+128]=dq.astype(BF); dz_ref[0,:,D+b:D+b+128]=dk.astype(BF); dz_ref[0,:,2*D+b:2*D+b+128]=dv.astype(BF)

def kd(qkv,do):
    n=do.shape[0]; S=jax.ShapeDtypeStruct
    return pl.pallas_call(kd_kernel,grid=(n,),in_specs=[img(3*D),img(D)],out_specs=[img(3*D),full((16,D))],
        out_shape=[S((n,RP,3*D),BF),S((16,D),F32)],compiler_params=PAR)(qkv,do)

def kf_kernel(dz_ref,h_ref,dh1_ref,w_ref,vec_ref,dh_ref,dv_ref):
    @pl.when(pl.program_id(0)==0)
    def _(): dv_ref[...]=jnp.zeros_like(dv_ref)
    da=dot_t(dz_ref[0],w_ref[...])
    dx,dg,dc=norm_back(h_ref[0].astype(F32),vec_ref[0:1],da)
    dv_ref[0:1]+=dg; dv_ref[1:2]+=dc
    rows=dh_ref.shape[1]
    dh_ref[0]=(dh1_ref[0]+dx)[:rows]

def kf(dz,h,dh1,w,vec,rows=RP):
    n=dz.shape[0]; S=jax.ShapeDtypeStruct
    return pl.pallas_call(kf_kernel,grid=(n,),in_specs=[img(3*D),img(D),img(D),full(w.shape),full(vec.shape)],
        out_specs=[pl.BlockSpec((1,rows,D),lambda i:(i,0,0)),full((16,D))],
        out_shape=[S((n,rows,D),F32),S((16,D),F32)],compiler_params=PAR)(dz,h,dh1,w,vec)

def dw_kernel(l_ref,r_ref,o_ref):
    o_ref[...]=dot_0(l_ref[...],r_ref[...]).astype(BF)
def dw(l,r,MB=256):
    M=l.shape[-1]; N=r.shape[-1]; K=l.shape[0]*RP
    l=l.reshape(K,M); r=r.reshape(K,N)
    return pl.pallas_call(dw_kernel,grid=(M//MB,),in_specs=[pl.BlockSpec((K,MB),lambda i:(0,i)),pl.BlockSpec((K,N),lambda i:(0,0))],
       out_specs=pl.BlockSpec((MB,N),lambda i:(i,0)),out_shape=jax.ShapeDtypeStruct((M,N),BF),compiler_params=PAR)(l,r)


LAYERS = 2
MESH = pl.DeviceIdType.MESH
CH = 96
NC = 12


def plane():
    f = lax.axis_index("fsdp")
    core, x, y = f % 2, (f // 2) % 2, f // 4
    return f, core, x, y


def chunk_rows(c, f):
    layer, j = c // NC, c % NC
    early = 1 - (j + 9) // 12
    late = j // 8
    mid = 1 - early - late
    base = layer * NC * D
    return pl.multiple_of(base + early * (j * D + CH * f) + late * ((j - 5) * D + CH * f)
                          + mid * (7 * D + 5 * CH * f + CH * (j - 3)), 16)


def fwd_kernel(img_ref, win_ref, wout_ref, vs_ref, hs_ref, qkv_ref, a1_ref, o_ref, h1_ref, a2_ref, e_ref, g_ref, enc_ref, wo_ref, vo_ref,
               w, hb, ob, ab, vg, vec, st, lsem, ssem, rsem, vssem, vrsem, osem, vosem):
    l, s = pl.program_id(0), pl.program_id(1)
    f, core, x, y = plane()
    fc, fx, fy = f + 1 - 2 * core, f + 2 - 4 * x, f + 4 - 8 * y
    fd = fx + fy - f
    z = lax.axis_index("rep")
    side = z % 2
    zp = z + 1 - 2 * side
    part = pl.ds(pl.multiple_of(256 * side, 128), 512)
    give = pl.ds(pl.multiple_of(512 * side, 128), 256)

    def wrow(c, who, lo=0, n=CH):
        return pl.ds(pl.multiple_of(chunk_rows(c, who) + lo, 16), n)

    def send(c, kind, where, **to):
        return pltpu.make_async_remote_copy(src_ref=w.at[where], dst_ref=w.at[where], send_sem=ssem.at[c % 12, kind], recv_sem=rsem.at[c % 12, kind],
                                            device_id=to, device_id_type=MESH)

    def fetch(c, act):
        layer, j = c // NC, c % NC
        mid = (j >= 3) & (j < 8)

        @pl.when(mid)
        def _():
            act(pltpu.make_async_copy(wout_ref.at[layer, pl.ds(pl.multiple_of((j - 3) * CH, 8), CH)], st.at[c % 4], lsem.at[c % 4]))

        @pl.when(jnp.logical_not(mid))
        def _():
            act(pltpu.make_async_copy(win_ref.at[layer, :, pl.ds(pl.multiple_of((j - 5 * (j // 8)) * D, 128), D)], st.at[c % 4], lsem.at[c % 4]))

    def kinds(c):
        half = CH // 2
        return [lambda: send(c, 0, (wrow(c, f), part), fsdp=fx), lambda: send(c, 1, (wrow(c, f), part), fsdp=fy),
                lambda: send(c, 2, (wrow(c, f),), fsdp=fc),
                lambda: send(c, 3, (wrow(c, fx, 0, half), part), fsdp=fy), lambda: send(c, 4, (wrow(c, fy, half, half), part), fsdp=fx),
                lambda: send(c, 5, (wrow(c, fx), give), rep=zp), lambda: send(c, 6, (wrow(c, fy), give), rep=zp),
                lambda: send(c, 7, (wrow(c, fd), give), rep=zp),
                lambda: send(c, 8, (wrow(c, fx),), fsdp=fc), lambda: send(c, 9, (wrow(c, fy),), fsdp=fc), lambda: send(c, 10, (wrow(c, fd),), fsdp=fc)]

    def start(c, which):
        k = kinds(c)
        for i in which:
            k[i]().start()

    def wait(c, which):
        k = kinds(c)
        for i in which:
            k[i]().wait()

    def tick(t):
        @pl.when((t >= 7) & (t < 31))
        def _():
            wait(t - 7, (2, 8, 9, 10))

        @pl.when((t >= 6) & (t < 30))
        def _():
            wait(t - 6, (7,))
            start(t - 6, (10,))

        @pl.when((t >= 4) & (t < 28))
        def _():
            wait(t - 4, (3, 4, 5, 6))
            start(t - 4, (7, 8, 9))

        @pl.when((t >= 2) & (t < 26))
        def _():
            wait(t - 2, (0, 1))
            start(t - 2, (3, 4, 5, 6))

        def launch(c):
            fetch(c, lambda a: a.wait())
            w[pl.ds(chunk_rows(c, f), CH)] = st[c % 4].astype(BF)
            start(c, (0, 1, 2))

        @pl.when(t <= 8)
        def _():
            launch(t)

        @pl.when((t >= 8) & (t < 23))
        def _():
            launch(t + 1)

        @pl.when(t < 21)
        def _():
            fetch(t + 3, lambda a: a.start())

    def out_copy(b, n):
        return pltpu.make_async_copy(w.at[pl.ds(b, n)], wo_ref.at[pl.ds(b, n)], osem)

    @pl.when((l == 0) & (s == 0))
    def _():
        for c in range(3):
            fetch(jnp.int32(c), lambda a: a.start())
        bar = pltpu.get_barrier_semaphore()
        for k in range(1, 8):
            pl.semaphore_signal(bar, inc=1, device_id={"fsdp": (f + k) % 8}, device_id_type=MESH)
        pl.semaphore_signal(bar, inc=1, device_id={"rep": zp}, device_id_type=MESH)
        pl.semaphore_wait(bar, 8)

        def vcopy(k):
            return pltpu.make_async_remote_copy(src_ref=vs_ref, dst_ref=vg.at[f], send_sem=vssem.at[k - 1], recv_sem=vrsem.at[k - 1],
                                                device_id={"fsdp": (f + k) % 8}, device_id_type=MESH)
        for k in range(1, 8):
            vcopy(k).start()
        vg[f] = vs_ref[...]

        @pl.loop(0, 10)
        def _(t):
            tick(t)

            @pl.when(t == 0)
            def _():
                hb[...] = jnp.zeros_like(hb)

            @pl.when(t == 3)
            def _():
                for k in range(1, 8):
                    vcopy(k).wait()
                for layer in range(LAYERS):
                    for c in range(72):
                        vec[layer, c // 6:c // 6 + 1, 128 * (c % 6):128 * (c % 6) + 128] = vg[c // 9, layer, c % 9:c % 9 + 1, :]
                pltpu.make_async_copy(vec, vo_ref, vosem).start()

    early = s <= 5
    late = (s == 8) | ((s >= 10) & (s + l <= 13))
    t = jnp.where(early, (1 - l) * (s + 9) + l * (s + 21), jnp.where(s == 8, 15 + 12 * l, (1 - l) * (s + 6 + s // 12) + l * (s + 18)))

    @pl.when((early & (l + s > 0)) | late)
    def _():
        tick(t)

    @pl.when(s < 5)
    def _():
        @pl.when(l == 0)
        def _():
            hb[s, 0:SEQ, :] = img_ref[s].astype(F32)
        h = hb[s]
        hs_ref[0, 0] = h
        xc, rs = norm_stats(h)
        a1_ref[0, 0] = (xc * rs * vec[l, 0:1] + vec[l, 1:2]).astype(BF)
        a = a1_ref[0, 0]
        wb = l * NC * D

        def wq(part, c):
            return w[pl.ds(pl.multiple_of(wb + part * D, 16), D), 256 * c:256 * c + 256]
        for c in range(3):
            cs = slice(256 * c, 256 * c + 256)
            qkv_ref[0, 0, :, cs] = (dot(a, wq(0, c)) + vec[l, 2:3, cs]).astype(BF)
            qkv_ref[0, 0, :, D + 256 * c:D + 256 * c + 256] = dot(a, wq(1, c)).astype(BF)
            qkv_ref[0, 0, :, 2 * D + 256 * c:2 * D + 256 * c + 256] = (dot(a, wq(2, c)) + vec[l, 3:4, cs]).astype(BF)
            for p in range(2):
                b = 256 * c + 128 * p
                o = attn_fwd(qkv_ref[0, 0, :, b:b + 128], qkv_ref[0, 0, :, D + b:D + b + 128], qkv_ref[0, 0, :, 2 * D + b:2 * D + b + 128])
                o_ref[0, 0, :, b:b + 128] = o
                ob[s, :, b:b + 128] = o

    @pl.when((s >= 5) & (s < 10))
    def _():
        i = s - 5
        wo = w[pl.ds(pl.multiple_of((l * NC + 7) * D, 16), D), :]
        h1 = hb[i] + dot(ob[i], wo) + vec[l, 4:5]
        h1_ref[0, 0] = h1
        hb[i] = h1 + vec[l, 7:8]
        xc, rs = norm_stats(h1)
        a = (xc * rs * vec[l, 5:6] + vec[l, 6:7]).astype(BF)
        a2_ref[0, 0] = a
        ab[i] = a

    @pl.when(s >= 10)
    def _():
        j = s - 10
        up = pl.multiple_of((l * NC + 3 + j) * D, 16)
        down = pl.multiple_of((l * NC + 8 + j) * D, 16)

        bias = vec[l, pl.ds(8 + j, 1), :]
        n = hb.shape[0]
        u = dot(ab[0], w[pl.ds(up, D), :])
        for i in range(n):
            later = dot(ab[i + 1], w[pl.ds(up, D), :]) if i < n - 1 else None
            e, g = gelu_parts(u + bias)
            e = e.astype(BF)
            e_ref[0, i] = e
            g_ref[0, i] = g.astype(BF)
            hb[i] += dot(e, w[pl.ds(down, D), :])
            u = later
            if i == 2:
                @pl.when((s == 11) & (l == 0))
                def _():
                    tick(18)

        @pl.when((l == 1) & (s == 13))
        def _():
            for i in range(n):
                enc_ref[i] = hb[i, 0:SEQ, :].astype(BF)

    for layer in range(LAYERS):
        base = layer * NC * D

        @pl.when((l == layer) & (s == 4))
        def _():
            out_copy(base, 3 * D).start()

        @pl.when((l == layer) & (s == 9))
        def _():
            out_copy(base + 7 * D, 5 * D).start()

        for j in range(4):
            @pl.when((l == layer) & (s == 10 + j))
            def _():
                out_copy(base + (3 + j) * D, D).start()

    @pl.when((l == 1) & (s == 13))
    def _():
        pltpu.make_async_copy(w, wo_ref, osem).wait()
        pltpu.make_async_copy(vec, vo_ref, vosem).wait()


def fwd(images, weight_in, weight_out, vshard):
    n = images.shape[0]
    S = jax.ShapeDtypeStruct
    one = lambda cols: pl.BlockSpec((1, 1, RP, cols), lambda l, s: (l, jnp.minimum(s, 4), 0, 0))
    two = lambda cols: pl.BlockSpec((1, 1, RP, cols), lambda l, s: (l, jnp.clip(s - 5, 0, 4), 0, 0))
    wide = pl.BlockSpec((1, n, RP, D), lambda l, s: (l, 0, 0, jnp.clip(s - 10, 0, 3)))
    anyw = pl.BlockSpec(memory_space=pl.ANY)
    rows = LAYERS * NC * D
    return pl.pallas_call(
        fwd_kernel, grid=(LAYERS, 14),
        in_specs=[pl.BlockSpec(images.shape, lambda l, s: (0, 0, 0)), anyw, anyw, pl.BlockSpec(vshard.shape, lambda l, s: (0, 0, 0))],
        out_specs=[one(D), one(3 * D), one(D), one(D), two(D), two(D), wide, wide, pl.BlockSpec(images.shape, lambda l, s: (0, 0, 0)), anyw, anyw],
        out_shape=[S((LAYERS, n, RP, D), F32), S((LAYERS, n, RP, 3 * D), BF), S((LAYERS, n, RP, D), BF), S((LAYERS, n, RP, D), BF),
                   S((LAYERS, n, RP, D), F32), S((LAYERS, n, RP, D), BF), S((LAYERS, n, RP, 4 * D), BF), S((LAYERS, n, RP, 4 * D), BF),
                   S(images.shape, BF), S((rows, D), BF), S((LAYERS, 16, D), F32)],
        scratch_shapes=[pltpu.VMEM((rows, D), BF), pltpu.VMEM((n, RP, D), F32), pltpu.VMEM((n, RP, D), BF), pltpu.VMEM((n, RP, D), BF),
                        pltpu.VMEM((8, LAYERS, 16, 128), F32), pltpu.VMEM((LAYERS, 16, D), F32), pltpu.VMEM((4, CH, D), F32),
                        pltpu.SemaphoreType.DMA((4,)), pltpu.SemaphoreType.DMA((12, 11)), pltpu.SemaphoreType.DMA((12, 11)),
                        pltpu.SemaphoreType.DMA((7,)), pltpu.SemaphoreType.DMA((7,)), pltpu.SemaphoreType.DMA, pltpu.SemaphoreType.DMA],
        compiler_params=pltpu.CompilerParams(collective_id=0, has_side_effects=True, vmem_limit_bytes=62 * 2**20),
    )(images, weight_in, weight_out, vshard)


def bwd_kernel(cot_ref, w_ref, vec_ref, hs_ref, h1_ref, g_ref, e_ref, qkv_ref, a2_ref, o_ref, a1_ref,
               di_ref, gin_ref, gout_ref, gv_ref,
               wk, d, acc, db, du, ab, gb, dv, rc, s2, ra, rb, s3a, s3b, r3a, r3b, s4, rz, s5, ry, s6, rw, fin,
               vs, vr, vz, wsem, asem, ssem, rsem, osem, vssem, vrsem):
    lr, s = pl.program_id(0), pl.program_id(1)
    l = LAYERS - 1 - lr
    f, core, x, y = plane()
    z = lax.axis_index("rep")
    fc, fx, fy = f + 1 - 2 * core, f + 2 - 4 * x, f + 4 - 8 * y
    z1, z3 = z + 1 - 2 * (z % 2), 3 - z
    half = CH // 2
    mine = pl.multiple_of(((z + 1) // 2 % 2) * half, 16)
    theirs = pl.multiple_of(half - (z + 1) // 2 % 2 * half, 16)
    n = d.shape[0]
    rows = n * RP

    def load(layer, block, n, at):
        return pltpu.make_async_copy(w_ref.at[pl.ds(pl.multiple_of((layer * NC + block) * D, 16), n * D)], wk.at[pl.ds(at * D, n * D)], wsem.at[0 if at else 1])

    def fetch(src, slot, layer):
        return pltpu.make_async_copy(src.at[layer], ab.at[slot], asem.at[slot])

    def remote(kind, p, src, dst, **to):
        return pltpu.make_async_remote_copy(src_ref=src, dst_ref=dst, send_sem=ssem.at[p, kind], recv_sem=rsem.at[p, kind],
                                            device_id=to, device_id_type=MESH)

    def live(v):
        return (v >= 0) & (v < 24)

    def kind(n, v):
        p, q = v % 2, v % 4
        if n == 0:
            lc = v % NC
            return remote(0, q, gb.at[lc - 9 * (lc // 9), :, 1 - core], rc.at[p], fsdp=fc)
        if n == 1:
            return remote(1, q, s2.at[p, :, 1 - x, pl.ds(0, half)], ra.at[q], fsdp=fx)
        if n == 2:
            return remote(2, q, s2.at[p, 1 - y, :, pl.ds(half, half)], rb.at[q], fsdp=fy)
        if n == 3:
            return remote(3, q, s3a.at[p, 1 - y], r3a.at[q], fsdp=fy)
        if n == 4:
            return remote(4, q, s3b.at[p, 1 - x], r3b.at[q], fsdp=fx)
        if n == 5:
            return remote(5, q, s4.at[p, pl.ds(theirs, half)], rz.at[q], rep=z1)
        if n == 6:
            return remote(6, q, s5.at[p], ry.at[q], rep=z3)
        return remote(7, q, s6.at[p], rw.at[q], rep=z1)

    def put(v, act):
        lc, layer = v % NC, LAYERS - 1 - v // NC
        p = v % 2
        out = (lc >= 4) & (lc < 9)

        @pl.when(out)
        def _():
            act(pltpu.make_async_copy(fin.at[p], gout_ref.at[layer, pl.ds(pl.multiple_of((lc - 4) * CH, 16), CH)], osem.at[p]))

        @pl.when(jnp.logical_not(out))
        def _():
            j = lc + 3 - 9 * (lc // 9)
            j = j - 3 * (lc // 9)
            act(pltpu.make_async_copy(fin.at[p], gin_ref.at[layer, :, pl.ds(pl.multiple_of(j * D, 128), D)], osem.at[p]))

    def add(a, b):
        return a + b

    def tick(t):
        @pl.when(live(t - 12))
        def _():
            put(t - 12, lambda a: a.wait())

        @pl.when(live(t - 11))
        def _():
            v = t - 11
            p = v % 2
            kind(7, v).wait()
            fin[p, pl.ds(mine, half)] = s6[p]
            fin[p, pl.ds(theirs, half)] = rw[v % 4]
            put(v, lambda a: a.start())

        @pl.when(live(t - 9))
        def _():
            v = t - 9
            p = v % 2
            kind(6, v).wait()
            s6[p] = add(s5[p], ry[v % 4]).astype(BF)
            kind(7, v).start()

        @pl.when(live(t - 7))
        def _():
            v = t - 7
            p = v % 2
            kind(5, v).wait()
            s5[p] = add(s4[p, pl.ds(mine, half)], rz[v % 4]).astype(BF)
            kind(6, v).start()

        @pl.when(live(t - 5))
        def _():
            v = t - 5
            p, q = v % 2, v % 4
            kind(3, v).wait()
            kind(4, v).wait()
            s4[p, 0:half] = add(s3a[p, y], r3a[q]).astype(BF)
            s4[p, half:CH] = add(s3b[p, x], r3b[q]).astype(BF)
            kind(5, v).start()

        @pl.when(live(t - 3))
        def _():
            v = t - 3
            p, q = v % 2, v % 4
            kind(1, v).wait()
            kind(2, v).wait()
            for i in range(2):
                s3a[p, i] = add(s2[p, i, x, 0:half], ra[q, i]).astype(BF)
                s3b[p, i] = add(s2[p, y, i, half:CH], rb[q, i]).astype(BF)
            kind(3, v).start()
            kind(4, v).start()

        @pl.when(live(t - 1))
        def _():
            v = t - 1
            p = v % 2
            kind(0, v).wait()
            lc = v % NC
            for i in range(4):
                s2[p, i // 2, i % 2] = add(gb[lc - 9 * (lc // 9), i, core], rc[p, i]).astype(BF)
            kind(1, v).start()
            kind(2, v).start()

        @pl.when(live(t))
        def _():
            kind(0, t).start()

    @pl.when((lr == 0) & (s == 0))
    def _():
        load(l, 3, 9, 0).start()
        bar = pltpu.get_barrier_semaphore()
        for k in range(1, 8):
            pl.semaphore_signal(bar, inc=1, device_id={"fsdp": (f + k) % 8}, device_id_type=MESH)
        for k in range(1, 4):
            pl.semaphore_signal(bar, inc=1, device_id={"rep": (z + k) % 4}, device_id_type=MESH)
        pl.semaphore_wait(bar, 10)
        dv[...] = jnp.zeros_like(dv)
        fetch(a2_ref, 0, l).start()
        for i in range(n):
            d[i] = jnp.zeros((RP, D), F32)
            d[i, 0:SEQ, :] = cot_ref[i].astype(F32)

    @pl.when(s == 0)
    def _():
        fetch(o_ref, 1, l).start()

    @pl.when(s == 4)
    def _():
        fetch(a2_ref, 0, l).wait()

        @pl.when(lr == 0)
        def _():
            load(l, 3, 9, 0).wait()

        @pl.when(lr == 1)
        def _():
            load(l, 3, 3, 0).wait()
            load(l, 6, 6, 3).wait()

    @pl.when(s == 8)
    def _():
        fetch(a1_ref, 0, l).start()
        load(l, 0, 3, 0).start()

    @pl.when(s == 13)
    def _():
        fetch(o_ref, 1, l).wait()

        @pl.when(lr == 0)
        def _():
            load(l - 1, 6, 6, 3).start()

    @pl.when(s == 19)
    def _():
        fetch(a1_ref, 0, l).wait()
        load(l, 0, 3, 0).wait()

    @pl.when((s == 20) & (lr == 0))
    def _():
        fetch(a2_ref, 0, l - 1).start()
        load(l - 1, 3, 3, 0).start()

    one = (s >= 5) & (s <= 8)
    two = (s >= 14) & (s <= 19) & (s != 16)
    three = (lr == 0) & (s == 21)
    four = (lr == 1) & ((s == 0) | (s == 2))
    five = (lr == 1) & (s >= 20)
    back = s - 14
    t = jnp.where(one, 12 * lr + s - 5, jnp.where(two, 12 * lr + 4 + back - (back + 1) // 4, jnp.where(three, 9, jnp.where(four, 10 + s // 2, s + 3))))

    @pl.when(one | two | three | four | five)
    def _():
        tick(t)

    @pl.when(s == 0)
    def _():
        for i in range(n):
            up = d[i]
            db[i] = up.astype(BF)
            acc[i] = jnp.zeros((RP, D), F32)
            dv[l, 7:8] += rsum(up)

    @pl.when((s >= 4) & (s < 8))
    def _():
        j = s - 4
        whole = db[...].reshape(rows, D)
        cols = pl.multiple_of(j * D, 128)
        for q in range(3):
            t1 = dot_t(whole, wk[pl.ds(pl.multiple_of((5 + j) * D + 256 * q, 16), 256), :])
            t1 = t1 * g_ref[0, :, :, 256 * q:256 * q + 256].reshape(rows, 256).astype(F32)
            dv[l, pl.ds(8 + j, 1), 256 * q:256 * q + 256] += rsum(t1)
            du[:, :, pl.ds(pl.multiple_of(cols + 256 * q, 128), 256)] = t1.astype(BF).reshape(n, RP, 256)
        acc[...] += dot_t(du[:, :, pl.ds(cols, D)].reshape(rows, D), wk[pl.ds(pl.multiple_of(j * D, 16), D), :]).reshape(n, RP, D)

    @pl.when((s >= 8) & (s < 13))
    def _():
        i = s - 8
        dx, dg, dc = norm_back(h1_ref[0, 0], vec_ref[l, 5:6], acc[i])
        dv[l, 5:6] += dg
        dv[l, 6:7] += dc
        dh1 = d[i] + dx
        d[i] = dh1
        dv[l, 4:5] += rsum(dh1)
        du[i, :, 0:D] = dh1.astype(BF)
        du[i, :, 3 * D:4 * D] = dot_t(du[i, :, 0:D], wk[4 * D:5 * D, :]).astype(BF)

    def grad(lhs, rhs, store):
        for m in range(2):
            r = dot_0(lhs(384 * m), rhs).astype(BF).reshape(4, CH, D)
            store(4 * m, r)

    def inner(slot, j):
        def store(m, r):
            gb[slot, m // 2, 0] = r[0]
            gb[slot, m // 2, 1] = r[1]
            gb[slot, m // 2 + 1, 0] = r[2]
            gb[slot, m // 2 + 1, 1] = r[3]
        grad(lambda m: ab[0, :, :, m:m + 384].reshape(rows, 384), du[:, :, pl.ds(pl.multiple_of(D * j, 128), D)].reshape(rows, D), store)

    def outer(step, lhs, rhs):
        def store(m, r):
            for q in range(4):
                b = 8 * step + m + q
                gb[4 + b % 5, b // 10, (b // 5) % 2] = r[q]
        grad(lhs, rhs.reshape(rows, D), store)

    @pl.when((s >= 4) & (s < 8))
    def _():
        inner(s - 4, s - 4)

    @pl.when(s == 13)
    def _():
        outer(0, lambda m: ab[1, :, :, m:m + 384].reshape(rows, 384), du[:, :, 0:D])

    @pl.when(s < 4)
    def _():
        outer(s + 1, lambda m: e_ref[0, :, :, m:m + 384].reshape(rows, 384), db[...])

    @pl.when((s >= 14) & (s < 19))
    def _():
        i = s - 14
        for p in range(6):
            b = 128 * p
            dq, dk, dvv = attn_bwd(qkv_ref[0, 0, :, b:b + 128], qkv_ref[0, 0, :, D + b:D + b + 128], qkv_ref[0, 0, :, 2 * D + b:2 * D + b + 128],
                                   du[i, :, 3 * D + b:3 * D + b + 128])
            dv[l, 2:3, b:b + 128] += rsum(dq)
            dv[l, 3:4, b:b + 128] += rsum(dvv)
            du[i, :, b:b + 128] = dq.astype(BF)
            du[i, :, D + b:D + b + 128] = dk.astype(BF)
            du[i, :, 2 * D + b:2 * D + b + 128] = dvv.astype(BF)

    @pl.when(s == 19)
    def _():
        @pl.loop(0, 3)
        def _(j):
            inner(j, j)

            @pl.when((lr == 1) & (j >= 1))
            def _():
                tick(20 + j)
        acc[...] = dot_t(du[:, :, 0:D].reshape(rows, D), wk[0:D, :]).reshape(n, RP, D)
        acc[...] += dot_t(du[:, :, D:2 * D].reshape(rows, D), wk[D:2 * D, :]).reshape(n, RP, D)
        acc[...] += dot_t(du[:, :, 2 * D:3 * D].reshape(rows, D), wk[2 * D:3 * D, :]).reshape(n, RP, D)

    @pl.when(s >= 20)
    def _():
        i = s - 20
        dx, dg, dc = norm_back(hs_ref[0, 0], vec_ref[l, 0:1], acc[i])
        dv[l, 0:1] += dg
        dv[l, 1:2] += dc
        dh = d[i] + dx
        d[i] = dh
        di_ref[0] = dh[0:SEQ]

    @pl.when((lr == 1) & (s == 24))
    def _():
        for layer in range(LAYERS):
            for c in range(72):
                vs[c // 9, layer, c % 9:c % 9 + 1, :] = dv[layer, c // 6:c // 6 + 1, 128 * (c % 6):128 * (c % 6) + 128]

        def vcopy(k):
            to = (f + k) % 8
            return pltpu.make_async_remote_copy(src_ref=vs.at[to], dst_ref=vr.at[k - 1], send_sem=vssem.at[k - 1], recv_sem=vrsem.at[k - 1],
                                                device_id={"fsdp": to}, device_id_type=MESH)

        def zcopy(k):
            return pltpu.make_async_remote_copy(src_ref=vz.at[z], dst_ref=vz.at[z], send_sem=vssem.at[6 + k], recv_sem=vrsem.at[6 + k],
                                                device_id={"rep": (z + k) % 4}, device_id_type=MESH)
        for k in range(1, 8):
            vcopy(k).start()

        @pl.loop(28, 36)
        def _(t):
            @pl.when(t == 30)
            def _():
                for k in range(1, 8):
                    vcopy(k).wait()
                total = vs[f]
                for k in range(7):
                    total = total + vr[k]
                vz[z] = total
                for k in range(1, 4):
                    zcopy(k).start()
            tick(t)

        for k in range(1, 4):
            zcopy(k).wait()
        gv_ref[...] = (vz[0] + vz[1]) + (vz[2] + vz[3])


def bwd(cotangent, w, vec, hs, h1, g, e, qkv, a2, o, a1, shard_in, shard_out):
    n = cotangent.shape[0]
    S = jax.ShapeDtypeStruct
    anyw = pl.BlockSpec(memory_space=pl.ANY)
    row = lambda cols, at: pl.BlockSpec((1, 1, RP, cols), lambda lr, s: (LAYERS - 1 - lr, jnp.clip(s - at, 0, 4), 0, 0))
    cols = lambda at: pl.BlockSpec((1, n, RP, D), lambda lr, s: (LAYERS - 1 - lr, 0, 0, jnp.clip(s - at, 0, 3)))
    tok = lambda index: pl.BlockSpec((1, SEQ, D), index)
    VB = lambda *shape: pltpu.VMEM(shape, BF)
    half = CH // 2
    return pl.pallas_call(
        bwd_kernel, grid=(LAYERS, 25),
        in_specs=[pl.BlockSpec(cotangent.shape, lambda lr, s: (0, 0, 0), pipeline_mode=pl.Buffered(1)), anyw, pl.BlockSpec(vec.shape, lambda lr, s: (0, 0, 0)),
                  row(D, 20), row(D, 8), cols(4), cols(0), row(3 * D, 14), anyw, anyw, anyw],
        out_specs=[tok(lambda lr, s: (lr * jnp.clip(s - 20, 0, 4), 0, 0)), anyw, anyw, pl.BlockSpec((LAYERS, 16, 128), lambda lr, s: (0, 0, 0))],
        out_shape=[S(cotangent.shape, F32), S(shard_in, BF), S(shard_out, BF), S((LAYERS, 16, 128), F32)],
        scratch_shapes=[VB(9 * D, D), pltpu.VMEM((n, RP, D), F32), pltpu.VMEM((n, RP, D), F32), VB(n, RP, D), VB(n, RP, 4 * D), VB(2, n, RP, D),
                        VB(9, 4, 2, CH, D), pltpu.VMEM((LAYERS, 16, D), F32),
                        VB(2, 4, CH, D), VB(2, 2, 2, CH, D), VB(4, 2, half, D), VB(4, 2, half, D), VB(2, 2, half, D), VB(2, 2, half, D),
                        VB(4, half, D), VB(4, half, D), VB(2, CH, D), VB(4, half, D), VB(2, half, D), VB(4, half, D), VB(2, half, D), VB(4, half, D),
                        VB(2, CH, D),
                        pltpu.VMEM((8, LAYERS, 16, 128), F32), pltpu.VMEM((7, LAYERS, 16, 128), F32), pltpu.VMEM((4, LAYERS, 16, 128), F32),
                        pltpu.SemaphoreType.DMA((2,)), pltpu.SemaphoreType.DMA((2,)), pltpu.SemaphoreType.DMA((4, 8)), pltpu.SemaphoreType.DMA((4, 8)),
                        pltpu.SemaphoreType.DMA((2,)), pltpu.SemaphoreType.DMA((10,)), pltpu.SemaphoreType.DMA((10,))],
        compiler_params=pltpu.CompilerParams(collective_id=1, has_side_effects=True, vmem_limit_bytes=63 * 2**20),
    )(cotangent, w, vec, hs, h1, g, e, qkv, a2, o, a1)


STEP = 3
beta_one = 0.9
beta_two = 0.999
matrix_rate = 0.03
vector_rate = 0.2
matrix_decay = 0.05
adam_eps = 1e-8


def adam_update(master, gradient, moment_one, moment_two, rate, decay_rate):
    moment_one = beta_one * moment_one + (1.0 - beta_one) * gradient
    moment_two = beta_two * moment_two + (1.0 - beta_two) * gradient * gradient
    corr_one = 1.0 - beta_one**STEP
    corr_two = 1.0 - beta_two**STEP
    adam_move = moment_one / corr_one / (jnp.sqrt(moment_two / corr_two) + adam_eps)
    return (master - rate * (adam_move + decay_rate * master), moment_one, moment_two)


def adam_kernel(g_ref, w_ref, m_ref, v_ref, go_ref, wo_ref, mo_ref, vo_ref, enc_ref, dim_ref,
                g_out, w_out, m_out, v_out, go_out, wo_out, mo_out, vo_out, enc_out, dim_out, steps):
    i = pl.program_id(0)

    def update(g, w, m, v, outs):
        grad = g[...].astype(F32)
        new, moment, square = adam_update(w[...], grad, m[...], v[...], matrix_rate, matrix_decay)
        outs[0][...], outs[1][...], outs[2][...], outs[3][...] = grad, new, moment, square

    @pl.when(i < steps)
    def _():
        update(g_ref, w_ref, m_ref, v_ref, (g_out, w_out, m_out, v_out))

    @pl.when(i >= steps)
    def _():
        update(go_ref, wo_ref, mo_ref, vo_ref, (go_out, wo_out, mo_out, vo_out))

    @pl.when(i < enc_steps)
    def _():
        enc_out[...] = enc_ref[...]
        dim_out[...] = dim_ref[...]


enc_steps = 5


def adam_all(ins, outs, encoded, dimg):
    a, b = ins[0].shape, outs[0].shape
    steps = 2 * LAYERS
    first = pl.BlockSpec((1, a[1] // 2, a[2]), lambda i: (jnp.minimum(i, steps - 1) // 2, jnp.minimum(i, steps - 1) % 2, 0))
    second = pl.BlockSpec((1, b[1] // 2, b[2]), lambda i: (jnp.maximum(i - steps, 0) // 2, jnp.maximum(i - steps, 0) % 2, 0))
    tok = pl.BlockSpec((1,) + encoded.shape[1:], lambda i: (jnp.minimum(i, enc_steps - 1), 0, 0))
    S = jax.ShapeDtypeStruct
    return pl.pallas_call(
        functools.partial(adam_kernel, steps=steps), grid=(2 * steps,),
        in_specs=[first] * 4 + [second] * 4 + [tok] * 2, out_specs=[first] * 4 + [second] * 4 + [tok] * 2,
        out_shape=[S(a, F32)] * 4 + [S(b, F32)] * 4 + [S(encoded.shape, BF), S(dimg.shape, F32)],
        compiler_params=PAR,
    )(*ins, *outs, encoded, dimg)


def swap(x, axis, size, mask):
    return lax.ppermute(x, axis, [(i, i ^ mask) for i in range(size)])


def halve(x, order, size):
    bits = size.bit_length() - 1
    me = lax.axis_index("fsdp")
    x = x.reshape((2,) * bits + x.shape[1:])
    left = list(range(bits))[::-1]
    for bit in order:
        at = left.index(bit)
        mine = (me >> bit) & 1
        keep = lax.dynamic_index_in_dim(x, mine, at, keepdims=False)
        send = lax.dynamic_index_in_dim(x, 1 - mine, at, keepdims=False)
        got = swap(send, "fsdp", size, 1 << bit)
        x = (keep.astype(F32) + got.astype(F32)).astype(BF)
        left.remove(bit)
    return x


def reduce_all(x, nf, nr):
    bits = nf.bit_length() - 1
    rows, cols = x.shape
    x = x.reshape(nf, rows // nf, cols)
    half = cols // 2 // 128 * 128
    up = [0] + list(range(1, bits))
    down = [0] + list(range(1, bits))[::-1]
    x = jnp.concatenate([halve(x[..., :half], up, nf), halve(x[..., half:], down, nf)], axis=-1)
    mask = 1
    while mask < nr:
        got = swap(x, "rep", nr, 2 * mask - 1)
        y = x.astype(F32) + got.astype(F32)
        x = y.astype(BF)
        mask *= 2
    return y


def fused_step(images, cotangent, weight_in, weight_out, vector_params):
    vs = jnp.pad(vector_params.astype(BF).astype(F32).reshape(LAYERS, 9, 128), ((0, 0), (0, 7), (0, 0)))
    hs, qkv, a1, o, h1, a2, e, g, encoded, w, vec = fwd(images, weight_in, weight_out, vs)
    dimg, gi, go, gv = bwd(cotangent, w, vec, hs, h1, g, e, qkv, a2, o, a1, weight_in.shape, weight_out.shape)
    return encoded, dimg, gi, go, gv[:, :9].reshape(vector_params.shape)


def plain_step(nf, nr, images, cotangent, weight_in, weight_out, vector_params):
    pad = lambda a: jnp.pad(a, ((0, 0), (0, RP - SEQ), (0, 0)))
    vec_all = lax.all_gather(vector_params.astype(BF), "fsdp", axis=1, tiled=True).astype(F32)
    h = pad(images)
    ct = pad(cotangent)
    saved = []
    for l in range(LAYERS):
        win = lax.all_gather(weight_in[l].astype(BF), "fsdp", axis=0, tiled=True)
        wout = lax.all_gather(weight_out[l].astype(BF), "fsdp", axis=0, tiled=True)
        vec = jnp.pad(vec_all[l].reshape(12, D), ((0, 4), (0, 0)))
        wqkv, w1, wo, w2 = win[:, : 3 * D], win[:, 3 * D :], wout[:D], wout[D:]
        qkv, o, a1 = ka(h, wqkv, vec)
        h1, a2, e, g, h2 = kb(h, o, wo, w1, w2, vec)
        saved.append((h, wqkv, w1, wo, w2, vec, qkv, o, a1, h1, a2, e, g))
        h = h2
    encoded = h[:, :SEQ].astype(BF)
    d = ct
    gin, gout, gvec = [None] * LAYERS, [None] * LAYERS, [None] * LAYERS
    for l in reversed(range(LAYERS)):
        h, wqkv, w1, wo, w2, vec, qkv, o, a1, h1, a2, e, g = saved[l]
        db, du, dh1, dh1b, do, dv1 = kc(d, h1, g, wo, w1, w2, vec)
        g1 = reduce_all(dw(a2, du), nf, nr)
        go = reduce_all(jnp.concatenate([dw(o, dh1b), dw(e, db)], axis=0), nf, nr)
        dz, dv2 = kd(qkv, do)
        gq = reduce_all(dw(a1, dz), nf, nr)
        d, dv3 = kf(dz, h, dh1, wqkv, vec, RP if l else SEQ)
        gin[l] = jnp.concatenate([gq, g1], axis=1)
        gout[l] = go
        gvec[l] = (dv1 + dv2 + dv3)[:12].reshape(-1)
    gv = lax.psum(jnp.stack(gvec), ("fsdp", "rep"))
    wide = gv.shape[1] // nf
    gv = lax.dynamic_slice_in_dim(gv, lax.axis_index("fsdp") * wide, wide, 1)
    return encoded, d, jnp.stack(gin), jnp.stack(gout), gv


def make_shards(nf, nr):
    def shards(images, cotangent, weight_in, weight_out, vector_params, first_in, first_out, first_vec, second_in, second_out, second_vec):
        if nf == 8 and nr == 4:
            encoded, d, gi, go, gv = fused_step(images, cotangent, weight_in, weight_out, vector_params)
            gi, new_in, moment_in, square_in, go, new_out, moment_out, square_out, encoded, d = adam_all(
                (gi, weight_in, first_in, second_in), (go, weight_out, first_out, second_out), encoded, d)
        else:
            encoded, d, gi, go, gv = plain_step(nf, nr, images, cotangent, weight_in, weight_out, vector_params)
            new_in, moment_in, square_in = adam_update(weight_in, gi, first_in, second_in, matrix_rate, matrix_decay)
            new_out, moment_out, square_out = adam_update(weight_out, go, first_out, second_out, matrix_rate, matrix_decay)
        new_vec, moment_vec, square_vec = adam_update(vector_params, gv, first_vec, second_vec, vector_rate, 0.0)
        return (encoded, d, gi, go, gv, new_in, new_out, new_vec, moment_in, moment_out, moment_vec, square_in, square_out, square_vec)

    return shards


def solution(mesh):
    tokens = P(("fsdp", "rep"), None, None)
    matrix = P(None, "fsdp", None)
    vector = P(None, "fsdp")
    in_specs = (tokens, tokens) + (matrix, matrix, vector) * 3
    out_specs = (tokens, tokens) + (matrix, matrix, vector) * 4
    return jax.shard_map(make_shards(mesh.shape["fsdp"], mesh.shape["rep"]), mesh=mesh, in_specs=in_specs, out_specs=out_specs, check_vma=False)
```

```python
import functools
import jax, jax.numpy as jnp
from jax import lax
from jax.experimental import pallas as pl
from jax.experimental.pallas import tpu as pltpu
from jax.sharding import PartitionSpec as P

D=768; HD=64; SEQ=197; RP=208; EPS=1e-6
BF=jnp.bfloat16; F32=jnp.float32
def dot(a,b): return jnp.dot(a,b,preferred_element_type=F32)
def dot_t(a,b): return lax.dot_general(a,b,(((1,),(1,)),((),())),preferred_element_type=F32)
def dot_0(a,b): return lax.dot_general(a,b,(((0,),(0,)),((),())),preferred_element_type=F32)

def norm_stats(x):
    mean=jnp.mean(x,axis=-1,keepdims=True); xc=x-mean
    var=jnp.mean(xc*xc,axis=-1,keepdims=True)
    return xc, lax.rsqrt(var+EPS)

def head_masks(scale):
    lane = lax.broadcasted_iota(jnp.int32, (1, 128), 1)
    return jnp.where(lane < 64, scale, 0.0).astype(BF), jnp.where(lane < 64, 0.0, scale).astype(BF)


def weights_t(q, k, masks):
    row = lax.broadcasted_iota(jnp.int32, (RP, 1), 0)
    s = [jnp.where(row < SEQ, dot_t(k, q * m), -1e30) for m in masks]
    e = [jnp.exp(x - jnp.max(x, axis=0, keepdims=True)) for x in s]
    return [x * (1.0 / jnp.sum(x, axis=0, keepdims=True)) for x in e]


def attn_fwd(q, k, v):
    ones = head_masks(1.0)
    row = lax.broadcasted_iota(jnp.int32, (16, 1), 0)
    ps = []
    for m in head_masks(0.125):
        s = dot_t(k, q * m)
        s = jnp.concatenate([s[:RP - 16], jnp.where(row < SEQ - RP + 16, s[RP - 16:], -1e30)], axis=0)
        e = jnp.exp(s - jnp.max(s, axis=0, keepdims=True))
        ps.append((e * (1.0 / jnp.sum(e, axis=0, keepdims=True))).astype(BF))
    return (dot_0(ps[0], v * ones[0]) + dot_0(ps[1], v * ones[1])).astype(BF)


def attn_bwd(q, k, v, do):
    scaled, ones = head_masks(0.125), head_masks(1.0)
    p = weights_t(q, k, scaled)
    dos = [do * m for m in ones]
    dp = [dot_t(v, x) for x in dos]
    pb = [x.astype(BF) for x in p]
    ds = [(a * (b - jnp.sum(a * b, axis=0, keepdims=True))).astype(BF) for a, b in zip(p, dp)]
    dv = dot(pb[0], dos[0]) + dot(pb[1], dos[1])
    dk = dot(ds[0], q * scaled[0]) + dot(ds[1], q * scaled[1])
    dq = dot_0(ds[0], k * scaled[0]) + dot_0(ds[1], k * scaled[1])
    return dq, dk, dv


TAIL = SEQ - RP + 16


def fold_rows(first, last):
    r = lax.broadcasted_iota(jnp.int32, (16, 16), 0)
    c = lax.broadcasted_iota(jnp.int32, (16, 16), 1)
    move = jnp.where((r == c + TAIL) & (c < TAIL), 1.0, 0.0).astype(BF)
    row = lax.broadcasted_iota(jnp.int32, (16, 1), 0)
    return jnp.where((row >= TAIL) & (row < 2 * TAIL), dot(move, last), first.astype(F32)).astype(BF)


def clear_rows(first):
    row = lax.broadcasted_iota(jnp.int32, (16, 1), 0)
    return jnp.where(row < TAIL, first.astype(F32), 0.0).astype(BF)


def ka_kernel(h_ref,w_ref,vec_ref,qkv_ref,o_ref,a_ref):
    h=h_ref[0].astype(F32)
    xc,rs=norm_stats(h)
    a_ref[0]=(xc*rs*vec_ref[0:1]+vec_ref[1:2]).astype(BF)
    a=a_ref[0]
    for c in range(3):
        cs=slice(256*c,256*c+256)
        qkv_ref[0,:,256*c:256*c+256]=(dot(a,w_ref[:,256*c:256*c+256])+vec_ref[2:3,cs]).astype(BF)
        qkv_ref[0,:,D+256*c:D+256*c+256]=dot(a,w_ref[:,D+256*c:D+256*c+256]).astype(BF)
        qkv_ref[0,:,2*D+256*c:2*D+256*c+256]=(dot(a,w_ref[:,2*D+256*c:2*D+256*c+256])+vec_ref[3:4,cs]).astype(BF)
        for p in range(2):
            b=256*c+128*p
            o_ref[0,:,b:b+128]=attn_fwd(qkv_ref[0,:,b:b+128],qkv_ref[0,:,D+b:D+b+128],qkv_ref[0,:,2*D+b:2*D+b+128])

def img(n,dt=None): return pl.BlockSpec((1,RP,n),lambda i:(i,0,0))
def full(shape): return pl.BlockSpec(shape,lambda i:(0,)*len(shape))
PAR=pltpu.CompilerParams(vmem_limit_bytes=60*2**20)

def ka(h,w,vec):
    n=h.shape[0]
    return pl.pallas_call(ka_kernel,grid=(n,),in_specs=[img(D),full(w.shape),full(vec.shape)],
        out_specs=[img(3*D),img(D),img(D)],
        out_shape=[jax.ShapeDtypeStruct((n,RP,3*D),BF),jax.ShapeDtypeStruct((n,RP,D),BF),jax.ShapeDtypeStruct((n,RP,D),BF)],
        compiler_params=PAR)(h,w,vec)

def gelu_parts(u):
    c=0.5*(1.0+lax.erf(u*0.7071067811865476))
    g=c+u*(jnp.exp(-0.5*u*u)*0.3989422804014327)
    return u*c,g

def kb_kernel(FC,h_ref,o_ref,wo_ref,w1_ref,w2_ref,vec_ref,h1_ref,a_ref,e_ref,g_ref,h2_ref):
    h1=h_ref[0].astype(F32)+dot(o_ref[0],wo_ref[...])+vec_ref[4:5]
    h1_ref[0]=h1
    xc,rs=norm_stats(h1)
    a_ref[0]=(xc*rs*vec_ref[5:6]+vec_ref[6:7]).astype(BF)
    a=a_ref[0]
    h2_ref[0]=h1+vec_ref[7:8]
    for j in range(3072//FC):
        lo=FC*j
        u=dot(a,w1_ref[:,lo:lo+FC])+vec_ref[8+lo//D:9+lo//D,lo%D:lo%D+FC]
        e,g=gelu_parts(u)
        e_ref[0,:,lo:lo+FC]=e.astype(BF); g_ref[0,:,lo:lo+FC]=g.astype(BF)
        h2_ref[0]+=dot(e_ref[0,:,lo:lo+FC],w2_ref[lo:lo+FC,:])

def kb(h,o,wo,w1,w2,vec,FC=256):
    n=h.shape[0]
    S=jax.ShapeDtypeStruct
    return pl.pallas_call(functools.partial(kb_kernel,FC),grid=(n,),in_specs=[img(D),img(D),full(wo.shape),full(w1.shape),full(w2.shape),full(vec.shape)],
        out_specs=[img(D),img(D),img(3072),img(3072),img(D)],
        out_shape=[S((n,RP,D),F32),S((n,RP,D),BF),S((n,RP,3072),BF),S((n,RP,3072),BF),S((n,RP,D),F32)],
        compiler_params=PAR)(h,o,wo,w1,w2,vec)

def rsum(x): return jnp.sum(x,axis=0,keepdims=True)
def norm_back(x,gain,dy):
    xc,rs=norm_stats(x); xh=xc*rs
    dyg=dy*gain
    dx=rs*(dyg-jnp.mean(dyg,axis=-1,keepdims=True)-xh*jnp.mean(dyg*xh,axis=-1,keepdims=True))
    return dx, rsum(dy*xh), rsum(dy)

def kc_kernel(FC,d_ref,h1_ref,g_ref,wo_ref,w1_ref,w2_ref,vec_ref,db_ref,du_ref,dh1_ref,dh1b_ref,do_ref,dv_ref,acc_ref):
    @pl.when(pl.program_id(0)==0)
    def _(): dv_ref[...]=jnp.zeros_like(dv_ref)
    d=d_ref[0].astype(F32)
    db_ref[0]=d.astype(BF)
    db=db_ref[0]
    dv_ref[7:8]+=rsum(d)
    for j in range(3072//FC):
        lo=FC*j
        du=dot_t(db,w2_ref[lo:lo+FC,:])*g_ref[0,:,lo:lo+FC].astype(F32)
        dv_ref[8+lo//D:9+lo//D,lo%D:lo%D+FC]+=rsum(du)
        du_ref[0,:,lo:lo+FC]=du.astype(BF)
        t=dot_t(du_ref[0,:,lo:lo+FC],w1_ref[:,lo:lo+FC])
        if j==0: acc_ref[...]=t
        else: acc_ref[...]+=t
    dx,dg,dc=norm_back(h1_ref[0],vec_ref[5:6],acc_ref[...])
    dv_ref[5:6]+=dg; dv_ref[6:7]+=dc
    dh1=d_ref[0].astype(F32)+dx
    dh1_ref[0]=dh1
    dv_ref[4:5]+=rsum(dh1)
    dh1b_ref[0]=dh1.astype(BF)
    do_ref[0]=dot_t(dh1b_ref[0],wo_ref[...]).astype(BF)

def kc(d,h1,g,wo,w1,w2,vec,FC=256):
    n=d.shape[0]; S=jax.ShapeDtypeStruct
    return pl.pallas_call(functools.partial(kc_kernel,FC),grid=(n,),in_specs=[img(D),img(D),img(3072),full(wo.shape),full(w1.shape),full(w2.shape),full(vec.shape)],
        out_specs=[img(D),img(3072),img(D),img(D),img(D),full((16,D))],
        out_shape=[S((n,RP,D),BF),S((n,RP,3072),BF),S((n,RP,D),F32),S((n,RP,D),BF),S((n,RP,D),BF),S((16,D),F32)],
        scratch_shapes=[pltpu.VMEM((RP,D),F32)],
        compiler_params=PAR)(d,h1,g,wo,w1,w2,vec)

def kd_kernel(qkv_ref,do_ref,dz_ref,dv_ref):
    @pl.when(pl.program_id(0)==0)
    def _(): dv_ref[...]=jnp.zeros_like(dv_ref)
    for p in range(6):
        b=128*p
        dq,dk,dv=attn_bwd(qkv_ref[0,:,b:b+128],qkv_ref[0,:,D+b:D+b+128],qkv_ref[0,:,2*D+b:2*D+b+128],do_ref[0,:,b:b+128])
        dv_ref[2:3,b:b+128]+=rsum(dq); dv_ref[3:4,b:b+128]+=rsum(dv)
        dz_ref[0,:,b:b+128]=dq.astype(BF); dz_ref[0,:,D+b:D+b+128]=dk.astype(BF); dz_ref[0,:,2*D+b:2*D+b+128]=dv.astype(BF)

def kd(qkv,do):
    n=do.shape[0]; S=jax.ShapeDtypeStruct
    return pl.pallas_call(kd_kernel,grid=(n,),in_specs=[img(3*D),img(D)],out_specs=[img(3*D),full((16,D))],
        out_shape=[S((n,RP,3*D),BF),S((16,D),F32)],compiler_params=PAR)(qkv,do)

def kf_kernel(dz_ref,h_ref,dh1_ref,w_ref,vec_ref,dh_ref,dv_ref):
    @pl.when(pl.program_id(0)==0)
    def _(): dv_ref[...]=jnp.zeros_like(dv_ref)
    da=dot_t(dz_ref[0],w_ref[...])
    dx,dg,dc=norm_back(h_ref[0].astype(F32),vec_ref[0:1],da)
    dv_ref[0:1]+=dg; dv_ref[1:2]+=dc
    rows=dh_ref.shape[1]
    dh_ref[0]=(dh1_ref[0]+dx)[:rows]

def kf(dz,h,dh1,w,vec,rows=RP):
    n=dz.shape[0]; S=jax.ShapeDtypeStruct
    return pl.pallas_call(kf_kernel,grid=(n,),in_specs=[img(3*D),img(D),img(D),full(w.shape),full(vec.shape)],
        out_specs=[pl.BlockSpec((1,rows,D),lambda i:(i,0,0)),full((16,D))],
        out_shape=[S((n,rows,D),F32),S((16,D),F32)],compiler_params=PAR)(dz,h,dh1,w,vec)

def dw_kernel(l_ref,r_ref,o_ref):
    o_ref[...]=dot_0(l_ref[...],r_ref[...]).astype(BF)
def dw(l,r,MB=256):
    M=l.shape[-1]; N=r.shape[-1]; K=l.shape[0]*RP
    l=l.reshape(K,M); r=r.reshape(K,N)
    return pl.pallas_call(dw_kernel,grid=(M//MB,),in_specs=[pl.BlockSpec((K,MB),lambda i:(0,i)),pl.BlockSpec((K,N),lambda i:(0,0))],
       out_specs=pl.BlockSpec((MB,N),lambda i:(i,0)),out_shape=jax.ShapeDtypeStruct((M,N),BF),compiler_params=PAR)(l,r)


LAYERS = 2
MESH = pl.DeviceIdType.MESH
CH = 96
NC = 12


def plane():
    f = lax.axis_index("fsdp")
    core, x, y = f % 2, (f // 2) % 2, f // 4
    return f, core, x, y


def chunk_rows(c, f):
    layer, j = c // NC, c % NC
    early = 1 - (j + 9) // 12
    late = j // 8
    mid = 1 - early - late
    base = layer * NC * D
    return pl.multiple_of(base + early * (j * D + CH * f) + late * ((j - 5) * D + CH * f)
                          + mid * (7 * D + 5 * CH * f + CH * (j - 3)), 16)


def fwd_kernel(img_ref, win_ref, wout_ref, vs_ref, hs_ref, qkv_ref, a1_ref, o_ref, h1_ref, a2_ref, e_ref, g_ref, enc_ref, wo_ref, vo_ref,
               w, hb, ob, ab, vg, vec, st, lsem, ssem, rsem, vssem, vrsem, osem, vosem):
    l, s = pl.program_id(0), pl.program_id(1)
    f, core, x, y = plane()
    fc, fx, fy = f + 1 - 2 * core, f + 2 - 4 * x, f + 4 - 8 * y
    fd = fx + fy - f
    z = lax.axis_index("rep")
    side = z % 2
    zp = z + 1 - 2 * side
    part = pl.ds(pl.multiple_of(256 * side, 128), 512)
    give = pl.ds(pl.multiple_of(512 * side, 128), 256)

    def wrow(c, who, lo=0, n=CH):
        return pl.ds(pl.multiple_of(chunk_rows(c, who) + lo, 16), n)

    def send(c, kind, where, **to):
        return pltpu.make_async_remote_copy(src_ref=w.at[where], dst_ref=w.at[where], send_sem=ssem.at[c % 12, kind], recv_sem=rsem.at[c % 12, kind],
                                            device_id=to, device_id_type=MESH)

    def fetch(c, act):
        layer, j = c // NC, c % NC
        mid = (j >= 3) & (j < 8)

        @pl.when(mid)
        def _():
            act(pltpu.make_async_copy(wout_ref.at[layer, pl.ds(pl.multiple_of((j - 3) * CH, 8), CH)], st.at[c % 4], lsem.at[c % 4]))

        @pl.when(jnp.logical_not(mid))
        def _():
            act(pltpu.make_async_copy(win_ref.at[layer, :, pl.ds(pl.multiple_of((j - 5 * (j // 8)) * D, 128), D)], st.at[c % 4], lsem.at[c % 4]))

    def kinds(c):
        half = CH // 2
        return [lambda: send(c, 0, (wrow(c, f), part), fsdp=fx), lambda: send(c, 1, (wrow(c, f), part), fsdp=fy),
                lambda: send(c, 2, (wrow(c, f),), fsdp=fc),
                lambda: send(c, 3, (wrow(c, fx, 0, half), part), fsdp=fy), lambda: send(c, 4, (wrow(c, fy, half, half), part), fsdp=fx),
                lambda: send(c, 5, (wrow(c, fx), give), rep=zp), lambda: send(c, 6, (wrow(c, fy), give), rep=zp),
                lambda: send(c, 7, (wrow(c, fd), give), rep=zp),
                lambda: send(c, 8, (wrow(c, fx),), fsdp=fc), lambda: send(c, 9, (wrow(c, fy),), fsdp=fc), lambda: send(c, 10, (wrow(c, fd),), fsdp=fc)]

    def start(c, which):
        k = kinds(c)
        for i in which:
            k[i]().start()

    def wait(c, which):
        k = kinds(c)
        for i in which:
            k[i]().wait()

    def tick(t):
        @pl.when((t >= 7) & (t < 31))
        def _():
            wait(t - 7, (2, 8, 9, 10))

        @pl.when((t >= 6) & (t < 30))
        def _():
            wait(t - 6, (7,))
            start(t - 6, (10,))

        @pl.when((t >= 4) & (t < 28))
        def _():
            wait(t - 4, (3, 4, 5, 6))
            start(t - 4, (7, 8, 9))

        @pl.when((t >= 2) & (t < 26))
        def _():
            wait(t - 2, (0, 1))
            start(t - 2, (3, 4, 5, 6))

        def launch(c):
            fetch(c, lambda a: a.wait())
            w[pl.ds(chunk_rows(c, f), CH)] = st[c % 4].astype(BF)
            start(c, (0, 1, 2))

        @pl.when(t < 24)
        def _():
            launch(t)

        @pl.when(t < 21)
        def _():
            fetch(t + 3, lambda a: a.start())

    def out_copy(b, n):
        return pltpu.make_async_copy(w.at[pl.ds(b, n)], wo_ref.at[pl.ds(b, n)], osem)

    @pl.when((l == 0) & (s == 0))
    def _():
        for c in range(3):
            fetch(jnp.int32(c), lambda a: a.start())
        bar = pltpu.get_barrier_semaphore()
        for k in range(1, 8):
            pl.semaphore_signal(bar, inc=1, device_id={"fsdp": (f + k) % 8}, device_id_type=MESH)
        pl.semaphore_signal(bar, inc=1, device_id={"rep": zp}, device_id_type=MESH)
        pl.semaphore_wait(bar, 8)

        def vcopy(k):
            return pltpu.make_async_remote_copy(src_ref=vs_ref, dst_ref=vg.at[f], send_sem=vssem.at[k - 1], recv_sem=vrsem.at[k - 1],
                                                device_id={"fsdp": (f + k) % 8}, device_id_type=MESH)
        for k in range(1, 8):
            vcopy(k).start()
        vg[f] = vs_ref[...]

        @pl.loop(0, 10)
        def _(t):
            tick(t)

            @pl.when(t == 0)
            def _():
                hb[...] = jnp.zeros_like(hb)

            @pl.when(t == 3)
            def _():
                for k in range(1, 8):
                    vcopy(k).wait()
                for layer in range(LAYERS):
                    for c in range(72):
                        vec[layer, c // 6:c // 6 + 1, 128 * (c % 6):128 * (c % 6) + 128] = vg[c // 9, layer, c % 9:c % 9 + 1, :]
                pltpu.make_async_copy(vec, vo_ref, vosem).start()

    early = s <= 5
    late = (s == 8) | ((s >= 10) & (s + l <= 13))
    t = jnp.where(early, (1 - l) * (s + 9) + l * (s + 21), jnp.where(s == 8, 15 + 12 * l, (1 - l) * (s + 6 + s // 12) + l * (s + 18)))

    @pl.when((early & (l + s > 0)) | late)
    def _():
        tick(t)

    @pl.when(s < 5)
    def _():
        @pl.when(l == 0)
        def _():
            hb[s, 0:SEQ, :] = img_ref[s].astype(F32)
        h = hb[s]
        hs_ref[0, 0] = h
        xc, rs = norm_stats(h)
        a1_ref[0, 0] = (xc * rs * vec[l, 0:1] + vec[l, 1:2]).astype(BF)
        a = a1_ref[0, 0]
        wb = l * NC * D

        def wq(part, c):
            return w[pl.ds(pl.multiple_of(wb + part * D, 16), D), 256 * c:256 * c + 256]
        for c in range(3):
            cs = slice(256 * c, 256 * c + 256)
            qkv_ref[0, 0, :, cs] = (dot(a, wq(0, c)) + vec[l, 2:3, cs]).astype(BF)
            qkv_ref[0, 0, :, D + 256 * c:D + 256 * c + 256] = dot(a, wq(1, c)).astype(BF)
            qkv_ref[0, 0, :, 2 * D + 256 * c:2 * D + 256 * c + 256] = (dot(a, wq(2, c)) + vec[l, 3:4, cs]).astype(BF)
            for p in range(2):
                b = 256 * c + 128 * p
                o = attn_fwd(qkv_ref[0, 0, :, b:b + 128], qkv_ref[0, 0, :, D + b:D + b + 128], qkv_ref[0, 0, :, 2 * D + b:2 * D + b + 128])
                o_ref[0, 0, :, b:b + 128] = o
                ob[s, :, b:b + 128] = o

    @pl.when((s >= 5) & (s < 10))
    def _():
        i = s - 5
        wo = w[pl.ds(pl.multiple_of((l * NC + 7) * D, 16), D), :]
        h1 = hb[i] + dot(ob[i], wo) + vec[l, 4:5]
        h1_ref[0, 0] = h1
        hb[i] = h1 + vec[l, 7:8]
        xc, rs = norm_stats(h1)
        a = (xc * rs * vec[l, 5:6] + vec[l, 6:7]).astype(BF)
        a2_ref[0, 0] = a
        ab[i] = a

    @pl.when(s >= 10)
    def _():
        j = s - 10
        up = pl.multiple_of((l * NC + 3 + j) * D, 16)
        down = pl.multiple_of((l * NC + 8 + j) * D, 16)

        bias = vec[l, pl.ds(8 + j, 1), :]
        n = hb.shape[0]
        u = dot(ab[0], w[pl.ds(up, D), :])
        for i in range(n):
            later = dot(ab[i + 1], w[pl.ds(up, D), :]) if i < n - 1 else None
            e, g = gelu_parts(u + bias)
            e = e.astype(BF)
            e_ref[0, i] = e
            g_ref[0, i] = g.astype(BF)
            hb[i] += dot(e, w[pl.ds(down, D), :])
            u = later
            if i == 2:
                @pl.when((s == 11) & (l == 0))
                def _():
                    tick(18)

        e_ref[0, 0, RP - 16:RP] = fold_rows(e_ref[0, 0, RP - 16:RP], e_ref[0, n - 1, RP - 16:RP])

        @pl.when((l == 1) & (s == 13))
        def _():
            for i in range(n):
                enc_ref[i] = hb[i, 0:SEQ, :].astype(BF)

    for layer in range(LAYERS):
        base = layer * NC * D

        @pl.when((l == layer) & (s == 4))
        def _():
            out_copy(base, 3 * D).start()

        @pl.when((l == layer) & (s == 9))
        def _():
            out_copy(base + 7 * D, 5 * D).start()

        for j in range(4):
            @pl.when((l == layer) & (s == 10 + j))
            def _():
                out_copy(base + (3 + j) * D, D).start()

    @pl.when((l == 1) & (s == 13))
    def _():
        pltpu.make_async_copy(w, wo_ref, osem).wait()
        pltpu.make_async_copy(vec, vo_ref, vosem).wait()


def fwd(images, weight_in, weight_out, vshard):
    n = images.shape[0]
    S = jax.ShapeDtypeStruct
    one = lambda cols: pl.BlockSpec((1, 1, RP, cols), lambda l, s: (l, jnp.minimum(s, 4), 0, 0))
    two = lambda cols: pl.BlockSpec((1, 1, RP, cols), lambda l, s: (l, jnp.clip(s - 5, 0, 4), 0, 0))
    wide = pl.BlockSpec((1, n, RP, D), lambda l, s: (l, 0, 0, jnp.clip(s - 10, 0, 3)))
    anyw = pl.BlockSpec(memory_space=pl.ANY)
    rows = LAYERS * NC * D
    return pl.pallas_call(
        fwd_kernel, grid=(LAYERS, 14),
        in_specs=[pl.BlockSpec(images.shape, lambda l, s: (0, 0, 0)), anyw, anyw, pl.BlockSpec(vshard.shape, lambda l, s: (0, 0, 0))],
        out_specs=[one(D), one(3 * D), one(D), one(D), two(D), two(D), wide, wide, pl.BlockSpec(images.shape, lambda l, s: (0, 0, 0)), anyw, anyw],
        out_shape=[S((LAYERS, n, RP, D), F32), S((LAYERS, n, RP, 3 * D), BF), S((LAYERS, n, RP, D), BF), S((LAYERS, n, RP, D), BF),
                   S((LAYERS, n, RP, D), F32), S((LAYERS, n, RP, D), BF), S((LAYERS, n, RP, 4 * D), BF), S((LAYERS, n, RP, 4 * D), BF),
                   S(images.shape, BF), S((rows, D), BF), S((LAYERS, 16, D), F32)],
        scratch_shapes=[pltpu.VMEM((rows, D), BF), pltpu.VMEM((n, RP, D), F32), pltpu.VMEM((n, RP, D), BF), pltpu.VMEM((n, RP, D), BF),
                        pltpu.VMEM((8, LAYERS, 16, 128), F32), pltpu.VMEM((LAYERS, 16, D), F32), pltpu.VMEM((4, CH, D), F32),
                        pltpu.SemaphoreType.DMA((4,)), pltpu.SemaphoreType.DMA((12, 11)), pltpu.SemaphoreType.DMA((12, 11)),
                        pltpu.SemaphoreType.DMA((7,)), pltpu.SemaphoreType.DMA((7,)), pltpu.SemaphoreType.DMA, pltpu.SemaphoreType.DMA],
        compiler_params=pltpu.CompilerParams(collective_id=0, has_side_effects=True, vmem_limit_bytes=62 * 2**20),
    )(images, weight_in, weight_out, vshard)


def bwd_kernel(cot_ref, w_ref, vec_ref, hs_ref, h1_ref, g_ref, e_ref, qkv_ref, a2_ref, o_ref, a1_ref,
               di_ref, gin_ref, gout_ref, gv_ref,
               wk, d, acc, db, du, ab, gb, dv, rc, s2, ra, rb, s3a, s3b, r3a, r3b, s4, rz, s5, ry, s6, rw, fin,
               vs, vr, vz, wsem, asem, ssem, rsem, osem, vssem, vrsem):
    lr, s = pl.program_id(0), pl.program_id(1)
    l = LAYERS - 1 - lr
    f, core, x, y = plane()
    z = lax.axis_index("rep")
    fc, fx, fy = f + 1 - 2 * core, f + 2 - 4 * x, f + 4 - 8 * y
    z1, z3 = z + 1 - 2 * (z % 2), 3 - z
    half = CH // 2
    mine = pl.multiple_of(((z + 1) // 2 % 2) * half, 16)
    theirs = pl.multiple_of(half - (z + 1) // 2 % 2 * half, 16)
    n = d.shape[0]
    rows = n * RP

    def load(layer, block, n, at):
        return pltpu.make_async_copy(w_ref.at[pl.ds(pl.multiple_of((layer * NC + block) * D, 16), n * D)], wk.at[pl.ds(at * D, n * D)], wsem.at[0 if at else 1])

    def fetch(src, slot, layer):
        return pltpu.make_async_copy(src.at[layer], ab.at[slot], asem.at[slot])

    def remote(kind, p, src, dst, **to):
        return pltpu.make_async_remote_copy(src_ref=src, dst_ref=dst, send_sem=ssem.at[p, kind], recv_sem=rsem.at[p, kind],
                                            device_id=to, device_id_type=MESH)

    def live(v):
        return (v >= 0) & (v < 24)

    def kind(n, v):
        p, q = v % 2, v % 4
        if n == 0:
            lc = v % NC
            return remote(0, q, gb.at[lc - 9 * (lc // 9), :, 1 - core], rc.at[p], fsdp=fc)
        if n == 1:
            return remote(1, q, s2.at[p, :, 1 - x, pl.ds(0, half)], ra.at[q], fsdp=fx)
        if n == 2:
            return remote(2, q, s2.at[p, 1 - y, :, pl.ds(half, half)], rb.at[q], fsdp=fy)
        if n == 3:
            return remote(3, q, s3a.at[p, 1 - y], r3a.at[q], fsdp=fy)
        if n == 4:
            return remote(4, q, s3b.at[p, 1 - x], r3b.at[q], fsdp=fx)
        if n == 5:
            return remote(5, q, s4.at[p, pl.ds(theirs, half)], rz.at[q], rep=z1)
        if n == 6:
            return remote(6, q, s5.at[p], ry.at[q], rep=z3)
        return remote(7, q, s6.at[p], rw.at[q], rep=z1)

    def put(v, act):
        lc, layer = v % NC, LAYERS - 1 - v // NC
        p = v % 2
        out = (lc >= 4) & (lc < 9)

        @pl.when(out)
        def _():
            act(pltpu.make_async_copy(fin.at[p], gout_ref.at[layer, pl.ds(pl.multiple_of((lc - 4) * CH, 16), CH)], osem.at[p]))

        @pl.when(jnp.logical_not(out))
        def _():
            j = lc + 3 - 9 * (lc // 9)
            j = j - 3 * (lc // 9)
            act(pltpu.make_async_copy(fin.at[p], gin_ref.at[layer, :, pl.ds(pl.multiple_of(j * D, 128), D)], osem.at[p]))

    def add(a, b):
        return a + b

    def tick(t):
        @pl.when(live(t - 12))
        def _():
            put(t - 12, lambda a: a.wait())

        @pl.when(live(t - 11))
        def _():
            v = t - 11
            p = v % 2
            kind(7, v).wait()
            fin[p, pl.ds(mine, half)] = s6[p]
            fin[p, pl.ds(theirs, half)] = rw[v % 4]
            put(v, lambda a: a.start())

        @pl.when(live(t - 9))
        def _():
            v = t - 9
            p = v % 2
            kind(6, v).wait()
            s6[p] = add(s5[p], ry[v % 4]).astype(BF)
            kind(7, v).start()

        @pl.when(live(t - 7))
        def _():
            v = t - 7
            p = v % 2
            kind(5, v).wait()
            s5[p] = add(s4[p, pl.ds(mine, half)], rz[v % 4]).astype(BF)
            kind(6, v).start()

        @pl.when(live(t - 5))
        def _():
            v = t - 5
            p, q = v % 2, v % 4
            kind(3, v).wait()
            kind(4, v).wait()
            s4[p, 0:half] = add(s3a[p, y], r3a[q]).astype(BF)
            s4[p, half:CH] = add(s3b[p, x], r3b[q]).astype(BF)
            kind(5, v).start()

        @pl.when(live(t - 3))
        def _():
            v = t - 3
            p, q = v % 2, v % 4
            kind(1, v).wait()
            kind(2, v).wait()
            for i in range(2):
                s3a[p, i] = add(s2[p, i, x, 0:half], ra[q, i]).astype(BF)
                s3b[p, i] = add(s2[p, y, i, half:CH], rb[q, i]).astype(BF)
            kind(3, v).start()
            kind(4, v).start()

        @pl.when(live(t - 1))
        def _():
            v = t - 1
            p = v % 2
            kind(0, v).wait()
            lc = v % NC
            for i in range(4):
                s2[p, i // 2, i % 2] = add(gb[lc - 9 * (lc // 9), i, core], rc[p, i]).astype(BF)
            kind(1, v).start()
            kind(2, v).start()

        @pl.when(live(t))
        def _():
            kind(0, t).start()

    @pl.when((lr == 0) & (s == 0))
    def _():
        load(l, 3, 9, 0).start()
        bar = pltpu.get_barrier_semaphore()
        for k in range(1, 8):
            pl.semaphore_signal(bar, inc=1, device_id={"fsdp": (f + k) % 8}, device_id_type=MESH)
        for k in range(1, 4):
            pl.semaphore_signal(bar, inc=1, device_id={"rep": (z + k) % 4}, device_id_type=MESH)
        pl.semaphore_wait(bar, 10)
        dv[...] = jnp.zeros_like(dv)
        fetch(a2_ref, 0, l).start()
        for i in range(n):
            d[i] = jnp.zeros((RP, D), F32)
            d[i, 0:SEQ, :] = cot_ref[i].astype(F32)

    @pl.when(s == 0)
    def _():
        fetch(o_ref, 1, l).start()

    @pl.when(s == 4)
    def _():
        fetch(a2_ref, 0, l).wait()
        ab[0, 0, RP - 16:RP] = fold_rows(ab[0, 0, RP - 16:RP], ab[0, n - 1, RP - 16:RP])

        @pl.when(lr == 0)
        def _():
            load(l, 3, 9, 0).wait()

        @pl.when(lr == 1)
        def _():
            load(l, 3, 3, 0).wait()
            load(l, 6, 6, 3).wait()

    @pl.when(s == 8)
    def _():
        fetch(a1_ref, 0, l).start()
        load(l, 0, 3, 0).start()

    @pl.when(s == 13)
    def _():
        fetch(o_ref, 1, l).wait()
        ab[1, 0, RP - 16:RP] = fold_rows(ab[1, 0, RP - 16:RP], ab[1, n - 1, RP - 16:RP])

        @pl.when(lr == 0)
        def _():
            load(l - 1, 6, 6, 3).start()

    @pl.when(s == 19)
    def _():
        fetch(a1_ref, 0, l).wait()
        ab[0, 0, RP - 16:RP] = fold_rows(ab[0, 0, RP - 16:RP], ab[0, n - 1, RP - 16:RP])
        load(l, 0, 3, 0).wait()

    @pl.when((s == 20) & (lr == 0))
    def _():
        fetch(a2_ref, 0, l - 1).start()
        load(l - 1, 3, 3, 0).start()

    one = (s >= 5) & (s <= 8)
    two = (s >= 14) & (s <= 18)
    three = (lr == 0) & ((s == 20) | (s == 23))
    four = (lr == 1) & (s == 1)
    five = (lr == 1) & (s >= 20)
    t = jnp.where(one, 12 * lr + s - 5, jnp.where(two, 12 * lr + s - 10, jnp.where(three, 9 + (s - 20) // 3, jnp.where(four, 11, s + 4))))

    @pl.when(one | two | three | four | five)
    def _():
        tick(t)

    @pl.when(s == 0)
    def _():
        for i in range(n):
            up = d[i]
            db[i] = up.astype(BF)
            acc[i] = jnp.zeros((RP, D), F32)
            dv[l, 7:8] += rsum(up)
        db[0, RP - 16:RP] = fold_rows(db[0, RP - 16:RP], db[n - 1, RP - 16:RP])

    @pl.when(s == 4)
    def _():
        db[0, RP - 16:RP] = clear_rows(db[0, RP - 16:RP])

    @pl.when((s >= 4) & (s < 8))
    def _():
        j = s - 4
        whole = db[...].reshape(rows, D)
        cols = pl.multiple_of(j * D, 128)
        for q in range(3):
            t1 = dot_t(whole, wk[pl.ds(pl.multiple_of((5 + j) * D + 256 * q, 16), 256), :])
            t1 = t1 * g_ref[0, :, :, 256 * q:256 * q + 256].reshape(rows, 256).astype(F32)
            dv[l, pl.ds(8 + j, 1), 256 * q:256 * q + 256] += rsum(t1)
            du[:, :, pl.ds(pl.multiple_of(cols + 256 * q, 128), 256)] = t1.astype(BF).reshape(n, RP, 256)
        acc[...] += dot_t(du[:, :, pl.ds(cols, D)].reshape(rows, D), wk[pl.ds(pl.multiple_of(j * D, 16), D), :]).reshape(n, RP, D)

    @pl.when((s >= 8) & (s < 13))
    def _():
        i = s - 8
        dx, dg, dc = norm_back(h1_ref[0, 0], vec_ref[l, 5:6], acc[i])
        dv[l, 5:6] += dg
        dv[l, 6:7] += dc
        dh1 = d[i] + dx
        d[i] = dh1
        dv[l, 4:5] += rsum(dh1)
        du[i, :, 0:D] = dh1.astype(BF)
        du[i, :, 3 * D:4 * D] = dot_t(du[i, :, 0:D], wk[4 * D:5 * D, :]).astype(BF)

    def grad(lhs, rhs, store):
        rhs = rhs[:rows - 16]
        for m in range(2):
            r = dot_0(lhs(384 * m)[:rows - 16], rhs).astype(BF).reshape(4, CH, D)
            store(4 * m, r)

    def inner(slot, j):
        def store(m, r):
            gb[slot, m // 2, 0] = r[0]
            gb[slot, m // 2, 1] = r[1]
            gb[slot, m // 2 + 1, 0] = r[2]
            gb[slot, m // 2 + 1, 1] = r[3]
        grad(lambda m: ab[0, :, :, m:m + 384].reshape(rows, 384), du[:, :, pl.ds(pl.multiple_of(D * j, 128), D)].reshape(rows, D), store)

    def outer(step, lhs, rhs):
        def store(m, r):
            for q in range(4):
                b = 8 * step + m + q
                gb[4 + b % 5, b // 10, (b // 5) % 2] = r[q]
        grad(lhs, rhs.reshape(rows, D), store)

    @pl.when((s >= 4) & (s < 8))
    def _():
        at = pl.ds(pl.multiple_of((s - 4) * D, 128), D)
        du[0, RP - 16:RP, at] = fold_rows(du[0, RP - 16:RP, at], du[n - 1, RP - 16:RP, at])
        inner(s - 4, s - 4)

    @pl.when(s == 13)
    def _():
        du[0, RP - 16:RP, 0:D] = fold_rows(du[0, RP - 16:RP, 0:D], du[n - 1, RP - 16:RP, 0:D])
        outer(0, lambda m: ab[1, :, :, m:m + 384].reshape(rows, 384), du[:, :, 0:D])

    @pl.when(s < 4)
    def _():
        outer(s + 1, lambda m: e_ref[0, :, :, m:m + 384].reshape(rows, 384), db[...])

    @pl.when((s >= 14) & (s < 19))
    def _():
        i = s - 14
        for p in range(6):
            b = 128 * p
            dq, dk, dvv = attn_bwd(qkv_ref[0, 0, :, b:b + 128], qkv_ref[0, 0, :, D + b:D + b + 128], qkv_ref[0, 0, :, 2 * D + b:2 * D + b + 128],
                                   du[i, :, 3 * D + b:3 * D + b + 128])
            dv[l, 2:3, b:b + 128] += rsum(dq)
            dv[l, 3:4, b:b + 128] += rsum(dvv)
            du[i, :, b:b + 128] = dq.astype(BF)
            du[i, :, D + b:D + b + 128] = dk.astype(BF)
            du[i, :, 2 * D + b:2 * D + b + 128] = dvv.astype(BF)

    @pl.when(s == 19)
    def _():
        du[0, RP - 16:RP, 0:3 * D] = fold_rows(du[0, RP - 16:RP, 0:3 * D], du[n - 1, RP - 16:RP, 0:3 * D])

        @pl.loop(0, 3)
        def _(j):
            inner(j, j)

            @pl.when(lr == 1)
            def _():
                tick(21 + j)
        du[0, RP - 16:RP, 0:3 * D] = clear_rows(du[0, RP - 16:RP, 0:3 * D])
        acc[...] = dot_t(du[:, :, 0:D].reshape(rows, D), wk[0:D, :]).reshape(n, RP, D)
        acc[...] += dot_t(du[:, :, D:2 * D].reshape(rows, D), wk[D:2 * D, :]).reshape(n, RP, D)
        acc[...] += dot_t(du[:, :, 2 * D:3 * D].reshape(rows, D), wk[2 * D:3 * D, :]).reshape(n, RP, D)

    @pl.when(s >= 20)
    def _():
        i = s - 20
        dx, dg, dc = norm_back(hs_ref[0, 0], vec_ref[l, 0:1], acc[i])
        dv[l, 0:1] += dg
        dv[l, 1:2] += dc
        dh = d[i] + dx
        d[i] = dh
        di_ref[0] = dh[0:SEQ]

    @pl.when((lr == 1) & (s == 24))
    def _():
        for layer in range(LAYERS):
            for c in range(72):
                vs[c // 9, layer, c % 9:c % 9 + 1, :] = dv[layer, c // 6:c // 6 + 1, 128 * (c % 6):128 * (c % 6) + 128]

        def vcopy(k):
            to = (f + k) % 8
            return pltpu.make_async_remote_copy(src_ref=vs.at[to], dst_ref=vr.at[k - 1], send_sem=vssem.at[k - 1], recv_sem=vrsem.at[k - 1],
                                                device_id={"fsdp": to}, device_id_type=MESH)

        def zcopy(k):
            return pltpu.make_async_remote_copy(src_ref=vz.at[z], dst_ref=vz.at[z], send_sem=vssem.at[6 + k], recv_sem=vrsem.at[6 + k],
                                                device_id={"rep": (z + k) % 4}, device_id_type=MESH)
        for k in range(1, 8):
            vcopy(k).start()

        @pl.loop(29, 36)
        def _(t):
            @pl.when(t == 30)
            def _():
                for k in range(1, 8):
                    vcopy(k).wait()
                total = vs[f]
                for k in range(7):
                    total = total + vr[k]
                vz[z] = total
                for k in range(1, 4):
                    zcopy(k).start()
            tick(t)

        for k in range(1, 4):
            zcopy(k).wait()
        gv_ref[...] = (vz[0] + vz[1]) + (vz[2] + vz[3])


def bwd(cotangent, w, vec, hs, h1, g, e, qkv, a2, o, a1, shard_in, shard_out):
    n = cotangent.shape[0]
    S = jax.ShapeDtypeStruct
    anyw = pl.BlockSpec(memory_space=pl.ANY)
    row = lambda cols, at: pl.BlockSpec((1, 1, RP, cols), lambda lr, s: (LAYERS - 1 - lr, jnp.clip(s - at, 0, 4), 0, 0))
    cols = lambda at: pl.BlockSpec((1, n, RP, D), lambda lr, s: (LAYERS - 1 - lr, 0, 0, jnp.clip(s - at, 0, 3)))
    tok = lambda index: pl.BlockSpec((1, SEQ, D), index)
    VB = lambda *shape: pltpu.VMEM(shape, BF)
    half = CH // 2
    return pl.pallas_call(
        bwd_kernel, grid=(LAYERS, 25),
        in_specs=[pl.BlockSpec(cotangent.shape, lambda lr, s: (0, 0, 0), pipeline_mode=pl.Buffered(1)), anyw, pl.BlockSpec(vec.shape, lambda lr, s: (0, 0, 0)),
                  row(D, 20), row(D, 8), cols(4), cols(0), row(3 * D, 14), anyw, anyw, anyw],
        out_specs=[tok(lambda lr, s: (lr * jnp.clip(s - 20, 0, 4), 0, 0)), anyw, anyw, pl.BlockSpec((LAYERS, 16, 128), lambda lr, s: (0, 0, 0))],
        out_shape=[S(cotangent.shape, F32), S(shard_in, BF), S(shard_out, BF), S((LAYERS, 16, 128), F32)],
        scratch_shapes=[VB(9 * D, D), pltpu.VMEM((n, RP, D), F32), pltpu.VMEM((n, RP, D), F32), VB(n, RP, D), VB(n, RP, 4 * D), VB(2, n, RP, D),
                        VB(9, 4, 2, CH, D), pltpu.VMEM((LAYERS, 16, D), F32),
                        VB(2, 4, CH, D), VB(2, 2, 2, CH, D), VB(4, 2, half, D), VB(4, 2, half, D), VB(2, 2, half, D), VB(2, 2, half, D),
                        VB(4, half, D), VB(4, half, D), VB(2, CH, D), VB(4, half, D), VB(2, half, D), VB(4, half, D), VB(2, half, D), VB(4, half, D),
                        VB(2, CH, D),
                        pltpu.VMEM((8, LAYERS, 16, 128), F32), pltpu.VMEM((7, LAYERS, 16, 128), F32), pltpu.VMEM((4, LAYERS, 16, 128), F32),
                        pltpu.SemaphoreType.DMA((2,)), pltpu.SemaphoreType.DMA((2,)), pltpu.SemaphoreType.DMA((4, 8)), pltpu.SemaphoreType.DMA((4, 8)),
                        pltpu.SemaphoreType.DMA((2,)), pltpu.SemaphoreType.DMA((10,)), pltpu.SemaphoreType.DMA((10,))],
        compiler_params=pltpu.CompilerParams(collective_id=1, has_side_effects=True, vmem_limit_bytes=63 * 2**20),
    )(cotangent, w, vec, hs, h1, g, e, qkv, a2, o, a1)


STEP = 3
beta_one = 0.9
beta_two = 0.999
matrix_rate = 0.03
vector_rate = 0.2
matrix_decay = 0.05
adam_eps = 1e-8


def adam_update(master, gradient, moment_one, moment_two, rate, decay_rate):
    moment_one = beta_one * moment_one + (1.0 - beta_one) * gradient
    moment_two = beta_two * moment_two + (1.0 - beta_two) * gradient * gradient
    corr_one = 1.0 - beta_one**STEP
    corr_two = 1.0 - beta_two**STEP
    adam_move = moment_one / corr_one / (jnp.sqrt(moment_two / corr_two) + adam_eps)
    return (master - rate * (adam_move + decay_rate * master), moment_one, moment_two)


def adam_kernel(g_ref, w_ref, m_ref, v_ref, go_ref, wo_ref, mo_ref, vo_ref, enc_ref, dim_ref,
                g_out, w_out, m_out, v_out, go_out, wo_out, mo_out, vo_out, enc_out, dim_out, steps):
    i = pl.program_id(0)

    def update(g, w, m, v, outs):
        grad = g[...].astype(F32)
        new, moment, square = adam_update(w[...], grad, m[...], v[...], matrix_rate, matrix_decay)
        outs[0][...], outs[1][...], outs[2][...], outs[3][...] = grad, new, moment, square

    @pl.when(i < steps)
    def _():
        update(g_ref, w_ref, m_ref, v_ref, (g_out, w_out, m_out, v_out))

    @pl.when(i >= steps)
    def _():
        update(go_ref, wo_ref, mo_ref, vo_ref, (go_out, wo_out, mo_out, vo_out))

    @pl.when(i < enc_steps)
    def _():
        enc_out[...] = enc_ref[...]
        dim_out[...] = dim_ref[...]


enc_steps = 5


def adam_all(ins, outs, encoded, dimg):
    a, b = ins[0].shape, outs[0].shape
    steps = 2 * LAYERS
    first = pl.BlockSpec((1, a[1] // 2, a[2]), lambda i: (jnp.minimum(i, steps - 1) // 2, jnp.minimum(i, steps - 1) % 2, 0))
    second = pl.BlockSpec((1, b[1] // 2, b[2]), lambda i: (jnp.maximum(i - steps, 0) // 2, jnp.maximum(i - steps, 0) % 2, 0))
    tok = pl.BlockSpec((1,) + encoded.shape[1:], lambda i: (jnp.minimum(i, enc_steps - 1), 0, 0))
    S = jax.ShapeDtypeStruct
    return pl.pallas_call(
        functools.partial(adam_kernel, steps=steps), grid=(2 * steps,),
        in_specs=[first] * 4 + [second] * 4 + [tok] * 2, out_specs=[first] * 4 + [second] * 4 + [tok] * 2,
        out_shape=[S(a, F32)] * 4 + [S(b, F32)] * 4 + [S(encoded.shape, BF), S(dimg.shape, F32)],
        compiler_params=PAR,
    )(*ins, *outs, encoded, dimg)


def swap(x, axis, size, mask):
    return lax.ppermute(x, axis, [(i, i ^ mask) for i in range(size)])


def halve(x, order, size):
    bits = size.bit_length() - 1
    me = lax.axis_index("fsdp")
    x = x.reshape((2,) * bits + x.shape[1:])
    left = list(range(bits))[::-1]
    for bit in order:
        at = left.index(bit)
        mine = (me >> bit) & 1
        keep = lax.dynamic_index_in_dim(x, mine, at, keepdims=False)
        send = lax.dynamic_index_in_dim(x, 1 - mine, at, keepdims=False)
        got = swap(send, "fsdp", size, 1 << bit)
        x = (keep.astype(F32) + got.astype(F32)).astype(BF)
        left.remove(bit)
    return x


def reduce_all(x, nf, nr):
    bits = nf.bit_length() - 1
    rows, cols = x.shape
    x = x.reshape(nf, rows // nf, cols)
    half = cols // 2 // 128 * 128
    up = [0] + list(range(1, bits))
    down = [0] + list(range(1, bits))[::-1]
    x = jnp.concatenate([halve(x[..., :half], up, nf), halve(x[..., half:], down, nf)], axis=-1)
    mask = 1
    while mask < nr:
        got = swap(x, "rep", nr, 2 * mask - 1)
        y = x.astype(F32) + got.astype(F32)
        x = y.astype(BF)
        mask *= 2
    return y


def fused_step(images, cotangent, weight_in, weight_out, vector_params):
    vs = jnp.pad(vector_params.astype(BF).astype(F32).reshape(LAYERS, 9, 128), ((0, 0), (0, 7), (0, 0)))
    hs, qkv, a1, o, h1, a2, e, g, encoded, w, vec = fwd(images, weight_in, weight_out, vs)
    dimg, gi, go, gv = bwd(cotangent, w, vec, hs, h1, g, e, qkv, a2, o, a1, weight_in.shape, weight_out.shape)
    return encoded, dimg, gi, go, gv[:, :9].reshape(vector_params.shape)


def plain_step(nf, nr, images, cotangent, weight_in, weight_out, vector_params):
    pad = lambda a: jnp.pad(a, ((0, 0), (0, RP - SEQ), (0, 0)))
    vec_all = lax.all_gather(vector_params.astype(BF), "fsdp", axis=1, tiled=True).astype(F32)
    h = pad(images)
    ct = pad(cotangent)
    saved = []
    for l in range(LAYERS):
        win = lax.all_gather(weight_in[l].astype(BF), "fsdp", axis=0, tiled=True)
        wout = lax.all_gather(weight_out[l].astype(BF), "fsdp", axis=0, tiled=True)
        vec = jnp.pad(vec_all[l].reshape(12, D), ((0, 4), (0, 0)))
        wqkv, w1, wo, w2 = win[:, : 3 * D], win[:, 3 * D :], wout[:D], wout[D:]
        qkv, o, a1 = ka(h, wqkv, vec)
        h1, a2, e, g, h2 = kb(h, o, wo, w1, w2, vec)
        saved.append((h, wqkv, w1, wo, w2, vec, qkv, o, a1, h1, a2, e, g))
        h = h2
    encoded = h[:, :SEQ].astype(BF)
    d = ct
    gin, gout, gvec = [None] * LAYERS, [None] * LAYERS, [None] * LAYERS
    for l in reversed(range(LAYERS)):
        h, wqkv, w1, wo, w2, vec, qkv, o, a1, h1, a2, e, g = saved[l]
        db, du, dh1, dh1b, do, dv1 = kc(d, h1, g, wo, w1, w2, vec)
        g1 = reduce_all(dw(a2, du), nf, nr)
        go = reduce_all(jnp.concatenate([dw(o, dh1b), dw(e, db)], axis=0), nf, nr)
        dz, dv2 = kd(qkv, do)
        gq = reduce_all(dw(a1, dz), nf, nr)
        d, dv3 = kf(dz, h, dh1, wqkv, vec, RP if l else SEQ)
        gin[l] = jnp.concatenate([gq, g1], axis=1)
        gout[l] = go
        gvec[l] = (dv1 + dv2 + dv3)[:12].reshape(-1)
    gv = lax.psum(jnp.stack(gvec), ("fsdp", "rep"))
    wide = gv.shape[1] // nf
    gv = lax.dynamic_slice_in_dim(gv, lax.axis_index("fsdp") * wide, wide, 1)
    return encoded, d, jnp.stack(gin), jnp.stack(gout), gv


def make_shards(nf, nr):
    def shards(images, cotangent, weight_in, weight_out, vector_params, first_in, first_out, first_vec, second_in, second_out, second_vec):
        if nf == 8 and nr == 4:
            encoded, d, gi, go, gv = fused_step(images, cotangent, weight_in, weight_out, vector_params)
            gi, new_in, moment_in, square_in, go, new_out, moment_out, square_out, encoded, d = adam_all(
                (gi, weight_in, first_in, second_in), (go, weight_out, first_out, second_out), encoded, d)
        else:
            encoded, d, gi, go, gv = plain_step(nf, nr, images, cotangent, weight_in, weight_out, vector_params)
            new_in, moment_in, square_in = adam_update(weight_in, gi, first_in, second_in, matrix_rate, matrix_decay)
            new_out, moment_out, square_out = adam_update(weight_out, go, first_out, second_out, matrix_rate, matrix_decay)
        new_vec, moment_vec, square_vec = adam_update(vector_params, gv, first_vec, second_vec, vector_rate, 0.0)
        return (encoded, d, gi, go, gv, new_in, new_out, new_vec, moment_in, moment_out, moment_vec, square_in, square_out, square_vec)

    return shards


def solution(mesh):
    tokens = P(("fsdp", "rep"), None, None)
    matrix = P(None, "fsdp", None)
    vector = P(None, "fsdp")
    in_specs = (tokens, tokens) + (matrix, matrix, vector) * 3
    out_specs = (tokens, tokens) + (matrix, matrix, vector) * 4
    return jax.shard_map(make_shards(mesh.shape["fsdp"], mesh.shape["rep"]), mesh=mesh, in_specs=in_specs, out_specs=out_specs, check_vma=False)
```

```python
import functools
import jax, jax.numpy as jnp
from jax import lax
from jax.experimental import pallas as pl
from jax.experimental.pallas import tpu as pltpu
from jax.sharding import PartitionSpec as P

D=768; HD=64; SEQ=197; RP=208; EPS=1e-6
BF=jnp.bfloat16; F32=jnp.float32
def dot(a,b): return jnp.dot(a,b,preferred_element_type=F32)
def dot_t(a,b): return lax.dot_general(a,b,(((1,),(1,)),((),())),preferred_element_type=F32)
def dot_0(a,b): return lax.dot_general(a,b,(((0,),(0,)),((),())),preferred_element_type=F32)

def norm_stats(x):
    mean=jnp.mean(x,axis=-1,keepdims=True); xc=x-mean
    var=jnp.mean(xc*xc,axis=-1,keepdims=True)
    return xc, lax.rsqrt(var+EPS)

def head_masks(scale):
    lane = lax.broadcasted_iota(jnp.int32, (1, 128), 1)
    return jnp.where(lane < 64, scale, 0.0).astype(BF), jnp.where(lane < 64, 0.0, scale).astype(BF)


def attn_fwd(q, k, v):
    ones = head_masks(1.0)
    row = lax.broadcasted_iota(jnp.int32, (16, 1), 0)
    ps = []
    for m in head_masks(0.125):
        s = dot_t(k, q * m)
        s = jnp.concatenate([s[:RP - 16], jnp.where(row < SEQ - RP + 16, s[RP - 16:], -1e30)], axis=0)
        e = jnp.exp(s - jnp.max(s, axis=0, keepdims=True))
        ps.append((e * (1.0 / jnp.sum(e, axis=0, keepdims=True))).astype(BF))
    return (dot_0(ps[0], v * ones[0]) + dot_0(ps[1], v * ones[1])).astype(BF)


def attn_bwd_products(q, k, v, do):
    scaled, ones = head_masks(0.125), head_masks(1.0)
    row = lax.broadcasted_iota(jnp.int32, (RP, 1), 0)
    qs, ks, dos = [q * m for m in scaled], [k * m for m in scaled], [do * m for m in ones]
    s = [jnp.where(row < SEQ, dot_t(k, x), -1e30) for x in qs]
    return qs, ks, dos, s, [dot_t(v, x) for x in dos]


def attn_bwd_rest(qs, ks, dos, s, dp):
    e = [jnp.exp(x - jnp.max(x, axis=0, keepdims=True)) for x in s]
    p = [x * (1.0 / jnp.sum(x, axis=0, keepdims=True)) for x in e]
    pb = [x.astype(BF) for x in p]
    ds = [(a * (b - jnp.sum(a * b, axis=0, keepdims=True))).astype(BF) for a, b in zip(p, dp)]
    dv = dot(pb[0], dos[0]) + dot(pb[1], dos[1])
    dk = dot(ds[0], qs[0]) + dot(ds[1], qs[1])
    dq = dot_0(ds[0], ks[0]) + dot_0(ds[1], ks[1])
    return dq, dk, dv


def attn_bwd(q, k, v, do):
    return attn_bwd_rest(*attn_bwd_products(q, k, v, do))


TAIL = SEQ - RP + 16


def fold_rows(first, last):
    r = lax.broadcasted_iota(jnp.int32, (16, 16), 0)
    c = lax.broadcasted_iota(jnp.int32, (16, 16), 1)
    move = jnp.where((r == c + TAIL) & (c < TAIL), 1.0, 0.0).astype(BF)
    row = lax.broadcasted_iota(jnp.int32, (16, 1), 0)
    return jnp.where((row >= TAIL) & (row < 2 * TAIL), dot(move, last), first.astype(F32)).astype(BF)


def clear_rows(first):
    row = lax.broadcasted_iota(jnp.int32, (16, 1), 0)
    return jnp.where(row < TAIL, first.astype(F32), 0.0).astype(BF)


def ka_kernel(h_ref,w_ref,vec_ref,qkv_ref,o_ref,a_ref):
    h=h_ref[0].astype(F32)
    xc,rs=norm_stats(h)
    a_ref[0]=(xc*rs*vec_ref[0:1]+vec_ref[1:2]).astype(BF)
    a=a_ref[0]
    for c in range(3):
        cs=slice(256*c,256*c+256)
        qkv_ref[0,:,256*c:256*c+256]=(dot(a,w_ref[:,256*c:256*c+256])+vec_ref[2:3,cs]).astype(BF)
        qkv_ref[0,:,D+256*c:D+256*c+256]=dot(a,w_ref[:,D+256*c:D+256*c+256]).astype(BF)
        qkv_ref[0,:,2*D+256*c:2*D+256*c+256]=(dot(a,w_ref[:,2*D+256*c:2*D+256*c+256])+vec_ref[3:4,cs]).astype(BF)
        for p in range(2):
            b=256*c+128*p
            o_ref[0,:,b:b+128]=attn_fwd(qkv_ref[0,:,b:b+128],qkv_ref[0,:,D+b:D+b+128],qkv_ref[0,:,2*D+b:2*D+b+128])

def img(n,dt=None): return pl.BlockSpec((1,RP,n),lambda i:(i,0,0))
def full(shape): return pl.BlockSpec(shape,lambda i:(0,)*len(shape))
PAR=pltpu.CompilerParams(vmem_limit_bytes=60*2**20)

def ka(h,w,vec):
    n=h.shape[0]
    return pl.pallas_call(ka_kernel,grid=(n,),in_specs=[img(D),full(w.shape),full(vec.shape)],
        out_specs=[img(3*D),img(D),img(D)],
        out_shape=[jax.ShapeDtypeStruct((n,RP,3*D),BF),jax.ShapeDtypeStruct((n,RP,D),BF),jax.ShapeDtypeStruct((n,RP,D),BF)],
        compiler_params=PAR)(h,w,vec)

def gelu_parts(u):
    c=0.5*(1.0+lax.erf(u*0.7071067811865476))
    g=c+u*(jnp.exp(-0.5*u*u)*0.3989422804014327)
    return u*c,g

def kb_kernel(FC,h_ref,o_ref,wo_ref,w1_ref,w2_ref,vec_ref,h1_ref,a_ref,e_ref,g_ref,h2_ref):
    h1=h_ref[0].astype(F32)+dot(o_ref[0],wo_ref[...])+vec_ref[4:5]
    h1_ref[0]=h1
    xc,rs=norm_stats(h1)
    a_ref[0]=(xc*rs*vec_ref[5:6]+vec_ref[6:7]).astype(BF)
    a=a_ref[0]
    h2_ref[0]=h1+vec_ref[7:8]
    for j in range(3072//FC):
        lo=FC*j
        u=dot(a,w1_ref[:,lo:lo+FC])+vec_ref[8+lo//D:9+lo//D,lo%D:lo%D+FC]
        e,g=gelu_parts(u)
        e_ref[0,:,lo:lo+FC]=e.astype(BF); g_ref[0,:,lo:lo+FC]=g.astype(BF)
        h2_ref[0]+=dot(e_ref[0,:,lo:lo+FC],w2_ref[lo:lo+FC,:])

def kb(h,o,wo,w1,w2,vec,FC=256):
    n=h.shape[0]
    S=jax.ShapeDtypeStruct
    return pl.pallas_call(functools.partial(kb_kernel,FC),grid=(n,),in_specs=[img(D),img(D),full(wo.shape),full(w1.shape),full(w2.shape),full(vec.shape)],
        out_specs=[img(D),img(D),img(3072),img(3072),img(D)],
        out_shape=[S((n,RP,D),F32),S((n,RP,D),BF),S((n,RP,3072),BF),S((n,RP,3072),BF),S((n,RP,D),F32)],
        compiler_params=PAR)(h,o,wo,w1,w2,vec)

def rsum(x): return jnp.sum(x,axis=0,keepdims=True)
def norm_back(x,gain,dy):
    xc,rs=norm_stats(x); xh=xc*rs
    dyg=dy*gain
    dx=rs*(dyg-jnp.mean(dyg,axis=-1,keepdims=True)-xh*jnp.mean(dyg*xh,axis=-1,keepdims=True))
    return dx, rsum(dy*xh), rsum(dy)

def kc_kernel(FC,d_ref,h1_ref,g_ref,wo_ref,w1_ref,w2_ref,vec_ref,db_ref,du_ref,dh1_ref,dh1b_ref,do_ref,dv_ref,acc_ref):
    @pl.when(pl.program_id(0)==0)
    def _(): dv_ref[...]=jnp.zeros_like(dv_ref)
    d=d_ref[0].astype(F32)
    db_ref[0]=d.astype(BF)
    db=db_ref[0]
    dv_ref[7:8]+=rsum(d)
    for j in range(3072//FC):
        lo=FC*j
        du=dot_t(db,w2_ref[lo:lo+FC,:])*g_ref[0,:,lo:lo+FC].astype(F32)
        dv_ref[8+lo//D:9+lo//D,lo%D:lo%D+FC]+=rsum(du)
        du_ref[0,:,lo:lo+FC]=du.astype(BF)
        t=dot_t(du_ref[0,:,lo:lo+FC],w1_ref[:,lo:lo+FC])
        if j==0: acc_ref[...]=t
        else: acc_ref[...]+=t
    dx,dg,dc=norm_back(h1_ref[0],vec_ref[5:6],acc_ref[...])
    dv_ref[5:6]+=dg; dv_ref[6:7]+=dc
    dh1=d_ref[0].astype(F32)+dx
    dh1_ref[0]=dh1
    dv_ref[4:5]+=rsum(dh1)
    dh1b_ref[0]=dh1.astype(BF)
    do_ref[0]=dot_t(dh1b_ref[0],wo_ref[...]).astype(BF)

def kc(d,h1,g,wo,w1,w2,vec,FC=256):
    n=d.shape[0]; S=jax.ShapeDtypeStruct
    return pl.pallas_call(functools.partial(kc_kernel,FC),grid=(n,),in_specs=[img(D),img(D),img(3072),full(wo.shape),full(w1.shape),full(w2.shape),full(vec.shape)],
        out_specs=[img(D),img(3072),img(D),img(D),img(D),full((16,D))],
        out_shape=[S((n,RP,D),BF),S((n,RP,3072),BF),S((n,RP,D),F32),S((n,RP,D),BF),S((n,RP,D),BF),S((16,D),F32)],
        scratch_shapes=[pltpu.VMEM((RP,D),F32)],
        compiler_params=PAR)(d,h1,g,wo,w1,w2,vec)

def kd_kernel(qkv_ref,do_ref,dz_ref,dv_ref):
    @pl.when(pl.program_id(0)==0)
    def _(): dv_ref[...]=jnp.zeros_like(dv_ref)
    for p in range(6):
        b=128*p
        dq,dk,dv=attn_bwd(qkv_ref[0,:,b:b+128],qkv_ref[0,:,D+b:D+b+128],qkv_ref[0,:,2*D+b:2*D+b+128],do_ref[0,:,b:b+128])
        dv_ref[2:3,b:b+128]+=rsum(dq); dv_ref[3:4,b:b+128]+=rsum(dv)
        dz_ref[0,:,b:b+128]=dq.astype(BF); dz_ref[0,:,D+b:D+b+128]=dk.astype(BF); dz_ref[0,:,2*D+b:2*D+b+128]=dv.astype(BF)

def kd(qkv,do):
    n=do.shape[0]; S=jax.ShapeDtypeStruct
    return pl.pallas_call(kd_kernel,grid=(n,),in_specs=[img(3*D),img(D)],out_specs=[img(3*D),full((16,D))],
        out_shape=[S((n,RP,3*D),BF),S((16,D),F32)],compiler_params=PAR)(qkv,do)

def kf_kernel(dz_ref,h_ref,dh1_ref,w_ref,vec_ref,dh_ref,dv_ref):
    @pl.when(pl.program_id(0)==0)
    def _(): dv_ref[...]=jnp.zeros_like(dv_ref)
    da=dot_t(dz_ref[0],w_ref[...])
    dx,dg,dc=norm_back(h_ref[0].astype(F32),vec_ref[0:1],da)
    dv_ref[0:1]+=dg; dv_ref[1:2]+=dc
    rows=dh_ref.shape[1]
    dh_ref[0]=(dh1_ref[0]+dx)[:rows]

def kf(dz,h,dh1,w,vec,rows=RP):
    n=dz.shape[0]; S=jax.ShapeDtypeStruct
    return pl.pallas_call(kf_kernel,grid=(n,),in_specs=[img(3*D),img(D),img(D),full(w.shape),full(vec.shape)],
        out_specs=[pl.BlockSpec((1,rows,D),lambda i:(i,0,0)),full((16,D))],
        out_shape=[S((n,rows,D),F32),S((16,D),F32)],compiler_params=PAR)(dz,h,dh1,w,vec)

def dw_kernel(l_ref,r_ref,o_ref):
    o_ref[...]=dot_0(l_ref[...],r_ref[...]).astype(BF)
def dw(l,r,MB=256):
    M=l.shape[-1]; N=r.shape[-1]; K=l.shape[0]*RP
    l=l.reshape(K,M); r=r.reshape(K,N)
    return pl.pallas_call(dw_kernel,grid=(M//MB,),in_specs=[pl.BlockSpec((K,MB),lambda i:(0,i)),pl.BlockSpec((K,N),lambda i:(0,0))],
       out_specs=pl.BlockSpec((MB,N),lambda i:(i,0)),out_shape=jax.ShapeDtypeStruct((M,N),BF),compiler_params=PAR)(l,r)


LAYERS = 2
MESH = pl.DeviceIdType.MESH
CH = 96
NC = 12


def plane():
    f = lax.axis_index("fsdp")
    core, x, y = f % 2, (f // 2) % 2, f // 4
    return f, core, x, y


def chunk_rows(c, f):
    layer, j = c // NC, c % NC
    early = 1 - (j + 9) // 12
    late = j // 8
    mid = 1 - early - late
    base = layer * NC * D
    return pl.multiple_of(base + early * (j * D + CH * f) + late * ((j - 5) * D + CH * f)
                          + mid * (7 * D + 5 * CH * f + CH * (j - 3)), 16)


def fwd_kernel(img_ref, win_ref, wout_ref, vs_ref, hs_ref, qkv_ref, a1_ref, o_ref, h1_ref, a2_ref, e_ref, g_ref, enc_ref, wo_ref, vo_ref,
               w, hb, ob, ab, vg, vec, st, lsem, ssem, rsem, vssem, vrsem, osem, vosem):
    l, s = pl.program_id(0), pl.program_id(1)
    f, core, x, y = plane()
    fc, fx, fy = f + 1 - 2 * core, f + 2 - 4 * x, f + 4 - 8 * y
    fd = fx + fy - f
    z = lax.axis_index("rep")
    side = z % 2
    zp = z + 1 - 2 * side
    part = pl.ds(pl.multiple_of(256 * side, 128), 512)
    give = pl.ds(pl.multiple_of(512 * side, 128), 256)

    def wrow(c, who, lo=0, n=CH):
        return pl.ds(pl.multiple_of(chunk_rows(c, who) + lo, 16), n)

    def send(c, kind, where, **to):
        return pltpu.make_async_remote_copy(src_ref=w.at[where], dst_ref=w.at[where], send_sem=ssem.at[c % 12, kind], recv_sem=rsem.at[c % 12, kind],
                                            device_id=to, device_id_type=MESH)

    def fetch(c, act):
        layer, j = c // NC, c % NC
        mid = (j >= 3) & (j < 8)

        @pl.when(mid)
        def _():
            act(pltpu.make_async_copy(wout_ref.at[layer, pl.ds(pl.multiple_of((j - 3) * CH, 8), CH)], st.at[c % 4], lsem.at[c % 4]))

        @pl.when(jnp.logical_not(mid))
        def _():
            act(pltpu.make_async_copy(win_ref.at[layer, :, pl.ds(pl.multiple_of((j - 5 * (j // 8)) * D, 128), D)], st.at[c % 4], lsem.at[c % 4]))

    def kinds(c):
        half = CH // 2
        return [lambda: send(c, 0, (wrow(c, f), part), fsdp=fx), lambda: send(c, 1, (wrow(c, f), part), fsdp=fy),
                lambda: send(c, 2, (wrow(c, f),), fsdp=fc),
                lambda: send(c, 3, (wrow(c, fx, 0, half), part), fsdp=fy), lambda: send(c, 4, (wrow(c, fy, half, half), part), fsdp=fx),
                lambda: send(c, 5, (wrow(c, fx), give), rep=zp), lambda: send(c, 6, (wrow(c, fy), give), rep=zp),
                lambda: send(c, 7, (wrow(c, fd), give), rep=zp),
                lambda: send(c, 8, (wrow(c, fx),), fsdp=fc), lambda: send(c, 9, (wrow(c, fy),), fsdp=fc), lambda: send(c, 10, (wrow(c, fd),), fsdp=fc)]

    def start(c, which):
        k = kinds(c)
        for i in which:
            k[i]().start()

    def wait(c, which):
        k = kinds(c)
        for i in which:
            k[i]().wait()

    def tick(t):
        @pl.when((t >= 7) & (t < 31))
        def _():
            wait(t - 7, (2, 8, 9, 10))

        @pl.when((t >= 6) & (t < 30))
        def _():
            wait(t - 6, (7,))
            start(t - 6, (10,))

        @pl.when((t >= 4) & (t < 28))
        def _():
            wait(t - 4, (3, 4, 5, 6))
            start(t - 4, (7, 8, 9))

        @pl.when((t >= 2) & (t < 26))
        def _():
            wait(t - 2, (0, 1))
            start(t - 2, (3, 4, 5, 6))

        def launch(c):
            fetch(c, lambda a: a.wait())
            w[pl.ds(chunk_rows(c, f), CH)] = st[c % 4].astype(BF)
            start(c, (0, 1, 2))

        @pl.when(t < 24)
        def _():
            launch(t)

        @pl.when(t < 21)
        def _():
            fetch(t + 3, lambda a: a.start())

    def out_copy(b, n):
        return pltpu.make_async_copy(w.at[pl.ds(b, n)], wo_ref.at[pl.ds(b, n)], osem)

    @pl.when((l == 0) & (s == 0))
    def _():
        for c in range(3):
            fetch(jnp.int32(c), lambda a: a.start())
        bar = pltpu.get_barrier_semaphore()
        for k in range(1, 8):
            pl.semaphore_signal(bar, inc=1, device_id={"fsdp": (f + k) % 8}, device_id_type=MESH)
        pl.semaphore_signal(bar, inc=1, device_id={"rep": zp}, device_id_type=MESH)
        pl.semaphore_wait(bar, 8)

        def vcopy(k):
            return pltpu.make_async_remote_copy(src_ref=vs_ref, dst_ref=vg.at[f], send_sem=vssem.at[k - 1], recv_sem=vrsem.at[k - 1],
                                                device_id={"fsdp": (f + k) % 8}, device_id_type=MESH)
        for k in range(1, 8):
            vcopy(k).start()
        vg[f] = vs_ref[...]

        @pl.loop(0, 10)
        def _(t):
            tick(t)

            @pl.when(t == 0)
            def _():
                hb[...] = jnp.zeros_like(hb)

            @pl.when(t == 3)
            def _():
                for k in range(1, 8):
                    vcopy(k).wait()
                for layer in range(LAYERS):
                    for c in range(72):
                        vec[layer, c // 6:c // 6 + 1, 128 * (c % 6):128 * (c % 6) + 128] = vg[c // 9, layer, c % 9:c % 9 + 1, :]
                pltpu.make_async_copy(vec, vo_ref, vosem).start()

    early = s <= 5
    late = (s == 8) | ((s >= 10) & (s + l <= 13))
    t = jnp.where(early, (1 - l) * (s + 9) + l * (s + 21), jnp.where(s == 8, 15 + 12 * l, (1 - l) * (s + 6 + s // 12) + l * (s + 18)))

    @pl.when((early & (l + s > 0)) | late)
    def _():
        tick(t)

    @pl.when(s < 5)
    def _():
        @pl.when(l == 0)
        def _():
            hb[s, 0:SEQ, :] = img_ref[s].astype(F32)
        h = hb[s]
        hs_ref[0, 0] = h
        xc, rs = norm_stats(h)
        a1_ref[0, 0] = (xc * rs * vec[l, 0:1] + vec[l, 1:2]).astype(BF)
        a = a1_ref[0, 0]
        wb = l * NC * D

        def wq(part, c):
            return w[pl.ds(pl.multiple_of(wb + part * D, 16), D), 256 * c:256 * c + 256]
        for c in range(3):
            cs = slice(256 * c, 256 * c + 256)
            qkv_ref[0, 0, :, cs] = (dot(a, wq(0, c)) + vec[l, 2:3, cs]).astype(BF)
            qkv_ref[0, 0, :, D + 256 * c:D + 256 * c + 256] = dot(a, wq(1, c)).astype(BF)
            qkv_ref[0, 0, :, 2 * D + 256 * c:2 * D + 256 * c + 256] = (dot(a, wq(2, c)) + vec[l, 3:4, cs]).astype(BF)
            for p in range(2):
                b = 256 * c + 128 * p
                o = attn_fwd(qkv_ref[0, 0, :, b:b + 128], qkv_ref[0, 0, :, D + b:D + b + 128], qkv_ref[0, 0, :, 2 * D + b:2 * D + b + 128])
                o_ref[0, 0, :, b:b + 128] = o
                ob[s, :, b:b + 128] = o

    @pl.when((s >= 5) & (s < 10))
    def _():
        i = s - 5
        wo = w[pl.ds(pl.multiple_of((l * NC + 7) * D, 16), D), :]
        h1 = hb[i] + dot(ob[i], wo) + vec[l, 4:5]
        h1_ref[0, 0] = h1
        hb[i] = h1 + vec[l, 7:8]
        xc, rs = norm_stats(h1)
        a = (xc * rs * vec[l, 5:6] + vec[l, 6:7]).astype(BF)
        a2_ref[0, 0] = a
        ab[i] = a

    @pl.when(s >= 10)
    def _():
        j = s - 10
        up = pl.multiple_of((l * NC + 3 + j) * D, 16)
        down = pl.multiple_of((l * NC + 8 + j) * D, 16)

        bias = vec[l, pl.ds(8 + j, 1), :]
        n = hb.shape[0]
        u = dot(ab[0], w[pl.ds(up, D), :])
        for i in range(n):
            later = dot(ab[i + 1], w[pl.ds(up, D), :]) if i < n - 1 else None
            e, g = gelu_parts(u + bias)
            e = e.astype(BF)
            e_ref[0, i] = e
            g_ref[0, i] = g.astype(BF)
            hb[i] += dot(e, w[pl.ds(down, D), :])
            u = later
            if i == 2:
                @pl.when((s == 11) & (l == 0))
                def _():
                    tick(18)

        e_ref[0, 0, RP - 16:RP] = fold_rows(e_ref[0, 0, RP - 16:RP], e_ref[0, n - 1, RP - 16:RP])

        @pl.when((l == 1) & (s == 13))
        def _():
            for i in range(n):
                enc_ref[i] = hb[i, 0:SEQ, :].astype(BF)

    for layer in range(LAYERS):
        base = layer * NC * D

        @pl.when((l == layer) & (s == 4))
        def _():
            out_copy(base, 3 * D).start()

        @pl.when((l == layer) & (s == 9))
        def _():
            out_copy(base + 7 * D, 5 * D).start()

        for j in range(4):
            @pl.when((l == layer) & (s == 10 + j))
            def _():
                out_copy(base + (3 + j) * D, D).start()

    @pl.when((l == 1) & (s == 13))
    def _():
        pltpu.make_async_copy(w, wo_ref, osem).wait()
        pltpu.make_async_copy(vec, vo_ref, vosem).wait()


def fwd(images, weight_in, weight_out, vshard):
    n = images.shape[0]
    S = jax.ShapeDtypeStruct
    one = lambda cols: pl.BlockSpec((1, 1, RP, cols), lambda l, s: (l, jnp.minimum(s, 4), 0, 0))
    two = lambda cols: pl.BlockSpec((1, 1, RP, cols), lambda l, s: (l, jnp.clip(s - 5, 0, 4), 0, 0))
    wide = pl.BlockSpec((1, n, RP, D), lambda l, s: (l, 0, 0, jnp.clip(s - 10, 0, 3)))
    anyw = pl.BlockSpec(memory_space=pl.ANY)
    rows = LAYERS * NC * D
    return pl.pallas_call(
        fwd_kernel, grid=(LAYERS, 14),
        in_specs=[pl.BlockSpec(images.shape, lambda l, s: (0, 0, 0)), anyw, anyw, pl.BlockSpec(vshard.shape, lambda l, s: (0, 0, 0))],
        out_specs=[one(D), one(3 * D), one(D), one(D), two(D), two(D), wide, wide, pl.BlockSpec(images.shape, lambda l, s: (0, 0, 0)), anyw, anyw],
        out_shape=[S((LAYERS, n, RP, D), F32), S((LAYERS, n, RP, 3 * D), BF), S((LAYERS, n, RP, D), BF), S((LAYERS, n, RP, D), BF),
                   S((LAYERS, n, RP, D), F32), S((LAYERS, n, RP, D), BF), S((LAYERS, n, RP, 4 * D), BF), S((LAYERS, n, RP, 4 * D), BF),
                   S(images.shape, BF), S((rows, D), BF), S((LAYERS, 16, D), F32)],
        scratch_shapes=[pltpu.VMEM((rows, D), BF), pltpu.VMEM((n, RP, D), F32), pltpu.VMEM((n, RP, D), BF), pltpu.VMEM((n, RP, D), BF),
                        pltpu.VMEM((8, LAYERS, 16, 128), F32), pltpu.VMEM((LAYERS, 16, D), F32), pltpu.VMEM((4, CH, D), F32),
                        pltpu.SemaphoreType.DMA((4,)), pltpu.SemaphoreType.DMA((12, 11)), pltpu.SemaphoreType.DMA((12, 11)),
                        pltpu.SemaphoreType.DMA((7,)), pltpu.SemaphoreType.DMA((7,)), pltpu.SemaphoreType.DMA, pltpu.SemaphoreType.DMA],
        compiler_params=pltpu.CompilerParams(collective_id=0, has_side_effects=True, vmem_limit_bytes=62 * 2**20),
    )(images, weight_in, weight_out, vshard)


def bwd_kernel(cot_ref, w_ref, vec_ref, hs_ref, h1_ref, g_ref, e_ref, qkv_ref, a2_ref, o_ref, a1_ref,
               di_ref, gin_ref, gout_ref, gv_ref,
               wk, d, acc, db, du, ab, gb, dv, rc, s2, ra, rb, s3a, s3b, r3a, r3b, s4, rz, s5, ry, s6, rw, fin,
               vs, vr, vz, wsem, asem, ssem, rsem, osem, vssem, vrsem):
    lr, s = pl.program_id(0), pl.program_id(1)
    l = LAYERS - 1 - lr
    f, core, x, y = plane()
    z = lax.axis_index("rep")
    fc, fx, fy = f + 1 - 2 * core, f + 2 - 4 * x, f + 4 - 8 * y
    z1, z3 = z + 1 - 2 * (z % 2), 3 - z
    half = CH // 2
    mine = pl.multiple_of(((z + 1) // 2 % 2) * half, 16)
    theirs = pl.multiple_of(half - (z + 1) // 2 % 2 * half, 16)
    n = d.shape[0]
    rows = n * RP

    def load(layer, block, n, at):
        return pltpu.make_async_copy(w_ref.at[pl.ds(pl.multiple_of((layer * NC + block) * D, 16), n * D)], wk.at[pl.ds(at * D, n * D)], wsem.at[0 if at else 1])

    def fetch(src, slot, layer):
        return pltpu.make_async_copy(src.at[layer], ab.at[slot], asem.at[slot])

    def remote(kind, p, src, dst, **to):
        return pltpu.make_async_remote_copy(src_ref=src, dst_ref=dst, send_sem=ssem.at[p, kind], recv_sem=rsem.at[p, kind],
                                            device_id=to, device_id_type=MESH)

    def live(v):
        return (v >= 0) & (v < 24)

    def kind(n, v):
        p, q = v % 2, v % 4
        if n == 0:
            lc = v % NC
            return remote(0, q, gb.at[lc - 9 * (lc // 9), :, 1 - core], rc.at[p], fsdp=fc)
        if n == 1:
            return remote(1, q, s2.at[p, :, 1 - x, pl.ds(0, half)], ra.at[q], fsdp=fx)
        if n == 2:
            return remote(2, q, s2.at[p, 1 - y, :, pl.ds(half, half)], rb.at[q], fsdp=fy)
        if n == 3:
            return remote(3, q, s3a.at[p, 1 - y], r3a.at[q], fsdp=fy)
        if n == 4:
            return remote(4, q, s3b.at[p, 1 - x], r3b.at[q], fsdp=fx)
        if n == 5:
            return remote(5, q, s4.at[p, pl.ds(theirs, half)], rz.at[q], rep=z1)
        if n == 6:
            return remote(6, q, s5.at[p], ry.at[q], rep=z3)
        return remote(7, q, s6.at[p], rw.at[q], rep=z1)

    def put(v, act):
        lc, layer = v % NC, LAYERS - 1 - v // NC
        p = v % 2
        out = (lc >= 4) & (lc < 9)

        @pl.when(out)
        def _():
            act(pltpu.make_async_copy(fin.at[p], gout_ref.at[layer, pl.ds(pl.multiple_of((lc - 4) * CH, 16), CH)], osem.at[p]))

        @pl.when(jnp.logical_not(out))
        def _():
            j = lc + 3 - 9 * (lc // 9)
            j = j - 3 * (lc // 9)
            act(pltpu.make_async_copy(fin.at[p], gin_ref.at[layer, :, pl.ds(pl.multiple_of(j * D, 128), D)], osem.at[p]))

    def add(a, b):
        return a + b

    def tick(t):
        @pl.when(live(t - 12))
        def _():
            put(t - 12, lambda a: a.wait())

        @pl.when(live(t - 11))
        def _():
            v = t - 11
            p = v % 2
            kind(7, v).wait()
            fin[p, pl.ds(mine, half)] = s6[p]
            fin[p, pl.ds(theirs, half)] = rw[v % 4]
            put(v, lambda a: a.start())

        @pl.when(live(t - 9))
        def _():
            v = t - 9
            p = v % 2
            kind(6, v).wait()
            s6[p] = add(s5[p], ry[v % 4]).astype(BF)
            kind(7, v).start()

        @pl.when(live(t - 7))
        def _():
            v = t - 7
            p = v % 2
            kind(5, v).wait()
            s5[p] = add(s4[p, pl.ds(mine, half)], rz[v % 4]).astype(BF)
            kind(6, v).start()

        @pl.when(live(t - 5))
        def _():
            v = t - 5
            p, q = v % 2, v % 4
            kind(3, v).wait()
            kind(4, v).wait()
            s4[p, 0:half] = add(s3a[p, y], r3a[q]).astype(BF)
            s4[p, half:CH] = add(s3b[p, x], r3b[q]).astype(BF)
            kind(5, v).start()

        @pl.when(live(t - 3))
        def _():
            v = t - 3
            p, q = v % 2, v % 4
            kind(1, v).wait()
            kind(2, v).wait()
            for i in range(2):
                s3a[p, i] = add(s2[p, i, x, 0:half], ra[q, i]).astype(BF)
                s3b[p, i] = add(s2[p, y, i, half:CH], rb[q, i]).astype(BF)
            kind(3, v).start()
            kind(4, v).start()

        @pl.when(live(t - 1))
        def _():
            v = t - 1
            p = v % 2
            kind(0, v).wait()
            lc = v % NC
            for i in range(4):
                s2[p, i // 2, i % 2] = add(gb[lc - 9 * (lc // 9), i, core], rc[p, i]).astype(BF)
            kind(1, v).start()
            kind(2, v).start()

        @pl.when(live(t))
        def _():
            kind(0, t).start()

    @pl.when((lr == 0) & (s == 0))
    def _():
        load(l, 3, 9, 0).start()
        bar = pltpu.get_barrier_semaphore()
        for k in range(1, 8):
            pl.semaphore_signal(bar, inc=1, device_id={"fsdp": (f + k) % 8}, device_id_type=MESH)
        for k in range(1, 4):
            pl.semaphore_signal(bar, inc=1, device_id={"rep": (z + k) % 4}, device_id_type=MESH)
        pl.semaphore_wait(bar, 10)
        dv[...] = jnp.zeros_like(dv)
        fetch(a2_ref, 0, l).start()
        for i in range(n):
            d[i] = jnp.zeros((RP, D), F32)
            d[i, 0:SEQ, :] = cot_ref[i].astype(F32)

    @pl.when(s == 0)
    def _():
        fetch(o_ref, 1, l).start()

    @pl.when(s == 4)
    def _():
        fetch(a2_ref, 0, l).wait()
        ab[0, 0, RP - 16:RP] = fold_rows(ab[0, 0, RP - 16:RP], ab[0, n - 1, RP - 16:RP])

        @pl.when(lr == 0)
        def _():
            load(l, 3, 9, 0).wait()

        @pl.when(lr == 1)
        def _():
            load(l, 3, 3, 0).wait()
            load(l, 6, 6, 3).wait()

    @pl.when(s == 8)
    def _():
        fetch(a1_ref, 0, l).start()
        load(l, 0, 3, 0).start()

    @pl.when(s == 13)
    def _():
        fetch(o_ref, 1, l).wait()
        ab[1, 0, RP - 16:RP] = fold_rows(ab[1, 0, RP - 16:RP], ab[1, n - 1, RP - 16:RP])

        @pl.when(lr == 0)
        def _():
            load(l - 1, 6, 6, 3).start()

    @pl.when(s == 19)
    def _():
        fetch(a1_ref, 0, l).wait()
        ab[0, 0, RP - 16:RP] = fold_rows(ab[0, 0, RP - 16:RP], ab[0, n - 1, RP - 16:RP])
        load(l, 0, 3, 0).wait()

    @pl.when((s == 20) & (lr == 0))
    def _():
        fetch(a2_ref, 0, l - 1).start()
        load(l - 1, 3, 3, 0).start()

    one = (s >= 5) & (s <= 8)
    two = (lr == 1) & (s >= 14) & (s <= 18)
    three = (lr == 0) & ((s == 14) | (s == 16) | (s == 18) | (s == 19))
    four = ((lr == 0) & (s == 21)) | ((lr == 1) & ((s == 0) | (s == 2)))
    five = (lr == 1) & (s >= 20)
    t = jnp.where(one, 12 * lr + s - 5, jnp.where(two, s + 2, jnp.where(three, 4 + (s - 14) // 2 + s // 19, jnp.where(four, 9 + lr * (1 + s // 2), s + 4))))

    @pl.when(one | two | three | four | five)
    def _():
        tick(t)

    @pl.when(s == 0)
    def _():
        for i in range(n):
            up = d[i]
            db[i] = up.astype(BF)
            acc[i] = jnp.zeros((RP, D), F32)
            dv[l, 7:8] += rsum(up)
        db[0, RP - 16:RP] = fold_rows(db[0, RP - 16:RP], db[n - 1, RP - 16:RP])

    @pl.when(s == 4)
    def _():
        db[0, RP - 16:RP] = clear_rows(db[0, RP - 16:RP])

    @pl.when((s >= 4) & (s < 8))
    def _():
        j = s - 4
        whole = db[...].reshape(rows, D)
        cols = pl.multiple_of(j * D, 128)
        for q in range(3):
            t1 = dot_t(whole, wk[pl.ds(pl.multiple_of((5 + j) * D + 256 * q, 16), 256), :])
            t1 = t1 * g_ref[0, :, :, 256 * q:256 * q + 256].reshape(rows, 256).astype(F32)
            dv[l, pl.ds(8 + j, 1), 256 * q:256 * q + 256] += rsum(t1)
            du[:, :, pl.ds(pl.multiple_of(cols + 256 * q, 128), 256)] = t1.astype(BF).reshape(n, RP, 256)
        acc[...] += dot_t(du[:, :, pl.ds(cols, D)].reshape(rows, D), wk[pl.ds(pl.multiple_of(j * D, 16), D), :]).reshape(n, RP, D)

    @pl.when((s >= 8) & (s < 13))
    def _():
        i = s - 8
        dx, dg, dc = norm_back(h1_ref[0, 0], vec_ref[l, 5:6], acc[i])
        dv[l, 5:6] += dg
        dv[l, 6:7] += dc
        dh1 = d[i] + dx
        d[i] = dh1
        dv[l, 4:5] += rsum(dh1)
        du[i, :, 0:D] = dh1.astype(BF)
        du[i, :, 3 * D:4 * D] = dot_t(du[i, :, 0:D], wk[4 * D:5 * D, :]).astype(BF)

    def grad(lhs, rhs, store):
        rhs = rhs[:rows - 16]
        for m in range(2):
            r = dot_0(lhs(384 * m)[:rows - 16], rhs).astype(BF).reshape(4, CH, D)
            store(4 * m, r)

    def inner(slot, j):
        def store(m, r):
            gb[slot, m // 2, 0] = r[0]
            gb[slot, m // 2, 1] = r[1]
            gb[slot, m // 2 + 1, 0] = r[2]
            gb[slot, m // 2 + 1, 1] = r[3]
        grad(lambda m: ab[0, :, :, m:m + 384].reshape(rows, 384), du[:, :, pl.ds(pl.multiple_of(D * j, 128), D)].reshape(rows, D), store)

    def outer(step, lhs, rhs):
        def store(m, r):
            for q in range(4):
                b = 8 * step + m + q
                gb[4 + b % 5, b // 10, (b // 5) % 2] = r[q]
        grad(lhs, rhs.reshape(rows, D), store)

    @pl.when((s >= 4) & (s < 8))
    def _():
        at = pl.ds(pl.multiple_of((s - 4) * D, 128), D)
        du[0, RP - 16:RP, at] = fold_rows(du[0, RP - 16:RP, at], du[n - 1, RP - 16:RP, at])
        inner(s - 4, s - 4)

    @pl.when(s == 13)
    def _():
        du[0, RP - 16:RP, 0:D] = fold_rows(du[0, RP - 16:RP, 0:D], du[n - 1, RP - 16:RP, 0:D])
        outer(0, lambda m: ab[1, :, :, m:m + 384].reshape(rows, 384), du[:, :, 0:D])

    @pl.when(s < 4)
    def _():
        outer(s + 1, lambda m: e_ref[0, :, :, m:m + 384].reshape(rows, 384), db[...])

    @pl.when((s >= 14) & (s < 19))
    def _():
        i = s - 14

        def products(p):
            b = 128 * p
            return attn_bwd_products(qkv_ref[0, 0, :, b:b + 128], qkv_ref[0, 0, :, D + b:D + b + 128], qkv_ref[0, 0, :, 2 * D + b:2 * D + b + 128],
                                     du[i, :, 3 * D + b:3 * D + b + 128])
        later = products(0)
        for p in range(6):
            b = 128 * p
            now, later = later, (products(p + 1) if p < 5 else None)
            dq, dk, dvv = attn_bwd_rest(*now)
            dv[l, 2:3, b:b + 128] += rsum(dq)
            dv[l, 3:4, b:b + 128] += rsum(dvv)
            du[i, :, b:b + 128] = dq.astype(BF)
            du[i, :, D + b:D + b + 128] = dk.astype(BF)
            du[i, :, 2 * D + b:2 * D + b + 128] = dvv.astype(BF)

    @pl.when(s == 19)
    def _():
        du[0, RP - 16:RP, 0:3 * D] = fold_rows(du[0, RP - 16:RP, 0:3 * D], du[n - 1, RP - 16:RP, 0:3 * D])

        @pl.loop(0, 3)
        def _(j):
            inner(j, j)

            @pl.when((lr == 1) | (j == 1))
            def _():
                tick(lr * (21 + j) + (1 - lr) * 8)
        du[0, RP - 16:RP, 0:3 * D] = clear_rows(du[0, RP - 16:RP, 0:3 * D])
        acc[...] = dot_t(du[:, :, 0:D].reshape(rows, D), wk[0:D, :]).reshape(n, RP, D)
        acc[...] += dot_t(du[:, :, D:2 * D].reshape(rows, D), wk[D:2 * D, :]).reshape(n, RP, D)
        acc[...] += dot_t(du[:, :, 2 * D:3 * D].reshape(rows, D), wk[2 * D:3 * D, :]).reshape(n, RP, D)

    @pl.when(s >= 20)
    def _():
        i = s - 20
        dx, dg, dc = norm_back(hs_ref[0, 0], vec_ref[l, 0:1], acc[i])
        dv[l, 0:1] += dg
        dv[l, 1:2] += dc
        dh = d[i] + dx
        d[i] = dh
        di_ref[0] = dh[0:SEQ]

    @pl.when((lr == 1) & (s == 24))
    def _():
        for layer in range(LAYERS):
            for c in range(72):
                vs[c // 9, layer, c % 9:c % 9 + 1, :] = dv[layer, c // 6:c // 6 + 1, 128 * (c % 6):128 * (c % 6) + 128]

        def vcopy(k):
            to = (f + k) % 8
            return pltpu.make_async_remote_copy(src_ref=vs.at[to], dst_ref=vr.at[k - 1], send_sem=vssem.at[k - 1], recv_sem=vrsem.at[k - 1],
                                                device_id={"fsdp": to}, device_id_type=MESH)

        def zcopy(k):
            return pltpu.make_async_remote_copy(src_ref=vz.at[z], dst_ref=vz.at[z], send_sem=vssem.at[6 + k], recv_sem=vrsem.at[6 + k],
                                                device_id={"rep": (z + k) % 4}, device_id_type=MESH)
        for k in range(1, 8):
            vcopy(k).start()

        @pl.loop(29, 36)
        def _(t):
            @pl.when(t == 30)
            def _():
                for k in range(1, 8):
                    vcopy(k).wait()
                total = vs[f]
                for k in range(7):
                    total = total + vr[k]
                vz[z] = total
                for k in range(1, 4):
                    zcopy(k).start()
            tick(t)

        for k in range(1, 4):
            zcopy(k).wait()
        gv_ref[...] = (vz[0] + vz[1]) + (vz[2] + vz[3])


def bwd(cotangent, w, vec, hs, h1, g, e, qkv, a2, o, a1, shard_in, shard_out):
    n = cotangent.shape[0]
    S = jax.ShapeDtypeStruct
    anyw = pl.BlockSpec(memory_space=pl.ANY)
    row = lambda cols, at: pl.BlockSpec((1, 1, RP, cols), lambda lr, s: (LAYERS - 1 - lr, jnp.clip(s - at, 0, 4), 0, 0))
    cols = lambda at: pl.BlockSpec((1, n, RP, D), lambda lr, s: (LAYERS - 1 - lr, 0, 0, jnp.clip(s - at, 0, 3)))
    tok = lambda index: pl.BlockSpec((1, SEQ, D), index)
    VB = lambda *shape: pltpu.VMEM(shape, BF)
    half = CH // 2
    return pl.pallas_call(
        bwd_kernel, grid=(LAYERS, 25),
        in_specs=[pl.BlockSpec(cotangent.shape, lambda lr, s: (0, 0, 0), pipeline_mode=pl.Buffered(1)), anyw, pl.BlockSpec(vec.shape, lambda lr, s: (0, 0, 0)),
                  row(D, 20), row(D, 8), cols(4), cols(0), row(3 * D, 14), anyw, anyw, anyw],
        out_specs=[tok(lambda lr, s: (lr * jnp.clip(s - 20, 0, 4), 0, 0)), anyw, anyw, pl.BlockSpec((LAYERS, 16, 128), lambda lr, s: (0, 0, 0))],
        out_shape=[S(cotangent.shape, F32), S(shard_in, BF), S(shard_out, BF), S((LAYERS, 16, 128), F32)],
        scratch_shapes=[VB(9 * D, D), pltpu.VMEM((n, RP, D), F32), pltpu.VMEM((n, RP, D), F32), VB(n, RP, D), VB(n, RP, 4 * D), VB(2, n, RP, D),
                        VB(9, 4, 2, CH, D), pltpu.VMEM((LAYERS, 16, D), F32),
                        VB(2, 4, CH, D), VB(2, 2, 2, CH, D), VB(4, 2, half, D), VB(4, 2, half, D), VB(2, 2, half, D), VB(2, 2, half, D),
                        VB(4, half, D), VB(4, half, D), VB(2, CH, D), VB(4, half, D), VB(2, half, D), VB(4, half, D), VB(2, half, D), VB(4, half, D),
                        VB(2, CH, D),
                        pltpu.VMEM((8, LAYERS, 16, 128), F32), pltpu.VMEM((7, LAYERS, 16, 128), F32), pltpu.VMEM((4, LAYERS, 16, 128), F32),
                        pltpu.SemaphoreType.DMA((2,)), pltpu.SemaphoreType.DMA((2,)), pltpu.SemaphoreType.DMA((4, 8)), pltpu.SemaphoreType.DMA((4, 8)),
                        pltpu.SemaphoreType.DMA((2,)), pltpu.SemaphoreType.DMA((10,)), pltpu.SemaphoreType.DMA((10,))],
        compiler_params=pltpu.CompilerParams(collective_id=1, has_side_effects=True, vmem_limit_bytes=63 * 2**20),
    )(cotangent, w, vec, hs, h1, g, e, qkv, a2, o, a1)


STEP = 3
beta_one = 0.9
beta_two = 0.999
matrix_rate = 0.03
vector_rate = 0.2
matrix_decay = 0.05
adam_eps = 1e-8


def adam_update(master, gradient, moment_one, moment_two, rate, decay_rate):
    moment_one = beta_one * moment_one + (1.0 - beta_one) * gradient
    moment_two = beta_two * moment_two + (1.0 - beta_two) * gradient * gradient
    corr_one = 1.0 - beta_one**STEP
    corr_two = 1.0 - beta_two**STEP
    adam_move = moment_one / corr_one / (jnp.sqrt(moment_two / corr_two) + adam_eps)
    return (master - rate * (adam_move + decay_rate * master), moment_one, moment_two)


def adam_kernel(g_ref, w_ref, m_ref, v_ref, go_ref, wo_ref, mo_ref, vo_ref, enc_ref, dim_ref,
                g_out, w_out, m_out, v_out, go_out, wo_out, mo_out, vo_out, enc_out, dim_out, steps):
    i = pl.program_id(0)

    def update(g, w, m, v, outs):
        grad = g[...].astype(F32)
        new, moment, square = adam_update(w[...], grad, m[...], v[...], matrix_rate, matrix_decay)
        outs[0][...], outs[1][...], outs[2][...], outs[3][...] = grad, new, moment, square

    @pl.when(i < steps)
    def _():
        update(g_ref, w_ref, m_ref, v_ref, (g_out, w_out, m_out, v_out))

    @pl.when(i >= steps)
    def _():
        update(go_ref, wo_ref, mo_ref, vo_ref, (go_out, wo_out, mo_out, vo_out))

    @pl.when(i < enc_steps)
    def _():
        enc_out[...] = enc_ref[...]
        dim_out[...] = dim_ref[...]


enc_steps = 5


def adam_all(ins, outs, encoded, dimg):
    a, b = ins[0].shape, outs[0].shape
    steps = 2 * LAYERS
    first = pl.BlockSpec((1, a[1] // 2, a[2]), lambda i: (jnp.minimum(i, steps - 1) // 2, jnp.minimum(i, steps - 1) % 2, 0))
    second = pl.BlockSpec((1, b[1] // 2, b[2]), lambda i: (jnp.maximum(i - steps, 0) // 2, jnp.maximum(i - steps, 0) % 2, 0))
    tok = pl.BlockSpec((1,) + encoded.shape[1:], lambda i: (jnp.minimum(i, enc_steps - 1), 0, 0))
    S = jax.ShapeDtypeStruct
    return pl.pallas_call(
        functools.partial(adam_kernel, steps=steps), grid=(2 * steps,),
        in_specs=[first] * 4 + [second] * 4 + [tok] * 2, out_specs=[first] * 4 + [second] * 4 + [tok] * 2,
        out_shape=[S(a, F32)] * 4 + [S(b, F32)] * 4 + [S(encoded.shape, BF), S(dimg.shape, F32)],
        compiler_params=PAR,
    )(*ins, *outs, encoded, dimg)


def swap(x, axis, size, mask):
    return lax.ppermute(x, axis, [(i, i ^ mask) for i in range(size)])


def halve(x, order, size):
    bits = size.bit_length() - 1
    me = lax.axis_index("fsdp")
    x = x.reshape((2,) * bits + x.shape[1:])
    left = list(range(bits))[::-1]
    for bit in order:
        at = left.index(bit)
        mine = (me >> bit) & 1
        keep = lax.dynamic_index_in_dim(x, mine, at, keepdims=False)
        send = lax.dynamic_index_in_dim(x, 1 - mine, at, keepdims=False)
        got = swap(send, "fsdp", size, 1 << bit)
        x = (keep.astype(F32) + got.astype(F32)).astype(BF)
        left.remove(bit)
    return x


def reduce_all(x, nf, nr):
    bits = nf.bit_length() - 1
    rows, cols = x.shape
    x = x.reshape(nf, rows // nf, cols)
    half = cols // 2 // 128 * 128
    up = [0] + list(range(1, bits))
    down = [0] + list(range(1, bits))[::-1]
    x = jnp.concatenate([halve(x[..., :half], up, nf), halve(x[..., half:], down, nf)], axis=-1)
    mask = 1
    while mask < nr:
        got = swap(x, "rep", nr, 2 * mask - 1)
        y = x.astype(F32) + got.astype(F32)
        x = y.astype(BF)
        mask *= 2
    return y


def fused_step(images, cotangent, weight_in, weight_out, vector_params):
    vs = jnp.pad(vector_params.astype(BF).astype(F32).reshape(LAYERS, 9, 128), ((0, 0), (0, 7), (0, 0)))
    hs, qkv, a1, o, h1, a2, e, g, encoded, w, vec = fwd(images, weight_in, weight_out, vs)
    dimg, gi, go, gv = bwd(cotangent, w, vec, hs, h1, g, e, qkv, a2, o, a1, weight_in.shape, weight_out.shape)
    return encoded, dimg, gi, go, gv[:, :9].reshape(vector_params.shape)


def plain_step(nf, nr, images, cotangent, weight_in, weight_out, vector_params):
    pad = lambda a: jnp.pad(a, ((0, 0), (0, RP - SEQ), (0, 0)))
    vec_all = lax.all_gather(vector_params.astype(BF), "fsdp", axis=1, tiled=True).astype(F32)
    h = pad(images)
    ct = pad(cotangent)
    saved = []
    for l in range(LAYERS):
        win = lax.all_gather(weight_in[l].astype(BF), "fsdp", axis=0, tiled=True)
        wout = lax.all_gather(weight_out[l].astype(BF), "fsdp", axis=0, tiled=True)
        vec = jnp.pad(vec_all[l].reshape(12, D), ((0, 4), (0, 0)))
        wqkv, w1, wo, w2 = win[:, : 3 * D], win[:, 3 * D :], wout[:D], wout[D:]
        qkv, o, a1 = ka(h, wqkv, vec)
        h1, a2, e, g, h2 = kb(h, o, wo, w1, w2, vec)
        saved.append((h, wqkv, w1, wo, w2, vec, qkv, o, a1, h1, a2, e, g))
        h = h2
    encoded = h[:, :SEQ].astype(BF)
    d = ct
    gin, gout, gvec = [None] * LAYERS, [None] * LAYERS, [None] * LAYERS
    for l in reversed(range(LAYERS)):
        h, wqkv, w1, wo, w2, vec, qkv, o, a1, h1, a2, e, g = saved[l]
        db, du, dh1, dh1b, do, dv1 = kc(d, h1, g, wo, w1, w2, vec)
        g1 = reduce_all(dw(a2, du), nf, nr)
        go = reduce_all(jnp.concatenate([dw(o, dh1b), dw(e, db)], axis=0), nf, nr)
        dz, dv2 = kd(qkv, do)
        gq = reduce_all(dw(a1, dz), nf, nr)
        d, dv3 = kf(dz, h, dh1, wqkv, vec, RP if l else SEQ)
        gin[l] = jnp.concatenate([gq, g1], axis=1)
        gout[l] = go
        gvec[l] = (dv1 + dv2 + dv3)[:12].reshape(-1)
    gv = lax.psum(jnp.stack(gvec), ("fsdp", "rep"))
    wide = gv.shape[1] // nf
    gv = lax.dynamic_slice_in_dim(gv, lax.axis_index("fsdp") * wide, wide, 1)
    return encoded, d, jnp.stack(gin), jnp.stack(gout), gv


def make_shards(nf, nr):
    def shards(images, cotangent, weight_in, weight_out, vector_params, first_in, first_out, first_vec, second_in, second_out, second_vec):
        if nf == 8 and nr == 4:
            encoded, d, gi, go, gv = fused_step(images, cotangent, weight_in, weight_out, vector_params)
            gi, new_in, moment_in, square_in, go, new_out, moment_out, square_out, encoded, d = adam_all(
                (gi, weight_in, first_in, second_in), (go, weight_out, first_out, second_out), encoded, d)
        else:
            encoded, d, gi, go, gv = plain_step(nf, nr, images, cotangent, weight_in, weight_out, vector_params)
            new_in, moment_in, square_in = adam_update(weight_in, gi, first_in, second_in, matrix_rate, matrix_decay)
            new_out, moment_out, square_out = adam_update(weight_out, go, first_out, second_out, matrix_rate, matrix_decay)
        new_vec, moment_vec, square_vec = adam_update(vector_params, gv, first_vec, second_vec, vector_rate, 0.0)
        return (encoded, d, gi, go, gv, new_in, new_out, new_vec, moment_in, moment_out, moment_vec, square_in, square_out, square_vec)

    return shards


def solution(mesh):
    tokens = P(("fsdp", "rep"), None, None)
    matrix = P(None, "fsdp", None)
    vector = P(None, "fsdp")
    in_specs = (tokens, tokens) + (matrix, matrix, vector) * 3
    out_specs = (tokens, tokens) + (matrix, matrix, vector) * 4
    return jax.shard_map(make_shards(mesh.shape["fsdp"], mesh.shape["rep"]), mesh=mesh, in_specs=in_specs, out_specs=out_specs, check_vma=False)
```

```python
import functools
import jax, jax.numpy as jnp
from jax import lax
from jax.experimental import pallas as pl
from jax.experimental.pallas import tpu as pltpu
from jax.sharding import PartitionSpec as P

D=768; HD=64; SEQ=197; RP=208; EPS=1e-6
BF=jnp.bfloat16; F32=jnp.float32
def dot(a,b): return jnp.dot(a,b,preferred_element_type=F32)
def dot_t(a,b): return lax.dot_general(a,b,(((1,),(1,)),((),())),preferred_element_type=F32)
def dot_0(a,b): return lax.dot_general(a,b,(((0,),(0,)),((),())),preferred_element_type=F32)

def norm_stats(x):
    mean=jnp.mean(x,axis=-1,keepdims=True); xc=x-mean
    var=jnp.mean(xc*xc,axis=-1,keepdims=True)
    return xc, lax.rsqrt(var+EPS)

def head_masks(scale):
    lane = lax.broadcasted_iota(jnp.int32, (1, 128), 1)
    return jnp.where(lane < 64, scale, 0.0).astype(BF), jnp.where(lane < 64, 0.0, scale).astype(BF)


def attn_fwd(q, k, v):
    ones = head_masks(1.0)
    row = lax.broadcasted_iota(jnp.int32, (16, 1), 0)
    ps = []
    for m in head_masks(0.125):
        s = dot_t(k, q * m)
        s = jnp.concatenate([s[:RP - 16], jnp.where(row < SEQ - RP + 16, s[RP - 16:], -1e30)], axis=0)
        e = jnp.exp(s - jnp.max(s, axis=0, keepdims=True))
        ps.append((e * (1.0 / jnp.sum(e, axis=0, keepdims=True))).astype(BF))
    return (dot_0(ps[0], v * ones[0]) + dot_0(ps[1], v * ones[1])).astype(BF)


def attn_bwd_products(q, k, v, do):
    scaled, ones = head_masks(0.125), head_masks(1.0)
    row = lax.broadcasted_iota(jnp.int32, (RP, 1), 0)
    qs, ks, dos = [q * m for m in scaled], [k * m for m in scaled], [do * m for m in ones]
    s = [jnp.where(row < SEQ, dot_t(k, x), -1e30) for x in qs]
    return qs, ks, dos, s, [dot_t(v, x) for x in dos]


def attn_bwd_rest(qs, ks, dos, s, dp):
    e = [jnp.exp(x - jnp.max(x, axis=0, keepdims=True)) for x in s]
    p = [x * (1.0 / jnp.sum(x, axis=0, keepdims=True)) for x in e]
    pb = [x.astype(BF) for x in p]
    ds = [(a * (b - jnp.sum(a * b, axis=0, keepdims=True))).astype(BF) for a, b in zip(p, dp)]
    dv = dot(pb[0], dos[0]) + dot(pb[1], dos[1])
    dk = dot(ds[0], qs[0]) + dot(ds[1], qs[1])
    dq = dot_0(ds[0], ks[0]) + dot_0(ds[1], ks[1])
    return dq, dk, dv


def attn_bwd(q, k, v, do):
    return attn_bwd_rest(*attn_bwd_products(q, k, v, do))


TAIL = SEQ - RP + 16


def fold_rows(first, last):
    r = lax.broadcasted_iota(jnp.int32, (16, 16), 0)
    c = lax.broadcasted_iota(jnp.int32, (16, 16), 1)
    move = jnp.where((r == c + TAIL) & (c < TAIL), 1.0, 0.0).astype(BF)
    row = lax.broadcasted_iota(jnp.int32, (16, 1), 0)
    return jnp.where((row >= TAIL) & (row < 2 * TAIL), dot(move, last), first.astype(F32)).astype(BF)


def clear_rows(first):
    row = lax.broadcasted_iota(jnp.int32, (16, 1), 0)
    return jnp.where(row < TAIL, first.astype(F32), 0.0).astype(BF)


def ka_kernel(h_ref,w_ref,vec_ref,qkv_ref,o_ref,a_ref):
    h=h_ref[0].astype(F32)
    xc,rs=norm_stats(h)
    a_ref[0]=(xc*rs*vec_ref[0:1]+vec_ref[1:2]).astype(BF)
    a=a_ref[0]
    for c in range(3):
        cs=slice(256*c,256*c+256)
        qkv_ref[0,:,256*c:256*c+256]=(dot(a,w_ref[:,256*c:256*c+256])+vec_ref[2:3,cs]).astype(BF)
        qkv_ref[0,:,D+256*c:D+256*c+256]=dot(a,w_ref[:,D+256*c:D+256*c+256]).astype(BF)
        qkv_ref[0,:,2*D+256*c:2*D+256*c+256]=(dot(a,w_ref[:,2*D+256*c:2*D+256*c+256])+vec_ref[3:4,cs]).astype(BF)
        for p in range(2):
            b=256*c+128*p
            o_ref[0,:,b:b+128]=attn_fwd(qkv_ref[0,:,b:b+128],qkv_ref[0,:,D+b:D+b+128],qkv_ref[0,:,2*D+b:2*D+b+128])

def img(n,dt=None): return pl.BlockSpec((1,RP,n),lambda i:(i,0,0))
def full(shape): return pl.BlockSpec(shape,lambda i:(0,)*len(shape))
PAR=pltpu.CompilerParams(vmem_limit_bytes=60*2**20)

def ka(h,w,vec):
    n=h.shape[0]
    return pl.pallas_call(ka_kernel,grid=(n,),in_specs=[img(D),full(w.shape),full(vec.shape)],
        out_specs=[img(3*D),img(D),img(D)],
        out_shape=[jax.ShapeDtypeStruct((n,RP,3*D),BF),jax.ShapeDtypeStruct((n,RP,D),BF),jax.ShapeDtypeStruct((n,RP,D),BF)],
        compiler_params=PAR)(h,w,vec)

def gelu_parts(u):
    c=0.5*(1.0+lax.erf(u*0.7071067811865476))
    g=c+u*(jnp.exp(-0.5*u*u)*0.3989422804014327)
    return u*c,g

def kb_kernel(FC,h_ref,o_ref,wo_ref,w1_ref,w2_ref,vec_ref,h1_ref,a_ref,e_ref,g_ref,h2_ref):
    h1=h_ref[0].astype(F32)+dot(o_ref[0],wo_ref[...])+vec_ref[4:5]
    h1_ref[0]=h1
    xc,rs=norm_stats(h1)
    a_ref[0]=(xc*rs*vec_ref[5:6]+vec_ref[6:7]).astype(BF)
    a=a_ref[0]
    h2_ref[0]=h1+vec_ref[7:8]
    for j in range(3072//FC):
        lo=FC*j
        u=dot(a,w1_ref[:,lo:lo+FC])+vec_ref[8+lo//D:9+lo//D,lo%D:lo%D+FC]
        e,g=gelu_parts(u)
        e_ref[0,:,lo:lo+FC]=e.astype(BF); g_ref[0,:,lo:lo+FC]=g.astype(BF)
        h2_ref[0]+=dot(e_ref[0,:,lo:lo+FC],w2_ref[lo:lo+FC,:])

def kb(h,o,wo,w1,w2,vec,FC=256):
    n=h.shape[0]
    S=jax.ShapeDtypeStruct
    return pl.pallas_call(functools.partial(kb_kernel,FC),grid=(n,),in_specs=[img(D),img(D),full(wo.shape),full(w1.shape),full(w2.shape),full(vec.shape)],
        out_specs=[img(D),img(D),img(3072),img(3072),img(D)],
        out_shape=[S((n,RP,D),F32),S((n,RP,D),BF),S((n,RP,3072),BF),S((n,RP,3072),BF),S((n,RP,D),F32)],
        compiler_params=PAR)(h,o,wo,w1,w2,vec)

def rsum(x): return jnp.sum(x,axis=0,keepdims=True)
def norm_back(x,gain,dy):
    xc,rs=norm_stats(x); xh=xc*rs
    dyg=dy*gain
    dx=rs*(dyg-jnp.mean(dyg,axis=-1,keepdims=True)-xh*jnp.mean(dyg*xh,axis=-1,keepdims=True))
    return dx, rsum(dy*xh), rsum(dy)

def kc_kernel(FC,d_ref,h1_ref,g_ref,wo_ref,w1_ref,w2_ref,vec_ref,db_ref,du_ref,dh1_ref,dh1b_ref,do_ref,dv_ref,acc_ref):
    @pl.when(pl.program_id(0)==0)
    def _(): dv_ref[...]=jnp.zeros_like(dv_ref)
    d=d_ref[0].astype(F32)
    db_ref[0]=d.astype(BF)
    db=db_ref[0]
    dv_ref[7:8]+=rsum(d)
    for j in range(3072//FC):
        lo=FC*j
        du=dot_t(db,w2_ref[lo:lo+FC,:])*g_ref[0,:,lo:lo+FC].astype(F32)
        dv_ref[8+lo//D:9+lo//D,lo%D:lo%D+FC]+=rsum(du)
        du_ref[0,:,lo:lo+FC]=du.astype(BF)
        t=dot_t(du_ref[0,:,lo:lo+FC],w1_ref[:,lo:lo+FC])
        if j==0: acc_ref[...]=t
        else: acc_ref[...]+=t
    dx,dg,dc=norm_back(h1_ref[0],vec_ref[5:6],acc_ref[...])
    dv_ref[5:6]+=dg; dv_ref[6:7]+=dc
    dh1=d_ref[0].astype(F32)+dx
    dh1_ref[0]=dh1
    dv_ref[4:5]+=rsum(dh1)
    dh1b_ref[0]=dh1.astype(BF)
    do_ref[0]=dot_t(dh1b_ref[0],wo_ref[...]).astype(BF)

def kc(d,h1,g,wo,w1,w2,vec,FC=256):
    n=d.shape[0]; S=jax.ShapeDtypeStruct
    return pl.pallas_call(functools.partial(kc_kernel,FC),grid=(n,),in_specs=[img(D),img(D),img(3072),full(wo.shape),full(w1.shape),full(w2.shape),full(vec.shape)],
        out_specs=[img(D),img(3072),img(D),img(D),img(D),full((16,D))],
        out_shape=[S((n,RP,D),BF),S((n,RP,3072),BF),S((n,RP,D),F32),S((n,RP,D),BF),S((n,RP,D),BF),S((16,D),F32)],
        scratch_shapes=[pltpu.VMEM((RP,D),F32)],
        compiler_params=PAR)(d,h1,g,wo,w1,w2,vec)

def kd_kernel(qkv_ref,do_ref,dz_ref,dv_ref):
    @pl.when(pl.program_id(0)==0)
    def _(): dv_ref[...]=jnp.zeros_like(dv_ref)
    for p in range(6):
        b=128*p
        dq,dk,dv=attn_bwd(qkv_ref[0,:,b:b+128],qkv_ref[0,:,D+b:D+b+128],qkv_ref[0,:,2*D+b:2*D+b+128],do_ref[0,:,b:b+128])
        dv_ref[2:3,b:b+128]+=rsum(dq); dv_ref[3:4,b:b+128]+=rsum(dv)
        dz_ref[0,:,b:b+128]=dq.astype(BF); dz_ref[0,:,D+b:D+b+128]=dk.astype(BF); dz_ref[0,:,2*D+b:2*D+b+128]=dv.astype(BF)

def kd(qkv,do):
    n=do.shape[0]; S=jax.ShapeDtypeStruct
    return pl.pallas_call(kd_kernel,grid=(n,),in_specs=[img(3*D),img(D)],out_specs=[img(3*D),full((16,D))],
        out_shape=[S((n,RP,3*D),BF),S((16,D),F32)],compiler_params=PAR)(qkv,do)

def kf_kernel(dz_ref,h_ref,dh1_ref,w_ref,vec_ref,dh_ref,dv_ref):
    @pl.when(pl.program_id(0)==0)
    def _(): dv_ref[...]=jnp.zeros_like(dv_ref)
    da=dot_t(dz_ref[0],w_ref[...])
    dx,dg,dc=norm_back(h_ref[0].astype(F32),vec_ref[0:1],da)
    dv_ref[0:1]+=dg; dv_ref[1:2]+=dc
    rows=dh_ref.shape[1]
    dh_ref[0]=(dh1_ref[0]+dx)[:rows]

def kf(dz,h,dh1,w,vec,rows=RP):
    n=dz.shape[0]; S=jax.ShapeDtypeStruct
    return pl.pallas_call(kf_kernel,grid=(n,),in_specs=[img(3*D),img(D),img(D),full(w.shape),full(vec.shape)],
        out_specs=[pl.BlockSpec((1,rows,D),lambda i:(i,0,0)),full((16,D))],
        out_shape=[S((n,rows,D),F32),S((16,D),F32)],compiler_params=PAR)(dz,h,dh1,w,vec)

def dw_kernel(l_ref,r_ref,o_ref):
    o_ref[...]=dot_0(l_ref[...],r_ref[...]).astype(BF)
def dw(l,r,MB=256):
    M=l.shape[-1]; N=r.shape[-1]; K=l.shape[0]*RP
    l=l.reshape(K,M); r=r.reshape(K,N)
    return pl.pallas_call(dw_kernel,grid=(M//MB,),in_specs=[pl.BlockSpec((K,MB),lambda i:(0,i)),pl.BlockSpec((K,N),lambda i:(0,0))],
       out_specs=pl.BlockSpec((MB,N),lambda i:(i,0)),out_shape=jax.ShapeDtypeStruct((M,N),BF),compiler_params=PAR)(l,r)


LAYERS = 2
MESH = pl.DeviceIdType.MESH
CH = 96
NC = 12


def plane():
    f = lax.axis_index("fsdp")
    core, x, y = f % 2, (f // 2) % 2, f // 4
    return f, core, x, y


def chunk_rows(c, f):
    layer, j = c // NC, c % NC
    early = 1 - (j + 9) // 12
    late = j // 8
    mid = 1 - early - late
    base = layer * NC * D
    return pl.multiple_of(base + early * (j * D + CH * f) + late * ((j - 5) * D + CH * f)
                          + mid * (7 * D + 5 * CH * f + CH * (j - 3)), 16)


def fwd_kernel(img_ref, win_ref, wout_ref, vs_ref, hs_ref, qkv_ref, a1_ref, o_ref, h1_ref, a2_ref, e_ref, g_ref, enc_ref, wo_ref, vo_ref,
               w, hb, ob, ab, vg, vec, st, lsem, ssem, rsem, vssem, vrsem, osem, vosem):
    l, s = pl.program_id(0), pl.program_id(1)
    f, core, x, y = plane()
    fc, fx, fy = f + 1 - 2 * core, f + 2 - 4 * x, f + 4 - 8 * y
    fd = fx + fy - f
    z = lax.axis_index("rep")
    side = z % 2
    zp = z + 1 - 2 * side
    part = pl.ds(pl.multiple_of(256 * side, 128), 512)
    give = pl.ds(pl.multiple_of(512 * side, 128), 256)

    def wrow(c, who, lo=0, n=CH):
        return pl.ds(pl.multiple_of(chunk_rows(c, who) + lo, 16), n)

    def send(c, kind, where, **to):
        return pltpu.make_async_remote_copy(src_ref=w.at[where], dst_ref=w.at[where], send_sem=ssem.at[c % 12, kind], recv_sem=rsem.at[c % 12, kind],
                                            device_id=to, device_id_type=MESH)

    def fetch(c, act):
        layer, j = c // NC, c % NC
        mid = (j >= 3) & (j < 8)

        @pl.when(mid)
        def _():
            act(pltpu.make_async_copy(wout_ref.at[layer, pl.ds(pl.multiple_of((j - 3) * CH, 8), CH)], st.at[c % 4], lsem.at[c % 4]))

        @pl.when(jnp.logical_not(mid))
        def _():
            act(pltpu.make_async_copy(win_ref.at[layer, :, pl.ds(pl.multiple_of((j - 5 * (j // 8)) * D, 128), D)], st.at[c % 4], lsem.at[c % 4]))

    def kinds(c):
        half = CH // 2
        return [lambda: send(c, 0, (wrow(c, f), part), fsdp=fx), lambda: send(c, 1, (wrow(c, f), part), fsdp=fy),
                lambda: send(c, 2, (wrow(c, f),), fsdp=fc),
                lambda: send(c, 3, (wrow(c, fx, 0, half), part), fsdp=fy), lambda: send(c, 4, (wrow(c, fy, half, half), part), fsdp=fx),
                lambda: send(c, 5, (wrow(c, fx), give), rep=zp), lambda: send(c, 6, (wrow(c, fy), give), rep=zp),
                lambda: send(c, 7, (wrow(c, fd), give), rep=zp),
                lambda: send(c, 8, (wrow(c, fx),), fsdp=fc), lambda: send(c, 9, (wrow(c, fy),), fsdp=fc), lambda: send(c, 10, (wrow(c, fd),), fsdp=fc)]

    def start(c, which):
        k = kinds(c)
        for i in which:
            k[i]().start()

    def wait(c, which):
        k = kinds(c)
        for i in which:
            k[i]().wait()

    def tick(t):
        @pl.when((t >= 7) & (t < 31))
        def _():
            wait(t - 7, (2, 8, 9, 10))

        @pl.when((t >= 6) & (t < 30))
        def _():
            wait(t - 6, (7,))
            start(t - 6, (10,))

        @pl.when((t >= 4) & (t < 28))
        def _():
            wait(t - 4, (3, 4, 5, 6))
            start(t - 4, (7, 8, 9))

        @pl.when((t >= 2) & (t < 26))
        def _():
            wait(t - 2, (0, 1))
            start(t - 2, (3, 4, 5, 6))

        def launch(c):
            fetch(c, lambda a: a.wait())
            w[pl.ds(chunk_rows(c, f), CH)] = st[c % 4].astype(BF)
            start(c, (0, 1, 2))

        @pl.when(t < 24)
        def _():
            launch(t)

        @pl.when(t < 21)
        def _():
            fetch(t + 3, lambda a: a.start())

    def out_copy(b, n):
        return pltpu.make_async_copy(w.at[pl.ds(b, n)], wo_ref.at[pl.ds(b, n)], osem)

    @pl.when((l == 0) & (s == 0))
    def _():
        for c in range(3):
            fetch(jnp.int32(c), lambda a: a.start())
        bar = pltpu.get_barrier_semaphore()
        for k in range(1, 8):
            pl.semaphore_signal(bar, inc=1, device_id={"fsdp": (f + k) % 8}, device_id_type=MESH)
        pl.semaphore_signal(bar, inc=1, device_id={"rep": zp}, device_id_type=MESH)
        pl.semaphore_wait(bar, 8)

        def vcopy(k):
            return pltpu.make_async_remote_copy(src_ref=vs_ref, dst_ref=vg.at[f], send_sem=vssem.at[k - 1], recv_sem=vrsem.at[k - 1],
                                                device_id={"fsdp": (f + k) % 8}, device_id_type=MESH)
        for k in range(1, 8):
            vcopy(k).start()
        vg[f] = vs_ref[...]

        @pl.loop(0, 10)
        def _(t):
            tick(t)

            @pl.when(t == 0)
            def _():
                hb[...] = jnp.zeros_like(hb)

            @pl.when(t == 3)
            def _():
                for k in range(1, 8):
                    vcopy(k).wait()
                for layer in range(LAYERS):
                    for c in range(72):
                        vec[layer, c // 6:c // 6 + 1, 128 * (c % 6):128 * (c % 6) + 128] = vg[c // 9, layer, c % 9:c % 9 + 1, :]
                pltpu.make_async_copy(vec, vo_ref, vosem).start()

    early = s <= 5
    late = (s == 8) | ((s >= 10) & (s + l <= 13))
    t = jnp.where(early, (1 - l) * (s + 9) + l * (s + 21), jnp.where(s == 8, 15 + 12 * l, (1 - l) * (s + 6 + s // 12) + l * (s + 18)))

    @pl.when((early & (l + s > 0)) | late)
    def _():
        tick(t)

    @pl.when(s < 5)
    def _():
        @pl.when(l == 0)
        def _():
            hb[s, 0:SEQ, :] = img_ref[s].astype(F32)
        h = hb[s]
        hs_ref[0, 0] = h
        xc, rs = norm_stats(h)
        a1_ref[0, 0] = (xc * rs * vec[l, 0:1] + vec[l, 1:2]).astype(BF)
        a = a1_ref[0, 0]
        wb = l * NC * D

        def wq(part, c):
            return w[pl.ds(pl.multiple_of(wb + part * D, 16), D), 256 * c:256 * c + 256]
        for c in range(3):
            cs = slice(256 * c, 256 * c + 256)
            qkv_ref[0, 0, :, cs] = (dot(a, wq(0, c)) + vec[l, 2:3, cs]).astype(BF)
            qkv_ref[0, 0, :, D + 256 * c:D + 256 * c + 256] = dot(a, wq(1, c)).astype(BF)
            qkv_ref[0, 0, :, 2 * D + 256 * c:2 * D + 256 * c + 256] = (dot(a, wq(2, c)) + vec[l, 3:4, cs]).astype(BF)
            for p in range(2):
                b = 256 * c + 128 * p
                o = attn_fwd(qkv_ref[0, 0, :, b:b + 128], qkv_ref[0, 0, :, D + b:D + b + 128], qkv_ref[0, 0, :, 2 * D + b:2 * D + b + 128])
                o_ref[0, 0, :, b:b + 128] = o
                ob[s, :, b:b + 128] = o

    @pl.when((s >= 5) & (s < 10))
    def _():
        i = s - 5
        wo = w[pl.ds(pl.multiple_of((l * NC + 7) * D, 16), D), :]
        h1 = hb[i] + dot(ob[i], wo) + vec[l, 4:5]
        h1_ref[0, 0] = h1
        hb[i] = h1 + vec[l, 7:8]
        xc, rs = norm_stats(h1)
        a = (xc * rs * vec[l, 5:6] + vec[l, 6:7]).astype(BF)
        a2_ref[0, 0] = a
        ab[i] = a

    @pl.when(s >= 10)
    def _():
        j = s - 10
        up = pl.multiple_of((l * NC + 3 + j) * D, 16)
        down = pl.multiple_of((l * NC + 8 + j) * D, 16)

        bias = vec[l, pl.ds(8 + j, 1), :]
        n = hb.shape[0]
        u = dot(ab[0], w[pl.ds(up, D), :])
        for i in range(n):
            later = dot(ab[i + 1], w[pl.ds(up, D), :]) if i < n - 1 else None
            e, g = gelu_parts(u + bias)
            e = e.astype(BF)
            e_ref[0, i] = e
            g_ref[0, i] = g.astype(BF)
            hb[i] += dot(e, w[pl.ds(down, D), :])
            u = later
            if i == 2:
                @pl.when((s == 11) & (l == 0))
                def _():
                    tick(18)

        e_ref[0, 0, RP - 16:RP] = fold_rows(e_ref[0, 0, RP - 16:RP], e_ref[0, n - 1, RP - 16:RP])

        @pl.when((l == 1) & (s == 13))
        def _():
            for i in range(n):
                enc_ref[i] = hb[i, 0:SEQ, :].astype(BF)

    for layer in range(LAYERS):
        base = layer * NC * D

        @pl.when((l == layer) & (s == 4))
        def _():
            out_copy(base, 3 * D).start()

        @pl.when((l == layer) & (s == 9))
        def _():
            out_copy(base + 7 * D, 5 * D).start()

        for j in range(4):
            @pl.when((l == layer) & (s == 10 + j))
            def _():
                out_copy(base + (3 + j) * D, D).start()

    @pl.when((l == 1) & (s == 13))
    def _():
        pltpu.make_async_copy(w, wo_ref, osem).wait()
        pltpu.make_async_copy(vec, vo_ref, vosem).wait()


def fwd(images, weight_in, weight_out, vshard):
    n = images.shape[0]
    S = jax.ShapeDtypeStruct
    one = lambda cols: pl.BlockSpec((1, 1, RP, cols), lambda l, s: (l, jnp.minimum(s, 4), 0, 0))
    two = lambda cols: pl.BlockSpec((1, 1, RP, cols), lambda l, s: (l, jnp.clip(s - 5, 0, 4), 0, 0))
    wide = pl.BlockSpec((1, n, RP, D), lambda l, s: (l, 0, 0, jnp.clip(s - 10, 0, 3)))
    anyw = pl.BlockSpec(memory_space=pl.ANY)
    rows = LAYERS * NC * D
    return pl.pallas_call(
        fwd_kernel, grid=(LAYERS, 14),
        in_specs=[pl.BlockSpec(images.shape, lambda l, s: (0, 0, 0)), anyw, anyw, pl.BlockSpec(vshard.shape, lambda l, s: (0, 0, 0))],
        out_specs=[one(D), one(3 * D), one(D), one(D), two(D), two(D), wide, wide, pl.BlockSpec(images.shape, lambda l, s: (0, 0, 0)), anyw, anyw],
        out_shape=[S((LAYERS, n, RP, D), F32), S((LAYERS, n, RP, 3 * D), BF), S((LAYERS, n, RP, D), BF), S((LAYERS, n, RP, D), BF),
                   S((LAYERS, n, RP, D), F32), S((LAYERS, n, RP, D), BF), S((LAYERS, n, RP, 4 * D), BF), S((LAYERS, n, RP, 4 * D), BF),
                   S(images.shape, BF), S((rows, D), BF), S((LAYERS, 16, D), F32)],
        scratch_shapes=[pltpu.VMEM((rows, D), BF), pltpu.VMEM((n, RP, D), F32), pltpu.VMEM((n, RP, D), BF), pltpu.VMEM((n, RP, D), BF),
                        pltpu.VMEM((8, LAYERS, 16, 128), F32), pltpu.VMEM((LAYERS, 16, D), F32), pltpu.VMEM((4, CH, D), F32),
                        pltpu.SemaphoreType.DMA((4,)), pltpu.SemaphoreType.DMA((12, 11)), pltpu.SemaphoreType.DMA((12, 11)),
                        pltpu.SemaphoreType.DMA((7,)), pltpu.SemaphoreType.DMA((7,)), pltpu.SemaphoreType.DMA, pltpu.SemaphoreType.DMA],
        compiler_params=pltpu.CompilerParams(collective_id=0, has_side_effects=True, vmem_limit_bytes=62 * 2**20),
    )(images, weight_in, weight_out, vshard)


def bwd_kernel(cot_ref, w_ref, vec_ref, hs_ref, h1_ref, g_ref, e_ref, qkv_ref, a2_ref, o_ref, a1_ref,
               di_ref, gin_ref, gout_ref, gv_ref,
               wk, d, acc, db, du, ab, gb, dv, rc, s2, ra, rb, s3a, s3b, r3a, r3b, s4, rz, s5, ry, s6, rw, fin,
               vs, vr, vz, wsem, asem, ssem, rsem, osem, vssem, vrsem):
    lr, s = pl.program_id(0), pl.program_id(1)
    l = LAYERS - 1 - lr
    f, core, x, y = plane()
    z = lax.axis_index("rep")
    fc, fx, fy = f + 1 - 2 * core, f + 2 - 4 * x, f + 4 - 8 * y
    z1, z3 = z + 1 - 2 * (z % 2), 3 - z
    half = CH // 2
    mine = pl.multiple_of(((z + 1) // 2 % 2) * half, 16)
    theirs = pl.multiple_of(half - (z + 1) // 2 % 2 * half, 16)
    n = d.shape[0]
    rows = n * RP

    def load(layer, block, n, at):
        return pltpu.make_async_copy(w_ref.at[pl.ds(pl.multiple_of((layer * NC + block) * D, 16), n * D)], wk.at[pl.ds(at * D, n * D)], wsem.at[0 if at else 1])

    def fetch(src, slot, layer):
        return pltpu.make_async_copy(src.at[layer], ab.at[slot], asem.at[slot])

    def remote(kind, p, src, dst, **to):
        return pltpu.make_async_remote_copy(src_ref=src, dst_ref=dst, send_sem=ssem.at[p, kind], recv_sem=rsem.at[p, kind],
                                            device_id=to, device_id_type=MESH)

    def live(v):
        return (v >= 0) & (v < 24)

    def kind(n, v):
        p, q = v % 2, v % 4
        if n == 0:
            lc = v % NC
            return remote(0, q, gb.at[lc - 9 * (lc // 9), :, 1 - core], rc.at[p], fsdp=fc)
        if n == 1:
            return remote(1, q, s2.at[p, :, 1 - x, pl.ds(0, half)], ra.at[q], fsdp=fx)
        if n == 2:
            return remote(2, q, s2.at[p, 1 - y, :, pl.ds(half, half)], rb.at[q], fsdp=fy)
        if n == 3:
            return remote(3, q, s3a.at[p, 1 - y], r3a.at[q], fsdp=fy)
        if n == 4:
            return remote(4, q, s3b.at[p, 1 - x], r3b.at[q], fsdp=fx)
        if n == 5:
            return remote(5, q, s4.at[p, pl.ds(theirs, half)], rz.at[q], rep=z1)
        if n == 6:
            return remote(6, q, s5.at[p], ry.at[q], rep=z3)
        return remote(7, q, s6.at[p], rw.at[q], rep=z1)

    def put(v, act):
        lc, layer = v % NC, LAYERS - 1 - v // NC
        p = v % 2
        out = (lc >= 4) & (lc < 9)

        @pl.when(out)
        def _():
            act(pltpu.make_async_copy(fin.at[p], gout_ref.at[layer, pl.ds(pl.multiple_of((lc - 4) * CH, 16), CH)], osem.at[p]))

        @pl.when(jnp.logical_not(out))
        def _():
            j = lc + 3 - 9 * (lc // 9)
            j = j - 3 * (lc // 9)
            act(pltpu.make_async_copy(fin.at[p], gin_ref.at[layer, :, pl.ds(pl.multiple_of(j * D, 128), D)], osem.at[p]))

    def add(a, b):
        return a + b

    def tick(t):
        @pl.when(live(t - 12))
        def _():
            put(t - 12, lambda a: a.wait())

        @pl.when(live(t - 11))
        def _():
            v = t - 11
            p = v % 2
            kind(7, v).wait()
            fin[p, pl.ds(mine, half)] = s6[p]
            fin[p, pl.ds(theirs, half)] = rw[v % 4]
            put(v, lambda a: a.start())

        @pl.when(live(t - 9))
        def _():
            v = t - 9
            p = v % 2
            kind(6, v).wait()
            s6[p] = add(s5[p], ry[v % 4]).astype(BF)
            kind(7, v).start()

        @pl.when(live(t - 7))
        def _():
            v = t - 7
            p = v % 2
            kind(5, v).wait()
            s5[p] = add(s4[p, pl.ds(mine, half)], rz[v % 4]).astype(BF)
            kind(6, v).start()

        @pl.when(live(t - 5))
        def _():
            v = t - 5
            p, q = v % 2, v % 4
            kind(3, v).wait()
            kind(4, v).wait()
            s4[p, 0:half] = add(s3a[p, y], r3a[q]).astype(BF)
            s4[p, half:CH] = add(s3b[p, x], r3b[q]).astype(BF)
            kind(5, v).start()

        @pl.when(live(t - 3))
        def _():
            v = t - 3
            p, q = v % 2, v % 4
            kind(1, v).wait()
            kind(2, v).wait()
            for i in range(2):
                s3a[p, i] = add(s2[p, i, x, 0:half], ra[q, i]).astype(BF)
                s3b[p, i] = add(s2[p, y, i, half:CH], rb[q, i]).astype(BF)
            kind(3, v).start()
            kind(4, v).start()

        @pl.when(live(t - 1))
        def _():
            v = t - 1
            p = v % 2
            kind(0, v).wait()
            lc = v % NC
            for i in range(4):
                s2[p, i // 2, i % 2] = add(gb[lc - 9 * (lc // 9), i, core], rc[p, i]).astype(BF)
            kind(1, v).start()
            kind(2, v).start()

        @pl.when(live(t))
        def _():
            kind(0, t).start()

    @pl.when((lr == 0) & (s == 0))
    def _():
        load(l, 3, 9, 0).start()
        bar = pltpu.get_barrier_semaphore()
        for k in range(1, 8):
            pl.semaphore_signal(bar, inc=1, device_id={"fsdp": (f + k) % 8}, device_id_type=MESH)
        for k in range(1, 4):
            pl.semaphore_signal(bar, inc=1, device_id={"rep": (z + k) % 4}, device_id_type=MESH)
        dv[...] = jnp.zeros_like(dv)
        fetch(a2_ref, 0, l).start()
        for i in range(n):
            d[i] = jnp.zeros((RP, D), F32)
            d[i, 0:SEQ, :] = cot_ref[i].astype(F32)

    @pl.when(s == 0)
    def _():
        fetch(o_ref, 1, l).start()

    @pl.when(s == 4)
    def _():
        fetch(a2_ref, 0, l).wait()
        ab[0, 0, RP - 16:RP] = fold_rows(ab[0, 0, RP - 16:RP], ab[0, n - 1, RP - 16:RP])

        @pl.when(lr == 0)
        def _():
            load(l, 3, 9, 0).wait()

        @pl.when(lr == 1)
        def _():
            load(l, 3, 3, 0).wait()
            load(l, 6, 6, 3).wait()

    @pl.when(s == 8)
    def _():
        fetch(a1_ref, 0, l).start()
        load(l, 0, 3, 0).start()

    @pl.when(s == 13)
    def _():
        fetch(o_ref, 1, l).wait()
        ab[1, 0, RP - 16:RP] = fold_rows(ab[1, 0, RP - 16:RP], ab[1, n - 1, RP - 16:RP])

        @pl.when(lr == 0)
        def _():
            load(l - 1, 6, 6, 3).start()

    @pl.when(s == 19)
    def _():
        fetch(a1_ref, 0, l).wait()
        ab[0, 0, RP - 16:RP] = fold_rows(ab[0, 0, RP - 16:RP], ab[0, n - 1, RP - 16:RP])
        load(l, 0, 3, 0).wait()

    @pl.when((s == 20) & (lr == 0))
    def _():
        fetch(a2_ref, 0, l - 1).start()
        load(l - 1, 3, 3, 0).start()

    @pl.when((lr == 0) & (s == 5))
    def _():
        pl.semaphore_wait(pltpu.get_barrier_semaphore(), 10)

    one = (s >= 5) & (s <= 8)
    two = (lr == 1) & (s >= 14) & (s <= 18)
    three = (lr == 0) & ((s == 14) | (s == 16) | (s == 18) | (s == 19))
    four = ((lr == 0) & (s == 21)) | ((lr == 1) & ((s == 0) | (s == 2)))
    five = (lr == 1) & (s >= 20)
    t = jnp.where(one, 12 * lr + s - 5, jnp.where(two, s + 2, jnp.where(three, 4 + (s - 14) // 2 + s // 19, jnp.where(four, 9 + lr * (1 + s // 2), s + 4))))

    @pl.when(one | two | three | four | five)
    def _():
        tick(t)

    @pl.when(s == 0)
    def _():
        for i in range(n):
            up = d[i]
            db[i] = up.astype(BF)
            acc[i] = jnp.zeros((RP, D), F32)
            dv[l, 7:8] += rsum(up)
        db[0, RP - 16:RP] = fold_rows(db[0, RP - 16:RP], db[n - 1, RP - 16:RP])

    @pl.when(s == 4)
    def _():
        db[0, RP - 16:RP] = clear_rows(db[0, RP - 16:RP])

    @pl.when((s >= 4) & (s < 8))
    def _():
        j = s - 4
        whole = db[...].reshape(rows, D)
        cols = pl.multiple_of(j * D, 128)
        for q in range(3):
            t1 = dot_t(whole, wk[pl.ds(pl.multiple_of((5 + j) * D + 256 * q, 16), 256), :])
            t1 = t1 * g_ref[0, :, :, 256 * q:256 * q + 256].reshape(rows, 256).astype(F32)
            dv[l, pl.ds(8 + j, 1), 256 * q:256 * q + 256] += rsum(t1)
            du[:, :, pl.ds(pl.multiple_of(cols + 256 * q, 128), 256)] = t1.astype(BF).reshape(n, RP, 256)
        acc[...] += dot_t(du[:, :, pl.ds(cols, D)].reshape(rows, D), wk[pl.ds(pl.multiple_of(j * D, 16), D), :]).reshape(n, RP, D)

    @pl.when((s >= 8) & (s < 13))
    def _():
        i = s - 8
        dx, dg, dc = norm_back(h1_ref[0, 0], vec_ref[l, 5:6], acc[i])
        dv[l, 5:6] += dg
        dv[l, 6:7] += dc
        dh1 = d[i] + dx
        d[i] = dh1
        dv[l, 4:5] += rsum(dh1)
        du[i, :, 0:D] = dh1.astype(BF)
        du[i, :, 3 * D:4 * D] = dot_t(du[i, :, 0:D], wk[4 * D:5 * D, :]).astype(BF)

    def grad(lhs, rhs, store):
        rhs = rhs[:rows - 16]
        for m in range(2):
            r = dot_0(lhs(384 * m)[:rows - 16], rhs).astype(BF).reshape(4, CH, D)
            store(4 * m, r)

    def inner(slot, j):
        def store(m, r):
            gb[slot, m // 2, 0] = r[0]
            gb[slot, m // 2, 1] = r[1]
            gb[slot, m // 2 + 1, 0] = r[2]
            gb[slot, m // 2 + 1, 1] = r[3]
        grad(lambda m: ab[0, :, :, m:m + 384].reshape(rows, 384), du[:, :, pl.ds(pl.multiple_of(D * j, 128), D)].reshape(rows, D), store)

    def outer(step, lhs, rhs):
        def store(m, r):
            for q in range(4):
                b = 8 * step + m + q
                gb[4 + b % 5, b // 10, (b // 5) % 2] = r[q]
        grad(lhs, rhs.reshape(rows, D), store)

    @pl.when((s >= 4) & (s < 8))
    def _():
        at = pl.ds(pl.multiple_of((s - 4) * D, 128), D)
        du[0, RP - 16:RP, at] = fold_rows(du[0, RP - 16:RP, at], du[n - 1, RP - 16:RP, at])
        inner(s - 4, s - 4)

    @pl.when(s == 13)
    def _():
        du[0, RP - 16:RP, 0:D] = fold_rows(du[0, RP - 16:RP, 0:D], du[n - 1, RP - 16:RP, 0:D])
        outer(0, lambda m: ab[1, :, :, m:m + 384].reshape(rows, 384), du[:, :, 0:D])

    @pl.when(s < 4)
    def _():
        outer(s + 1, lambda m: e_ref[0, :, :, m:m + 384].reshape(rows, 384), db[...])

    @pl.when((s >= 14) & (s < 19))
    def _():
        i = s - 14

        def products(p):
            b = 128 * p
            return attn_bwd_products(qkv_ref[0, 0, :, b:b + 128], qkv_ref[0, 0, :, D + b:D + b + 128], qkv_ref[0, 0, :, 2 * D + b:2 * D + b + 128],
                                     du[i, :, 3 * D + b:3 * D + b + 128])
        later = products(0)
        for p in range(6):
            b = 128 * p
            now, later = later, (products(p + 1) if p < 5 else None)
            dq, dk, dvv = attn_bwd_rest(*now)
            dv[l, 2:3, b:b + 128] += rsum(dq)
            dv[l, 3:4, b:b + 128] += rsum(dvv)
            du[i, :, b:b + 128] = dq.astype(BF)
            du[i, :, D + b:D + b + 128] = dk.astype(BF)
            du[i, :, 2 * D + b:2 * D + b + 128] = dvv.astype(BF)

    @pl.when(s == 19)
    def _():
        du[0, RP - 16:RP, 0:3 * D] = fold_rows(du[0, RP - 16:RP, 0:3 * D], du[n - 1, RP - 16:RP, 0:3 * D])

        @pl.loop(0, 3)
        def _(j):
            inner(j, j)

            @pl.when((lr == 1) | (j == 1))
            def _():
                tick(lr * (21 + j) + (1 - lr) * 8)
        du[0, RP - 16:RP, 0:3 * D] = clear_rows(du[0, RP - 16:RP, 0:3 * D])
        acc[...] = dot_t(du[:, :, 0:D].reshape(rows, D), wk[0:D, :]).reshape(n, RP, D)
        acc[...] += dot_t(du[:, :, D:2 * D].reshape(rows, D), wk[D:2 * D, :]).reshape(n, RP, D)
        acc[...] += dot_t(du[:, :, 2 * D:3 * D].reshape(rows, D), wk[2 * D:3 * D, :]).reshape(n, RP, D)

    @pl.when(s >= 20)
    def _():
        i = s - 20
        dx, dg, dc = norm_back(hs_ref[0, 0], vec_ref[l, 0:1], acc[i])
        dv[l, 0:1] += dg
        dv[l, 1:2] += dc
        dh = d[i] + dx
        d[i] = dh
        di_ref[0] = dh[0:SEQ]

    @pl.when((lr == 1) & (s == 24))
    def _():
        for layer in range(LAYERS):
            for c in range(72):
                vs[c // 9, layer, c % 9:c % 9 + 1, :] = dv[layer, c // 6:c // 6 + 1, 128 * (c % 6):128 * (c % 6) + 128]

        def vcopy(k):
            to = (f + k) % 8
            return pltpu.make_async_remote_copy(src_ref=vs.at[to], dst_ref=vr.at[k - 1], send_sem=vssem.at[k - 1], recv_sem=vrsem.at[k - 1],
                                                device_id={"fsdp": to}, device_id_type=MESH)

        def zcopy(k):
            return pltpu.make_async_remote_copy(src_ref=vz.at[z], dst_ref=vz.at[z], send_sem=vssem.at[6 + k], recv_sem=vrsem.at[6 + k],
                                                device_id={"rep": (z + k) % 4}, device_id_type=MESH)
        for k in range(1, 8):
            vcopy(k).start()

        @pl.loop(29, 36)
        def _(t):
            @pl.when(t == 30)
            def _():
                for k in range(1, 8):
                    vcopy(k).wait()
                total = vs[f]
                for k in range(7):
                    total = total + vr[k]
                vz[z] = total
                for k in range(1, 4):
                    zcopy(k).start()
            tick(t)

        for k in range(1, 4):
            zcopy(k).wait()
        gv_ref[...] = (vz[0] + vz[1]) + (vz[2] + vz[3])


def bwd(cotangent, w, vec, hs, h1, g, e, qkv, a2, o, a1, shard_in, shard_out):
    n = cotangent.shape[0]
    S = jax.ShapeDtypeStruct
    anyw = pl.BlockSpec(memory_space=pl.ANY)
    row = lambda cols, at: pl.BlockSpec((1, 1, RP, cols), lambda lr, s: (LAYERS - 1 - lr, jnp.clip(s - at, 0, 4), 0, 0))
    cols = lambda at: pl.BlockSpec((1, n, RP, D), lambda lr, s: (LAYERS - 1 - lr, 0, 0, jnp.clip(s - at, 0, 3)))
    tok = lambda index: pl.BlockSpec((1, SEQ, D), index)
    VB = lambda *shape: pltpu.VMEM(shape, BF)
    half = CH // 2
    return pl.pallas_call(
        bwd_kernel, grid=(LAYERS, 25),
        in_specs=[pl.BlockSpec(cotangent.shape, lambda lr, s: (0, 0, 0), pipeline_mode=pl.Buffered(1)), anyw, pl.BlockSpec(vec.shape, lambda lr, s: (0, 0, 0)),
                  row(D, 20), row(D, 8), cols(4), cols(0), row(3 * D, 14), anyw, anyw, anyw],
        out_specs=[tok(lambda lr, s: (lr * jnp.clip(s - 20, 0, 4), 0, 0)), anyw, anyw, pl.BlockSpec((LAYERS, 16, 128), lambda lr, s: (0, 0, 0))],
        out_shape=[S(cotangent.shape, F32), S(shard_in, BF), S(shard_out, BF), S((LAYERS, 16, 128), F32)],
        scratch_shapes=[VB(9 * D, D), pltpu.VMEM((n, RP, D), F32), pltpu.VMEM((n, RP, D), F32), VB(n, RP, D), VB(n, RP, 4 * D), VB(2, n, RP, D),
                        VB(9, 4, 2, CH, D), pltpu.VMEM((LAYERS, 16, D), F32),
                        VB(2, 4, CH, D), VB(2, 2, 2, CH, D), VB(4, 2, half, D), VB(4, 2, half, D), VB(2, 2, half, D), VB(2, 2, half, D),
                        VB(4, half, D), VB(4, half, D), VB(2, CH, D), VB(4, half, D), VB(2, half, D), VB(4, half, D), VB(2, half, D), VB(4, half, D),
                        VB(2, CH, D),
                        pltpu.VMEM((8, LAYERS, 16, 128), F32), pltpu.VMEM((7, LAYERS, 16, 128), F32), pltpu.VMEM((4, LAYERS, 16, 128), F32),
                        pltpu.SemaphoreType.DMA((2,)), pltpu.SemaphoreType.DMA((2,)), pltpu.SemaphoreType.DMA((4, 8)), pltpu.SemaphoreType.DMA((4, 8)),
                        pltpu.SemaphoreType.DMA((2,)), pltpu.SemaphoreType.DMA((10,)), pltpu.SemaphoreType.DMA((10,))],
        compiler_params=pltpu.CompilerParams(collective_id=1, has_side_effects=True, vmem_limit_bytes=63 * 2**20),
    )(cotangent, w, vec, hs, h1, g, e, qkv, a2, o, a1)


STEP = 3
beta_one = 0.9
beta_two = 0.999
matrix_rate = 0.03
vector_rate = 0.2
matrix_decay = 0.05
adam_eps = 1e-8


def adam_update(master, gradient, moment_one, moment_two, rate, decay_rate):
    moment_one = beta_one * moment_one + (1.0 - beta_one) * gradient
    moment_two = beta_two * moment_two + (1.0 - beta_two) * gradient * gradient
    corr_one = 1.0 - beta_one**STEP
    corr_two = 1.0 - beta_two**STEP
    adam_move = moment_one / corr_one / (jnp.sqrt(moment_two / corr_two) + adam_eps)
    return (master - rate * (adam_move + decay_rate * master), moment_one, moment_two)


def adam_kernel(g_ref, w_ref, m_ref, v_ref, go_ref, wo_ref, mo_ref, vo_ref, enc_ref, dim_ref,
                g_out, w_out, m_out, v_out, go_out, wo_out, mo_out, vo_out, enc_out, dim_out, steps):
    i = pl.program_id(0)

    def update(g, w, m, v, outs):
        grad = g[...].astype(F32)
        new, moment, square = adam_update(w[...], grad, m[...], v[...], matrix_rate, matrix_decay)
        outs[0][...], outs[1][...], outs[2][...], outs[3][...] = grad, new, moment, square

    @pl.when(i < steps)
    def _():
        update(g_ref, w_ref, m_ref, v_ref, (g_out, w_out, m_out, v_out))

    @pl.when(i >= steps)
    def _():
        update(go_ref, wo_ref, mo_ref, vo_ref, (go_out, wo_out, mo_out, vo_out))

    @pl.when(i < enc_steps)
    def _():
        enc_out[...] = enc_ref[...]
        dim_out[...] = dim_ref[...]


enc_steps = 5


def adam_all(ins, outs, encoded, dimg):
    a, b = ins[0].shape, outs[0].shape
    steps = 2 * LAYERS
    first = pl.BlockSpec((1, a[1] // 2, a[2]), lambda i: (jnp.minimum(i, steps - 1) // 2, jnp.minimum(i, steps - 1) % 2, 0))
    second = pl.BlockSpec((1, b[1] // 2, b[2]), lambda i: (jnp.maximum(i - steps, 0) // 2, jnp.maximum(i - steps, 0) % 2, 0))
    tok = pl.BlockSpec((1,) + encoded.shape[1:], lambda i: (jnp.minimum(i, enc_steps - 1), 0, 0))
    S = jax.ShapeDtypeStruct
    return pl.pallas_call(
        functools.partial(adam_kernel, steps=steps), grid=(2 * steps,),
        in_specs=[first] * 4 + [second] * 4 + [tok] * 2, out_specs=[first] * 4 + [second] * 4 + [tok] * 2,
        out_shape=[S(a, F32)] * 4 + [S(b, F32)] * 4 + [S(encoded.shape, BF), S(dimg.shape, F32)],
        compiler_params=PAR,
    )(*ins, *outs, encoded, dimg)


def swap(x, axis, size, mask):
    return lax.ppermute(x, axis, [(i, i ^ mask) for i in range(size)])


def halve(x, order, size):
    bits = size.bit_length() - 1
    me = lax.axis_index("fsdp")
    x = x.reshape((2,) * bits + x.shape[1:])
    left = list(range(bits))[::-1]
    for bit in order:
        at = left.index(bit)
        mine = (me >> bit) & 1
        keep = lax.dynamic_index_in_dim(x, mine, at, keepdims=False)
        send = lax.dynamic_index_in_dim(x, 1 - mine, at, keepdims=False)
        got = swap(send, "fsdp", size, 1 << bit)
        x = (keep.astype(F32) + got.astype(F32)).astype(BF)
        left.remove(bit)
    return x


def reduce_all(x, nf, nr):
    bits = nf.bit_length() - 1
    rows, cols = x.shape
    x = x.reshape(nf, rows // nf, cols)
    half = cols // 2 // 128 * 128
    up = [0] + list(range(1, bits))
    down = [0] + list(range(1, bits))[::-1]
    x = jnp.concatenate([halve(x[..., :half], up, nf), halve(x[..., half:], down, nf)], axis=-1)
    mask = 1
    while mask < nr:
        got = swap(x, "rep", nr, 2 * mask - 1)
        y = x.astype(F32) + got.astype(F32)
        x = y.astype(BF)
        mask *= 2
    return y


def fused_step(images, cotangent, weight_in, weight_out, vector_params):
    vs = jnp.pad(vector_params.astype(BF).astype(F32).reshape(LAYERS, 9, 128), ((0, 0), (0, 7), (0, 0)))
    hs, qkv, a1, o, h1, a2, e, g, encoded, w, vec = fwd(images, weight_in, weight_out, vs)
    dimg, gi, go, gv = bwd(cotangent, w, vec, hs, h1, g, e, qkv, a2, o, a1, weight_in.shape, weight_out.shape)
    return encoded, dimg, gi, go, gv[:, :9].reshape(vector_params.shape)


def plain_step(nf, nr, images, cotangent, weight_in, weight_out, vector_params):
    pad = lambda a: jnp.pad(a, ((0, 0), (0, RP - SEQ), (0, 0)))
    vec_all = lax.all_gather(vector_params.astype(BF), "fsdp", axis=1, tiled=True).astype(F32)
    h = pad(images)
    ct = pad(cotangent)
    saved = []
    for l in range(LAYERS):
        win = lax.all_gather(weight_in[l].astype(BF), "fsdp", axis=0, tiled=True)
        wout = lax.all_gather(weight_out[l].astype(BF), "fsdp", axis=0, tiled=True)
        vec = jnp.pad(vec_all[l].reshape(12, D), ((0, 4), (0, 0)))
        wqkv, w1, wo, w2 = win[:, : 3 * D], win[:, 3 * D :], wout[:D], wout[D:]
        qkv, o, a1 = ka(h, wqkv, vec)
        h1, a2, e, g, h2 = kb(h, o, wo, w1, w2, vec)
        saved.append((h, wqkv, w1, wo, w2, vec, qkv, o, a1, h1, a2, e, g))
        h = h2
    encoded = h[:, :SEQ].astype(BF)
    d = ct
    gin, gout, gvec = [None] * LAYERS, [None] * LAYERS, [None] * LAYERS
    for l in reversed(range(LAYERS)):
        h, wqkv, w1, wo, w2, vec, qkv, o, a1, h1, a2, e, g = saved[l]
        db, du, dh1, dh1b, do, dv1 = kc(d, h1, g, wo, w1, w2, vec)
        g1 = reduce_all(dw(a2, du), nf, nr)
        go = reduce_all(jnp.concatenate([dw(o, dh1b), dw(e, db)], axis=0), nf, nr)
        dz, dv2 = kd(qkv, do)
        gq = reduce_all(dw(a1, dz), nf, nr)
        d, dv3 = kf(dz, h, dh1, wqkv, vec, RP if l else SEQ)
        gin[l] = jnp.concatenate([gq, g1], axis=1)
        gout[l] = go
        gvec[l] = (dv1 + dv2 + dv3)[:12].reshape(-1)
    gv = lax.psum(jnp.stack(gvec), ("fsdp", "rep"))
    wide = gv.shape[1] // nf
    gv = lax.dynamic_slice_in_dim(gv, lax.axis_index("fsdp") * wide, wide, 1)
    return encoded, d, jnp.stack(gin), jnp.stack(gout), gv


def make_shards(nf, nr):
    def shards(images, cotangent, weight_in, weight_out, vector_params, first_in, first_out, first_vec, second_in, second_out, second_vec):
        if nf == 8 and nr == 4:
            encoded, d, gi, go, gv = fused_step(images, cotangent, weight_in, weight_out, vector_params)
            gi, new_in, moment_in, square_in, go, new_out, moment_out, square_out, encoded, d = adam_all(
                (gi, weight_in, first_in, second_in), (go, weight_out, first_out, second_out), encoded, d)
        else:
            encoded, d, gi, go, gv = plain_step(nf, nr, images, cotangent, weight_in, weight_out, vector_params)
            new_in, moment_in, square_in = adam_update(weight_in, gi, first_in, second_in, matrix_rate, matrix_decay)
            new_out, moment_out, square_out = adam_update(weight_out, go, first_out, second_out, matrix_rate, matrix_decay)
        new_vec, moment_vec, square_vec = adam_update(vector_params, gv, first_vec, second_vec, vector_rate, 0.0)
        return (encoded, d, gi, go, gv, new_in, new_out, new_vec, moment_in, moment_out, moment_vec, square_in, square_out, square_vec)

    return shards


def solution(mesh):
    tokens = P(("fsdp", "rep"), None, None)
    matrix = P(None, "fsdp", None)
    vector = P(None, "fsdp")
    in_specs = (tokens, tokens) + (matrix, matrix, vector) * 3
    out_specs = (tokens, tokens) + (matrix, matrix, vector) * 4
    return jax.shard_map(make_shards(mesh.shape["fsdp"], mesh.shape["rep"]), mesh=mesh, in_specs=in_specs, out_specs=out_specs, check_vma=False)
```
